32 devices in a mesh: rep: 4 (over x, core), shard: 8 (over z, y).
Axes of the slice: x: 2, y: 2, z: 4, core: 2. Of those that a mesh axis runs over, the one named last changes fastest.
Arguments:
- token_ids: int32 [2, 8, 512], P(None, 'shard', 'rep'), may hold values from 0 to 50303
- pic_start: int32 [2, 8], P(None, 'shard'), may hold values from 0 to 256
- comp_pos: int32 [2, 8, 128], P(None, 'shard', 'rep'), may hold values from 0 to 128, as said below
- comp_tgt: int32 [2, 8, 128], P(None, 'shard', 'rep'), may hold values from 0 to 50303
- proj_in: float32 [1024, 7168], P('shard'), may hold values from -0.1875 to 0.1875
- proj_back: float32 [5120, 1024], P('shard')
- small_params: float32 [14336], P('shard')
- head_table: float32 [1024, 50304], P(None, 'shard')
- embed_table: float32 [1024, 50304], P('shard'), may hold values from -6 to 6
- first_in: float32 [1024, 7168], P('shard'), may hold values from -0.00015258789 to 0.00015258789
- second_in: float32 [1024, 7168], P('shard'), may hold values from 5.1894206e-10 to 1.729807e-09
- first_back: float32 [5120, 1024], P('shard'), may hold values from -0.00015258789 to 0.00015258789
- second_back: float32 [5120, 1024], P('shard'), may hold values from 5.1894206e-10 to 1.729807e-09
- first_small: float32 [14336], P('shard'), may hold values from -0.0007324219 to 0.0007324219
- second_small: float32 [14336], P('shard'), may hold values from 1.2973552e-08 to 4.3245173e-08
- first_head: float32 [1024, 50304], P(None, 'shard'), may hold values from -0.00015258789 to 0.00015258789
- second_head: float32 [1024, 50304], P(None, 'shard'), may hold values from 5.1894206e-10 to 1.729807e-09
- first_embed: float32 [1024, 50304], P('shard'), may hold values from -0.00015258789 to 0.00015258789
- second_embed: float32 [1024, 50304], P('shard'), may hold values from 5.1894206e-10 to 1.729807e-09
Outputs:
- loss_parts: float32 [2], replicated
- grad_norm: float32 [1], replicated
- next_in: float32 [1024, 7168], P('shard')
- moment_in: float32 [1024, 7168], P('shard')
- square_in: float32 [1024, 7168], P('shard')
- next_back: float32 [5120, 1024], P('shard')
- moment_back: float32 [5120, 1024], P('shard')
- square_back: float32 [5120, 1024], P('shard')
- next_small: float32 [14336], P('shard')
- moment_small: float32 [14336], P('shard')
- square_small: float32 [14336], P('shard')
- next_head: float32 [1024, 50304], P(None, 'shard')
- moment_head: float32 [1024, 50304], P(None, 'shard')
- square_head: float32 [1024, 50304], P(None, 'shard')
- next_embed: float32 [1024, 50304], P('shard')
- moment_embed: float32 [1024, 50304], P('shard')
- square_embed: float32 [1024, 50304], P('shard')
The draws below stay inside these ranges and needn't reach their ends.
Inputs may be any that keep to these rules, and one draw needn't show every extreme that they name: `comp_pos`: in each block of 32 slots the used slots come first and name distinct positions below 128; the other slots hold 128. Every block uses at least one slot, and the last block of the last sequence of every micro-batch uses all 32.
All inputs are finite; a program needn't handle non-finite values.
Results may differ from the reference program's by a relative error of at most 0.003.
The reference program's roundings to bfloat16 on the way count: a program that leaves them out, or rounds other values in their place, can miss the bound.
Values may be sent and summed in bfloat16 or wider, within the bound.
A program may use at most 432 MiB of HBM per device.

```python
import math
import jax
import jax.numpy as jnp
import numpy as np
from jax import lax

D = 1024
H = 16
HD = 64
ROT = 16
FF = 4096
V = 50304
SEQ_DEV = 128
PIC = 256
MB = 2
STEP = 10
SEQS = 8
REPS = 4
SEQ = 512
COMP = 32
NPARAM = 115619840


def draw_proj_back(key, part):
    key = jax.random.fold_in(key, 3)
    attend_spread = (SEQ / 4.0) ** 0.5 / D ** 0.5
    hidden_spread = (2.0 / FF) ** 0.5
    spreads = jnp.concatenate([jnp.full((D, 1), attend_spread, jnp.float32), jnp.full((FF, 1), hidden_spread, jnp.float32)], axis=0)
    values = jax.random.normal(key, (D + FF, D), jnp.float32)
    return (values * spreads).astype(jnp.float32)


def draw_small_params(key, part):
    key = jax.random.fold_in(key, 7)
    key_list = jax.random.split(key, 2)
    ramp_up = jnp.arange(D).astype(jnp.float32) / D
    rising = 0.5 + ramp_up
    shifts = 0.2 * jax.random.normal(key_list[1], (10 * D + FF,), jnp.float32)
    jitter = jax.random.uniform(key_list[0], (3, D), jnp.float32, 0.8, 1.2)
    pieces = [rising * jitter[0], shifts[:D], rising * jitter[1], shifts[D:2 * D], jitter[2], shifts[2 * D:3 * D], 0.5 * shifts[3 * D:7 * D + FF]]
    return jnp.concatenate(pieces).astype(jnp.float32)


def draw_head_table(key, part):
    key = jax.random.fold_in(key, 9)
    ramp_up = jnp.arange(V).astype(jnp.float32) / V
    values = jax.random.normal(key, (D, V), jnp.float32)
    rising = 1.0 + 2.0 * ramp_up
    return (values * rising[None, :] / D ** 0.5).astype(jnp.float32)


def permute_one(row_key):
    return jax.random.permutation(row_key, SEQ_DEV)


def draw_comp_pos(key, part):
    key = jax.random.fold_in(key, 5)
    key_perm, key_jit = jax.random.split(key)
    total_rows = MB * SEQS * REPS
    orders = jax.vmap(permute_one)(jax.random.split(key_perm, total_rows))[:, :COMP]
    row_ids = jnp.arange(total_rows)
    shard_at = row_ids // REPS % SEQS
    rep_at = row_ids % REPS
    shard_span = max(SEQS - 1, 1)
    rep_span = max(REPS - 1, 1)
    position_sum = shard_at * rep_span + rep_at * shard_span
    base_count = COMP // 3 + 2 * COMP * position_sum // (3 * shard_span * rep_span)
    jitter = jax.random.randint(key_jit, (total_rows,), -(COMP // 8), COMP // 8 + 1)
    counts = jnp.clip(base_count + jitter, 1, COMP)
    counts = jnp.where(position_sum == 2 * shard_span * rep_span, COMP, counts)
    slot_ids = jnp.arange(COMP)
    chosen = jnp.where(slot_ids[None, :] < counts[:, None], orders, SEQ_DEV)
    return chosen.reshape(MB, SEQS, REPS * COMP).astype(jnp.int32)


def plant(values, rng, low, high):
    longest = values.shape.index(max(values.shape))
    spots = []
    for shift in (0, 1):
        where = [jax.random.randint(jax.random.fold_in(rng, axis), (), 0, length) for axis, length in enumerate(values.shape)]
        where[longest] = (where[longest] + shift) % values.shape[longest]
        spots.append(tuple(where))
    return values.at[spots[0]].set(low).at[spots[1]].set(high)


def levels(key, shape, shards, smallest, largest):
    level, own = 1.0, jax.random.fold_in(key, 6)
    for dim, blocks in shards:
        heights = jnp.exp(jax.random.uniform(jax.random.fold_in(own, dim), (blocks,), jnp.float32, smallest / len(shards), largest / len(shards)))
        level = level * jnp.repeat(heights, shape[dim] // blocks).reshape([-1 if axis == dim else 1 for axis in range(len(shape))])
    return level


def cumulative_ranks(amount, slope):
    weights = [(1 << 20) // math.isqrt(rank ** slope) + 1 for rank in range(1, amount + 1)]
    deviation = 1 + sum(weights) // (1 << 30)
    return np.cumsum(np.array([max(1, weight // deviation) for weight in weights]))


def ranked(rng, dims, number_of, skew):
    grid = cumulative_ranks(number_of, skew)
    lot = jax.random.randint(jax.random.fold_in(rng, 1), dims, 0, int(grid[number_of - 1]))
    standing = jnp.searchsorted(jnp.asarray(grid, jnp.int32), lot, side="right")
    return jax.random.permutation(jax.random.fold_in(rng, 2), number_of)[standing].astype(jnp.int32)


def scatter_about(stream_key, shape, scale, limit, cuts=(), dtype=jnp.bfloat16):
    entries = jax.random.normal(stream_key, shape, jnp.float32) * scale
    if len(cuts) > 0:
        entries = levels(stream_key, shape, cuts, -0.22, 0.18) * entries
    return jnp.clip(entries, min=-limit, max=limit).astype(dtype)


def setup_inputs(seed: int = 0) -> dict:
    arg_keys = jax.random.split(jax.random.key(seed), 20)
    token_ids = plant(ranked(arg_keys[0], (MB, SEQS, SEQ), V, 2), jax.random.fold_in(arg_keys[0], 3), 0, V - 1).astype(jnp.int32)
    pic_start = plant(jax.random.randint(arg_keys[1], (MB, SEQS), 0, SEQ - PIC + 1), jax.random.fold_in(arg_keys[1], 1), 0, SEQ - PIC).astype(jnp.int32)
    comp_pos = draw_comp_pos(jax.random.fold_in(arg_keys[19], 71), 0)
    comp_tgt = plant(ranked(arg_keys[3], (MB, SEQS, REPS * COMP), V, 2), jax.random.fold_in(arg_keys[3], 3), 0, V - 1).astype(jnp.int32)
    proj_in = scatter_about(arg_keys[4], (D, 3 * D + FF), D ** -0.5, 0.1875, ((0, 8),), jnp.float32)
    proj_back = draw_proj_back(jax.random.fold_in(arg_keys[19], 71), 0)
    small_params = draw_small_params(jax.random.fold_in(arg_keys[19], 71), 0)
    head_table = draw_head_table(jax.random.fold_in(arg_keys[19], 71), 0)
    embed_table = scatter_about(arg_keys[8], (D, V), 1.0, 6.0, ((0, 8),), jnp.float32)
    first_in = scatter_about(arg_keys[9], (D, 3 * D + FF), (0.11 / NPARAM ** 0.5), 0.00015258789, ((0, 8),), jnp.float32)
    second_in = jnp.clip(jnp.exp(math.log(1.729806964334557e-09) - 1.20397287 * jax.random.uniform(arg_keys[10], (D, 3 * D + FF), jnp.float32) ** levels(arg_keys[10], (D, 3 * D + FF), ((0, 8),), -0.2, 0.2)), 5.189420559936764e-10, 1.729806964334557e-09)
    first_back = scatter_about(arg_keys[11], (D + FF, D), (0.11 / NPARAM ** 0.5), 0.00015258789, ((0, 8),), jnp.float32)
    second_back = jnp.clip(jnp.exp(math.log(1.729806964334557e-09) - 1.20397287 * jax.random.uniform(arg_keys[12], (D + FF, D), jnp.float32) ** levels(arg_keys[12], (D + FF, D), ((0, 8),), -0.2, 0.2)), 5.189420559936764e-10, 1.729806964334557e-09)
    first_small = scatter_about(arg_keys[13], (10 * D + FF,), (0.55 / NPARAM ** 0.5), 0.0007324219, ((0, 8),), jnp.float32)
    second_small = jnp.clip(jnp.exp(math.log(4.32451727760963e-08) - 1.2039728 * jax.random.uniform(arg_keys[14], (10 * D + FF,), jnp.float32) ** levels(arg_keys[14], (10 * D + FF,), ((0, 8),), -0.2, 0.2)), 1.2973552010464573e-08, 4.32451727760963e-08)
    first_head = scatter_about(arg_keys[15], (D, V), (0.11 / NPARAM ** 0.5), 0.00015258789, ((1, 8),), jnp.float32)
    second_head = jnp.clip(jnp.exp(math.log(1.729806964334557e-09) - 1.20397287 * jax.random.uniform(arg_keys[16], (D, V), jnp.float32) ** levels(arg_keys[16], (D, V), ((1, 8),), -0.2, 0.2)), 5.189420559936764e-10, 1.729806964334557e-09)
    first_embed = scatter_about(arg_keys[17], (D, V), (0.11 / NPARAM ** 0.5), 0.00015258789, ((0, 8),), jnp.float32)
    second_embed = jnp.clip(jnp.exp(math.log(1.729806964334557e-09) - 1.20397287 * jax.random.uniform(arg_keys[18], (D, V), jnp.float32) ** levels(arg_keys[18], (D, V), ((0, 8),), -0.2, 0.2)), 5.189420559936764e-10, 1.729806964334557e-09)
    return {"token_ids": token_ids, "pic_start": pic_start, "comp_pos": comp_pos, "comp_tgt": comp_tgt, "proj_in": proj_in, "proj_back": proj_back, "small_params": small_params, "head_table": head_table, "embed_table": embed_table, "first_in": first_in, "second_in": second_in, "first_back": first_back, "second_back": second_back, "first_small": first_small, "second_small": second_small, "first_head": first_head, "second_head": second_head, "first_embed": first_embed, "second_embed": second_embed}


@jax.custom_vjp
def low(v):
    return lax.optimization_barrier(v.astype(jnp.bfloat16)).astype(jnp.float32)

@jax.custom_vjp
def low_back(v):
    return v

def low_keep(v):
    return (low(v), None)

def low_pass(kept, grad):
    return (grad,)

def back_keep(v):
    return (v, None)

def back_low(kept, grad):
    return (low(grad),)
low.defvjp(low_keep, low_pass)
low_back.defvjp(back_keep, back_low)
NORM_EPS = 1e-05
CLIP_LEVEL = 1.0
BETA_FIRST = 0.9
BETA_SECOND = 0.95
ADAM_EPS = 1e-08
DECAY_RATE = 0.01
RATE_IN = 0.01
RATE_BACK = 0.05
RATE_SMALL = 0.3
RATE_HEAD = 0.01
RATE_EMBED = 0.3
HIGHEST = lax.Precision.HIGHEST

def matmul(left, right):
    return jnp.dot(left, right, precision=HIGHEST)

def norm_rows(values, gain_vec, shift_vec):
    centred = values - lax.optimization_barrier(jnp.mean(values, axis=-1, keepdims=True))
    spread = lax.optimization_barrier(jnp.mean(centred * centred, axis=-1, keepdims=True))
    return centred * lax.rsqrt(spread + NORM_EPS) * gain_vec + shift_vec

def rotate(head_rows, place_vec):
    half_rot = ROT // 2
    exponent = jnp.arange(half_rot).astype(jnp.float32) * (2.0 / ROT)
    angles = place_vec[:, None] * jnp.exp(-exponent * jnp.log(10000.0))
    cosine = jnp.cos(angles)[:, None, :]
    sine_part = jnp.sin(angles)[:, None, :]
    front_part = head_rows[..., :half_rot]
    back_part = head_rows[..., half_rot:ROT]
    return jnp.concatenate([front_part * cosine - back_part * sine_part, back_part * cosine + front_part * sine_part, head_rows[..., ROT:]], axis=-1)

def split_small(gain_parts):
    marks = [0, D, 2 * D, 3 * D, 4 * D, 5 * D, 6 * D, 9 * D, 9 * D + FF, 10 * D + FF]
    return tuple((gain_parts[marks[number]:marks[number + 1]] for number in range(9)))

def sequence_loss(param_set, seq_ids, span_start, slot_places, slot_targets):
    wide_in, wide_back, gain_parts, head_low, table_low = param_set
    gain_one, shift_one, gain_two, shift_two, gain_last, shift_last, bias_qkv, bias_hidden, bias_out = split_small(gain_parts)
    int_places = jnp.arange(SEQ).astype(jnp.int32)
    float_places = int_places.astype(jnp.float32)
    residual = low_back(jnp.take(table_low, seq_ids, axis=1).T)
    normed_one = norm_rows(residual, gain_one, shift_one)
    normed_two = norm_rows(residual, gain_two, shift_two)
    projected = matmul(low(normed_one), wide_in[:, :3 * D]) + bias_qkv
    queries = low(rotate(low_back(projected[:, :D]).reshape(SEQ, H, HD), float_places))
    key_rows = low(rotate(low_back(projected[:, D:2 * D]).reshape(SEQ, H, HD), float_places))
    value_rows = low(low_back(projected[:, 2 * D:])).reshape(SEQ, H, HD)
    raw_scores = jnp.einsum('qhd,khd->hqk', queries, key_rows, precision=HIGHEST) * HD ** (-0.5)
    raw_scores = low_back(raw_scores)
    inside = (int_places >= span_start) & (int_places < span_start + PIC)
    allowed = (int_places[None, :] <= int_places[:, None]) | inside[:, None] & inside[None, :]
    masked = jnp.where(allowed[None], raw_scores, -1e+30)
    highest = lax.optimization_barrier(jnp.max(masked, axis=-1, keepdims=True))
    exponent = jnp.exp(masked - highest)
    attn_probs = low(exponent / lax.optimization_barrier(jnp.sum(exponent, axis=-1, keepdims=True)))
    attended = jnp.einsum('hqk,khd->qhd', attn_probs, value_rows, precision=HIGHEST).reshape(SEQ, D)
    attended = low(low_back(attended))
    hidden_pre = low_back(matmul(low(normed_two), wide_in[:, 3 * D:]) + bias_hidden)
    activation = low(jax.nn.gelu(hidden_pre, approximate=False))
    branch = low_back(matmul(jnp.concatenate([attended, activation], axis=1), wide_back) + bias_out)
    final_rows = norm_rows(residual + branch, gain_last, shift_last)
    block_ids = (jnp.arange(REPS * COMP) // COMP).astype(jnp.int32)
    used_slots = slot_places < SEQ_DEV
    row_at = block_ids * SEQ_DEV + jnp.minimum(slot_places, SEQ_DEV - 1)
    counted = used_slots.astype(jnp.float32)
    picked = jnp.take(final_rows, row_at, axis=0) * counted[:, None]
    logits = low_back(matmul(low(picked), head_low))
    row_top = lax.optimization_barrier(jnp.max(logits, axis=1))
    logsum = row_top + jnp.log(lax.optimization_barrier(jnp.sum(jnp.exp(logits - row_top[:, None]), axis=1)))
    row_target = jnp.take_along_axis(logits, slot_targets[:, None], axis=1)[:, 0]
    return (jnp.sum((logsum - row_target) * counted), jnp.sum(counted))

def total_loss(param_set, items):
    low_set = tuple((low(weight) for weight in param_set))

    def one_sequence(carry, sequence_item):
        part_loss, part_count = jax.checkpoint(sequence_loss)(low_set, sequence_item[0], sequence_item[1], sequence_item[2], sequence_item[3])
        return ((carry[0] + part_loss, carry[1] + part_count), None)
    start_carry = (jnp.zeros((), jnp.float32), jnp.zeros((), jnp.float32))
    (loss_sum, count_sum), _ = lax.scan(one_sequence, start_carry, items)
    return (loss_sum, count_sum)

def adamw(weight, gradient, moment, square, rate_value):
    moment = BETA_FIRST * moment + (1.0 - BETA_FIRST) * gradient
    square = BETA_SECOND * square + (1.0 - BETA_SECOND) * gradient * gradient
    moment_hat = moment / (1.0 - BETA_FIRST ** STEP)
    square_hat = square / (1.0 - BETA_SECOND ** STEP)
    weight = weight - rate_value * (moment_hat / (jnp.sqrt(square_hat) + ADAM_EPS) + DECAY_RATE * weight)
    return (weight, moment, square)

def reference(token_ids, pic_start, comp_pos, comp_tgt, proj_in, proj_back, small_params, head_table, embed_table, first_in, second_in, first_back, second_back, first_small, second_small, first_head, second_head, first_embed, second_embed):
    items = (token_ids.reshape(MB * SEQS, SEQ), pic_start.reshape(MB * SEQS), comp_pos.reshape(MB * SEQS, REPS * COMP), comp_tgt.reshape(MB * SEQS, REPS * COMP))
    param_set = (proj_in, proj_back, small_params, head_table, embed_table)
    loss_sum, pull, count_sum = jax.vjp(lambda weights: total_loss(weights, items), param_set, has_aux=True)
    gradients = pull(jnp.ones_like(loss_sum))[0]
    square_sum = jnp.sum(gradients[0] * gradients[0]) + jnp.sum(gradients[1] * gradients[1]) + jnp.sum(gradients[2] * gradients[2]) + jnp.sum(gradients[3] * gradients[3]) + jnp.sum(gradients[4] * gradients[4])
    norm_value = jnp.sqrt(square_sum)
    factor = CLIP_LEVEL / jnp.maximum(norm_value, CLIP_LEVEL)
    next_in, moment_in, square_in = adamw(proj_in, gradients[0] * factor, first_in, second_in, RATE_IN)
    next_back, moment_back, square_back = adamw(proj_back, gradients[1] * factor, first_back, second_back, RATE_BACK)
    next_small, moment_small, square_small = adamw(small_params, gradients[2] * factor, first_small, second_small, RATE_SMALL)
    next_head, moment_head, square_head = adamw(head_table, gradients[3] * factor, first_head, second_head, RATE_HEAD)
    next_embed, moment_embed, square_embed = adamw(embed_table, gradients[4] * factor, first_embed, second_embed, RATE_EMBED)
    return (jnp.stack([loss_sum, count_sum]), norm_value.reshape(1), next_in, moment_in, square_in, next_back, moment_back, square_back, next_small, moment_small, square_small, next_head, moment_head, square_head, next_embed, moment_embed, square_embed)
```

```python
import functools

import jax
import jax.numpy as jnp
from jax import lax
from jax.experimental import pallas as pl
from jax.experimental.pallas import tpu as pltpu
from jax.sharding import PartitionSpec as P

D = 1024
H = 16
HD = 64
ROT = 16
FF = 4096
PIC = 256
STEP = 10


NORM_EPS = 1e-05
CLIP_LEVEL = 1.0
BETA_FIRST = 0.9
BETA_SECOND = 0.95
ADAM_EPS = 1e-08
DECAY_RATE = 0.01
RATE_IN = 0.01
RATE_BACK = 0.05
RATE_SMALL = 0.3
RATE_HEAD = 0.01
RATE_EMBED = 0.3


def combined_all(part, axis, combine):
    gathered = jax.tree.map(lambda a: lax.all_gather(a, axis), part)

    def take(source):
        return jax.tree.map(lambda a: lax.dynamic_index_in_dim(a, source, 0, False), gathered)

    return lax.fori_loop(
        1, lax.axis_size(axis), lambda source, state: combine(state, take(source)), take(0)
    )


def norm_rows(values, gain_vec, shift_vec):
    centred = values - jnp.mean(values, axis=-1, keepdims=True)
    spread = jnp.mean(centred * centred, axis=-1, keepdims=True)
    return centred * lax.rsqrt(spread + NORM_EPS) * gain_vec + shift_vec


def rotate(head_rows, place_vec):
    half_rot = ROT // 2
    exponent = jnp.arange(half_rot).astype(jnp.float32) * (2.0 / ROT)
    angles = place_vec[:, None] * jnp.exp(-exponent * jnp.log(10000.0))
    cosine = jnp.cos(angles)[:, None, :]
    sine_part = jnp.sin(angles)[:, None, :]
    front_part = head_rows[..., :half_rot]
    back_part = head_rows[..., half_rot:ROT]
    return jnp.concatenate(
        [
            front_part * cosine - back_part * sine_part,
            back_part * cosine + front_part * sine_part,
            head_rows[..., ROT:],
        ],
        axis=-1,
    )


def split_small(gain_parts):
    marks = [0, D, 2 * D, 3 * D, 4 * D, 5 * D, 6 * D, 9 * D, 9 * D + FF, 10 * D + FF]
    return tuple((gain_parts[marks[number] : marks[number + 1]] for number in range(9)))


def gelu_exact(values):
    return jax.nn.gelu(values, approximate=False)


def combine_totals(earlier, later_part):
    highest = jnp.maximum(earlier[0], later_part[0])
    totals = earlier[1] * jnp.exp(earlier[0] - highest) + later_part[1] * jnp.exp(
        later_part[0] - highest
    )
    return (highest, totals, earlier[2] + later_part[2])


def allowed_mask(query_places, key_places, span_start):
    inside_query = (query_places >= span_start) & (query_places < span_start + PIC)
    inside_key = (key_places >= span_start) & (key_places < span_start + PIC)
    return (key_places[None, :] <= query_places[:, None]) | inside_query[:, None] & inside_key[
        None, :
    ]


def masked_scores(queries, keys_all, allowed):
    raw_scores = jnp.einsum(
        "qhd,khd->hqk", queries, keys_all, preferred_element_type=jnp.float32
    ) * HD ** (-0.5)
    return jnp.where(allowed[None], raw_scores, -1e30)


def adamw(weight, gradient, moment, square, rate_value):
    moment = BETA_FIRST * moment + (1.0 - BETA_FIRST) * gradient
    square = BETA_SECOND * square + (1.0 - BETA_SECOND) * gradient * gradient
    moment_hat = moment / (1.0 - BETA_FIRST**STEP)
    square_hat = square / (1.0 - BETA_SECOND**STEP)
    weight = weight - rate_value * (
        moment_hat / (jnp.sqrt(square_hat) + ADAM_EPS) + DECAY_RATE * weight
    )
    return (weight, moment, square)


def any_mesh(
    token_ids,
    pic_start,
    comp_pos,
    comp_tgt,
    proj_in,
    proj_back,
    small_params,
    head_table,
    embed_table,
    first_in,
    second_in,
    first_back,
    second_back,
    first_small,
    second_small,
    first_head,
    second_head,
    first_embed,
    second_embed,
):
    seq_dev = token_ids.shape[2]
    micro_count = token_ids.shape[0]
    vocab_dev = head_table.shape[1]
    rep_count = lax.axis_size("rep")
    seq_len = seq_dev * rep_count
    rep_at = lax.axis_index("rep")
    shard_at = lax.axis_index("shard")
    used_own = comp_pos[:, 0, :] < seq_dev
    marked = jnp.where(used_own, comp_tgt[:, 0, :], -1)
    ids_group, tgt_group = (
        lax.all_gather(token_ids[:, 0, :], "shard", axis=1, tiled=True),
        lax.all_gather(marked, "shard", axis=1, tiled=True),
    )
    in_low = proj_in.astype(jnp.bfloat16)
    back_low = proj_back.astype(jnp.bfloat16)
    small_low = small_params.astype(jnp.bfloat16)
    head_low = head_table.astype(jnp.bfloat16)
    table_low = embed_table.astype(jnp.bfloat16)
    own_places = rep_at * seq_dev + jnp.arange(seq_dev)
    key_places = jnp.arange(seq_len)
    own_float = own_places.astype(jnp.float32)
    vocab_ids = jnp.arange(vocab_dev)
    grad_in = jnp.zeros((D, 3 * D + FF), jnp.float32)
    grad_back = jnp.zeros((D + FF, D), jnp.float32)
    grad_small = jnp.zeros((10 * D + FF,), jnp.float32)
    grad_head = jnp.zeros(head_table.shape, jnp.float32)
    grad_embed = jnp.zeros(embed_table.shape, jnp.float32)
    loss_sum = jnp.zeros((), jnp.float32)
    count_sum = jnp.zeros((), jnp.float32)
    for micro_at in range(micro_count):
        wide_in, wide_back, wide_small = (
            lax.all_gather(in_low, "shard", axis=0, tiled=True),
            lax.all_gather(back_low, "shard", axis=0, tiled=True),
            lax.all_gather(small_low, "shard", axis=0, tiled=True),
        )
        (
            gain_one,
            shift_one,
            gain_two,
            shift_two,
            gain_last,
            shift_last,
            bias_qkv,
            bias_hidden,
            bias_out,
        ) = split_small(wide_small.astype(jnp.float32))
        columns = jnp.take(table_low, ids_group[micro_at], axis=1)
        arrived = lax.all_to_all(columns, "shard", split_axis=1, concat_axis=0, tiled=True)
        residual = arrived.T.astype(jnp.float32)
        normed_one = norm_rows(residual, gain_one, shift_one)
        normed_two = norm_rows(residual, gain_two, shift_two)
        low_one = normed_one.astype(jnp.bfloat16)
        low_two = normed_two.astype(jnp.bfloat16)
        projected = (
            jnp.dot(low_one, wide_in[:, : 3 * D], preferred_element_type=jnp.float32) + bias_qkv
        )
        queries = rotate(projected[:, :D].reshape(seq_dev, H, HD), own_float).astype(jnp.bfloat16)
        key_rows = (
            rotate(projected[:, D : 2 * D].reshape(seq_dev, H, HD), own_float)
            .astype(jnp.bfloat16)
            .reshape(seq_dev, D)
        )
        value_rows = projected[:, 2 * D :].astype(jnp.bfloat16)
        keys_all, values_all = (
            lax.all_gather(key_rows, "rep", axis=0, tiled=True),
            lax.all_gather(value_rows, "rep", axis=0, tiled=True),
        )
        keys_all = keys_all.reshape(seq_len, H, HD)
        values_all = values_all.reshape(seq_len, H, HD)
        allowed = allowed_mask(own_places, key_places, pic_start[micro_at, 0])
        scores = masked_scores(queries, keys_all, allowed)
        highest = jnp.max(scores, axis=-1, keepdims=True)
        exponent = jnp.exp(scores - highest)
        totals = jnp.sum(exponent, axis=-1, keepdims=True)
        logsum = highest + jnp.log(totals)
        attn_probs = (exponent / totals).astype(jnp.bfloat16)
        attended = (
            jnp.einsum("hqk,khd->qhd", attn_probs, values_all, preferred_element_type=jnp.float32)
            .reshape(seq_dev, D)
            .astype(jnp.bfloat16)
        )
        hidden_pre = (
            jnp.dot(low_two, wide_in[:, 3 * D :], preferred_element_type=jnp.float32) + bias_hidden
        )
        activation = gelu_exact(hidden_pre).astype(jnp.bfloat16)
        joined = jnp.concatenate([attended, activation], axis=1)
        after_add = (
            residual + jnp.dot(joined, wide_back, preferred_element_type=jnp.float32) + bias_out
        )
        final_rows = norm_rows(after_add, gain_last, shift_last)
        places = comp_pos[micro_at, 0]
        used_slots = (places < seq_dev).astype(jnp.float32)
        picked = (
            jnp.take(final_rows, jnp.minimum(places, seq_dev - 1), axis=0) * used_slots[:, None]
        ).astype(jnp.bfloat16)
        rows_all = lax.all_gather(picked, "shard", axis=0, tiled=True)
        logits = jnp.dot(rows_all, head_low, preferred_element_type=jnp.float32)
        targets = tgt_group[micro_at]
        matches = (targets - shard_at * vocab_dev)[:, None] == vocab_ids[None, :]
        row_top = jnp.max(logits, axis=1)
        row_total = jnp.sum(jnp.exp(logits - row_top[:, None]), axis=1)
        row_target = jnp.sum(jnp.where(matches, logits, 0.0), axis=1)
        row_top, row_total, row_target = combined_all(
            (row_top, row_total, row_target), "shard", combine_totals
        )
        logsum_rows = row_top + jnp.log(row_total)
        counted = (targets >= 0).astype(jnp.float32)
        loss_sum = loss_sum + jnp.sum((logsum_rows - row_target) * counted)
        count_sum = count_sum + jnp.sum(counted)
        d_logits = (
            (jnp.exp(logits - logsum_rows[:, None]) - matches.astype(jnp.float32))
            * counted[:, None]
        ).astype(jnp.bfloat16)
        grad_head = grad_head + jnp.einsum(
            "rd,rv->dv", rows_all, d_logits, preferred_element_type=jnp.float32
        )
        d_picked = lax.psum_scatter(
            jnp.einsum("rv,dv->rd", d_logits, head_low, preferred_element_type=jnp.float32),
            "shard",
            scatter_dimension=0,
            tiled=True,
        )
        d_final = jnp.zeros((seq_dev, D), jnp.float32).at[places].add(d_picked, mode="drop")
        back_in, back_back = (
            lax.all_gather(in_low, "shard", axis=0, tiled=True),
            lax.all_gather(back_low, "shard", axis=0, tiled=True),
        )
        _, pull_last = jax.vjp(norm_rows, after_add, gain_last, shift_last)
        d_after, d_gain_last, d_shift_last = pull_last(d_final)
        d_branch = d_after.astype(jnp.bfloat16)
        grad_back = grad_back + jnp.einsum(
            "sc,sd->cd", joined, d_branch, preferred_element_type=jnp.float32
        )
        d_joined = jnp.einsum("sd,cd->sc", d_branch, back_back, preferred_element_type=jnp.float32)
        d_attended = d_joined[:, :D].astype(jnp.bfloat16).reshape(seq_dev, H, HD)
        _, pull_gelu = jax.vjp(gelu_exact, hidden_pre)
        d_hidden = pull_gelu(d_joined[:, D:])[0].astype(jnp.bfloat16)
        probs_again = jnp.exp(masked_scores(queries, keys_all, allowed) - logsum)
        d_probs = jnp.einsum(
            "qhd,khd->hqk", d_attended, values_all, preferred_element_type=jnp.float32
        )
        d_scores = (
            probs_again * (d_probs - jnp.sum(probs_again * d_probs, axis=-1, keepdims=True))
        ).astype(jnp.bfloat16)
        d_queries = jnp.einsum(
            "hqk,khd->qhd", d_scores, keys_all, preferred_element_type=jnp.float32
        ) * HD ** (-0.5)
        low_probs = probs_again.astype(jnp.bfloat16)
        d_keys = jnp.einsum(
            "hqk,qhd->khd", d_scores, queries, preferred_element_type=jnp.float32
        ) * HD ** (-0.5)
        d_values = jnp.einsum(
            "hqk,qhd->khd", low_probs, d_attended, preferred_element_type=jnp.float32
        )
        key_grads = lax.psum_scatter(
            jnp.concatenate(
                [
                    d_keys.reshape(seq_dev * lax.axis_size("rep"), D),
                    d_values.reshape(seq_dev * lax.axis_size("rep"), D),
                ],
                axis=1,
            ),
            "rep",
            scatter_dimension=0,
            tiled=True,
        )
        d_key_rows = rotate(key_grads[:, :D].reshape(seq_dev, H, HD), -own_float).reshape(
            seq_dev, D
        )
        d_query_rows = rotate(d_queries, -own_float).reshape(seq_dev, D)
        d_projected = jnp.concatenate([d_query_rows, d_key_rows, key_grads[:, D:]], axis=1).astype(
            jnp.bfloat16
        )
        grad_in = grad_in + jnp.concatenate(
            [
                jnp.einsum("sd,sc->dc", low_one, d_projected, preferred_element_type=jnp.float32),
                jnp.einsum("sd,sc->dc", low_two, d_hidden, preferred_element_type=jnp.float32),
            ],
            axis=1,
        )
        d_normed_one = jnp.einsum(
            "sc,dc->sd", d_projected, back_in[:, : 3 * D], preferred_element_type=jnp.float32
        )
        d_normed_two = jnp.einsum(
            "sc,dc->sd", d_hidden, back_in[:, 3 * D :], preferred_element_type=jnp.float32
        )
        _, pull_one = jax.vjp(norm_rows, residual, gain_one, shift_one)
        d_resid_one, d_gain_one, d_shift_one = pull_one(d_normed_one)
        _, pull_two = jax.vjp(norm_rows, residual, gain_two, shift_two)
        d_resid_two, d_gain_two, d_shift_two = pull_two(d_normed_two)
        d_residual = (d_after + d_resid_one + d_resid_two).astype(jnp.bfloat16)
        returned = lax.all_to_all(d_residual.T, "shard", split_axis=0, concat_axis=1, tiled=True)
        grad_embed = grad_embed.at[:, ids_group[micro_at]].add(returned.astype(jnp.float32))
        grad_small = grad_small + jnp.concatenate(
            [
                d_gain_one,
                d_shift_one,
                d_gain_two,
                d_shift_two,
                d_gain_last,
                d_shift_last,
                jnp.sum(d_projected.astype(jnp.float32), axis=0),
                jnp.sum(d_hidden.astype(jnp.float32), axis=0),
                jnp.sum(d_branch.astype(jnp.float32), axis=0),
            ]
        )
    shard_in, shard_back, shard_small = (
        lax.psum_scatter(grad_in, "shard", scatter_dimension=0, tiled=True),
        lax.psum_scatter(grad_back, "shard", scatter_dimension=0, tiled=True),
        lax.psum_scatter(grad_small, "shard", scatter_dimension=0, tiled=True),
    )
    summed = lax.psum(
        (shard_in, shard_back, shard_small, grad_head, grad_embed, loss_sum, count_sum), "rep"
    )
    local_square = (
        jnp.sum(summed[0] * summed[0])
        + jnp.sum(summed[1] * summed[1])
        + jnp.sum(summed[2] * summed[2])
        + jnp.sum(summed[3] * summed[3])
        + jnp.sum(summed[4] * summed[4])
    )
    norm_value = jnp.sqrt(lax.psum(local_square, "shard"))
    factor = CLIP_LEVEL / jnp.maximum(norm_value, CLIP_LEVEL)
    next_in, moment_in, square_in = adamw(proj_in, summed[0] * factor, first_in, second_in, RATE_IN)
    next_back, moment_back, square_back = adamw(
        proj_back, summed[1] * factor, first_back, second_back, RATE_BACK
    )
    next_small, moment_small, square_small = adamw(
        small_params, summed[2] * factor, first_small, second_small, RATE_SMALL
    )
    next_head, moment_head, square_head = adamw(
        head_table, summed[3] * factor, first_head, second_head, RATE_HEAD
    )
    next_embed, moment_embed, square_embed = adamw(
        embed_table, summed[4] * factor, first_embed, second_embed, RATE_EMBED
    )
    return (
        jnp.stack([summed[5], summed[6]]),
        norm_value.reshape(1),
        next_in,
        moment_in,
        square_in,
        next_back,
        moment_back,
        square_back,
        next_small,
        moment_small,
        square_small,
        next_head,
        moment_head,
        square_head,
        next_embed,
        moment_embed,
        square_embed,
    )


MESH = pl.DeviceIdType.MESH
RG = 4
SG = 8


def whereabouts():
    rep = lax.axis_index("rep")
    shard = lax.axis_index("shard")
    core_twin = rep + 1 - 2 * lax.rem(rep, 2)
    x_twin = lax.rem(rep + 2, RG)
    y_twin = shard + 1 - 2 * lax.rem(shard, 2)
    return rep, shard, core_twin, x_twin, y_twin


def z_peer(shard, step):
    return lax.rem(shard + 2 * step, SG)


def shard_peer(shard, step):
    return lax.rem(shard + step, SG)


def greet(partners):
    barrier = pltpu.get_barrier_semaphore()
    for partner in partners:
        pl.semaphore_signal(barrier, inc=1, device_id=partner, device_id_type=MESH)
    pl.semaphore_wait(barrier, len(partners))


def remote(src, dst, send_sem, recv_sem, partner):
    return pltpu.make_async_remote_copy(
        src_ref=src,
        dst_ref=dst,
        send_sem=send_sem,
        recv_sem=recv_sem,
        device_id=partner,
        device_id_type=MESH,
    )


def comm_call(kernel, out_shape, scratch, number, args, spaces=None, out_spaces=None, limit=None):
    any_spec = pl.BlockSpec(memory_space=pl.ANY)
    vmem_spec = pl.BlockSpec(memory_space=pltpu.VMEM)
    pick = {"a": any_spec, "v": vmem_spec}
    spaces = spaces or "a" * len(args)
    out_spaces = out_spaces or "a" * len(out_shape)
    return pl.pallas_call(
        kernel,
        out_shape=out_shape,
        in_specs=[pick[space] for space in spaces],
        out_specs=[pick[space] for space in out_spaces],
        scratch_shapes=scratch,
        compiler_params=pltpu.CompilerParams(
            collective_id=number, has_side_effects=True, vmem_limit_bytes=limit
        ),
    )(*args)


def facts_kernel(ints, smalls, ints_all, smalls_all, send_int, recv_int, send_small, recv_small, send_rep, recv_rep, own):
    rep, shard, _, _, _ = whereabouts()
    shard_peers = [(rep, shard_peer(shard, step)) for step in range(1, SG)]
    rep_peers = [(lax.rem(rep + step, RG), shard) for step in range(1, RG)]
    greet(shard_peers + rep_peers)
    copies = []
    for at, peer in enumerate(shard_peers):
        copies.append(remote(ints, ints_all.at[rep, shard], send_int.at[at], recv_int.at[at], peer))
        copies[-1].start()
    small_copies = []
    for at, peer in enumerate(shard_peers):
        small_copies.append(remote(smalls, smalls_all.at[shard], send_small.at[at], recv_small.at[at], peer))
        small_copies[-1].start()
    keep_int = pltpu.make_async_copy(ints, ints_all.at[rep, shard], own.at[0])
    keep_small = pltpu.make_async_copy(smalls, smalls_all.at[shard], own.at[1])
    keep_int.start()
    keep_small.start()
    keep_int.wait()
    for copy in copies:
        copy.wait()
    rep_copies = []
    for at, peer in enumerate(rep_peers):
        rep_copies.append(remote(ints_all.at[rep], ints_all.at[rep], send_rep.at[at], recv_rep.at[at], peer))
        rep_copies[-1].start()
    keep_small.wait()
    for copy in small_copies + rep_copies:
        copy.wait()


def share_facts(ints, smalls, number):
    dma = pltpu.SemaphoreType.DMA
    return comm_call(
        facts_kernel,
        [
            jax.ShapeDtypeStruct((RG, SG) + ints.shape, ints.dtype),
            jax.ShapeDtypeStruct((SG,) + smalls.shape, smalls.dtype),
        ],
        [dma((SG - 1,))] * 4 + [dma((RG - 1,))] * 2 + [dma((2,))],
        number,
        (ints, smalls),
        "vv",
        "vv",
    )


def start_gather(source, out, slot, place, sems):
    send_z, recv_z, send_y, recv_y, own = sems
    rep, shard, _, _, y_twin = place
    keep = pltpu.make_async_copy(source, slot(out, shard), own)
    keep.start()
    first_y = remote(source, slot(out, shard), send_y.at[0], recv_y.at[0], (rep, y_twin))
    z_copies = [
        remote(source, slot(out, shard), send_z.at[step - 1], recv_z.at[step - 1], (rep, z_peer(shard, step)))
        for step in range(1, 4)
    ]
    for copy in z_copies:
        copy.start()
    first_y.start()
    return keep, first_y, z_copies


def finish_gather(started, out, slot, place, sems):
    send_z, recv_z, send_y, recv_y, own = sems
    rep, shard, _, _, y_twin = place
    keep, first_y, z_copies = started
    passed = []
    for step in range(1, 4):
        z_copies[step - 1].wait_recv()
        came_from = z_peer(shard, SG // 2 - step)
        passed.append(
            remote(slot(out, came_from), slot(out, came_from), send_y.at[step], recv_y.at[step], (rep, y_twin))
        )
        passed[-1].start()
    keep.wait()
    for copy in z_copies:
        copy.wait_send()
    first_y.wait()
    for copy in passed:
        copy.wait()


def gather_partners(place):
    rep, shard, _, _, y_twin = place
    return [(rep, z_peer(shard, step)) for step in range(1, 4)] + [(rep, y_twin)]


GATHER_SEMS = [pltpu.SemaphoreType.DMA((3,)), pltpu.SemaphoreType.DMA((3,)), pltpu.SemaphoreType.DMA((4,)), pltpu.SemaphoreType.DMA((4,)), pltpu.SemaphoreType.DMA]


def column_slot(out, index):
    width = out.shape[1] // SG
    return out.at[:, pl.ds(pl.multiple_of(index * width, width), width)]


def row_slot(out, index):
    height = out.shape[0] // SG
    return out.at[pl.ds(pl.multiple_of(index * height, height), height)]


def tile_user(tile):
    return jnp.where(tile < SG, tile, (tile - SG) // 4)


def tile_slot(tile):
    return jnp.where(tile < SG, 0, 1 + lax.rem(tile - SG + SG, 4))


def embed_kernel(rows, in_parts, back_tiles, out, in_all, back_all, *sems):
    gather_sems = sems[:5]
    send_in, recv_in, send_back, recv_back, own_in, send_pair, recv_pair = sems[5:]
    place = whereabouts()
    rep, shard, core_twin, _, _ = place
    half = lax.rem(rep, 2)
    greet([(rep, shard_peer(shard, step)) for step in range(1, SG)] + [(core_twin, shard)])
    started = start_gather(rows, out, column_slot, place, gather_sems)
    in_copies = []
    for step in range(1, SG):
        peer = shard_peer(shard, step)
        in_copies.append(
            remote(in_parts.at[peer, half], in_all.at[shard, half], send_in.at[step - 1], recv_in.at[step - 1], (rep, peer))
        )
        in_copies[-1].start()
    keep_in = pltpu.make_async_copy(in_parts.at[shard, half], in_all.at[shard, half], own_in)
    keep_in.start()
    moves = []
    for at in range(5):
        tile = 5 * shard + at
        user = tile_user(tile)
        slot = tile_slot(tile)
        there = remote(back_tiles.at[at, half], back_all.at[slot, half], send_back.at[at], recv_back.at[slot], (rep, user))
        here = pltpu.make_async_copy(back_tiles.at[at, half], back_all.at[slot, half], recv_back.at[slot])

        @pl.when(user == shard)
        def _():
            here.start()

        @pl.when(user != shard)
        def _():
            there.start()

        moves.append((user, there))
    finish_gather(started, out, column_slot, place, gather_sems)
    keep_in.wait()
    for copy in in_copies:
        copy.wait()
    for slot in range(5):
        pltpu.make_async_copy(back_tiles.at[0, half], back_all.at[slot, half], recv_back.at[slot]).wait()
    pair_in = remote(in_all.at[:, half], in_all.at[:, half], send_pair.at[0], recv_pair.at[0], (core_twin, shard))
    pair_back = remote(back_all.at[:, half], back_all.at[:, half], send_pair.at[1], recv_pair.at[1], (core_twin, shard))
    pair_in.start()
    pair_back.start()
    for user, there in moves:

        @pl.when(user != shard)
        def _():
            there.wait_send()

    pair_in.wait()
    pair_back.wait()


def share_embedding(rows, in_parts, back_tiles, number):
    dma = pltpu.SemaphoreType.DMA
    return comm_call(
        embed_kernel,
        [
            jax.ShapeDtypeStruct((rows.shape[0], SG * rows.shape[1]), rows.dtype),
            jax.ShapeDtypeStruct(in_parts.shape, in_parts.dtype),
            jax.ShapeDtypeStruct(back_tiles.shape, back_tiles.dtype),
        ],
        GATHER_SEMS + [dma((SG - 1,))] * 2 + [dma((5,))] * 2 + [dma] + [dma((2,))] * 2,
        number,
        (rows, in_parts, back_tiles),
    )


def gather_kernel(rows, out, *sems):
    place = whereabouts()
    greet(gather_partners(place))
    started = start_gather(rows, out, row_slot, place, sems)
    finish_gather(started, out, row_slot, place, sems)


def shard_gather(rows, number):
    return comm_call(
        gather_kernel,
        [jax.ShapeDtypeStruct((SG * rows.shape[0], rows.shape[1]), rows.dtype)],
        GATHER_SEMS,
        number,
        (rows,),
        "v",
        "v",
    )[0]


def stats_kernel(stats, out, send, recv):
    rep, shard, _, _, _ = whereabouts()
    peers = [(rep, shard_peer(shard, step)) for step in range(1, SG)]
    greet(peers)
    copies = [remote(stats, out.at[shard], send.at[at], recv.at[at], peer) for at, peer in enumerate(peers)]
    for copy in copies:
        copy.start()
    out[shard] = stats[...]
    for copy in copies:
        copy.wait()


def shard_stats(stats, number):
    dma = pltpu.SemaphoreType.DMA
    return comm_call(
        stats_kernel,
        [jax.ShapeDtypeStruct((SG,) + stats.shape, stats.dtype)],
        [dma((SG - 1,)), dma((SG - 1,))],
        number,
        (stats,),
        "v",
        "v",
    )[0]


def sum_sems():
    dma = pltpu.SemaphoreType.DMA
    return [dma((4,)), dma((4,)), dma((3,)), dma((3,))]


def sum_buffers(chunk):
    return [pltpu.VMEM((4,) + chunk, jnp.float32), pltpu.VMEM((4,) + chunk, jnp.float32), pltpu.VMEM((3,) + chunk, jnp.float32)]


def start_sum(parts, place, buffers, sems):
    rep, shard, _, _, y_twin = place
    from_y, own_sum, from_z = buffers
    send_y, recv_y, send_z, recv_z = sems
    y_copies = {}
    for step in (2, 1, 3, 0):
        y_copies[step] = remote(
            parts.at[z_peer(y_twin, step)], from_y.at[step], send_y.at[step], recv_y.at[step], (rep, y_twin)
        )
        y_copies[step].start()
    return y_copies


def finish_sum(y_copies, parts, out, place, buffers, sems, post=None):
    rep, shard, _, _, y_twin = place
    from_y, own_sum, from_z = buffers
    send_y, recv_y, send_z, recv_z = sems
    z_copies = []
    for step in (2, 1, 3):
        y_copies[step].wait_recv()
        own_sum[step] = parts[z_peer(shard, step)] + from_y[step]
        z_copies.append(
            remote(own_sum.at[step], from_z.at[step - 1], send_z.at[step - 1], recv_z.at[step - 1], (rep, z_peer(shard, step)))
        )
        z_copies[-1].start()
    y_copies[0].wait_recv()
    total = parts[shard] + from_y[0]
    for copy in z_copies:
        copy.wait_recv()
    out[...] = total + from_z[0] + from_z[1] + from_z[2]
    for step in range(4):
        y_copies[step].wait_send()
    for copy in z_copies:
        copy.wait_send()


def sum_kernel(parts, out, from_y, own_sum, from_z, *sems):
    place = whereabouts()
    greet(gather_partners(place))
    buffers = (from_y, own_sum, from_z)
    y_copies = start_sum(parts, place, buffers, sems)
    finish_sum(y_copies, parts, out, place, buffers, sems)


def shard_sum(parts, number):
    chunk = parts.shape[1:]
    return comm_call(
        sum_kernel,
        [jax.ShapeDtypeStruct(chunk, jnp.float32)],
        sum_buffers(chunk) + sum_sems(),
        number,
        (parts,),
        "v",
        "v",
        40 << 20,
    )[0]


def picked_kernel(parts, rows, facts, out, rows_all, facts_all, from_y, own_sum, from_z, *sems):
    place = whereabouts()
    rep, shard, core_twin, x_twin, _ = place
    sum_sem = sems[:4]
    send_row, recv_row, send_fact, recv_fact, own = sems[4:]
    rep_peers = [(lax.rem(rep + step, RG), shard) for step in range(1, RG)]
    greet(gather_partners(place) + rep_peers)
    buffers = (from_y, own_sum, from_z)
    y_copies = start_sum(parts, place, buffers, sum_sem)
    keep = pltpu.make_async_copy(rows, rows_all.at[rep], own)
    keep.start()
    to_x = remote(rows, rows_all.at[rep], send_row.at[0], recv_row.at[0], (x_twin, shard))
    to_core = remote(rows, rows_all.at[rep], send_row.at[1], recv_row.at[1], (core_twin, shard))
    to_x.start()
    to_core.start()
    fact_copies = [
        remote(facts, facts_all.at[rep], send_fact.at[at], recv_fact.at[at], peer) for at, peer in enumerate(rep_peers)
    ]
    for copy in fact_copies:
        copy.start()
    facts_all[rep] = facts[...]
    finish_sum(y_copies, parts, out, place, buffers, sum_sem)
    to_x.wait_recv()
    passed = remote(rows_all.at[x_twin], rows_all.at[x_twin], send_row.at[2], recv_row.at[2], (core_twin, shard))
    passed.start()
    keep.wait()
    to_x.wait_send()
    to_core.wait()
    for copy in fact_copies:
        copy.wait()
    passed.wait()


def sum_and_share(parts, rows, facts, number):
    dma = pltpu.SemaphoreType.DMA
    chunk = parts.shape[1:]
    return comm_call(
        picked_kernel,
        [
            jax.ShapeDtypeStruct(chunk, jnp.float32),
            jax.ShapeDtypeStruct((RG,) + rows.shape, rows.dtype),
            jax.ShapeDtypeStruct((RG,) + facts.shape, facts.dtype),
        ],
        sum_buffers(chunk) + sum_sems() + [dma((3,))] * 4 + [dma],
        number,
        (parts, rows, facts),
        "vvv",
        "vvv",
        40 << 20,
    )


def branch_kernel(rows, pieces, out, features, *sems):
    place = whereabouts()
    rep, shard, _, _, _ = place
    send, recv = sems[5:]
    peers = [(rep, shard_peer(shard, step)) for step in range(1, SG)]
    greet(peers)
    started = start_gather(rows, out, row_slot, place, sems[:5])
    copies = []
    for at, peer in enumerate(peers):
        copies.append(remote(pieces.at[peer[1]], features.at[shard], send.at[at], recv.at[at], peer))
        copies[-1].start()
    features[shard] = pieces[shard]
    finish_gather(started, out, row_slot, place, sems[:5])
    for copy in copies:
        copy.wait()


def share_branch(rows, pieces, number):
    dma = pltpu.SemaphoreType.DMA
    return comm_call(
        branch_kernel,
        [jax.ShapeDtypeStruct((SG * rows.shape[0], rows.shape[1]), rows.dtype), jax.ShapeDtypeStruct(pieces.shape, pieces.dtype)],
        GATHER_SEMS + [dma((SG - 1,))] * 2,
        number,
        (rows, pieces),
        "vv",
        "vv",
    )


def layer_kernel(parts, stats, grad_in, grad_back, smalls, out, stats_all, sum_in, sum_back, smalls_out,
                 from_y, own_sum, from_z, pair_in, pair_back, half_in, half_back, far_in, far_back, small_rep, small_sum, small_shard, *sems):
    place = whereabouts()
    rep, shard, core_twin, x_twin, _ = place
    sum_sem = sems[:4]
    send_stat, recv_stat, send_pair, recv_pair, send_far, recv_far, send_rep, recv_rep, send_small, recv_small = sems[4:]
    shard_peers = [(rep, shard_peer(shard, step)) for step in range(1, SG)]
    rep_peers = [(lax.rem(rep + step, RG), shard) for step in range(1, RG)]
    greet(shard_peers + rep_peers)
    buffers = (from_y, own_sum, from_z)
    rep_copies = [
        remote(smalls, small_rep.at[at], send_rep.at[at], recv_rep.at[at], peer) for at, peer in enumerate(rep_peers)
    ]
    for copy in rep_copies:
        copy.start()
    core_far = lax.rem(core_twin + 2, RG)
    pair_copies = [
        remote(grad_in.at[core_far], pair_in.at[1], send_pair.at[0], recv_pair.at[0], (core_twin, shard)),
        remote(grad_back.at[core_far], pair_back.at[1], send_pair.at[1], recv_pair.at[1], (core_twin, shard)),
        remote(grad_in.at[core_twin], pair_in.at[0], send_pair.at[2], recv_pair.at[2], (core_twin, shard)),
        remote(grad_back.at[core_twin], pair_back.at[0], send_pair.at[3], recv_pair.at[3], (core_twin, shard)),
    ]
    for copy in pair_copies:
        copy.start()
    y_copies = start_sum(parts, place, buffers, sum_sem)
    stat_copies = [
        remote(stats, stats_all.at[shard], send_stat.at[at], recv_stat.at[at], peer) for at, peer in enumerate(shard_peers)
    ]
    for copy in stat_copies:
        copy.start()
    stats_all[shard] = stats[...]
    pair_copies[0].wait()
    pair_copies[1].wait()
    half_in[...] = grad_in[x_twin] + pair_in[1]
    half_back[...] = grad_back[x_twin] + pair_back[1]
    far_copies = [
        remote(half_in, far_in, send_far.at[0], recv_far.at[0], (x_twin, shard)),
        remote(half_back, far_back, send_far.at[1], recv_far.at[1], (x_twin, shard)),
    ]
    for copy in far_copies:
        copy.start()
    for copy in rep_copies:
        copy.wait()
    small_sum[...] = smalls[...] + small_rep[0] + small_rep[1] + small_rep[2]
    small_copies = [
        remote(small_sum.at[peer[1]], small_shard.at[at], send_small.at[at], recv_small.at[at], peer)
        for at, peer in enumerate(shard_peers)
    ]
    for copy in small_copies:
        copy.start()
    finish_sum(y_copies, parts, out, place, buffers, sum_sem)
    pair_copies[2].wait()
    pair_copies[3].wait()
    for copy in far_copies:
        copy.wait()
    sum_in[...] = grad_in[rep] + pair_in[0] + far_in[...]
    sum_back[...] = grad_back[rep] + pair_back[0] + far_back[...]
    for copy in stat_copies + small_copies:
        copy.wait()
    total = small_sum[shard]
    for at in range(SG - 1):
        total = total + small_shard[at]
    smalls_out[...] = total


def layer_sums(parts, stats, grad_in, grad_back, smalls, number):
    dma = pltpu.SemaphoreType.DMA
    chunk = parts.shape[1:]
    quarter_in, quarter_back, piece = grad_in.shape[1:], grad_back.shape[1:], smalls.shape[1:]
    vmem = lambda shape: pltpu.VMEM(shape, jnp.float32)
    shape = lambda dims: jax.ShapeDtypeStruct(dims, jnp.float32)
    return comm_call(
        layer_kernel,
        [shape(chunk), shape((SG,) + stats.shape), shape(quarter_in), shape(quarter_back), shape(piece)],
        sum_buffers(chunk)
        + [vmem((2,) + quarter_in), vmem((2,) + quarter_back), vmem(quarter_in), vmem(quarter_back), vmem(quarter_in), vmem(quarter_back)]
        + [vmem((3,) + smalls.shape), vmem(smalls.shape), vmem((SG - 1,) + piece)]
        + sum_sems()
        + [dma((SG - 1,))] * 2 + [dma((4,))] * 2 + [dma((2,))] * 2 + [dma((3,))] * 2 + [dma((SG - 1,))] * 2,
        number,
        (parts, stats, grad_in, grad_back, smalls),
        "vvvvv",
        "vvvvv",
        62 << 20,
    )


def return_kernel(rows, sum_in, sum_back, rows_all, in_all, back_all, *sems):
    place = whereabouts()
    rep, shard, core_twin, x_twin, _ = place
    (send_row, recv_row, own, send_in, recv_in, send_back, recv_back, send_far, recv_far, send_pair, recv_pair) = sems
    greet([(rep, shard_peer(shard, step)) for step in range(1, SG)] + [(core_twin, shard), (x_twin, shard)])
    in_copies = []
    for step in range(1, SG):
        peer = shard_peer(shard, step)
        in_copies.append(
            remote(sum_in.at[peer], in_all.at[rep, shard], send_in.at[step - 1], recv_in.at[step - 1], (rep, peer))
        )
        in_copies[-1].start()
    keep_in = pltpu.make_async_copy(sum_in.at[shard], in_all.at[rep, shard], own.at[1])
    keep_in.start()
    moves = []
    for slot in range(5):
        tile = jnp.where(slot == 0, shard, SG + 4 * shard + slot - 1)
        owner = tile // 5
        at = lax.rem(tile, 5)
        there = remote(sum_back.at[slot], back_all.at[rep, at], send_back.at[slot], recv_back.at[at], (rep, owner))
        here = pltpu.make_async_copy(sum_back.at[slot], back_all.at[rep, at], recv_back.at[at])

        @pl.when(owner == shard)
        def _():
            here.start()

        @pl.when(owner != shard)
        def _():
            there.start()

        moves.append((owner, there))
    keep = pltpu.make_async_copy(rows, rows_all.at[rep], own.at[0])
    keep.start()
    to_x = remote(rows, rows_all.at[rep], send_row.at[0], recv_row.at[0], (x_twin, shard))
    to_core = remote(rows, rows_all.at[rep], send_row.at[1], recv_row.at[1], (core_twin, shard))
    to_x.start()
    to_core.start()
    keep_in.wait()
    for copy in in_copies:
        copy.wait()
    in_far = remote(in_all.at[rep], in_all.at[rep], send_far.at[0], recv_far.at[0], (x_twin, shard))
    in_pair = remote(in_all.at[rep], in_all.at[rep], send_pair.at[0], recv_pair.at[0], (core_twin, shard))
    in_far.start()
    in_pair.start()
    for at in range(5):
        pltpu.make_async_copy(sum_back.at[0], back_all.at[rep, at], recv_back.at[at]).wait()
    back_far = remote(back_all.at[rep], back_all.at[rep], send_far.at[1], recv_far.at[1], (x_twin, shard))
    back_pair = remote(back_all.at[rep], back_all.at[rep], send_pair.at[1], recv_pair.at[1], (core_twin, shard))
    back_far.start()
    back_pair.start()
    to_x.wait_recv()
    passed = remote(rows_all.at[x_twin], rows_all.at[x_twin], send_row.at[2], recv_row.at[2], (core_twin, shard))
    passed.start()
    in_far.wait_recv()
    in_passed = remote(in_all.at[x_twin], in_all.at[x_twin], send_pair.at[2], recv_pair.at[2], (core_twin, shard))
    in_passed.start()
    back_far.wait_recv()
    back_passed = remote(back_all.at[x_twin], back_all.at[x_twin], send_pair.at[3], recv_pair.at[3], (core_twin, shard))
    back_passed.start()
    for owner, there in moves:

        @pl.when(owner != shard)
        def _():
            there.wait_send()

    keep.wait()
    to_x.wait_send()
    to_core.wait()
    in_far.wait_send()
    back_far.wait_send()
    for copy in (in_pair, back_pair, passed, in_passed, back_passed):
        copy.wait()


def return_sums(rows, sum_in, sum_back, number):
    dma = pltpu.SemaphoreType.DMA
    shape = lambda dims, like: jax.ShapeDtypeStruct(dims, like.dtype)
    return comm_call(
        return_kernel,
        [shape((RG,) + rows.shape, rows), shape((RG,) + sum_in.shape, sum_in), shape((RG,) + sum_back.shape, sum_back)],
        [dma((3,))] * 2 + [dma((2,))] + [dma((SG - 1,))] * 2 + [dma((5,))] * 2 + [dma((2,))] * 2 + [dma((4,))] * 2,
        number,
        (rows, sum_in, sum_back),
    )


GROUP_HEADS = H // SG
HEAD_COLS = GROUP_HEADS * HD
UNITS = FF // SG
OWN_COLS = 3 * HEAD_COLS + UNITS
VOCAB_BLOCK = 512
TABLE_BLOCK = 4096
EMBED_BLOCK = 2048
EMBED_PART = 512
TOKEN_CHUNK = 128
VMEM_LIMIT = 60 << 20


def transposed_dot(left, right):
    return lax.dot_general(left, right, (((1,), (1,)), ((), ())), preferred_element_type=jnp.float32)


def first_dot(left, right):
    return lax.dot_general(left, right, (((0,), (0,)), ((), ())), preferred_element_type=jnp.float32)


def plain_dot(left, right):
    return jnp.dot(left, right, preferred_element_type=jnp.float32)


def table_kernel(ids, table, rows, turned, rows_wide):
    at = pl.program_id(0)
    block = table[...].astype(jnp.bfloat16).astype(jnp.float32)
    width = block.shape[1]
    turned[pl.ds(pl.multiple_of(at * width, width), width), :] = block.T

    @pl.when(at == pl.num_programs(0) - 1)
    def _():
        @pl.loop(0, rows.shape[0] // 16)
        def _(group):
            for lane in range(16):
                token = group * 16 + lane
                rows_wide[pl.ds(token, 1), :] = turned[pl.ds(ids[token], 1), :]

        rows[...] = rows_wide[...].astype(jnp.bfloat16)


def embedding_rows(ids, table):
    feats, vocab = table.shape
    blocks = pl.cdiv(vocab, TABLE_BLOCK)
    return pl.pallas_call(
        table_kernel,
        grid=(blocks,),
        in_specs=[
            pl.BlockSpec(memory_space=pltpu.SMEM),
            pl.BlockSpec((feats, TABLE_BLOCK), lambda at: (0, at)),
        ],
        out_specs=pl.BlockSpec((ids.shape[0], feats), lambda at: (0, 0)),
        out_shape=jax.ShapeDtypeStruct((ids.shape[0], feats), jnp.bfloat16),
        scratch_shapes=[
            pltpu.VMEM((blocks * TABLE_BLOCK, feats), jnp.float32),
            pltpu.VMEM((ids.shape[0], feats), jnp.float32),
        ],
        compiler_params=pltpu.CompilerParams(vmem_limit_bytes=VMEM_LIMIT),
    )(ids, table)


def vocab_rows(vocab, block):
    at = pl.program_id(0)
    places = at * VOCAB_BLOCK + lax.broadcasted_iota(jnp.int32, block.shape, 0)
    return places, jnp.where(places < vocab, block, jnp.zeros_like(block))


def top_kernel(vocab, rows, targets, head, stats, head_out, top, total, target):
    at = pl.program_id(0)

    @pl.when(at == 0)
    def _():
        top[...] = jnp.full_like(top, -1e30)
        total[...] = jnp.zeros_like(total)
        target[...] = jnp.zeros_like(target)

    low = head[...].astype(jnp.bfloat16)
    head_out[...] = low
    logits = transposed_dot(low, rows[...])
    places = at * VOCAB_BLOCK + lax.broadcasted_iota(jnp.int32, logits.shape, 0)
    valid = places < vocab
    masked = jnp.where(valid, logits, -1e30)
    highest = jnp.maximum(top[...], jnp.max(masked, axis=0, keepdims=True))
    weights = jnp.where(valid, jnp.exp(masked - highest), 0.0)
    total[...] = total[...] * jnp.exp(top[...] - highest) + jnp.sum(weights, axis=0, keepdims=True)
    top[...] = highest
    hits = (places == targets[...]) & valid
    target[...] += jnp.sum(jnp.where(hits, logits, 0.0), axis=0, keepdims=True)

    @pl.when(at == pl.num_programs(0) - 1)
    def _():
        stats[...] = jnp.zeros_like(stats)
        stats[0:1, :] = top[...]
        stats[1:2, :] = total[...]
        stats[2:3, :] = target[...]


def logit_stats(rows, targets, head):
    vocab, depth = head.shape
    count = rows.shape[0]
    line = pltpu.VMEM((1, count), jnp.float32)
    return pl.pallas_call(
        functools.partial(top_kernel, vocab),
        grid=(pl.cdiv(vocab, VOCAB_BLOCK),),
        in_specs=[
            pl.BlockSpec((count, depth), lambda at: (0, 0)),
            pl.BlockSpec((1, count), lambda at: (0, 0)),
            pl.BlockSpec((VOCAB_BLOCK, depth), lambda at: (at, 0)),
        ],
        out_specs=[
            pl.BlockSpec((8, count), lambda at: (0, 0)),
            pl.BlockSpec((VOCAB_BLOCK, depth), lambda at: (at, 0)),
        ],
        out_shape=[
            jax.ShapeDtypeStruct((8, count), jnp.float32),
            jax.ShapeDtypeStruct(head.shape, jnp.bfloat16),
        ],
        scratch_shapes=[line, line, line],
        compiler_params=pltpu.CompilerParams(vmem_limit_bytes=VMEM_LIMIT),
    )(rows, targets, head)


def logit_grads(vocab, low, rows, logsum, targets, counted):
    logits = transposed_dot(low, rows)
    places = pl.program_id(0) * VOCAB_BLOCK + lax.broadcasted_iota(jnp.int32, logits.shape, 0)
    hits = (places == targets).astype(jnp.float32)
    grads = (jnp.exp(logits - logsum) - hits) * counted
    return jnp.where(places < vocab, grads, 0.0).astype(jnp.bfloat16)


def rows_kernel(vocab, rows, facts, targets, head, out):
    @pl.when(pl.program_id(0) == 0)
    def _():
        out[...] = jnp.zeros_like(out)

    _, low = vocab_rows(vocab, head[...])
    grads = logit_grads(vocab, low, rows[...], facts[0:1, :], targets[...], facts[1:2, :])
    out[...] += first_dot(grads, low)


def picked_grads(rows, facts, targets, head):
    vocab, depth = head.shape
    count = rows.shape[0]
    return pl.pallas_call(
        functools.partial(rows_kernel, vocab),
        grid=(pl.cdiv(vocab, VOCAB_BLOCK),),
        in_specs=[
            pl.BlockSpec((count, depth), lambda at: (0, 0)),
            pl.BlockSpec((8, count), lambda at: (0, 0)),
            pl.BlockSpec((1, count), lambda at: (0, 0)),
            pl.BlockSpec((VOCAB_BLOCK, depth), lambda at: (at, 0)),
        ],
        out_specs=pl.BlockSpec((count, depth), lambda at: (0, 0)),
        out_shape=jax.ShapeDtypeStruct((count, depth), jnp.float32),
        compiler_params=pltpu.CompilerParams(vmem_limit_bytes=VMEM_LIMIT),
    )(rows, facts, targets, head)


def head_kernel(vocab, rows, facts, targets, head, out, squares):
    @pl.when(pl.program_id(0) == 0)
    def _():
        squares[...] = jnp.zeros_like(squares)

    _, low = vocab_rows(vocab, head[...])
    groups = rows.shape[0]
    total = None
    for group in range(groups):
        grads = logit_grads(
            vocab, low, rows[group], facts[group, 0:1, :], targets[group, 0:1, :], facts[group, 1:2, :]
        )
        term = plain_dot(grads, rows[group])
        total = term if total is None else total + term
    out[...] = total
    squares[0:1, :] += jnp.sum(total * total, axis=0, keepdims=True)


def head_grads(rows, facts, targets, head):
    vocab, depth = head.shape
    groups, count, _ = rows.shape
    return pl.pallas_call(
        functools.partial(head_kernel, vocab),
        grid=(pl.cdiv(vocab, VOCAB_BLOCK),),
        in_specs=[
            pl.BlockSpec((groups, count, depth), lambda at: (0, 0, 0)),
            pl.BlockSpec((groups, 8, count), lambda at: (0, 0, 0)),
            pl.BlockSpec((groups, 8, count), lambda at: (0, 0, 0)),
            pl.BlockSpec((VOCAB_BLOCK, depth), lambda at: (at, 0)),
        ],
        out_specs=[
            pl.BlockSpec((VOCAB_BLOCK, depth), lambda at: (at, 0)),
            pl.BlockSpec((8, depth), lambda at: (0, 0)),
        ],
        out_shape=[
            jax.ShapeDtypeStruct(head.shape, jnp.float32),
            jax.ShapeDtypeStruct((8, depth), jnp.float32),
        ],
        compiler_params=pltpu.CompilerParams(vmem_limit_bytes=VMEM_LIMIT),
    )(rows, facts, targets, head)


def embed_grad_kernel(starts, ids, rows, out, squares):
    at = pl.program_id(0)
    parts = EMBED_BLOCK // EMBED_PART

    @pl.when(at == 0)
    def _():
        squares[...] = jnp.zeros_like(squares)

    for part in range(parts):
        begin = starts[at * parts + part]
        end = starts[at * parts + part + 1]
        base = at * EMBED_BLOCK + part * EMBED_PART
        places = base + lax.broadcasted_iota(jnp.int32, (TOKEN_CHUNK, EMBED_PART), 1)

        def add(chunk, total):
            here = pl.ds(pl.multiple_of(chunk * TOKEN_CHUNK, TOKEN_CHUNK), TOKEN_CHUNK)
            hits = (ids[here, :] == places).astype(jnp.bfloat16)
            return total + first_dot(rows[here, :], hits)

        total = lax.fori_loop(
            begin // TOKEN_CHUNK,
            (end + TOKEN_CHUNK - 1) // TOKEN_CHUNK,
            add,
            jnp.zeros((rows.shape[1], EMBED_PART), jnp.float32),
        )
        out[:, part * EMBED_PART : (part + 1) * EMBED_PART] = total
        squares[...] += total * total


def embed_grads(starts, ids, rows, vocab):
    count, feats = rows.shape
    return pl.pallas_call(
        embed_grad_kernel,
        grid=(pl.cdiv(vocab, EMBED_BLOCK),),
        in_specs=[
            pl.BlockSpec(memory_space=pltpu.SMEM),
            pl.BlockSpec((count, 1), lambda at: (0, 0)),
            pl.BlockSpec((count, feats), lambda at: (0, 0)),
        ],
        out_specs=[
            pl.BlockSpec((feats, EMBED_BLOCK), lambda at: (0, at)),
            pl.BlockSpec((feats, EMBED_PART), lambda at: (0, 0)),
        ],
        out_shape=[
            jax.ShapeDtypeStruct((feats, vocab), jnp.float32),
            jax.ShapeDtypeStruct((feats, EMBED_PART), jnp.float32),
        ],
        compiler_params=pltpu.CompilerParams(vmem_limit_bytes=VMEM_LIMIT),
    )(starts, ids, rows)


def turn_tables(places):
    half_rot = ROT // 2
    lane = jnp.arange(HEAD_COLS) % HD
    exponent = (lane % half_rot).astype(jnp.float32) * (2.0 / ROT)
    angles = places[:, None] * jnp.exp(-exponent * jnp.log(10000.0))[None, :]
    cosine, sine = jnp.cos(angles), jnp.sin(angles)
    lane = lane[None, :]
    return (
        jnp.where(lane < ROT, cosine, 1.0),
        jnp.where(lane < half_rot, -sine, 0.0),
        jnp.where((lane >= half_rot) & (lane < ROT), sine, 0.0),
    )


def turn(rows, tables, sign):
    half_rot = ROT // 2
    own, after, before = tables
    return (
        rows * own
        + sign * jnp.roll(rows, -half_rot, axis=-1) * after
        + sign * jnp.roll(rows, half_rot, axis=-1) * before
    )


def centred_rows(values):
    centred = values - jnp.mean(values, axis=-1, keepdims=True)
    spread = jnp.mean(centred * centred, axis=-1, keepdims=True)
    scale = lax.rsqrt(spread + NORM_EPS)
    return centred * scale, scale


def group_plan(
    token_ids,
    pic_start,
    comp_pos,
    comp_tgt,
    proj_in,
    proj_back,
    small_params,
    head_table,
    embed_table,
    first_in,
    second_in,
    first_back,
    second_back,
    first_small,
    second_small,
    first_head,
    second_head,
    first_embed,
    second_embed,
):
    bf16 = jnp.bfloat16
    rep_at = lax.axis_index("rep")
    shard_at = lax.axis_index("shard")
    micro, _, seq_dev = token_ids.shape
    slots = comp_pos.shape[2]
    seq_len = seq_dev * RG
    lines = micro * SG // RG
    blocks = lines * RG
    own_blocks = blocks // SG
    tokens = lines * seq_len
    slot_count = blocks * slots
    own_slots = own_blocks * slots
    vocab_dev = head_table.shape[1]
    vocab = embed_table.shape[1]
    quarter = D // SG // RG

    place_line = jnp.concatenate([comp_pos[:, 0, :].reshape(-1), comp_tgt[:, 0, :].reshape(-1)])
    span_line = jnp.concatenate([pic_start[:, 0], jnp.zeros((seq_dev - micro,), jnp.int32)])
    ints = jnp.concatenate(
        [token_ids[:, 0, :], place_line[None], span_line[None], jnp.zeros((4, seq_dev), jnp.int32)]
    )
    small_low = small_params.astype(bf16).astype(jnp.float32).reshape(-1, 128)
    small_rows = small_low.shape[0]
    smalls = jnp.pad(small_low, ((0, 16 - small_rows), (0, 0)))
    ints_all, smalls_all = share_facts(ints, smalls, 1)
    wide_small = smalls_all[:, :small_rows].reshape(-1)
    (
        gain_one,
        shift_one,
        gain_two,
        shift_two,
        gain_last,
        shift_last,
        bias_qkv,
        bias_hidden,
        bias_out,
    ) = split_small(wide_small)
    head_cols = [
        lax.dynamic_slice(bias_qkv, (part * D + shard_at * HEAD_COLS,), (HEAD_COLS,)) for part in range(3)
    ]
    own_hidden = lax.dynamic_slice(bias_hidden, (shard_at * UNITS,), (UNITS,))

    by_group = ints_all.reshape(RG, RG, SG // RG, 8, seq_dev)
    ids_all = jnp.transpose(by_group[:, :, :, :micro], (1, 3, 2, 0, 4)).reshape(RG, tokens)
    slot_facts = jnp.transpose(
        by_group[:, :, :, 2].reshape(RG, RG, SG // RG, 2, micro, slots), (3, 1, 4, 2, 0, 5)
    ).reshape(2, RG, slot_count)
    used_all = slot_facts[0] < seq_dev
    targets_all = jnp.where(used_all, slot_facts[1] - shard_at * vocab_dev, -1)
    counted_all = used_all.astype(jnp.float32)
    ids_group = lax.dynamic_index_in_dim(ids_all, rep_at, 0, False)
    pos_group = lax.dynamic_index_in_dim(slot_facts[0], rep_at, 0, False)
    targets_group = lax.dynamic_index_in_dim(targets_all, rep_at, 0, False)
    counted_group = lax.dynamic_index_in_dim(counted_all, rep_at, 0, False)
    spans = lax.dynamic_index_in_dim(by_group[0, :, :, 3, :micro], rep_at, 0, False).T.reshape(lines)

    flat_ids = ids_all.reshape(-1)
    sorted_ids, order = lax.sort((flat_ids, jnp.arange(flat_ids.shape[0], dtype=jnp.int32)), num_keys=1)
    edges = jnp.arange(pl.cdiv(vocab, EMBED_BLOCK) * (EMBED_BLOCK // EMBED_PART) + 1) * EMBED_PART
    starts = jnp.sum((flat_ids[None, :] < edges[:, None]).astype(jnp.int32), axis=1)

    rows = embedding_rows(ids_group, embed_table)
    in_low = proj_in.astype(bf16)
    qkv_parts = in_low[:, : 3 * D].reshape(D // SG, 3, SG, HEAD_COLS)
    in_parts = jnp.concatenate(
        [
            jnp.transpose(qkv_parts, (2, 0, 1, 3)).reshape(SG, D // SG, 3 * HEAD_COLS),
            jnp.transpose(in_low[:, 3 * D :].reshape(D // SG, SG, UNITS), (1, 0, 2)),
        ],
        axis=2,
    ).reshape(SG, 2, D // SG // 2, OWN_COLS)
    back_tiles = proj_back.astype(bf16).reshape(5, 2, 64, D)
    residual_low, in_all, back_all = share_embedding(rows, in_parts, back_tiles, 2)
    own_in = in_all.reshape(D, OWN_COLS)
    own_back = back_all.reshape(5 * 128, D)

    residual = residual_low.astype(jnp.float32)
    unit_rows, unit_scale = centred_rows(residual)
    low_one = (unit_rows * gain_one + shift_one).astype(bf16)
    low_two = (unit_rows * gain_two + shift_two).astype(bf16)
    pick = (pos_group.reshape(blocks, slots, 1) == jnp.arange(seq_dev)[None, None, :]).astype(bf16)

    def pick_rows(values):
        blocked = values.reshape(blocks, seq_dev, values.shape[1])
        return jnp.einsum("bst,btd->bsd", pick, blocked, preferred_element_type=jnp.float32).reshape(
            slot_count, values.shape[1]
        )

    def put_rows(values):
        blocked = values.reshape(blocks, slots, values.shape[1])
        return jnp.einsum("bst,bsd->btd", pick, blocked, preferred_element_type=jnp.float32).reshape(
            tokens, values.shape[1]
        )

    picked_one = pick_rows(low_one).astype(bf16)
    picked_two = pick_rows(low_two).astype(bf16)
    slot_places = (
        (jnp.arange(blocks) % RG * seq_dev)[:, None] + jnp.minimum(pos_group.reshape(blocks, slots), seq_dev - 1)
    ).reshape(-1)
    key_places = jnp.arange(seq_len)
    query_turn = turn_tables(slot_places.astype(jnp.float32))
    key_turn = turn_tables(key_places.astype(jnp.float32))
    key_turn = tuple(jnp.tile(table, (lines, 1)) for table in key_turn)
    queries = turn(plain_dot(picked_one, own_in[:, :HEAD_COLS]) + head_cols[0], query_turn, 1.0).astype(bf16)
    key_values = plain_dot(low_one, own_in[:, HEAD_COLS : 3 * HEAD_COLS])
    keys = turn(key_values[:, :HEAD_COLS] + head_cols[1], key_turn, 1.0).astype(bf16)
    values = (key_values[:, HEAD_COLS:] + head_cols[2]).astype(bf16)
    line_slots = slot_count // lines
    queries = queries.reshape(lines, line_slots, GROUP_HEADS, HD)
    keys = keys.reshape(lines, seq_len, GROUP_HEADS, HD)
    values = values.reshape(lines, seq_len, GROUP_HEADS, HD)
    query_at = slot_places.reshape(lines, line_slots, 1)
    key_at = key_places[None, None, :]
    span_at = spans.reshape(lines, 1, 1)
    in_query = (query_at >= span_at) & (query_at < span_at + PIC)
    in_key = (key_at >= span_at) & (key_at < span_at + PIC)
    allowed = ((key_at <= query_at) | (in_query & in_key))[:, None]
    scores = jnp.einsum("nqhd,nkhd->nhqk", queries, keys, preferred_element_type=jnp.float32) * HD ** (-0.5)
    scores = jnp.where(allowed, scores, -1e30)
    highest = jnp.max(scores, axis=-1, keepdims=True)
    exponent = jnp.exp(scores - highest)
    probs = exponent / jnp.sum(exponent, axis=-1, keepdims=True)
    low_probs = probs.astype(bf16)
    attended = (
        jnp.einsum("nhqk,nkhd->nqhd", low_probs, values, preferred_element_type=jnp.float32)
        .reshape(slot_count, HEAD_COLS)
        .astype(bf16)
    )
    hidden_pre = plain_dot(picked_two, own_in[:, 3 * HEAD_COLS :]) + own_hidden
    activation = gelu_exact(hidden_pre).astype(bf16)
    joined = jnp.concatenate([attended, activation], axis=1)
    branch_parts = plain_dot(joined, own_back).reshape(SG, own_slots, D)
    branch = shard_sum(branch_parts, 3)

    own_pick = lax.dynamic_slice_in_dim(pick, shard_at * own_blocks, own_blocks, 0)
    own_residual = lax.dynamic_slice_in_dim(residual_low, shard_at * own_blocks * seq_dev, own_blocks * seq_dev, 0)
    own_residual = jnp.einsum(
        "bst,btd->bsd", own_pick, own_residual.reshape(own_blocks, seq_dev, D), preferred_element_type=jnp.float32
    ).reshape(own_slots, D)
    own_used = lax.dynamic_slice_in_dim(counted_group, shard_at * own_slots, own_slots, 0)
    after_add = own_residual + branch + bias_out
    final_rows, pull_last = jax.vjp(norm_rows, after_add, gain_last, shift_last)
    picked = (final_rows * own_used[:, None]).astype(bf16)
    rows_group = shard_gather(picked, 4)

    head_turned = head_table.T
    stats, head_low = logit_stats(rows_group, targets_group[None], head_turned)
    stats_all = shard_stats(stats, 5)
    tops = stats_all[:, 0]
    top = jnp.max(tops, axis=0)
    logsum = top + jnp.log(jnp.sum(stats_all[:, 1] * jnp.exp(tops - top), axis=0))
    row_target = jnp.sum(stats_all[:, 2], axis=0)
    facts = jnp.concatenate(
        [logsum[None], counted_group[None], row_target[None], jnp.zeros((5, slot_count), jnp.float32)]
    )
    picked_parts = picked_grads(rows_group, facts, targets_group[None], head_low)
    d_picked, rows_all, facts_all = sum_and_share(
        picked_parts.reshape(SG, own_slots, D), rows_group, facts, 6
    )
    loss_sum = jnp.sum((facts_all[:, 0] - facts_all[:, 2]) * facts_all[:, 1])
    count_sum = jnp.sum(facts_all[:, 1])
    targets_wide = jnp.broadcast_to(targets_all[:, None, :], (RG, 8, slot_count))
    grad_head, head_squares = head_grads(rows_all, facts_all, targets_wide, head_low)

    d_after, d_gain_last, d_shift_last = pull_last(d_picked)
    d_branch_own = d_after.astype(bf16)
    d_bias_out = jnp.sum(d_branch_own.astype(jnp.float32), axis=0)
    pieces = jnp.transpose(d_after.reshape(own_slots, SG, D // SG), (1, 0, 2))
    d_branch, after_pieces = share_branch(d_branch_own, pieces, 7)
    d_after_feats = after_pieces.reshape(slot_count, D // SG)

    d_joined = transposed_dot(d_branch, own_back)
    grad_back = first_dot(joined, d_branch)
    d_attended = d_joined[:, :HEAD_COLS].astype(bf16).reshape(lines, line_slots, GROUP_HEADS, HD)
    _, pull_gelu = jax.vjp(gelu_exact, hidden_pre)
    d_hidden = pull_gelu(d_joined[:, HEAD_COLS:])[0].astype(bf16)
    d_probs = jnp.einsum("nqhd,nkhd->nhqk", d_attended, values, preferred_element_type=jnp.float32)
    d_scores = (probs * (d_probs - jnp.sum(probs * d_probs, axis=-1, keepdims=True))).astype(bf16)
    d_queries = jnp.einsum("nhqk,nkhd->nqhd", d_scores, keys, preferred_element_type=jnp.float32) * HD ** (-0.5)
    d_keys = jnp.einsum("nhqk,nqhd->nkhd", d_scores, queries, preferred_element_type=jnp.float32) * HD ** (-0.5)
    d_values = jnp.einsum("nhqk,nqhd->nkhd", low_probs, d_attended, preferred_element_type=jnp.float32)
    d_query_rows = turn(d_queries.reshape(slot_count, HEAD_COLS), query_turn, -1.0).astype(bf16)
    d_key_rows = turn(d_keys.reshape(tokens, HEAD_COLS), key_turn, -1.0).astype(bf16)
    d_key_values = jnp.concatenate([d_key_rows, d_values.reshape(tokens, HEAD_COLS).astype(bf16)], axis=1)
    grad_in = jnp.concatenate(
        [first_dot(picked_one, d_query_rows), first_dot(low_one, d_key_values), first_dot(picked_two, d_hidden)],
        axis=1,
    )
    d_projected = jnp.concatenate([put_rows(d_query_rows).astype(bf16), d_key_values], axis=1)
    d_hidden_rows = put_rows(d_hidden).astype(bf16)
    d_normed_one = transposed_dot(d_projected, own_in[:, : 3 * HEAD_COLS])
    d_normed_two = transposed_dot(d_hidden_rows, own_in[:, 3 * HEAD_COLS :])
    d_unit = d_normed_one * gain_one + d_normed_two * gain_two
    norm_stats = jnp.stack([jnp.sum(d_unit, axis=1), jnp.sum(d_unit * unit_rows, axis=1)])
    norm_stats = jnp.pad(norm_stats, ((0, 6), (0, 0)))
    unit_parts = jnp.transpose(d_unit.reshape(tokens, SG, D // SG), (1, 0, 2))

    def whole(columns, length):
        start = shard_at * columns.shape[0]
        return lax.dynamic_update_slice(jnp.zeros((length,), jnp.float32), columns, (start,))

    d_bias_parts = [
        jnp.sum(d_query_rows.astype(jnp.float32), axis=0),
        jnp.sum(d_key_rows.astype(jnp.float32), axis=0),
        jnp.sum(d_key_values[:, HEAD_COLS:].astype(jnp.float32), axis=0),
    ]
    grad_small = jnp.concatenate(
        [
            jnp.sum(d_normed_one * unit_rows, axis=0),
            jnp.sum(d_normed_one, axis=0),
            jnp.sum(d_normed_two * unit_rows, axis=0),
            jnp.sum(d_normed_two, axis=0),
            d_gain_last,
            d_shift_last,
            *[whole(part, D) for part in d_bias_parts],
            whole(jnp.sum(d_hidden.astype(jnp.float32), axis=0), FF),
            d_bias_out,
        ]
    )
    grad_small = jnp.pad(grad_small.reshape(SG, small_rows, 128), ((0, 0), (0, 16 - small_rows), (0, 0)))
    in_quarters = jnp.transpose(grad_in.reshape(SG, RG, quarter, OWN_COLS), (1, 0, 2, 3))
    back_quarters = jnp.transpose(grad_back.reshape(5, RG, 32, D), (1, 0, 2, 3))
    d_unit_feats, norm_stats_all, in_sum, back_sum, small_sum = layer_sums(
        unit_parts, norm_stats, in_quarters, back_quarters, grad_small, 8
    )

    norm_sums = jnp.sum(norm_stats_all, axis=0)
    own_unit = lax.dynamic_slice_in_dim(residual_low, shard_at * (D // SG), D // SG, 1).astype(jnp.float32)
    row_mean = jnp.mean(residual, axis=-1, keepdims=True)
    own_unit = (own_unit - row_mean) * unit_scale
    d_rows = (
        d_unit_feats - norm_sums[0][:, None] / D - own_unit * (norm_sums[1][:, None] / D)
    ) * unit_scale
    d_after_rows = jnp.einsum(
        "bst,bsd->btd",
        pick.astype(jnp.float32),
        d_after_feats.reshape(blocks, slots, D // SG),
        precision=lax.Precision.HIGHEST,
    ).reshape(tokens, D // SG)
    d_rows = (d_after_rows + d_rows).astype(bf16)
    d_rows_all, in_grads, back_grads = return_sums(d_rows, in_sum, back_sum, 9)
    d_sorted = jnp.take(d_rows_all.reshape(RG * tokens, D // SG), order, axis=0)
    grad_embed, embed_squares = embed_grads(starts, sorted_ids[:, None], d_sorted, vocab)

    in_grads = jnp.transpose(in_grads, (0, 2, 1, 3)).reshape(D // SG, SG, OWN_COLS)
    qkv_grads = jnp.transpose(
        in_grads[:, :, : 3 * HEAD_COLS].reshape(D // SG, SG, 3, HEAD_COLS), (0, 2, 1, 3)
    ).reshape(D // SG, 3 * D)
    grad_in = jnp.concatenate([qkv_grads, in_grads[:, :, 3 * HEAD_COLS :].reshape(D // SG, FF)], axis=1)
    grad_back = jnp.transpose(back_grads, (1, 0, 2, 3)).reshape(proj_back.shape)
    grad_small = small_sum[:small_rows].reshape(-1)

    local_square = (
        jnp.sum(grad_in * grad_in)
        + jnp.sum(grad_back * grad_back)
        + jnp.sum(grad_small * grad_small)
        + jnp.sum(head_squares)
        + jnp.sum(embed_squares)
    )
    squares_all = shard_stats(jnp.broadcast_to(local_square, (8, 128)), 10)
    norm_value = jnp.sqrt(jnp.sum(squares_all[:, 0, 0]))
    factor = CLIP_LEVEL / jnp.maximum(norm_value, CLIP_LEVEL)
    next_in, moment_in, square_in = adamw(proj_in, grad_in * factor, first_in, second_in, RATE_IN)
    next_back, moment_back, square_back = adamw(
        proj_back, grad_back * factor, first_back, second_back, RATE_BACK
    )
    next_small, moment_small, square_small = adamw(
        small_params, grad_small * factor, first_small, second_small, RATE_SMALL
    )
    next_head, moment_head, square_head = adamw(
        head_table, grad_head.T * factor, first_head, second_head, RATE_HEAD
    )
    next_embed, moment_embed, square_embed = adamw(
        embed_table, grad_embed * factor, first_embed, second_embed, RATE_EMBED
    )
    return (
        jnp.stack([loss_sum, count_sum]),
        norm_value.reshape(1),
        next_in,
        moment_in,
        square_in,
        next_back,
        moment_back,
        square_back,
        next_small,
        moment_small,
        square_small,
        next_head,
        moment_head,
        square_head,
        next_embed,
        moment_embed,
        square_embed,
    )


def select_plan(mesh):
    if mesh.shape["rep"] == RG and mesh.shape["shard"] == SG:
        return group_plan
    return any_mesh


def solution(mesh):
    placed = (
        P(None, "shard", "rep"),
        P(None, "shard"),
        P(None, "shard", "rep"),
        P(None, "shard", "rep"),
        P("shard", None),
        P("shard", None),
        P("shard"),
        P(None, "shard"),
        P("shard", None),
        P("shard", None),
        P("shard", None),
        P("shard", None),
        P("shard", None),
        P("shard"),
        P("shard"),
        P(None, "shard"),
        P(None, "shard"),
        P("shard", None),
        P("shard", None),
    )
    return jax.shard_map(
        select_plan(mesh),
        mesh=mesh,
        in_specs=placed,
        out_specs=(
            P(),
            P(),
            P("shard", None),
            P("shard", None),
            P("shard", None),
            P("shard", None),
            P("shard", None),
            P("shard", None),
            P("shard"),
            P("shard"),
            P("shard"),
            P(None, "shard"),
            P(None, "shard"),
            P(None, "shard"),
            P("shard", None),
            P("shard", None),
            P("shard", None),
        ),
        check_vma=False,
    )
```

```python
import functools

import jax
import jax.numpy as jnp
from jax import lax
from jax.experimental import pallas as pl
from jax.experimental.pallas import tpu as pltpu
from jax.sharding import PartitionSpec as P

D = 1024
H = 16
HD = 64
ROT = 16
FF = 4096
PIC = 256
STEP = 10


NORM_EPS = 1e-05
CLIP_LEVEL = 1.0
BETA_FIRST = 0.9
BETA_SECOND = 0.95
ADAM_EPS = 1e-08
DECAY_RATE = 0.01
RATE_IN = 0.01
RATE_BACK = 0.05
RATE_SMALL = 0.3
RATE_HEAD = 0.01
RATE_EMBED = 0.3


def combined_all(part, axis, combine):
    gathered = jax.tree.map(lambda a: lax.all_gather(a, axis), part)

    def take(source):
        return jax.tree.map(lambda a: lax.dynamic_index_in_dim(a, source, 0, False), gathered)

    return lax.fori_loop(
        1, lax.axis_size(axis), lambda source, state: combine(state, take(source)), take(0)
    )


def norm_rows(values, gain_vec, shift_vec):
    centred = values - jnp.mean(values, axis=-1, keepdims=True)
    spread = jnp.mean(centred * centred, axis=-1, keepdims=True)
    return centred * lax.rsqrt(spread + NORM_EPS) * gain_vec + shift_vec


def rotate(head_rows, place_vec):
    half_rot = ROT // 2
    exponent = jnp.arange(half_rot).astype(jnp.float32) * (2.0 / ROT)
    angles = place_vec[:, None] * jnp.exp(-exponent * jnp.log(10000.0))
    cosine = jnp.cos(angles)[:, None, :]
    sine_part = jnp.sin(angles)[:, None, :]
    front_part = head_rows[..., :half_rot]
    back_part = head_rows[..., half_rot:ROT]
    return jnp.concatenate(
        [
            front_part * cosine - back_part * sine_part,
            back_part * cosine + front_part * sine_part,
            head_rows[..., ROT:],
        ],
        axis=-1,
    )


def split_small(gain_parts):
    marks = [0, D, 2 * D, 3 * D, 4 * D, 5 * D, 6 * D, 9 * D, 9 * D + FF, 10 * D + FF]
    return tuple((gain_parts[marks[number] : marks[number + 1]] for number in range(9)))


def gelu_exact(values):
    return jax.nn.gelu(values, approximate=False)


def combine_totals(earlier, later_part):
    highest = jnp.maximum(earlier[0], later_part[0])
    totals = earlier[1] * jnp.exp(earlier[0] - highest) + later_part[1] * jnp.exp(
        later_part[0] - highest
    )
    return (highest, totals, earlier[2] + later_part[2])


def allowed_mask(query_places, key_places, span_start):
    inside_query = (query_places >= span_start) & (query_places < span_start + PIC)
    inside_key = (key_places >= span_start) & (key_places < span_start + PIC)
    return (key_places[None, :] <= query_places[:, None]) | inside_query[:, None] & inside_key[
        None, :
    ]


def masked_scores(queries, keys_all, allowed):
    raw_scores = jnp.einsum(
        "qhd,khd->hqk", queries, keys_all, preferred_element_type=jnp.float32
    ) * HD ** (-0.5)
    return jnp.where(allowed[None], raw_scores, -1e30)


def adamw(weight, gradient, moment, square, rate_value):
    moment = BETA_FIRST * moment + (1.0 - BETA_FIRST) * gradient
    square = BETA_SECOND * square + (1.0 - BETA_SECOND) * gradient * gradient
    moment_hat = moment / (1.0 - BETA_FIRST**STEP)
    square_hat = square / (1.0 - BETA_SECOND**STEP)
    weight = weight - rate_value * (
        moment_hat / (jnp.sqrt(square_hat) + ADAM_EPS) + DECAY_RATE * weight
    )
    return (weight, moment, square)


def any_mesh(
    token_ids,
    pic_start,
    comp_pos,
    comp_tgt,
    proj_in,
    proj_back,
    small_params,
    head_table,
    embed_table,
    first_in,
    second_in,
    first_back,
    second_back,
    first_small,
    second_small,
    first_head,
    second_head,
    first_embed,
    second_embed,
):
    seq_dev = token_ids.shape[2]
    micro_count = token_ids.shape[0]
    vocab_dev = head_table.shape[1]
    rep_count = lax.axis_size("rep")
    seq_len = seq_dev * rep_count
    rep_at = lax.axis_index("rep")
    shard_at = lax.axis_index("shard")
    used_own = comp_pos[:, 0, :] < seq_dev
    marked = jnp.where(used_own, comp_tgt[:, 0, :], -1)
    ids_group, tgt_group = (
        lax.all_gather(token_ids[:, 0, :], "shard", axis=1, tiled=True),
        lax.all_gather(marked, "shard", axis=1, tiled=True),
    )
    in_low = proj_in.astype(jnp.bfloat16)
    back_low = proj_back.astype(jnp.bfloat16)
    small_low = small_params.astype(jnp.bfloat16)
    head_low = head_table.astype(jnp.bfloat16)
    table_low = embed_table.astype(jnp.bfloat16)
    own_places = rep_at * seq_dev + jnp.arange(seq_dev)
    key_places = jnp.arange(seq_len)
    own_float = own_places.astype(jnp.float32)
    vocab_ids = jnp.arange(vocab_dev)
    grad_in = jnp.zeros((D, 3 * D + FF), jnp.float32)
    grad_back = jnp.zeros((D + FF, D), jnp.float32)
    grad_small = jnp.zeros((10 * D + FF,), jnp.float32)
    grad_head = jnp.zeros(head_table.shape, jnp.float32)
    grad_embed = jnp.zeros(embed_table.shape, jnp.float32)
    loss_sum = jnp.zeros((), jnp.float32)
    count_sum = jnp.zeros((), jnp.float32)
    for micro_at in range(micro_count):
        wide_in, wide_back, wide_small = (
            lax.all_gather(in_low, "shard", axis=0, tiled=True),
            lax.all_gather(back_low, "shard", axis=0, tiled=True),
            lax.all_gather(small_low, "shard", axis=0, tiled=True),
        )
        (
            gain_one,
            shift_one,
            gain_two,
            shift_two,
            gain_last,
            shift_last,
            bias_qkv,
            bias_hidden,
            bias_out,
        ) = split_small(wide_small.astype(jnp.float32))
        columns = jnp.take(table_low, ids_group[micro_at], axis=1)
        arrived = lax.all_to_all(columns, "shard", split_axis=1, concat_axis=0, tiled=True)
        residual = arrived.T.astype(jnp.float32)
        normed_one = norm_rows(residual, gain_one, shift_one)
        normed_two = norm_rows(residual, gain_two, shift_two)
        low_one = normed_one.astype(jnp.bfloat16)
        low_two = normed_two.astype(jnp.bfloat16)
        projected = (
            jnp.dot(low_one, wide_in[:, : 3 * D], preferred_element_type=jnp.float32) + bias_qkv
        )
        queries = rotate(projected[:, :D].reshape(seq_dev, H, HD), own_float).astype(jnp.bfloat16)
        key_rows = (
            rotate(projected[:, D : 2 * D].reshape(seq_dev, H, HD), own_float)
            .astype(jnp.bfloat16)
            .reshape(seq_dev, D)
        )
        value_rows = projected[:, 2 * D :].astype(jnp.bfloat16)
        keys_all, values_all = (
            lax.all_gather(key_rows, "rep", axis=0, tiled=True),
            lax.all_gather(value_rows, "rep", axis=0, tiled=True),
        )
        keys_all = keys_all.reshape(seq_len, H, HD)
        values_all = values_all.reshape(seq_len, H, HD)
        allowed = allowed_mask(own_places, key_places, pic_start[micro_at, 0])
        scores = masked_scores(queries, keys_all, allowed)
        highest = jnp.max(scores, axis=-1, keepdims=True)
        exponent = jnp.exp(scores - highest)
        totals = jnp.sum(exponent, axis=-1, keepdims=True)
        logsum = highest + jnp.log(totals)
        attn_probs = (exponent / totals).astype(jnp.bfloat16)
        attended = (
            jnp.einsum("hqk,khd->qhd", attn_probs, values_all, preferred_element_type=jnp.float32)
            .reshape(seq_dev, D)
            .astype(jnp.bfloat16)
        )
        hidden_pre = (
            jnp.dot(low_two, wide_in[:, 3 * D :], preferred_element_type=jnp.float32) + bias_hidden
        )
        activation = gelu_exact(hidden_pre).astype(jnp.bfloat16)
        joined = jnp.concatenate([attended, activation], axis=1)
        after_add = (
            residual + jnp.dot(joined, wide_back, preferred_element_type=jnp.float32) + bias_out
        )
        final_rows = norm_rows(after_add, gain_last, shift_last)
        places = comp_pos[micro_at, 0]
        used_slots = (places < seq_dev).astype(jnp.float32)
        picked = (
            jnp.take(final_rows, jnp.minimum(places, seq_dev - 1), axis=0) * used_slots[:, None]
        ).astype(jnp.bfloat16)
        rows_all = lax.all_gather(picked, "shard", axis=0, tiled=True)
        logits = jnp.dot(rows_all, head_low, preferred_element_type=jnp.float32)
        targets = tgt_group[micro_at]
        matches = (targets - shard_at * vocab_dev)[:, None] == vocab_ids[None, :]
        row_top = jnp.max(logits, axis=1)
        row_total = jnp.sum(jnp.exp(logits - row_top[:, None]), axis=1)
        row_target = jnp.sum(jnp.where(matches, logits, 0.0), axis=1)
        row_top, row_total, row_target = combined_all(
            (row_top, row_total, row_target), "shard", combine_totals
        )
        logsum_rows = row_top + jnp.log(row_total)
        counted = (targets >= 0).astype(jnp.float32)
        loss_sum = loss_sum + jnp.sum((logsum_rows - row_target) * counted)
        count_sum = count_sum + jnp.sum(counted)
        d_logits = (
            (jnp.exp(logits - logsum_rows[:, None]) - matches.astype(jnp.float32))
            * counted[:, None]
        ).astype(jnp.bfloat16)
        grad_head = grad_head + jnp.einsum(
            "rd,rv->dv", rows_all, d_logits, preferred_element_type=jnp.float32
        )
        d_picked = lax.psum_scatter(
            jnp.einsum("rv,dv->rd", d_logits, head_low, preferred_element_type=jnp.float32),
            "shard",
            scatter_dimension=0,
            tiled=True,
        )
        d_final = jnp.zeros((seq_dev, D), jnp.float32).at[places].add(d_picked, mode="drop")
        back_in, back_back = (
            lax.all_gather(in_low, "shard", axis=0, tiled=True),
            lax.all_gather(back_low, "shard", axis=0, tiled=True),
        )
        _, pull_last = jax.vjp(norm_rows, after_add, gain_last, shift_last)
        d_after, d_gain_last, d_shift_last = pull_last(d_final)
        d_branch = d_after.astype(jnp.bfloat16)
        grad_back = grad_back + jnp.einsum(
            "sc,sd->cd", joined, d_branch, preferred_element_type=jnp.float32
        )
        d_joined = jnp.einsum("sd,cd->sc", d_branch, back_back, preferred_element_type=jnp.float32)
        d_attended = d_joined[:, :D].astype(jnp.bfloat16).reshape(seq_dev, H, HD)
        _, pull_gelu = jax.vjp(gelu_exact, hidden_pre)
        d_hidden = pull_gelu(d_joined[:, D:])[0].astype(jnp.bfloat16)
        probs_again = jnp.exp(masked_scores(queries, keys_all, allowed) - logsum)
        d_probs = jnp.einsum(
            "qhd,khd->hqk", d_attended, values_all, preferred_element_type=jnp.float32
        )
        d_scores = (
            probs_again * (d_probs - jnp.sum(probs_again * d_probs, axis=-1, keepdims=True))
        ).astype(jnp.bfloat16)
        d_queries = jnp.einsum(
            "hqk,khd->qhd", d_scores, keys_all, preferred_element_type=jnp.float32
        ) * HD ** (-0.5)
        low_probs = probs_again.astype(jnp.bfloat16)
        d_keys = jnp.einsum(
            "hqk,qhd->khd", d_scores, queries, preferred_element_type=jnp.float32
        ) * HD ** (-0.5)
        d_values = jnp.einsum(
            "hqk,qhd->khd", low_probs, d_attended, preferred_element_type=jnp.float32
        )
        key_grads = lax.psum_scatter(
            jnp.concatenate(
                [
                    d_keys.reshape(seq_dev * lax.axis_size("rep"), D),
                    d_values.reshape(seq_dev * lax.axis_size("rep"), D),
                ],
                axis=1,
            ),
            "rep",
            scatter_dimension=0,
            tiled=True,
        )
        d_key_rows = rotate(key_grads[:, :D].reshape(seq_dev, H, HD), -own_float).reshape(
            seq_dev, D
        )
        d_query_rows = rotate(d_queries, -own_float).reshape(seq_dev, D)
        d_projected = jnp.concatenate([d_query_rows, d_key_rows, key_grads[:, D:]], axis=1).astype(
            jnp.bfloat16
        )
        grad_in = grad_in + jnp.concatenate(
            [
                jnp.einsum("sd,sc->dc", low_one, d_projected, preferred_element_type=jnp.float32),
                jnp.einsum("sd,sc->dc", low_two, d_hidden, preferred_element_type=jnp.float32),
            ],
            axis=1,
        )
        d_normed_one = jnp.einsum(
            "sc,dc->sd", d_projected, back_in[:, : 3 * D], preferred_element_type=jnp.float32
        )
        d_normed_two = jnp.einsum(
            "sc,dc->sd", d_hidden, back_in[:, 3 * D :], preferred_element_type=jnp.float32
        )
        _, pull_one = jax.vjp(norm_rows, residual, gain_one, shift_one)
        d_resid_one, d_gain_one, d_shift_one = pull_one(d_normed_one)
        _, pull_two = jax.vjp(norm_rows, residual, gain_two, shift_two)
        d_resid_two, d_gain_two, d_shift_two = pull_two(d_normed_two)
        d_residual = (d_after + d_resid_one + d_resid_two).astype(jnp.bfloat16)
        returned = lax.all_to_all(d_residual.T, "shard", split_axis=0, concat_axis=1, tiled=True)
        grad_embed = grad_embed.at[:, ids_group[micro_at]].add(returned.astype(jnp.float32))
        grad_small = grad_small + jnp.concatenate(
            [
                d_gain_one,
                d_shift_one,
                d_gain_two,
                d_shift_two,
                d_gain_last,
                d_shift_last,
                jnp.sum(d_projected.astype(jnp.float32), axis=0),
                jnp.sum(d_hidden.astype(jnp.float32), axis=0),
                jnp.sum(d_branch.astype(jnp.float32), axis=0),
            ]
        )
    shard_in, shard_back, shard_small = (
        lax.psum_scatter(grad_in, "shard", scatter_dimension=0, tiled=True),
        lax.psum_scatter(grad_back, "shard", scatter_dimension=0, tiled=True),
        lax.psum_scatter(grad_small, "shard", scatter_dimension=0, tiled=True),
    )
    summed = lax.psum(
        (shard_in, shard_back, shard_small, grad_head, grad_embed, loss_sum, count_sum), "rep"
    )
    local_square = (
        jnp.sum(summed[0] * summed[0])
        + jnp.sum(summed[1] * summed[1])
        + jnp.sum(summed[2] * summed[2])
        + jnp.sum(summed[3] * summed[3])
        + jnp.sum(summed[4] * summed[4])
    )
    norm_value = jnp.sqrt(lax.psum(local_square, "shard"))
    factor = CLIP_LEVEL / jnp.maximum(norm_value, CLIP_LEVEL)
    next_in, moment_in, square_in = adamw(proj_in, summed[0] * factor, first_in, second_in, RATE_IN)
    next_back, moment_back, square_back = adamw(
        proj_back, summed[1] * factor, first_back, second_back, RATE_BACK
    )
    next_small, moment_small, square_small = adamw(
        small_params, summed[2] * factor, first_small, second_small, RATE_SMALL
    )
    next_head, moment_head, square_head = adamw(
        head_table, summed[3] * factor, first_head, second_head, RATE_HEAD
    )
    next_embed, moment_embed, square_embed = adamw(
        embed_table, summed[4] * factor, first_embed, second_embed, RATE_EMBED
    )
    return (
        jnp.stack([summed[5], summed[6]]),
        norm_value.reshape(1),
        next_in,
        moment_in,
        square_in,
        next_back,
        moment_back,
        square_back,
        next_small,
        moment_small,
        square_small,
        next_head,
        moment_head,
        square_head,
        next_embed,
        moment_embed,
        square_embed,
    )


MESH = pl.DeviceIdType.MESH
RG = 4
SG = 8


def whereabouts():
    rep = lax.axis_index("rep")
    shard = lax.axis_index("shard")
    core_twin = rep + 1 - 2 * lax.rem(rep, 2)
    x_twin = lax.rem(rep + 2, RG)
    y_twin = shard + 1 - 2 * lax.rem(shard, 2)
    return rep, shard, core_twin, x_twin, y_twin


def z_peer(shard, step):
    return lax.rem(shard + 2 * step, SG)


def shard_peer(shard, step):
    return lax.rem(shard + step, SG)


def greet(partners):
    barrier = pltpu.get_barrier_semaphore()
    for partner in partners:
        pl.semaphore_signal(barrier, inc=1, device_id=partner, device_id_type=MESH)
    pl.semaphore_wait(barrier, len(partners))


def remote(src, dst, send_sem, recv_sem, partner):
    return pltpu.make_async_remote_copy(
        src_ref=src,
        dst_ref=dst,
        send_sem=send_sem,
        recv_sem=recv_sem,
        device_id=partner,
        device_id_type=MESH,
    )


def comm_call(kernel, out_shape, scratch, number, args, spaces=None, out_spaces=None, limit=None, grid=()):
    pick = {
        "a": pl.BlockSpec(memory_space=pl.ANY),
        "v": pl.BlockSpec(memory_space=pltpu.VMEM),
    }
    choose = lambda space: pick[space] if isinstance(space, str) else space
    spaces = spaces or "a" * len(args)
    out_spaces = out_spaces or "a" * len(out_shape)
    return pl.pallas_call(
        kernel,
        grid=grid,
        out_shape=out_shape,
        in_specs=[choose(space) for space in spaces],
        out_specs=[choose(space) for space in out_spaces],
        scratch_shapes=scratch,
        compiler_params=pltpu.CompilerParams(
            collective_id=number, has_side_effects=True, vmem_limit_bytes=limit
        ),
    )(*args)


def start_gather(source, out, slot, place, sems):
    send_z, recv_z, send_y, recv_y, own = sems
    rep, shard, _, _, y_twin = place
    keep = pltpu.make_async_copy(source, slot(out, shard), own)
    keep.start()
    first_y = remote(source, slot(out, shard), send_y.at[0], recv_y.at[0], (rep, y_twin))
    z_copies = [
        remote(source, slot(out, shard), send_z.at[step - 1], recv_z.at[step - 1], (rep, z_peer(shard, step)))
        for step in range(1, 4)
    ]
    for copy in z_copies:
        copy.start()
    first_y.start()
    return keep, first_y, z_copies


def finish_gather(started, out, slot, place, sems):
    send_z, recv_z, send_y, recv_y, own = sems
    rep, shard, _, _, y_twin = place
    keep, first_y, z_copies = started
    passed = []
    for step in range(1, 4):
        z_copies[step - 1].wait_recv()
        came_from = z_peer(shard, SG // 2 - step)
        passed.append(
            remote(slot(out, came_from), slot(out, came_from), send_y.at[step], recv_y.at[step], (rep, y_twin))
        )
        passed[-1].start()
    keep.wait()
    for copy in z_copies:
        copy.wait_send()
    first_y.wait()
    for copy in passed:
        copy.wait()


def gather_partners(place):
    rep, shard, _, _, y_twin = place
    return [(rep, z_peer(shard, step)) for step in range(1, 4)] + [(rep, y_twin)]


GATHER_SEMS = [pltpu.SemaphoreType.DMA((3,)), pltpu.SemaphoreType.DMA((3,)), pltpu.SemaphoreType.DMA((4,)), pltpu.SemaphoreType.DMA((4,)), pltpu.SemaphoreType.DMA]


def row_slot(out, index):
    height = out.shape[0] // SG
    return out.at[pl.ds(pl.multiple_of(index * height, height), height)]


def tile_user(tile):
    return jnp.where(tile < SG, tile, (tile - SG) // 4)


def tile_slot(tile):
    return jnp.where(tile < SG, 0, 1 + lax.rem(tile - SG + SG, 4))


def entry_kernel(
    ints, smalls, in_parts, back_tiles, table,
    ints_out, smalls_out, out, in_all, back_all,
    ints_all, smalls_all, turned, wide, low, ids,
    send_int, recv_int, send_small, recv_small, send_rep, recv_rep,
    send_in, recv_in, send_back, recv_back, send_pair, recv_pair,
    send_z, recv_z, send_y, recv_y, own,
):
    at = pl.program_id(0)
    rep, shard, core_twin, _, y_twin = whereabouts()
    half = lax.rem(rep, 2)
    shard_peers = [(rep, shard_peer(shard, step)) for step in range(1, SG)]
    rep_peers = [(lax.rem(rep + step, RG), shard) for step in range(1, RG)]
    lines = low.shape[0]
    tokens = low.shape[1]

    def int_copies():
        return [
            remote(ints, ints_all.at[rep, shard], send_int.at[k], recv_int.at[k], peer)
            for k, peer in enumerate(shard_peers)
        ]

    def small_copies():
        return [
            remote(smalls, smalls_all.at[shard], send_small.at[k], recv_small.at[k], peer)
            for k, peer in enumerate(shard_peers)
        ]

    def rep_copies():
        return [
            remote(ints_all.at[rep], ints_all.at[rep], send_rep.at[k], recv_rep.at[k], peer)
            for k, peer in enumerate(rep_peers)
        ]

    def in_copies():
        return [
            remote(in_parts.at[peer[1], half], in_all.at[shard, half], send_in.at[k], recv_in.at[k], peer)
            for k, peer in enumerate(shard_peers)
        ]

    def own_in():
        return pltpu.make_async_copy(in_parts.at[shard, half], in_all.at[shard, half], own.at[0])

    def back_move(k):
        tile = 5 * shard + k
        user, slot = tile_user(tile), tile_slot(tile)
        there = remote(
            back_tiles.at[k, half], back_all.at[slot, half], send_back.at[k], recv_back.at[slot], (rep, user)
        )
        return user, slot, there

    @pl.when(at == 0)
    def _():
        greet(shard_peers + rep_peers)
        for copy in int_copies() + small_copies() + in_copies():
            copy.start()
        own_in().start()
        for k in range(5):
            user, slot, there = back_move(k)
            here = pltpu.make_async_copy(back_tiles.at[k, half], back_all.at[slot, half], recv_back.at[slot])
            pl.when(user == shard)(here.start)
            pl.when(user != shard)(there.start)
        ints_all[rep, shard] = ints[...]
        smalls_all[shard] = smalls[...]

    block = table[...].astype(jnp.bfloat16).astype(jnp.float32)
    width = block.shape[1]
    turned[pl.ds(pl.multiple_of(at * width, width), width), :] = block.T

    @pl.when(at == 4)
    def _():
        for copy in int_copies():
            copy.wait()
        for copy in rep_copies():
            copy.start()

    @pl.when(at == pl.num_programs(0) - 1)
    def _():
        for copy in rep_copies():
            copy.wait()
        to_scalars = pltpu.make_async_copy(ints_all.at[:, pl.ds(2 * rep, 2)], ids, own.at[1])
        to_scalars.start()
        to_scalars.wait()

        def slot(index, line):
            return out.at[
                pl.ds(line * tokens, tokens),
                pl.ds(pl.multiple_of(index * low.shape[2], low.shape[2]), low.shape[2]),
            ]

        def line_copies(line):
            z_copies = [
                remote(low.at[line], slot(shard, line), send_z.at[line, k - 1], recv_z.at[line, k - 1], (rep, z_peer(shard, k)))
                for k in range(1, 4)
            ]
            first_y = remote(low.at[line], slot(shard, line), send_y.at[line, 0], recv_y.at[line, 0], (rep, y_twin))
            keep = pltpu.make_async_copy(low.at[line], slot(shard, line), own.at[2 + line])
            return z_copies, first_y, keep

        started = []
        for line in range(lines):
            micro, member = line // 2, line % 2
            for block_at in range(RG):

                @pl.loop(0, 16)
                def _(group):
                    for k in range(8):
                        lane = group * 8 + k
                        wide[pl.ds(block_at * 128 + lane, 1), :] = turned[
                            pl.ds(ids[block_at, member, micro, lane], 1), :
                        ]

            low[line] = wide[...].astype(jnp.bfloat16)
            z_copies, first_y, keep = line_copies(line)
            for copy in z_copies + [first_y, keep]:
                copy.start()
            started.append((z_copies, first_y, keep))
        passed = []
        for line in range(lines):
            for k in range(1, 4):
                started[line][0][k - 1].wait_recv()
                came_from = z_peer(shard, 4 - k)
                copy = remote(
                    slot(came_from, line), slot(came_from, line), send_y.at[line, k], recv_y.at[line, k], (rep, y_twin)
                )
                copy.start()
                passed.append(copy)
        own_in().wait()
        for copy in in_copies():
            copy.wait()
        for k in range(5):
            pltpu.make_async_copy(back_tiles.at[0, half], back_all.at[k, half], recv_back.at[k]).wait()
        pair_in = remote(in_all.at[:, half], in_all.at[:, half], send_pair.at[0], recv_pair.at[0], (core_twin, shard))
        pair_back = remote(back_all.at[:, half], back_all.at[:, half], send_pair.at[1], recv_pair.at[1], (core_twin, shard))
        pair_in.start()
        pair_back.start()
        for copy in small_copies():
            copy.wait()
        ints_out[...] = ints_all[...]
        smalls_out[...] = smalls_all[...]
        for k in range(5):
            user, _, there = back_move(k)
            pl.when(user != shard)(there.wait_send)
        for z_copies, first_y, keep in started:
            keep.wait()
            first_y.wait()
            for copy in z_copies:
                copy.wait_send()
        for copy in passed:
            copy.wait()
        pair_in.wait()
        pair_back.wait()


def share_entry(ints, smalls, in_parts, back_tiles, table, tokens, number):
    dma = pltpu.SemaphoreType.DMA
    feats, vocab = table.shape
    blocks = pl.cdiv(vocab, TABLE_BLOCK)
    lines = 4
    per_line = tokens // lines
    return comm_call(
        entry_kernel,
        [
            jax.ShapeDtypeStruct((RG, SG) + ints.shape, ints.dtype),
            jax.ShapeDtypeStruct((SG,) + smalls.shape, smalls.dtype),
            jax.ShapeDtypeStruct((tokens, SG * feats), jnp.bfloat16),
            jax.ShapeDtypeStruct(in_parts.shape, in_parts.dtype),
            jax.ShapeDtypeStruct(back_tiles.shape, back_tiles.dtype),
        ],
        [
            pltpu.VMEM((RG, SG) + ints.shape, ints.dtype),
            pltpu.VMEM((SG,) + smalls.shape, smalls.dtype),
            pltpu.VMEM((blocks * TABLE_BLOCK, feats), jnp.float32),
            pltpu.VMEM((per_line, feats), jnp.float32),
            pltpu.VMEM((lines, per_line, feats), jnp.bfloat16),
            pltpu.SMEM((RG, 2) + ints.shape, jnp.int32),
        ]
        + [dma((SG - 1,))] * 4
        + [dma((RG - 1,))] * 2
        + [dma((SG - 1,))] * 2
        + [dma((5,))] * 2
        + [dma((2,))] * 2
        + [dma((lines, 3))] * 2
        + [dma((lines, 4))] * 2
        + [dma((2 + lines,))],
        number,
        (ints, smalls, in_parts, back_tiles, table),
        ["v", "v", "a", "a", pl.BlockSpec((feats, TABLE_BLOCK), lambda at: (0, at))],
        "vvaaa",
        VMEM_LIMIT,
        (blocks,),
    )


def gather_kernel(rows, out, *sems):
    place = whereabouts()
    greet(gather_partners(place))
    started = start_gather(rows, out, row_slot, place, sems)
    finish_gather(started, out, row_slot, place, sems)


def shard_gather(rows, number):
    return comm_call(
        gather_kernel,
        [jax.ShapeDtypeStruct((SG * rows.shape[0], rows.shape[1]), rows.dtype)],
        GATHER_SEMS,
        number,
        (rows,),
        "v",
        "v",
    )[0]


def stats_kernel(stats, out, send, recv):
    rep, shard, _, _, _ = whereabouts()
    peers = [(rep, shard_peer(shard, step)) for step in range(1, SG)]
    greet(peers)
    copies = [remote(stats, out.at[shard], send.at[at], recv.at[at], peer) for at, peer in enumerate(peers)]
    for copy in copies:
        copy.start()
    out[shard] = stats[...]
    for copy in copies:
        copy.wait()


def shard_stats(stats, number):
    dma = pltpu.SemaphoreType.DMA
    return comm_call(
        stats_kernel,
        [jax.ShapeDtypeStruct((SG,) + stats.shape, stats.dtype)],
        [dma((SG - 1,)), dma((SG - 1,))],
        number,
        (stats,),
        "v",
        "v",
    )[0]


def sum_sems():
    dma = pltpu.SemaphoreType.DMA
    return [dma((4,)), dma((4,)), dma((3,)), dma((3,))]


def sum_buffers(chunk):
    return [pltpu.VMEM((4,) + chunk, jnp.float32), pltpu.VMEM((4,) + chunk, jnp.float32), pltpu.VMEM((3,) + chunk, jnp.float32)]


def start_sum(parts, place, buffers, sems):
    rep, shard, _, _, y_twin = place
    from_y, own_sum, from_z = buffers
    send_y, recv_y, send_z, recv_z = sems
    y_copies = {}
    for step in (2, 1, 3, 0):
        y_copies[step] = remote(
            parts.at[z_peer(y_twin, step)], from_y.at[step], send_y.at[step], recv_y.at[step], (rep, y_twin)
        )
        y_copies[step].start()
    return y_copies


def finish_sum(y_copies, parts, out, place, buffers, sems, post=None):
    rep, shard, _, _, y_twin = place
    from_y, own_sum, from_z = buffers
    send_y, recv_y, send_z, recv_z = sems
    z_copies = []
    for step in (2, 1, 3):
        y_copies[step].wait_recv()
        own_sum[step] = parts[z_peer(shard, step)] + from_y[step]
        z_copies.append(
            remote(own_sum.at[step], from_z.at[step - 1], send_z.at[step - 1], recv_z.at[step - 1], (rep, z_peer(shard, step)))
        )
        z_copies[-1].start()
    y_copies[0].wait_recv()
    total = parts[shard] + from_y[0]
    for copy in z_copies:
        copy.wait_recv()
    out[...] = total + from_z[0] + from_z[1] + from_z[2]
    for step in range(4):
        y_copies[step].wait_send()
    for copy in z_copies:
        copy.wait_send()


def sum_kernel(parts, out, from_y, own_sum, from_z, *sems):
    place = whereabouts()
    greet(gather_partners(place))
    buffers = (from_y, own_sum, from_z)
    y_copies = start_sum(parts, place, buffers, sems)
    finish_sum(y_copies, parts, out, place, buffers, sems)


def shard_sum(parts, number):
    chunk = parts.shape[1:]
    return comm_call(
        sum_kernel,
        [jax.ShapeDtypeStruct(chunk, jnp.float32)],
        sum_buffers(chunk) + sum_sems(),
        number,
        (parts,),
        "v",
        "v",
        40 << 20,
    )[0]


def picked_kernel(parts, rows, facts, out, rows_all, facts_all, from_y, own_sum, from_z, *sems):
    place = whereabouts()
    rep, shard, core_twin, x_twin, _ = place
    sum_sem = sems[:4]
    send_row, recv_row, send_fact, recv_fact, own = sems[4:]
    rep_peers = [(lax.rem(rep + step, RG), shard) for step in range(1, RG)]
    greet(gather_partners(place) + rep_peers)
    buffers = (from_y, own_sum, from_z)
    y_copies = start_sum(parts, place, buffers, sum_sem)
    keep = pltpu.make_async_copy(rows, rows_all.at[rep], own)
    keep.start()
    to_x = remote(rows, rows_all.at[rep], send_row.at[0], recv_row.at[0], (x_twin, shard))
    to_core = remote(rows, rows_all.at[rep], send_row.at[1], recv_row.at[1], (core_twin, shard))
    to_x.start()
    to_core.start()
    fact_copies = [
        remote(facts, facts_all.at[rep], send_fact.at[at], recv_fact.at[at], peer) for at, peer in enumerate(rep_peers)
    ]
    for copy in fact_copies:
        copy.start()
    facts_all[rep] = facts[...]
    finish_sum(y_copies, parts, out, place, buffers, sum_sem)
    to_x.wait_recv()
    passed = remote(rows_all.at[x_twin], rows_all.at[x_twin], send_row.at[2], recv_row.at[2], (core_twin, shard))
    passed.start()
    keep.wait()
    to_x.wait_send()
    to_core.wait()
    for copy in fact_copies:
        copy.wait()
    passed.wait()


def sum_and_share(parts, rows, facts, number):
    dma = pltpu.SemaphoreType.DMA
    chunk = parts.shape[1:]
    return comm_call(
        picked_kernel,
        [
            jax.ShapeDtypeStruct(chunk, jnp.float32),
            jax.ShapeDtypeStruct((RG,) + rows.shape, rows.dtype),
            jax.ShapeDtypeStruct((RG,) + facts.shape, facts.dtype),
        ],
        sum_buffers(chunk) + sum_sems() + [dma((3,))] * 4 + [dma],
        number,
        (parts, rows, facts),
        "vvv",
        "vvv",
        40 << 20,
    )


def branch_kernel(rows, pieces, out, features, *sems):
    place = whereabouts()
    rep, shard, _, _, _ = place
    send, recv = sems[5:]
    peers = [(rep, shard_peer(shard, step)) for step in range(1, SG)]
    greet(peers)
    started = start_gather(rows, out, row_slot, place, sems[:5])
    copies = []
    for at, peer in enumerate(peers):
        copies.append(remote(pieces.at[peer[1]], features.at[shard], send.at[at], recv.at[at], peer))
        copies[-1].start()
    features[shard] = pieces[shard]
    finish_gather(started, out, row_slot, place, sems[:5])
    for copy in copies:
        copy.wait()


def share_branch(rows, pieces, number):
    dma = pltpu.SemaphoreType.DMA
    return comm_call(
        branch_kernel,
        [jax.ShapeDtypeStruct((SG * rows.shape[0], rows.shape[1]), rows.dtype), jax.ShapeDtypeStruct(pieces.shape, pieces.dtype)],
        GATHER_SEMS + [dma((SG - 1,))] * 2,
        number,
        (rows, pieces),
        "vv",
        "vv",
    )


def layer_kernel(
    vocab, parts, stats, grad_in, grad_back, smalls, rows, facts, targets, head,
    out, stats_out, sum_in, sum_back, smalls_out, head_out, squares,
    stats_all, from_y, own_sum, from_z, pair_in, pair_back, half_in, half_back, far_in, far_back, small_rep, small_sum, small_shard,
    send_y, recv_y, send_z, recv_z, send_stat, recv_stat, send_pair, recv_pair, send_far, recv_far,
    send_rep, recv_rep, send_small, recv_small,
):
    at = pl.program_id(0)
    last = pl.num_programs(0) - 1
    rep, shard, core_twin, x_twin, y_twin = whereabouts()
    core_far = lax.rem(core_twin + 2, RG)
    shard_peers = [(rep, shard_peer(shard, step)) for step in range(1, SG)]
    rep_peers = [(lax.rem(rep + step, RG), shard) for step in range(1, RG)]

    def rep_copies():
        return [
            remote(smalls, small_rep.at[k], send_rep.at[k], recv_rep.at[k], peer) for k, peer in enumerate(rep_peers)
        ]

    def pair_copies(which, slot):
        pairs = ((grad_in, pair_in), (grad_back, pair_back))
        return [
            remote(
                source.at[which], target.at[slot], send_pair.at[2 * slot + k], recv_pair.at[2 * slot + k],
                (core_twin, shard),
            )
            for k, (source, target) in enumerate(pairs)
        ]

    def y_copy(step):
        return remote(parts.at[z_peer(y_twin, step)], from_y.at[step], send_y.at[step], recv_y.at[step], (rep, y_twin))

    def z_copy(step):
        return remote(
            own_sum.at[step], from_z.at[step - 1], send_z.at[step - 1], recv_z.at[step - 1], (rep, z_peer(shard, step))
        )

    def stat_copies():
        return [
            remote(stats, stats_all.at[shard], send_stat.at[k], recv_stat.at[k], peer)
            for k, peer in enumerate(shard_peers)
        ]

    def far_copies():
        return [
            remote(half_in, far_in, send_far.at[0], recv_far.at[0], (x_twin, shard)),
            remote(half_back, far_back, send_far.at[1], recv_far.at[1], (x_twin, shard)),
        ]

    def small_copies():
        return [
            remote(small_sum.at[peer[1]], small_shard.at[k], send_small.at[k], recv_small.at[k], peer)
            for k, peer in enumerate(shard_peers)
        ]

    def pass_on(step):
        y_copy(step).wait_recv()
        own_sum[step] = parts[z_peer(shard, step)] + from_y[step]
        z_copy(step).start()

    @pl.when(at == 0)
    def _():
        greet(shard_peers + rep_peers)
        for step in (2, 1, 3, 0):
            y_copy(step).start()
        for copy in pair_copies(core_far, 1) + pair_copies(core_twin, 0) + rep_copies() + stat_copies():
            copy.start()
        stats_all[shard] = stats[...]
        squares[...] = jnp.zeros_like(squares)

    @pl.when(at == 2)
    def _():
        for copy in pair_copies(core_far, 1):
            copy.wait()
        half_in[...] = grad_in[x_twin] + pair_in[1]
        half_back[...] = grad_back[x_twin] + pair_back[1]
        for copy in far_copies():
            copy.start()
        for copy in rep_copies():
            copy.wait()
        small_sum[...] = smalls[...] + small_rep[0] + small_rep[1] + small_rep[2]
        for copy in small_copies():
            copy.start()

    pl.when(at == 5)(lambda: pass_on(2))
    pl.when(at == 9)(lambda: pass_on(1))

    _, low = vocab_rows(vocab, head[...])
    total = None
    for group in range(RG):
        grads = logit_grads(
            vocab, low, rows[group], facts[group, 0:1, :], targets[group, 0:1, :], facts[group, 1:2, :]
        )
        term = plain_dot(grads, rows[group])
        total = term if total is None else total + term
    head_out[...] = total
    squares[0:1, :] += jnp.sum(total * total, axis=0, keepdims=True)

    @pl.when(at == last)
    def _():
        pass_on(3)
        for copy in pair_copies(core_twin, 0):
            copy.wait()
        for copy in far_copies():
            copy.wait()
        sum_in[...] = grad_in[rep] + pair_in[0] + far_in[...]
        sum_back[...] = grad_back[rep] + pair_back[0] + far_back[...]
        for copy in stat_copies() + small_copies():
            copy.wait()
        stats_out[...] = stats_all[...]
        whole = small_sum[shard]
        for k in range(SG - 1):
            whole = whole + small_shard[k]
        smalls_out[...] = whole
        y_copy(0).wait_recv()
        own = parts[shard] + from_y[0]
        for step in (1, 2, 3):
            z_copy(step).wait()
        out[...] = own + from_z[0] + from_z[1] + from_z[2]
        for step in range(4):
            y_copy(step).wait_send()


def layer_sums(parts, stats, grad_in, grad_back, smalls, rows, facts, targets, head, number):
    dma = pltpu.SemaphoreType.DMA
    chunk = parts.shape[1:]
    quarter_in, quarter_back, piece = grad_in.shape[1:], grad_back.shape[1:], smalls.shape[1:]
    vocab, depth = head.shape
    vmem = lambda shape: pltpu.VMEM(shape, jnp.float32)
    shape = lambda dims: jax.ShapeDtypeStruct(dims, jnp.float32)
    block = pl.BlockSpec((VOCAB_BLOCK, depth), lambda at: (at, 0))
    return comm_call(
        functools.partial(layer_kernel, vocab),
        [shape(chunk), shape((SG,) + stats.shape), shape(quarter_in), shape(quarter_back), shape(piece), shape(head.shape), shape((8, depth))],
        [vmem((SG,) + stats.shape)]
        + sum_buffers(chunk)
        + [vmem((2,) + quarter_in), vmem((2,) + quarter_back), vmem(quarter_in), vmem(quarter_back), vmem(quarter_in), vmem(quarter_back)]
        + [vmem((3,) + smalls.shape), vmem(smalls.shape), vmem((SG - 1,) + piece)]
        + sum_sems()
        + [dma((SG - 1,))] * 2 + [dma((4,))] * 2 + [dma((2,))] * 2 + [dma((3,))] * 2 + [dma((SG - 1,))] * 2,
        number,
        (parts, stats, grad_in, grad_back, smalls, rows, facts, targets, head),
        ["v"] * 8 + [block],
        ["v"] * 5 + [block, "v"],
        62 << 20,
        (pl.cdiv(vocab, VOCAB_BLOCK),),
    )


def return_kernel(
    rows, sum_in, sum_back, rows_all, in_all, back_all, send_row, recv_row, own, send_in, recv_in, send_back, recv_back
):
    rep, shard, core_twin, x_twin, _ = whereabouts()
    shard_peers = [(rep, shard_peer(shard, step)) for step in range(1, SG)]
    greet(shard_peers + [(core_twin, shard), (x_twin, shard)])
    keep = pltpu.make_async_copy(rows, rows_all.at[rep], own.at[0])
    keep.start()
    to_x = remote(rows, rows_all.at[rep], send_row.at[0], recv_row.at[0], (x_twin, shard))
    to_core = remote(rows, rows_all.at[rep], send_row.at[1], recv_row.at[1], (core_twin, shard))
    to_x.start()
    to_core.start()
    in_copies = [
        remote(sum_in.at[peer[1]], in_all.at[shard], send_in.at[k], recv_in.at[k], peer)
        for k, peer in enumerate(shard_peers)
    ]
    for copy in in_copies:
        copy.start()
    keep_in = pltpu.make_async_copy(sum_in.at[shard], in_all.at[shard], own.at[1])
    keep_in.start()
    moves = []
    for slot in range(5):
        tile = shard if slot == 0 else SG + 4 * shard + slot - 1
        owner = tile // 5
        at = lax.rem(tile, 5)
        there = remote(sum_back.at[slot], back_all.at[at], send_back.at[slot], recv_back.at[at], (rep, owner))
        here = pltpu.make_async_copy(sum_back.at[slot], back_all.at[at], recv_back.at[at])
        pl.when(owner == shard)(here.start)
        pl.when(owner != shard)(there.start)
        moves.append((owner, there))
    to_x.wait_recv()
    passed = remote(rows_all.at[x_twin], rows_all.at[x_twin], send_row.at[2], recv_row.at[2], (core_twin, shard))
    passed.start()
    keep_in.wait()
    for copy in in_copies:
        copy.wait()
    for at in range(5):
        pltpu.make_async_copy(sum_back.at[0], back_all.at[at], recv_back.at[at]).wait()
    for owner, there in moves:
        pl.when(owner != shard)(there.wait_send)
    keep.wait()
    to_x.wait_send()
    to_core.wait()
    passed.wait()


def return_sums(rows, sum_in, sum_back, number):
    dma = pltpu.SemaphoreType.DMA
    shape = lambda dims, like: jax.ShapeDtypeStruct(dims, like.dtype)
    return comm_call(
        return_kernel,
        [shape((RG,) + rows.shape, rows), shape(sum_in.shape, sum_in), shape(sum_back.shape, sum_back)],
        [dma((3,))] * 2 + [dma((2,))] + [dma((SG - 1,))] * 2 + [dma((5,))] * 2,
        number,
        (rows, sum_in, sum_back),
    )


def total_kernel(value, out, from_rep, half, from_shard, send_rep, recv_rep, send_shard, recv_shard):
    rep, shard, _, _, _ = whereabouts()
    shard_peers = [(rep, shard_peer(shard, step)) for step in range(1, SG)]
    rep_peers = [(lax.rem(rep + step, RG), shard) for step in range(1, RG)]
    greet(shard_peers + rep_peers)
    copies = [
        remote(value, from_rep.at[rep], send_rep.at[k], recv_rep.at[k], peer) for k, peer in enumerate(rep_peers)
    ]
    for copy in copies:
        copy.start()
    from_rep[rep] = value[...]
    for copy in copies:
        copy.wait()
    half[...] = from_rep[0] + from_rep[1] + from_rep[2] + from_rep[3]
    copies = [
        remote(half, from_shard.at[shard], send_shard.at[k], recv_shard.at[k], peer)
        for k, peer in enumerate(shard_peers)
    ]
    for copy in copies:
        copy.start()
    from_shard[shard] = half[...]
    for copy in copies:
        copy.wait()
    total = from_shard[0]
    for k in range(1, SG):
        total = total + from_shard[k]
    out[...] = total


def total_everywhere(value, number):
    dma = pltpu.SemaphoreType.DMA
    return comm_call(
        total_kernel,
        [jax.ShapeDtypeStruct(value.shape, value.dtype)],
        [pltpu.VMEM((RG,) + value.shape, value.dtype), pltpu.VMEM(value.shape, value.dtype), pltpu.VMEM((SG,) + value.shape, value.dtype)]
        + [dma((RG - 1,))] * 2 + [dma((SG - 1,))] * 2,
        number,
        (value,),
        "v",
        "v",
    )[0]


GROUP_HEADS = H // SG
HEAD_COLS = GROUP_HEADS * HD
UNITS = FF // SG
OWN_COLS = 3 * HEAD_COLS + UNITS
VOCAB_BLOCK = 512
TABLE_BLOCK = 4096
VMEM_LIMIT = 60 << 20


def transposed_dot(left, right):
    return lax.dot_general(left, right, (((1,), (1,)), ((), ())), preferred_element_type=jnp.float32)


def first_dot(left, right):
    return lax.dot_general(left, right, (((0,), (0,)), ((), ())), preferred_element_type=jnp.float32)


def plain_dot(left, right):
    return jnp.dot(left, right, preferred_element_type=jnp.float32)


def vocab_rows(vocab, block):
    at = pl.program_id(0)
    places = at * VOCAB_BLOCK + lax.broadcasted_iota(jnp.int32, block.shape, 0)
    return places, jnp.where(places < vocab, block, jnp.zeros_like(block))


def top_kernel(vocab, rows, targets, head, stats, head_out, top, total, target):
    at = pl.program_id(0)

    @pl.when(at == 0)
    def _():
        top[...] = jnp.full_like(top, -1e30)
        total[...] = jnp.zeros_like(total)
        target[...] = jnp.zeros_like(target)

    low = head[...].astype(jnp.bfloat16)
    head_out[...] = low
    logits = transposed_dot(low, rows[...])
    places = at * VOCAB_BLOCK + lax.broadcasted_iota(jnp.int32, logits.shape, 0)
    valid = places < vocab
    masked = jnp.where(valid, logits, -1e30)
    highest = jnp.maximum(top[...], jnp.max(masked, axis=0, keepdims=True))
    weights = jnp.where(valid, jnp.exp(masked - highest), 0.0)
    total[...] = total[...] * jnp.exp(top[...] - highest) + jnp.sum(weights, axis=0, keepdims=True)
    top[...] = highest
    hits = (places == targets[...]) & valid
    target[...] += jnp.sum(jnp.where(hits, logits, 0.0), axis=0, keepdims=True)

    @pl.when(at == pl.num_programs(0) - 1)
    def _():
        stats[...] = jnp.zeros_like(stats)
        stats[0:1, :] = top[...]
        stats[1:2, :] = total[...]
        stats[2:3, :] = target[...]


def logit_stats(rows, targets, head):
    vocab, depth = head.shape
    count = rows.shape[0]
    line = pltpu.VMEM((1, count), jnp.float32)
    return pl.pallas_call(
        functools.partial(top_kernel, vocab),
        grid=(pl.cdiv(vocab, VOCAB_BLOCK),),
        in_specs=[
            pl.BlockSpec((count, depth), lambda at: (0, 0)),
            pl.BlockSpec((1, count), lambda at: (0, 0)),
            pl.BlockSpec((VOCAB_BLOCK, depth), lambda at: (at, 0)),
        ],
        out_specs=[
            pl.BlockSpec((8, count), lambda at: (0, 0)),
            pl.BlockSpec((VOCAB_BLOCK, depth), lambda at: (at, 0)),
        ],
        out_shape=[
            jax.ShapeDtypeStruct((8, count), jnp.float32),
            jax.ShapeDtypeStruct(head.shape, jnp.bfloat16),
        ],
        scratch_shapes=[line, line, line],
        compiler_params=pltpu.CompilerParams(vmem_limit_bytes=VMEM_LIMIT),
    )(rows, targets, head)


def logit_grads(vocab, low, rows, logsum, targets, counted):
    logits = transposed_dot(low, rows)
    places = pl.program_id(0) * VOCAB_BLOCK + lax.broadcasted_iota(jnp.int32, logits.shape, 0)
    hits = (places == targets).astype(jnp.float32)
    grads = (jnp.exp(logits - logsum) - hits) * counted
    return jnp.where(places < vocab, grads, 0.0).astype(jnp.bfloat16)


def rows_kernel(vocab, rows, facts, targets, head, out):
    at = pl.program_id(0)

    @pl.when(at == 0)
    def _():
        out[...] = jnp.zeros_like(out)

    _, low = vocab_rows(vocab, head[...])
    logits = transposed_dot(rows[...], low)
    places = at * VOCAB_BLOCK + lax.broadcasted_iota(jnp.int32, logits.shape, 1)
    hits = (places == targets[...]).astype(jnp.float32)
    grads = (jnp.exp(logits - facts[:, 0:1]) - hits) * facts[:, 1:2]
    grads = jnp.where(places < vocab, grads, 0.0).astype(jnp.bfloat16)
    out[...] += plain_dot(grads, low)


def picked_grads(rows, facts, targets, head):
    vocab, depth = head.shape
    count = rows.shape[0]
    return pl.pallas_call(
        functools.partial(rows_kernel, vocab),
        grid=(pl.cdiv(vocab, VOCAB_BLOCK),),
        in_specs=[
            pl.BlockSpec((count, depth), lambda at: (0, 0)),
            pl.BlockSpec((count, 8), lambda at: (0, 0)),
            pl.BlockSpec((count, 1), lambda at: (0, 0)),
            pl.BlockSpec((VOCAB_BLOCK, depth), lambda at: (at, 0)),
        ],
        out_specs=pl.BlockSpec((count, depth), lambda at: (0, 0)),
        out_shape=jax.ShapeDtypeStruct((count, depth), jnp.float32),
        compiler_params=pltpu.CompilerParams(vmem_limit_bytes=VMEM_LIMIT),
    )(rows, facts, targets, head)


def embed_grad_kernel(ids, rows, out, squares, table, wide):
    at = pl.program_id(0)
    width = out.shape[1]

    @pl.when(at == 0)
    def _():
        squares[...] = jnp.zeros_like(squares)
        wide[...] = rows[...].astype(jnp.float32)

        @pl.loop(0, table.shape[0] // 512)
        def _(part):
            table[pl.ds(pl.multiple_of(part * 512, 512), 512), :] = jnp.zeros((512, table.shape[1]), jnp.float32)

        @pl.loop(0, rows.shape[0] // 8)
        def _(group):
            for lane in range(8):
                token = group * 8 + lane
                here = pl.ds(ids[token], 1)
                table[here, :] = table[here, :] + wide[pl.ds(token, 1), :]

    block = table[pl.ds(pl.multiple_of(at * width, width), width), :]
    out[...] = block.T
    squares[...] += jnp.sum((block * block).reshape(width // 8, 8, block.shape[1]), axis=0)


def embed_grads(ids, rows, vocab):
    count, feats = rows.shape
    blocks = pl.cdiv(vocab, TABLE_BLOCK)
    return pl.pallas_call(
        embed_grad_kernel,
        grid=(blocks,),
        in_specs=[
            pl.BlockSpec(memory_space=pltpu.SMEM),
            pl.BlockSpec(memory_space=pltpu.VMEM),
        ],
        out_specs=[
            pl.BlockSpec((feats, TABLE_BLOCK), lambda at: (0, at)),
            pl.BlockSpec((8, feats), lambda at: (0, 0)),
        ],
        out_shape=[
            jax.ShapeDtypeStruct((feats, vocab), jnp.float32),
            jax.ShapeDtypeStruct((8, feats), jnp.float32),
        ],
        scratch_shapes=[
            pltpu.VMEM((blocks * TABLE_BLOCK, feats), jnp.float32),
            pltpu.VMEM((count, feats), jnp.float32),
        ],
        compiler_params=pltpu.CompilerParams(vmem_limit_bytes=VMEM_LIMIT),
    )(ids, rows)


def turn_tables(places):
    half_rot = ROT // 2
    lane = jnp.arange(HEAD_COLS) % HD
    exponent = (lane % half_rot).astype(jnp.float32) * (2.0 / ROT)
    angles = places[:, None] * jnp.exp(-exponent * jnp.log(10000.0))[None, :]
    cosine, sine = jnp.cos(angles), jnp.sin(angles)
    lane = lane[None, :]
    return (
        jnp.where(lane < ROT, cosine, 1.0),
        jnp.where(lane < half_rot, -sine, 0.0),
        jnp.where((lane >= half_rot) & (lane < ROT), sine, 0.0),
    )


def centred_rows(values):
    centred = values - jnp.mean(values, axis=-1, keepdims=True)
    spread = jnp.mean(centred * centred, axis=-1, keepdims=True)
    scale = lax.rsqrt(spread + NORM_EPS)
    return centred * scale, scale


def exact_dot(left, right):
    return jnp.dot(left, right, precision=lax.Precision.HIGHEST, preferred_element_type=jnp.float32)


def pick_matrix(places, tokens):
    lane = lax.broadcasted_iota(jnp.int32, (places.shape[0], tokens), 1)
    return (places == lane).astype(jnp.float32)


def turn(rows, tables, sign):
    half_rot = ROT // 2
    own, after, before = tables
    width = rows.shape[1]
    return (
        rows * own
        + sign * (pltpu.roll(rows, width - half_rot, 1) * after)
        + sign * (pltpu.roll(rows, half_rot, 1) * before)
    )


def head_lanes(rows, head):
    lane = lax.broadcasted_iota(jnp.int32, rows.shape, 1)
    return jnp.where(lane // HD == head, rows, jnp.zeros_like(rows))


def head_probs(queries, keys, allowed, head):
    scores = transposed_dot(head_lanes(queries, head), keys) * HD ** (-0.5)
    scores = jnp.where(allowed, scores, -1e30)
    exponent = jnp.exp(scores - jnp.max(scores, axis=-1, keepdims=True))
    return exponent / jnp.sum(exponent, axis=-1, keepdims=True)


def line_allowed(places, span, tokens):
    keys = lax.broadcasted_iota(jnp.int32, (places.shape[0], tokens), 1)
    in_query = (places >= span) & (places < span + PIC)
    in_key = (keys >= span) & (keys < span + PIC)
    return (keys <= places) | (in_query & in_key)


def forward_kernel(
    spans, residual, places, scales, bias, own, after, before, weights, back,
    queries, keys, values, hidden, joined, picked_one, picked_two, picked_rows, branch,
):
    bf16 = jnp.bfloat16
    tokens = residual.shape[0]
    span = spans[pl.program_id(0)]
    gain_one, shift_one = scales[0:1, :], scales[1:2, :]
    gain_two, shift_two = scales[2:3, :], scales[3:4, :]
    unit, _ = centred_rows(residual[...].astype(jnp.float32))
    low_one = (unit * gain_one + shift_one).astype(bf16)
    pick = pick_matrix(places[...], tokens)
    rows = plain_dot(pick.astype(bf16), residual[...])
    picked_rows[...] = rows.astype(bf16)
    unit, _ = centred_rows(rows)
    low_picked = (unit * gain_one + shift_one).astype(bf16)
    picked_one[...] = low_picked
    low_two = (unit * gain_two + shift_two).astype(bf16)
    picked_two[...] = low_two
    tables = (own[...], after[...], before[...])
    picked_tables = tuple(exact_dot(pick, table) for table in tables)
    two, three = 2 * HEAD_COLS, 3 * HEAD_COLS
    query = plain_dot(low_picked, weights[:, :HEAD_COLS]) + bias[:, :HEAD_COLS]
    query = turn(query, picked_tables, 1.0).astype(bf16)
    queries[...] = query
    key = plain_dot(low_one, weights[:, HEAD_COLS:two]) + bias[:, HEAD_COLS:two]
    key = turn(key, tables, 1.0).astype(bf16)
    keys[...] = key
    value = (plain_dot(low_one, weights[:, two:three]) + bias[:, two:three]).astype(bf16)
    values[...] = value
    allowed = line_allowed(places[...], span, tokens)
    attended = None
    for head in range(GROUP_HEADS):
        probs = head_probs(query, key, allowed, head).astype(bf16)
        term = head_lanes(plain_dot(probs, value), head)
        attended = term if attended is None else attended + term
    joined[:, :HEAD_COLS] = attended.astype(bf16)
    pre = plain_dot(low_two, weights[:, three:]) + bias[:, three:]
    hidden[...] = pre
    joined[:, HEAD_COLS:] = (0.5 * pre * (1.0 + lax.erf(pre * 0.5**0.5))).astype(bf16)
    branch[...] = plain_dot(joined[...], back[...])


def line_block(height, width):
    return pl.BlockSpec((height, width), lambda line: (line, 0))


def still(array):
    return pl.BlockSpec(array.shape, lambda line: (0,) * array.ndim)


def layer_forward(spans, residual, places, scales, bias, tables, weights, back):
    lines = spans.shape[0]
    tokens, slots = residual.shape[0] // lines, places.shape[0] // lines
    depth = residual.shape[1]
    bf16, f32 = jnp.bfloat16, jnp.float32
    outs = [
        (slots, HEAD_COLS, bf16),
        (tokens, HEAD_COLS, bf16),
        (tokens, HEAD_COLS, bf16),
        (slots, UNITS, f32),
        (slots, HEAD_COLS + UNITS, bf16),
        (slots, depth, bf16),
        (slots, depth, bf16),
        (slots, depth, bf16),
        (slots, depth, f32),
    ]
    return pl.pallas_call(
        forward_kernel,
        grid=(lines,),
        in_specs=[
            pl.BlockSpec(memory_space=pltpu.SMEM),
            line_block(tokens, depth),
            line_block(slots, 1),
            still(scales),
            still(bias),
            *[still(table) for table in tables],
            still(weights),
            still(back),
        ],
        out_specs=[line_block(height, width) for height, width, _ in outs],
        out_shape=[jax.ShapeDtypeStruct((lines * height, width), kind) for height, width, kind in outs],
        compiler_params=pltpu.CompilerParams(vmem_limit_bytes=VMEM_LIMIT),
    )(spans, residual, places, scales, bias, *tables, weights, back)


def backward_kernel(
    spans, residual, places, scales, own, after, before, weights, back,
    queries, keys, values, hidden, joined, picked_one, picked_two, d_branch,
    unit_parts, stats, grad_in, grad_back, grad_scales, grad_bias,
):
    bf16 = jnp.bfloat16
    line = pl.program_id(0)
    tokens = residual.shape[0]
    span = spans[line]
    gain_one, shift_one = scales[0:1, :], scales[1:2, :]
    gain_two = scales[2:3, :]

    @pl.when(line == 0)
    def _():
        for total in (grad_in, grad_back, grad_scales, grad_bias):
            total[...] = jnp.zeros_like(total)

    pick = pick_matrix(places[...], tokens)
    tables = (own[...], after[...], before[...])
    picked_tables = tuple(exact_dot(pick, table) for table in tables)
    pick = pick.astype(bf16)
    d_rows = d_branch[...]
    d_joined = transposed_dot(d_rows, back[...])
    grad_back[...] += first_dot(joined[...], d_rows)
    d_attended = d_joined[:, :HEAD_COLS].astype(bf16)
    pre = hidden[...]
    slope = 0.5 * (1.0 + lax.erf(pre * 0.5**0.5)) + pre * jnp.exp(-0.5 * pre * pre) * (2.0 * 3.141592653589793) ** -0.5
    d_hidden = (d_joined[:, HEAD_COLS:] * slope).astype(bf16)
    allowed = line_allowed(places[...], span, tokens)
    query, key, value = queries[...], keys[...], values[...]
    d_query = d_key = d_value = None
    for head in range(GROUP_HEADS):
        probs = head_probs(query, key, allowed, head)
        d_head = head_lanes(d_attended, head)
        d_probs = transposed_dot(d_head, value)
        d_scores = (probs * (d_probs - jnp.sum(probs * d_probs, axis=-1, keepdims=True))).astype(bf16)
        terms = (
            head_lanes(plain_dot(d_scores, key), head),
            first_dot(d_scores, head_lanes(query, head)),
            first_dot(probs.astype(bf16), d_head),
        )
        if d_query is None:
            d_query, d_key, d_value = terms
        else:
            d_query, d_key, d_value = d_query + terms[0], d_key + terms[1], d_value + terms[2]
    d_query = turn(d_query * HD ** (-0.5), picked_tables, -1.0).astype(bf16)
    d_key = turn(d_key * HD ** (-0.5), tables, -1.0).astype(bf16)
    d_value = d_value.astype(bf16)
    unit, _ = centred_rows(residual[...].astype(jnp.float32))
    low_one = (unit * gain_one + shift_one).astype(bf16)
    two, three = 2 * HEAD_COLS, 3 * HEAD_COLS
    grad_in[:, :HEAD_COLS] += first_dot(picked_one[...], d_query)
    grad_in[:, HEAD_COLS:two] += first_dot(low_one, d_key)
    grad_in[:, two:three] += first_dot(low_one, d_value)
    grad_in[:, three:] += first_dot(picked_two[...], d_hidden)

    def column_sum(rows):
        return jnp.sum(rows.astype(jnp.float32), axis=0, keepdims=True)

    grad_bias[0:1, :HEAD_COLS] += column_sum(d_query)
    grad_bias[0:1, HEAD_COLS:two] += column_sum(d_key)
    grad_bias[0:1, two:three] += column_sum(d_value)
    grad_bias[0:1, three:] += column_sum(d_hidden)
    d_normed = (
        transposed_dot(first_dot(pick, d_query).astype(bf16), weights[:, :HEAD_COLS])
        + transposed_dot(d_key, weights[:, HEAD_COLS:two])
        + transposed_dot(d_value, weights[:, two:three])
    )
    d_unit = d_normed * gain_one
    grad_scales[0:1, :] += column_sum(d_normed * unit)
    grad_scales[1:2, :] += column_sum(d_normed)
    d_normed = transposed_dot(first_dot(pick, d_hidden).astype(bf16), weights[:, three:])
    grad_scales[2:3, :] += column_sum(d_normed * unit)
    grad_scales[3:4, :] += column_sum(d_normed)
    d_unit = d_unit + d_normed * gain_two
    sum_one = jnp.sum(d_unit, axis=-1, keepdims=True)
    sum_two = jnp.sum(d_unit * unit, axis=-1, keepdims=True)
    lane = lax.broadcasted_iota(jnp.int32, (tokens, 128), 1)
    both = jnp.where(lane == 0, sum_one, jnp.where(lane == 1, sum_two, 0.0))
    stats[...] = both.T[:8, :]
    feats = unit_parts.shape[2]
    for part in range(unit_parts.shape[0]):
        unit_parts[part] = d_unit[:, part * feats : (part + 1) * feats]


def layer_backward(spans, residual, places, scales, tables, weights, back, kept, d_branch):
    lines = spans.shape[0]
    count, depth = residual.shape
    tokens, slots = count // lines, places.shape[0] // lines
    feats = depth // SG
    f32 = jnp.float32
    whole = lambda height, width: pl.BlockSpec((height, width), lambda line: (0, 0))
    return pl.pallas_call(
        backward_kernel,
        grid=(lines,),
        in_specs=[
            pl.BlockSpec(memory_space=pltpu.SMEM),
            line_block(tokens, depth),
            line_block(slots, 1),
            still(scales),
            *[still(table) for table in tables],
            still(weights),
            still(back),
            *[line_block(array.shape[0] // lines, array.shape[1]) for array in kept],
            line_block(slots, depth),
        ],
        out_specs=[
            pl.BlockSpec((SG, tokens, feats), lambda line: (0, line, 0)),
            pl.BlockSpec((8, tokens), lambda line: (0, line)),
            whole(depth, OWN_COLS),
            whole(HEAD_COLS + UNITS, depth),
            whole(8, depth),
            whole(8, OWN_COLS),
        ],
        out_shape=[
            jax.ShapeDtypeStruct((SG, count, feats), f32),
            jax.ShapeDtypeStruct((8, count), f32),
            jax.ShapeDtypeStruct((depth, OWN_COLS), f32),
            jax.ShapeDtypeStruct((HEAD_COLS + UNITS, depth), f32),
            jax.ShapeDtypeStruct((8, depth), f32),
            jax.ShapeDtypeStruct((8, OWN_COLS), f32),
        ],
        compiler_params=pltpu.CompilerParams(vmem_limit_bytes=VMEM_LIMIT),
    )(spans, residual, places, scales, *tables, weights, back, *kept, d_branch)


def group_plan(
    token_ids,
    pic_start,
    comp_pos,
    comp_tgt,
    proj_in,
    proj_back,
    small_params,
    head_table,
    embed_table,
    first_in,
    second_in,
    first_back,
    second_back,
    first_small,
    second_small,
    first_head,
    second_head,
    first_embed,
    second_embed,
):
    bf16 = jnp.bfloat16
    rep_at = lax.axis_index("rep")
    shard_at = lax.axis_index("shard")
    micro, _, seq_dev = token_ids.shape
    slots = comp_pos.shape[2]
    seq_len = seq_dev * RG
    lines = micro * SG // RG
    blocks = lines * RG
    own_blocks = blocks // SG
    tokens = lines * seq_len
    slot_count = blocks * slots
    own_slots = own_blocks * slots
    vocab_dev = head_table.shape[1]
    vocab = embed_table.shape[1]
    quarter = D // SG // RG

    place_line = jnp.concatenate([comp_pos[:, 0, :].reshape(-1), comp_tgt[:, 0, :].reshape(-1)])
    span_line = jnp.concatenate([pic_start[:, 0], jnp.zeros((seq_dev - micro,), jnp.int32)])
    ints = jnp.concatenate(
        [token_ids[:, 0, :], place_line[None], span_line[None], jnp.zeros((4, seq_dev), jnp.int32)]
    )
    small_low = small_params.astype(bf16).astype(jnp.float32).reshape(-1, 128)
    small_rows = small_low.shape[0]
    smalls = jnp.pad(small_low, ((0, 16 - small_rows), (0, 0)))
    in_low = proj_in.astype(bf16)
    qkv_parts = in_low[:, : 3 * D].reshape(D // SG, 3, SG, HEAD_COLS)
    in_parts = jnp.concatenate(
        [
            jnp.transpose(qkv_parts, (2, 0, 1, 3)).reshape(SG, D // SG, 3 * HEAD_COLS),
            jnp.transpose(in_low[:, 3 * D :].reshape(D // SG, SG, UNITS), (1, 0, 2)),
        ],
        axis=2,
    ).reshape(SG, 2, D // SG // 2, OWN_COLS)
    back_tiles = proj_back.astype(bf16).reshape(5, 2, 64, D)
    ints_all, smalls_all, residual_low, in_all, back_all = share_entry(
        ints, smalls, in_parts, back_tiles, embed_table, tokens, 1
    )
    own_in = in_all.reshape(D, OWN_COLS)
    own_back = back_all.reshape(5 * 128, D)
    wide_small = smalls_all[:, :small_rows].reshape(-1)
    (
        gain_one,
        shift_one,
        gain_two,
        shift_two,
        gain_last,
        shift_last,
        bias_qkv,
        bias_hidden,
        bias_out,
    ) = split_small(wide_small)
    head_cols = [
        lax.dynamic_slice(bias_qkv, (part * D + shard_at * HEAD_COLS,), (HEAD_COLS,)) for part in range(3)
    ]
    own_hidden = lax.dynamic_slice(bias_hidden, (shard_at * UNITS,), (UNITS,))

    by_group = ints_all.reshape(RG, RG, SG // RG, 8, seq_dev)
    ids_all = jnp.transpose(by_group[:, :, :, :micro], (1, 3, 2, 0, 4)).reshape(RG, tokens)
    slot_facts = jnp.transpose(
        by_group[:, :, :, 2].reshape(RG, RG, SG // RG, 2, micro, slots), (3, 1, 4, 2, 0, 5)
    ).reshape(2, RG, slot_count)
    used_all = slot_facts[0] < seq_dev
    targets_all = jnp.where(used_all, slot_facts[1] - shard_at * vocab_dev, -1)
    counted_all = used_all.astype(jnp.float32)
    pos_group = lax.dynamic_index_in_dim(slot_facts[0], rep_at, 0, False)
    targets_group = lax.dynamic_index_in_dim(targets_all, rep_at, 0, False)
    counted_group = lax.dynamic_index_in_dim(counted_all, rep_at, 0, False)
    spans = lax.dynamic_index_in_dim(by_group[0, :, :, 3, :micro], rep_at, 0, False).T.reshape(lines)

    block_starts = (jnp.arange(blocks) % RG * seq_dev)[:, None]
    slot_places = pos_group.reshape(blocks, slots)
    slot_places = jnp.where(slot_places < seq_dev, slot_places + block_starts, -1).reshape(slot_count, 1)
    tables = turn_tables(jnp.arange(seq_len).astype(jnp.float32))
    scales = jnp.stack([gain_one, shift_one, gain_two, shift_two] + [jnp.zeros_like(gain_one)] * 4)
    own_bias = jnp.concatenate(head_cols + [own_hidden])[None]
    *kept, picked_rows, branch_parts = layer_forward(
        spans, residual_low, slot_places, scales, own_bias, tables, own_in, own_back
    )
    branch = shard_sum(branch_parts.reshape(SG, own_slots, D), 3)

    own_residual = lax.dynamic_slice_in_dim(picked_rows, shard_at * own_slots, own_slots, 0).astype(jnp.float32)
    own_used = lax.dynamic_slice_in_dim(counted_group, shard_at * own_slots, own_slots, 0)
    after_add = own_residual + branch + bias_out
    final_rows, pull_last = jax.vjp(norm_rows, after_add, gain_last, shift_last)
    picked = (final_rows * own_used[:, None]).astype(bf16)
    rows_group = shard_gather(picked, 4)

    head_turned = head_table.T
    stats, head_low = logit_stats(rows_group, targets_group[None], head_turned)
    stats_all = shard_stats(stats, 5)
    tops = stats_all[:, 0]
    top = jnp.max(tops, axis=0)
    logsum = top + jnp.log(jnp.sum(stats_all[:, 1] * jnp.exp(tops - top), axis=0))
    row_target = jnp.sum(stats_all[:, 2], axis=0)
    facts = jnp.concatenate(
        [logsum[None], counted_group[None], row_target[None], jnp.zeros((5, slot_count), jnp.float32)]
    )
    picked_parts = picked_grads(rows_group, facts.T, targets_group[:, None], head_low)
    d_picked, rows_all, facts_all = sum_and_share(
        picked_parts.reshape(SG, own_slots, D), rows_group, facts, 6
    )
    loss_sum = jnp.sum((facts_all[:, 0] - facts_all[:, 2]) * facts_all[:, 1])
    count_sum = jnp.sum(facts_all[:, 1])
    targets_wide = jnp.broadcast_to(targets_all[:, None, :], (RG, 8, slot_count))

    d_after, d_gain_last, d_shift_last = pull_last(d_picked)
    d_branch_own = d_after.astype(bf16)
    d_bias_out = jnp.sum(d_branch_own.astype(jnp.float32), axis=0)
    pieces = jnp.transpose(d_after.reshape(own_slots, SG, D // SG), (1, 0, 2))
    d_branch, after_pieces = share_branch(d_branch_own, pieces, 7)
    d_after_feats = after_pieces.reshape(slot_count, D // SG)

    unit_parts, norm_stats, grad_in, grad_back, grad_scales, grad_bias = layer_backward(
        spans, residual_low, slot_places, scales, tables, own_in, own_back, kept, d_branch
    )

    def whole(columns, length):
        start = shard_at * columns.shape[0]
        return lax.dynamic_update_slice(jnp.zeros((length,), jnp.float32), columns, (start,))

    grad_small = jnp.concatenate(
        [
            grad_scales[:4].reshape(-1),
            d_gain_last,
            d_shift_last,
            *[whole(grad_bias[0, part * HEAD_COLS : (part + 1) * HEAD_COLS], D) for part in range(3)],
            whole(grad_bias[0, 3 * HEAD_COLS :], FF),
            d_bias_out,
        ]
    )
    grad_small = jnp.pad(grad_small.reshape(SG, small_rows, 128), ((0, 0), (0, 16 - small_rows), (0, 0)))
    in_quarters = jnp.transpose(grad_in.reshape(SG, RG, quarter, OWN_COLS), (1, 0, 2, 3))
    back_quarters = jnp.transpose(grad_back.reshape(5, RG, 32, D), (1, 0, 2, 3))
    d_unit_feats, norm_stats_all, in_sum, back_sum, small_sum, grad_head, head_squares = layer_sums(
        unit_parts, norm_stats, in_quarters, back_quarters, grad_small, rows_all, facts_all, targets_wide, head_low, 8
    )

    norm_sums = jnp.sum(norm_stats_all, axis=0)
    residual = residual_low.astype(jnp.float32)
    row_mean = jnp.mean(residual, axis=-1, keepdims=True)
    centred = residual - row_mean
    unit_scale = lax.rsqrt(jnp.mean(centred * centred, axis=-1, keepdims=True) + NORM_EPS)
    own_unit = lax.dynamic_slice_in_dim(residual_low, shard_at * (D // SG), D // SG, 1).astype(jnp.float32)
    own_unit = (own_unit - row_mean) * unit_scale
    d_rows = (
        d_unit_feats - norm_sums[0][:, None] / D - own_unit * (norm_sums[1][:, None] / D)
    ) * unit_scale
    pick = (pos_group.reshape(blocks, slots, 1) == jnp.arange(seq_dev)[None, None, :]).astype(jnp.float32)
    d_after_rows = jnp.einsum(
        "bst,bsd->btd",
        pick,
        d_after_feats.reshape(blocks, slots, D // SG),
        precision=lax.Precision.HIGHEST,
    ).reshape(tokens, D // SG)
    d_rows = (d_after_rows + d_rows).astype(bf16)
    d_rows_all, in_own, back_own = return_sums(d_rows, in_sum, back_sum, 9)
    in_grads = lax.all_gather(in_own, "rep")
    back_grads = lax.all_gather(back_own, "rep")
    grad_embed, embed_squares = embed_grads(ids_all.reshape(-1), d_rows_all.reshape(RG * tokens, D // SG), vocab)

    in_grads = jnp.transpose(in_grads, (0, 2, 1, 3)).reshape(D // SG, SG, OWN_COLS)
    qkv_grads = jnp.transpose(
        in_grads[:, :, : 3 * HEAD_COLS].reshape(D // SG, SG, 3, HEAD_COLS), (0, 2, 1, 3)
    ).reshape(D // SG, 3 * D)
    grad_in = jnp.concatenate([qkv_grads, in_grads[:, :, 3 * HEAD_COLS :].reshape(D // SG, FF)], axis=1)
    grad_back = jnp.transpose(back_grads, (1, 0, 2, 3)).reshape(proj_back.shape)
    grad_small = small_sum[:small_rows].reshape(-1)

    repeated_square = jnp.sum(grad_small * grad_small) + jnp.sum(head_squares) + jnp.sum(embed_squares)
    local_square = repeated_square / RG + jnp.sum(in_own * in_own) + jnp.sum(back_own * back_own)
    norm_value = jnp.sqrt(total_everywhere(jnp.broadcast_to(local_square, (8, 128)), 10)[0, 0])
    factor = CLIP_LEVEL / jnp.maximum(norm_value, CLIP_LEVEL)
    next_in, moment_in, square_in = adamw(proj_in, grad_in * factor, first_in, second_in, RATE_IN)
    next_back, moment_back, square_back = adamw(
        proj_back, grad_back * factor, first_back, second_back, RATE_BACK
    )
    next_small, moment_small, square_small = adamw(
        small_params, grad_small * factor, first_small, second_small, RATE_SMALL
    )
    next_head, moment_head, square_head = adamw(
        head_table, grad_head.T * factor, first_head, second_head, RATE_HEAD
    )
    next_embed, moment_embed, square_embed = adamw(
        embed_table, grad_embed * factor, first_embed, second_embed, RATE_EMBED
    )
    return (
        jnp.stack([loss_sum, count_sum]),
        norm_value.reshape(1),
        next_in,
        moment_in,
        square_in,
        next_back,
        moment_back,
        square_back,
        next_small,
        moment_small,
        square_small,
        next_head,
        moment_head,
        square_head,
        next_embed,
        moment_embed,
        square_embed,
    )


def select_plan(mesh):
    if mesh.shape["rep"] == RG and mesh.shape["shard"] == SG:
        return group_plan
    return any_mesh


def solution(mesh):
    placed = (
        P(None, "shard", "rep"),
        P(None, "shard"),
        P(None, "shard", "rep"),
        P(None, "shard", "rep"),
        P("shard", None),
        P("shard", None),
        P("shard"),
        P(None, "shard"),
        P("shard", None),
        P("shard", None),
        P("shard", None),
        P("shard", None),
        P("shard", None),
        P("shard"),
        P("shard"),
        P(None, "shard"),
        P(None, "shard"),
        P("shard", None),
        P("shard", None),
    )
    return jax.shard_map(
        select_plan(mesh),
        mesh=mesh,
        in_specs=placed,
        out_specs=(
            P(),
            P(),
            P("shard", None),
            P("shard", None),
            P("shard", None),
            P("shard", None),
            P("shard", None),
            P("shard", None),
            P("shard"),
            P("shard"),
            P("shard"),
            P(None, "shard"),
            P(None, "shard"),
            P(None, "shard"),
            P("shard", None),
            P("shard", None),
            P("shard", None),
        ),
        check_vma=False,
    )
```

```python
import functools

import jax
import jax.numpy as jnp
from jax import lax
from jax.experimental import pallas as pl
from jax.experimental.pallas import tpu as pltpu
from jax.sharding import PartitionSpec as P

D = 1024
H = 16
HD = 64
ROT = 16
FF = 4096
PIC = 256
STEP = 10


NORM_EPS = 1e-05
CLIP_LEVEL = 1.0
BETA_FIRST = 0.9
BETA_SECOND = 0.95
ADAM_EPS = 1e-08
DECAY_RATE = 0.01
RATE_IN = 0.01
RATE_BACK = 0.05
RATE_SMALL = 0.3
RATE_HEAD = 0.01
RATE_EMBED = 0.3


def combined_all(part, axis, combine):
    gathered = jax.tree.map(lambda a: lax.all_gather(a, axis), part)

    def take(source):
        return jax.tree.map(lambda a: lax.dynamic_index_in_dim(a, source, 0, False), gathered)

    return lax.fori_loop(
        1, lax.axis_size(axis), lambda source, state: combine(state, take(source)), take(0)
    )


def norm_rows(values, gain_vec, shift_vec):
    centred = values - jnp.mean(values, axis=-1, keepdims=True)
    spread = jnp.mean(centred * centred, axis=-1, keepdims=True)
    return centred * lax.rsqrt(spread + NORM_EPS) * gain_vec + shift_vec


def rotate(head_rows, place_vec):
    half_rot = ROT // 2
    exponent = jnp.arange(half_rot).astype(jnp.float32) * (2.0 / ROT)
    angles = place_vec[:, None] * jnp.exp(-exponent * jnp.log(10000.0))
    cosine = jnp.cos(angles)[:, None, :]
    sine_part = jnp.sin(angles)[:, None, :]
    front_part = head_rows[..., :half_rot]
    back_part = head_rows[..., half_rot:ROT]
    return jnp.concatenate(
        [
            front_part * cosine - back_part * sine_part,
            back_part * cosine + front_part * sine_part,
            head_rows[..., ROT:],
        ],
        axis=-1,
    )


def split_small(gain_parts):
    marks = [0, D, 2 * D, 3 * D, 4 * D, 5 * D, 6 * D, 9 * D, 9 * D + FF, 10 * D + FF]
    return tuple((gain_parts[marks[number] : marks[number + 1]] for number in range(9)))


def gelu_exact(values):
    return jax.nn.gelu(values, approximate=False)


def combine_totals(earlier, later_part):
    highest = jnp.maximum(earlier[0], later_part[0])
    totals = earlier[1] * jnp.exp(earlier[0] - highest) + later_part[1] * jnp.exp(
        later_part[0] - highest
    )
    return (highest, totals, earlier[2] + later_part[2])


def allowed_mask(query_places, key_places, span_start):
    inside_query = (query_places >= span_start) & (query_places < span_start + PIC)
    inside_key = (key_places >= span_start) & (key_places < span_start + PIC)
    return (key_places[None, :] <= query_places[:, None]) | inside_query[:, None] & inside_key[
        None, :
    ]


def masked_scores(queries, keys_all, allowed):
    raw_scores = jnp.einsum(
        "qhd,khd->hqk", queries, keys_all, preferred_element_type=jnp.float32
    ) * HD ** (-0.5)
    return jnp.where(allowed[None], raw_scores, -1e30)


def adamw(weight, gradient, moment, square, rate_value):
    moment = BETA_FIRST * moment + (1.0 - BETA_FIRST) * gradient
    square = BETA_SECOND * square + (1.0 - BETA_SECOND) * gradient * gradient
    moment_hat = moment / (1.0 - BETA_FIRST**STEP)
    square_hat = square / (1.0 - BETA_SECOND**STEP)
    weight = weight - rate_value * (
        moment_hat / (jnp.sqrt(square_hat) + ADAM_EPS) + DECAY_RATE * weight
    )
    return (weight, moment, square)


def any_mesh(
    token_ids,
    pic_start,
    comp_pos,
    comp_tgt,
    proj_in,
    proj_back,
    small_params,
    head_table,
    embed_table,
    first_in,
    second_in,
    first_back,
    second_back,
    first_small,
    second_small,
    first_head,
    second_head,
    first_embed,
    second_embed,
):
    seq_dev = token_ids.shape[2]
    micro_count = token_ids.shape[0]
    vocab_dev = head_table.shape[1]
    rep_count = lax.axis_size("rep")
    seq_len = seq_dev * rep_count
    rep_at = lax.axis_index("rep")
    shard_at = lax.axis_index("shard")
    used_own = comp_pos[:, 0, :] < seq_dev
    marked = jnp.where(used_own, comp_tgt[:, 0, :], -1)
    ids_group, tgt_group = (
        lax.all_gather(token_ids[:, 0, :], "shard", axis=1, tiled=True),
        lax.all_gather(marked, "shard", axis=1, tiled=True),
    )
    in_low = proj_in.astype(jnp.bfloat16)
    back_low = proj_back.astype(jnp.bfloat16)
    small_low = small_params.astype(jnp.bfloat16)
    head_low = head_table.astype(jnp.bfloat16)
    table_low = embed_table.astype(jnp.bfloat16)
    own_places = rep_at * seq_dev + jnp.arange(seq_dev)
    key_places = jnp.arange(seq_len)
    own_float = own_places.astype(jnp.float32)
    vocab_ids = jnp.arange(vocab_dev)
    grad_in = jnp.zeros((D, 3 * D + FF), jnp.float32)
    grad_back = jnp.zeros((D + FF, D), jnp.float32)
    grad_small = jnp.zeros((10 * D + FF,), jnp.float32)
    grad_head = jnp.zeros(head_table.shape, jnp.float32)
    grad_embed = jnp.zeros(embed_table.shape, jnp.float32)
    loss_sum = jnp.zeros((), jnp.float32)
    count_sum = jnp.zeros((), jnp.float32)
    for micro_at in range(micro_count):
        wide_in, wide_back, wide_small = (
            lax.all_gather(in_low, "shard", axis=0, tiled=True),
            lax.all_gather(back_low, "shard", axis=0, tiled=True),
            lax.all_gather(small_low, "shard", axis=0, tiled=True),
        )
        (
            gain_one,
            shift_one,
            gain_two,
            shift_two,
            gain_last,
            shift_last,
            bias_qkv,
            bias_hidden,
            bias_out,
        ) = split_small(wide_small.astype(jnp.float32))
        columns = jnp.take(table_low, ids_group[micro_at], axis=1)
        arrived = lax.all_to_all(columns, "shard", split_axis=1, concat_axis=0, tiled=True)
        residual = arrived.T.astype(jnp.float32)
        normed_one = norm_rows(residual, gain_one, shift_one)
        normed_two = norm_rows(residual, gain_two, shift_two)
        low_one = normed_one.astype(jnp.bfloat16)
        low_two = normed_two.astype(jnp.bfloat16)
        projected = (
            jnp.dot(low_one, wide_in[:, : 3 * D], preferred_element_type=jnp.float32) + bias_qkv
        )
        queries = rotate(projected[:, :D].reshape(seq_dev, H, HD), own_float).astype(jnp.bfloat16)
        key_rows = (
            rotate(projected[:, D : 2 * D].reshape(seq_dev, H, HD), own_float)
            .astype(jnp.bfloat16)
            .reshape(seq_dev, D)
        )
        value_rows = projected[:, 2 * D :].astype(jnp.bfloat16)
        keys_all, values_all = (
            lax.all_gather(key_rows, "rep", axis=0, tiled=True),
            lax.all_gather(value_rows, "rep", axis=0, tiled=True),
        )
        keys_all = keys_all.reshape(seq_len, H, HD)
        values_all = values_all.reshape(seq_len, H, HD)
        allowed = allowed_mask(own_places, key_places, pic_start[micro_at, 0])
        scores = masked_scores(queries, keys_all, allowed)
        highest = jnp.max(scores, axis=-1, keepdims=True)
        exponent = jnp.exp(scores - highest)
        totals = jnp.sum(exponent, axis=-1, keepdims=True)
        logsum = highest + jnp.log(totals)
        attn_probs = (exponent / totals).astype(jnp.bfloat16)
        attended = (
            jnp.einsum("hqk,khd->qhd", attn_probs, values_all, preferred_element_type=jnp.float32)
            .reshape(seq_dev, D)
            .astype(jnp.bfloat16)
        )
        hidden_pre = (
            jnp.dot(low_two, wide_in[:, 3 * D :], preferred_element_type=jnp.float32) + bias_hidden
        )
        activation = gelu_exact(hidden_pre).astype(jnp.bfloat16)
        joined = jnp.concatenate([attended, activation], axis=1)
        after_add = (
            residual + jnp.dot(joined, wide_back, preferred_element_type=jnp.float32) + bias_out
        )
        final_rows = norm_rows(after_add, gain_last, shift_last)
        places = comp_pos[micro_at, 0]
        used_slots = (places < seq_dev).astype(jnp.float32)
        picked = (
            jnp.take(final_rows, jnp.minimum(places, seq_dev - 1), axis=0) * used_slots[:, None]
        ).astype(jnp.bfloat16)
        rows_all = lax.all_gather(picked, "shard", axis=0, tiled=True)
        logits = jnp.dot(rows_all, head_low, preferred_element_type=jnp.float32)
        targets = tgt_group[micro_at]
        matches = (targets - shard_at * vocab_dev)[:, None] == vocab_ids[None, :]
        row_top = jnp.max(logits, axis=1)
        row_total = jnp.sum(jnp.exp(logits - row_top[:, None]), axis=1)
        row_target = jnp.sum(jnp.where(matches, logits, 0.0), axis=1)
        row_top, row_total, row_target = combined_all(
            (row_top, row_total, row_target), "shard", combine_totals
        )
        logsum_rows = row_top + jnp.log(row_total)
        counted = (targets >= 0).astype(jnp.float32)
        loss_sum = loss_sum + jnp.sum((logsum_rows - row_target) * counted)
        count_sum = count_sum + jnp.sum(counted)
        d_logits = (
            (jnp.exp(logits - logsum_rows[:, None]) - matches.astype(jnp.float32))
            * counted[:, None]
        ).astype(jnp.bfloat16)
        grad_head = grad_head + jnp.einsum(
            "rd,rv->dv", rows_all, d_logits, preferred_element_type=jnp.float32
        )
        d_picked = lax.psum_scatter(
            jnp.einsum("rv,dv->rd", d_logits, head_low, preferred_element_type=jnp.float32),
            "shard",
            scatter_dimension=0,
            tiled=True,
        )
        d_final = jnp.zeros((seq_dev, D), jnp.float32).at[places].add(d_picked, mode="drop")
        back_in, back_back = (
            lax.all_gather(in_low, "shard", axis=0, tiled=True),
            lax.all_gather(back_low, "shard", axis=0, tiled=True),
        )
        _, pull_last = jax.vjp(norm_rows, after_add, gain_last, shift_last)
        d_after, d_gain_last, d_shift_last = pull_last(d_final)
        d_branch = d_after.astype(jnp.bfloat16)
        grad_back = grad_back + jnp.einsum(
            "sc,sd->cd", joined, d_branch, preferred_element_type=jnp.float32
        )
        d_joined = jnp.einsum("sd,cd->sc", d_branch, back_back, preferred_element_type=jnp.float32)
        d_attended = d_joined[:, :D].astype(jnp.bfloat16).reshape(seq_dev, H, HD)
        _, pull_gelu = jax.vjp(gelu_exact, hidden_pre)
        d_hidden = pull_gelu(d_joined[:, D:])[0].astype(jnp.bfloat16)
        probs_again = jnp.exp(masked_scores(queries, keys_all, allowed) - logsum)
        d_probs = jnp.einsum(
            "qhd,khd->hqk", d_attended, values_all, preferred_element_type=jnp.float32
        )
        d_scores = (
            probs_again * (d_probs - jnp.sum(probs_again * d_probs, axis=-1, keepdims=True))
        ).astype(jnp.bfloat16)
        d_queries = jnp.einsum(
            "hqk,khd->qhd", d_scores, keys_all, preferred_element_type=jnp.float32
        ) * HD ** (-0.5)
        low_probs = probs_again.astype(jnp.bfloat16)
        d_keys = jnp.einsum(
            "hqk,qhd->khd", d_scores, queries, preferred_element_type=jnp.float32
        ) * HD ** (-0.5)
        d_values = jnp.einsum(
            "hqk,qhd->khd", low_probs, d_attended, preferred_element_type=jnp.float32
        )
        key_grads = lax.psum_scatter(
            jnp.concatenate(
                [
                    d_keys.reshape(seq_dev * lax.axis_size("rep"), D),
                    d_values.reshape(seq_dev * lax.axis_size("rep"), D),
                ],
                axis=1,
            ),
            "rep",
            scatter_dimension=0,
            tiled=True,
        )
        d_key_rows = rotate(key_grads[:, :D].reshape(seq_dev, H, HD), -own_float).reshape(
            seq_dev, D
        )
        d_query_rows = rotate(d_queries, -own_float).reshape(seq_dev, D)
        d_projected = jnp.concatenate([d_query_rows, d_key_rows, key_grads[:, D:]], axis=1).astype(
            jnp.bfloat16
        )
        grad_in = grad_in + jnp.concatenate(
            [
                jnp.einsum("sd,sc->dc", low_one, d_projected, preferred_element_type=jnp.float32),
                jnp.einsum("sd,sc->dc", low_two, d_hidden, preferred_element_type=jnp.float32),
            ],
            axis=1,
        )
        d_normed_one = jnp.einsum(
            "sc,dc->sd", d_projected, back_in[:, : 3 * D], preferred_element_type=jnp.float32
        )
        d_normed_two = jnp.einsum(
            "sc,dc->sd", d_hidden, back_in[:, 3 * D :], preferred_element_type=jnp.float32
        )
        _, pull_one = jax.vjp(norm_rows, residual, gain_one, shift_one)
        d_resid_one, d_gain_one, d_shift_one = pull_one(d_normed_one)
        _, pull_two = jax.vjp(norm_rows, residual, gain_two, shift_two)
        d_resid_two, d_gain_two, d_shift_two = pull_two(d_normed_two)
        d_residual = (d_after + d_resid_one + d_resid_two).astype(jnp.bfloat16)
        returned = lax.all_to_all(d_residual.T, "shard", split_axis=0, concat_axis=1, tiled=True)
        grad_embed = grad_embed.at[:, ids_group[micro_at]].add(returned.astype(jnp.float32))
        grad_small = grad_small + jnp.concatenate(
            [
                d_gain_one,
                d_shift_one,
                d_gain_two,
                d_shift_two,
                d_gain_last,
                d_shift_last,
                jnp.sum(d_projected.astype(jnp.float32), axis=0),
                jnp.sum(d_hidden.astype(jnp.float32), axis=0),
                jnp.sum(d_branch.astype(jnp.float32), axis=0),
            ]
        )
    shard_in, shard_back, shard_small = (
        lax.psum_scatter(grad_in, "shard", scatter_dimension=0, tiled=True),
        lax.psum_scatter(grad_back, "shard", scatter_dimension=0, tiled=True),
        lax.psum_scatter(grad_small, "shard", scatter_dimension=0, tiled=True),
    )
    summed = lax.psum(
        (shard_in, shard_back, shard_small, grad_head, grad_embed, loss_sum, count_sum), "rep"
    )
    local_square = (
        jnp.sum(summed[0] * summed[0])
        + jnp.sum(summed[1] * summed[1])
        + jnp.sum(summed[2] * summed[2])
        + jnp.sum(summed[3] * summed[3])
        + jnp.sum(summed[4] * summed[4])
    )
    norm_value = jnp.sqrt(lax.psum(local_square, "shard"))
    factor = CLIP_LEVEL / jnp.maximum(norm_value, CLIP_LEVEL)
    next_in, moment_in, square_in = adamw(proj_in, summed[0] * factor, first_in, second_in, RATE_IN)
    next_back, moment_back, square_back = adamw(
        proj_back, summed[1] * factor, first_back, second_back, RATE_BACK
    )
    next_small, moment_small, square_small = adamw(
        small_params, summed[2] * factor, first_small, second_small, RATE_SMALL
    )
    next_head, moment_head, square_head = adamw(
        head_table, summed[3] * factor, first_head, second_head, RATE_HEAD
    )
    next_embed, moment_embed, square_embed = adamw(
        embed_table, summed[4] * factor, first_embed, second_embed, RATE_EMBED
    )
    return (
        jnp.stack([summed[5], summed[6]]),
        norm_value.reshape(1),
        next_in,
        moment_in,
        square_in,
        next_back,
        moment_back,
        square_back,
        next_small,
        moment_small,
        square_small,
        next_head,
        moment_head,
        square_head,
        next_embed,
        moment_embed,
        square_embed,
    )


MESH = pl.DeviceIdType.MESH
RG = 4
SG = 8


def whereabouts():
    rep = lax.axis_index("rep")
    shard = lax.axis_index("shard")
    core_twin = rep + 1 - 2 * lax.rem(rep, 2)
    x_twin = lax.rem(rep + 2, RG)
    y_twin = shard + 1 - 2 * lax.rem(shard, 2)
    return rep, shard, core_twin, x_twin, y_twin


def z_peer(shard, step):
    return lax.rem(shard + 2 * step, SG)


def shard_peer(shard, step):
    return lax.rem(shard + step, SG)


def greet(partners):
    barrier = pltpu.get_barrier_semaphore()
    for partner in partners:
        pl.semaphore_signal(barrier, inc=1, device_id=partner, device_id_type=MESH)
    pl.semaphore_wait(barrier, len(partners))


def remote(src, dst, send_sem, recv_sem, partner):
    return pltpu.make_async_remote_copy(
        src_ref=src,
        dst_ref=dst,
        send_sem=send_sem,
        recv_sem=recv_sem,
        device_id=partner,
        device_id_type=MESH,
    )


def comm_call(kernel, out_shape, scratch, number, args, spaces=None, out_spaces=None, limit=None, grid=()):
    pick = {
        "a": pl.BlockSpec(memory_space=pl.ANY),
        "v": pl.BlockSpec(memory_space=pltpu.VMEM),
    }
    choose = lambda space: pick[space] if isinstance(space, str) else space
    spaces = spaces or "a" * len(args)
    out_spaces = out_spaces or "a" * len(out_shape)
    return pl.pallas_call(
        kernel,
        grid=grid,
        out_shape=out_shape,
        in_specs=[choose(space) for space in spaces],
        out_specs=[choose(space) for space in out_spaces],
        scratch_shapes=scratch,
        compiler_params=pltpu.CompilerParams(
            collective_id=number, has_side_effects=True, vmem_limit_bytes=limit
        ),
    )(*args)


def start_gather(source, out, slot, place, sems):
    send_z, recv_z, send_y, recv_y, own = sems
    rep, shard, _, _, y_twin = place
    keep = pltpu.make_async_copy(source, slot(out, shard), own)
    keep.start()
    first_y = remote(source, slot(out, shard), send_y.at[0], recv_y.at[0], (rep, y_twin))
    z_copies = [
        remote(source, slot(out, shard), send_z.at[step - 1], recv_z.at[step - 1], (rep, z_peer(shard, step)))
        for step in range(1, 4)
    ]
    for copy in z_copies:
        copy.start()
    first_y.start()
    return keep, first_y, z_copies


def finish_gather(started, out, slot, place, sems):
    send_z, recv_z, send_y, recv_y, own = sems
    rep, shard, _, _, y_twin = place
    keep, first_y, z_copies = started
    passed = []
    for step in range(1, 4):
        z_copies[step - 1].wait_recv()
        came_from = z_peer(shard, SG // 2 - step)
        passed.append(
            remote(slot(out, came_from), slot(out, came_from), send_y.at[step], recv_y.at[step], (rep, y_twin))
        )
        passed[-1].start()
    keep.wait()
    for copy in z_copies:
        copy.wait_send()
    first_y.wait()
    for copy in passed:
        copy.wait()


def gather_partners(place):
    rep, shard, _, _, y_twin = place
    return [(rep, z_peer(shard, step)) for step in range(1, 4)] + [(rep, y_twin)]


GATHER_SEMS = [pltpu.SemaphoreType.DMA((3,)), pltpu.SemaphoreType.DMA((3,)), pltpu.SemaphoreType.DMA((4,)), pltpu.SemaphoreType.DMA((4,)), pltpu.SemaphoreType.DMA]


def row_slot(out, index):
    height = out.shape[0] // SG
    return out.at[pl.ds(pl.multiple_of(index * height, height), height)]


def tile_user(tile):
    return jnp.where(tile < SG, tile, (tile - SG) // 4)


def tile_slot(tile):
    return jnp.where(tile < SG, 0, 1 + lax.rem(tile - SG + SG, 4))


def entry_kernel(
    table_steps, ints, smalls, weights_in, weights_back, table, head,
    ints_out, scales, bias, out, in_all, back_all, head_low,
    ints_all, smalls_all, in_parts, back_tiles, turned, wide, low, ids,
    send_int, recv_int, send_small, recv_small, send_rep, recv_rep,
    send_in, recv_in, send_back, recv_back, send_far, recv_far, send_pair, recv_pair,
    send_up, recv_up, send_down, recv_down, send_y, recv_y, own,
):
    at = pl.program_id(0)
    last = pl.num_programs(0) - 1
    rep, shard, core_twin, x_twin, y_twin = whereabouts()
    level, side = shard // 2, lax.rem(shard, 2)
    shard_peers = [(rep, shard_peer(shard, step)) for step in range(1, SG)]
    rep_peers = [(lax.rem(rep + step, RG), shard) for step in range(1, RG)]
    lines, tokens, feats = low.shape
    small_rows = 14

    def int_copies():
        return [
            remote(ints, ints_all.at[rep, shard], send_int.at[k], recv_int.at[k], peer)
            for k, peer in enumerate(shard_peers)
        ]

    def small_copies():
        return [
            remote(smalls, smalls_all.at[shard], send_small.at[k], recv_small.at[k], peer)
            for k, peer in enumerate(shard_peers)
        ]

    def rep_copies():
        return [
            remote(ints_all.at[rep], ints_all.at[rep], send_rep.at[k], recv_rep.at[k], peer)
            for k, peer in enumerate(rep_peers)
        ]

    def in_copies():
        return [
            remote(in_parts.at[peer[1], rep], in_all.at[shard, rep], send_in.at[k], recv_in.at[k], peer)
            for k, peer in enumerate(shard_peers)
        ]

    def own_in():
        return pltpu.make_async_copy(in_parts.at[shard, rep], in_all.at[shard, rep], own.at[0])

    def back_move(k):
        tile = 5 * shard + k
        user, slot = tile_user(tile), tile_slot(tile)
        there = remote(
            back_tiles.at[k, rep], back_all.at[slot, rep], send_back.at[k], recv_back.at[slot], (rep, user)
        )
        return user, slot, there

    def quarter_copies(quarter, sends, recvs, base, peer):
        return [
            remote(array.at[:, quarter], array.at[:, quarter], sends.at[base + k], recvs.at[base + k], (peer, shard))
            for k, array in enumerate((in_all, back_all))
        ]

    def far_copies():
        return quarter_copies(rep, send_far, recv_far, 0, x_twin)

    def pair_copies():
        return quarter_copies(rep, send_pair, recv_pair, 0, core_twin) + quarter_copies(
            x_twin, send_pair, recv_pair, 2, core_twin
        )

    def slot(line, z_at, y_at):
        index = 2 * z_at + y_at
        return out.at[pl.ds(line * tokens, tokens), pl.ds(pl.multiple_of(index * feats, feats), feats)]

    def up_copy(line, hop):
        here = slot(line, level - hop, side)
        source = low.at[line] if hop == 0 else here
        return remote(source, here, send_up.at[line, hop], recv_up.at[line, hop], (rep, shard + 2))

    def down_copy(line, hop):
        here = slot(line, level + hop, side)
        source = low.at[line] if hop == 0 else here
        return remote(source, here, send_down.at[line, hop], recv_down.at[line, hop], (rep, shard - 2))

    def side_copy(line, z_at, source=None):
        here = slot(line, z_at, side)
        return remote(
            here if source is None else source, here, send_y.at[line, z_at], recv_y.at[line, z_at], (rep, y_twin)
        )

    def keep_copy(line):
        return pltpu.make_async_copy(low.at[line], slot(line, level, side), own.at[2 + line])

    def pass_on(line, hop):
        @pl.when(level >= hop)
        def _():
            pltpu.make_async_copy(low.at[line], slot(line, level - hop, side), recv_up.at[line, hop - 1]).wait()
            if hop < 3:
                pl.when(level < 3)(lambda: up_copy(line, hop).start())
            side_copy(line, level - hop).start()

        @pl.when(level + hop <= 3)
        def _():
            pltpu.make_async_copy(low.at[line], slot(line, level + hop, side), recv_down.at[line, hop - 1]).wait()
            if hop < 3:
                pl.when(level > 0)(lambda: down_copy(line, hop).start())
            side_copy(line, level + hop).start()

    @pl.when(at == 0)
    def _():
        greet(shard_peers + rep_peers)
        for copy in int_copies() + small_copies():
            copy.start()
        for target in range(SG):
            for part in range(3):
                columns = weights_in[:, part * D + target * HEAD_COLS : part * D + (target + 1) * HEAD_COLS]
                in_parts[target, :, :, part * HEAD_COLS : (part + 1) * HEAD_COLS] = columns.astype(
                    in_parts.dtype
                ).reshape(RG, in_parts.shape[2], HEAD_COLS)
            columns = weights_in[:, 3 * D + target * UNITS : 3 * D + (target + 1) * UNITS]
            in_parts[target, :, :, 3 * HEAD_COLS :] = columns.astype(in_parts.dtype).reshape(
                RG, in_parts.shape[2], UNITS
            )
        back_tiles[...] = weights_back[...].astype(back_tiles.dtype).reshape(back_tiles.shape)
        for copy in in_copies():
            copy.start()
        own_in().start()
        for k in range(5):
            user, slot_at, there = back_move(k)
            here = pltpu.make_async_copy(back_tiles.at[k, rep], back_all.at[slot_at, rep], recv_back.at[slot_at])
            pl.when(user == shard)(here.start)
            pl.when(user != shard)(there.start)
        ints_all[rep, shard] = ints[...]
        smalls_all[shard] = smalls[...]

    @pl.when(at < table_steps)
    def _():
        block = table[...].astype(jnp.bfloat16).astype(jnp.float32)
        width = block.shape[1]
        turned[pl.ds(pl.multiple_of(at * width, width), width), :] = block.T

    @pl.when(at == 5)
    def _():
        for copy in int_copies():
            copy.wait()
        for copy in rep_copies():
            copy.start()

    @pl.when(at == table_steps)
    def _():
        for copy in rep_copies():
            copy.wait()
        to_scalars = pltpu.make_async_copy(ints_all.at[:, pl.ds(2 * rep, 2)], ids, own.at[1])
        to_scalars.start()
        to_scalars.wait()
        for line in range(lines):
            micro, member = line // 2, line % 2
            for block_at in range(RG):

                @pl.loop(0, 16)
                def _(group):
                    for k in range(8):
                        lane = group * 8 + k
                        wide[pl.ds(block_at * 128 + lane, 1), :] = turned[
                            pl.ds(ids[block_at, member, micro, lane], 1), :
                        ]

            low[line] = wide[...].astype(jnp.bfloat16)
            pl.when(level < 3)(lambda: up_copy(line, 0).start())
            pl.when(level > 0)(lambda: down_copy(line, 0).start())
            side_copy(line, level, low.at[line]).start()
            keep_copy(line).start()
        own_in().wait()
        for copy in in_copies():
            copy.wait()
        for k in range(5):
            pltpu.make_async_copy(back_tiles.at[0, rep], back_all.at[k, rep], recv_back.at[k]).wait()
        for copy in far_copies():
            copy.start()

    @pl.when(at >= table_steps)
    def _():
        head_low[...] = head[...].astype(jnp.bfloat16)

    order = sorted(((line, hop) for line in range(lines) for hop in range(1, 4)), key=lambda item: (sum(item), item[1]))
    for step, (line, hop) in enumerate(order):
        pl.when(at == table_steps + 1 + step)(functools.partial(pass_on, line, hop))

    @pl.when(at == last - 2)
    def _():
        for copy in far_copies():
            copy.wait()
        for copy in pair_copies():
            copy.start()

    @pl.when(at == last)
    def _():
        for copy in small_copies():
            copy.wait()
        ints_out[...] = ints_all[...]

        def small_row(row):
            return smalls_all[row // small_rows, pl.ds(lax.rem(row, small_rows), 1), :]

        scales[...] = jnp.zeros_like(scales)
        for vector, start in enumerate([8 * k for k in range(6)] + [8 * 13]):
            for part in range(8):
                row = start + part
                scales[vector : vector + 1, part * 128 : (part + 1) * 128] = smalls_all[
                    row // small_rows, row % small_rows : row % small_rows + 1, :
                ]
        for part in range(3):
            bias[:, part * 128 : (part + 1) * 128] = small_row(48 + 8 * part + shard)
        for part in range(4):
            bias[:, (3 + part) * 128 : (4 + part) * 128] = small_row(72 + 4 * shard + part)
        for k in range(5):
            user, _, there = back_move(k)
            pl.when(user != shard)(there.wait_send)
        for line in range(lines):
            keep_copy(line).wait()
            for hop in range(3):
                pl.when((level >= hop) & (level < 3))(lambda: up_copy(line, hop).wait_send())
                pl.when((level + hop <= 3) & (level > 0))(lambda: down_copy(line, hop).wait_send())
            for z_at in range(4):
                side_copy(line, z_at).wait()
        for copy in pair_copies():
            copy.wait()


def share_entry(ints, smalls, weights_in, weights_back, table, head, tokens, number):
    quarter = weights_in.shape[0] // RG
    in_shape = (SG, RG, quarter, OWN_COLS)
    back_shape = (5, RG, 32, weights_back.shape[1])
    dma = pltpu.SemaphoreType.DMA
    feats, vocab = table.shape
    blocks = pl.cdiv(vocab, TABLE_BLOCK)
    head_blocks = max(pl.cdiv(head.shape[0], CAST_BLOCK), 13)
    lines = 4
    per_line = tokens // lines
    head_spec = pl.BlockSpec(
        (CAST_BLOCK, head.shape[1]),
        lambda at: (jnp.clip(at - blocks, 0, pl.cdiv(head.shape[0], CAST_BLOCK) - 1), 0),
    )
    return comm_call(
        functools.partial(entry_kernel, blocks),
        [
            jax.ShapeDtypeStruct((RG, SG) + ints.shape, ints.dtype),
            jax.ShapeDtypeStruct((8, SG * feats), jnp.float32),
            jax.ShapeDtypeStruct((1, OWN_COLS), jnp.float32),
            jax.ShapeDtypeStruct((tokens, SG * feats), jnp.bfloat16),
            jax.ShapeDtypeStruct(in_shape, jnp.bfloat16),
            jax.ShapeDtypeStruct(back_shape, jnp.bfloat16),
            jax.ShapeDtypeStruct(head.shape, jnp.bfloat16),
        ],
        [
            pltpu.VMEM((RG, SG) + ints.shape, ints.dtype),
            pltpu.VMEM((SG,) + smalls.shape, smalls.dtype),
            pltpu.VMEM(in_shape, jnp.bfloat16),
            pltpu.VMEM(back_shape, jnp.bfloat16),
            pltpu.VMEM((blocks * TABLE_BLOCK, feats), jnp.float32),
            pltpu.VMEM((per_line, feats), jnp.float32),
            pltpu.VMEM((lines, per_line, feats), jnp.bfloat16),
            pltpu.SMEM((RG, 2) + ints.shape, jnp.int32),
        ]
        + [dma((SG - 1,))] * 4
        + [dma((RG - 1,))] * 2
        + [dma((SG - 1,))] * 2
        + [dma((5,))] * 2
        + [dma((2,))] * 2
        + [dma((4,))] * 2
        + [dma((lines, 3))] * 4
        + [dma((lines, 4))] * 2
        + [dma((2 + lines,))],
        number,
        (ints, smalls, weights_in, weights_back, table, head),
        ["v", "v", "v", "v", pl.BlockSpec((feats, TABLE_BLOCK), lambda at: (0, jnp.minimum(at, blocks - 1))), head_spec],
        ["v", "v", "v", "a", "a", "a", head_spec],
        VMEM_LIMIT,
        (blocks + head_blocks,),
    )


def gather_kernel(rows, out, *sems):
    place = whereabouts()
    greet(gather_partners(place))
    started = start_gather(rows, out, row_slot, place, sems)
    finish_gather(started, out, row_slot, place, sems)


def shard_gather(rows, number):
    return comm_call(
        gather_kernel,
        [jax.ShapeDtypeStruct((SG * rows.shape[0], rows.shape[1]), rows.dtype)],
        GATHER_SEMS,
        number,
        (rows,),
        "v",
        "v",
    )[0]


def stats_kernel(stats, out, send, recv):
    rep, shard, _, _, _ = whereabouts()
    peers = [(rep, shard_peer(shard, step)) for step in range(1, SG)]
    greet(peers)
    copies = [remote(stats, out.at[shard], send.at[at], recv.at[at], peer) for at, peer in enumerate(peers)]
    for copy in copies:
        copy.start()
    out[shard] = stats[...]
    for copy in copies:
        copy.wait()


def shard_stats(stats, number):
    dma = pltpu.SemaphoreType.DMA
    return comm_call(
        stats_kernel,
        [jax.ShapeDtypeStruct((SG,) + stats.shape, stats.dtype)],
        [dma((SG - 1,)), dma((SG - 1,))],
        number,
        (stats,),
        "v",
        "v",
    )[0]


def sum_sems():
    dma = pltpu.SemaphoreType.DMA
    return [dma((4,)), dma((4,)), dma((3,)), dma((3,))]


def sum_buffers(chunk):
    return [pltpu.VMEM((4,) + chunk, jnp.float32), pltpu.VMEM((4,) + chunk, jnp.float32), pltpu.VMEM((3,) + chunk, jnp.float32)]


def start_sum(parts, place, buffers, sems):
    rep, shard, _, _, y_twin = place
    from_y, own_sum, from_z = buffers
    send_y, recv_y, send_z, recv_z = sems
    y_copies = {}
    for step in (2, 1, 3, 0):
        y_copies[step] = remote(
            parts.at[z_peer(y_twin, step)], from_y.at[step], send_y.at[step], recv_y.at[step], (rep, y_twin)
        )
        y_copies[step].start()
    return y_copies


def finish_sum(y_copies, parts, out, place, buffers, sems, post=None):
    rep, shard, _, _, y_twin = place
    from_y, own_sum, from_z = buffers
    send_y, recv_y, send_z, recv_z = sems
    z_copies = []
    for step in (2, 1, 3):
        y_copies[step].wait_recv()
        own_sum[step] = parts[z_peer(shard, step)] + from_y[step]
        z_copies.append(
            remote(own_sum.at[step], from_z.at[step - 1], send_z.at[step - 1], recv_z.at[step - 1], (rep, z_peer(shard, step)))
        )
        z_copies[-1].start()
    y_copies[0].wait_recv()
    total = parts[shard] + from_y[0]
    for copy in z_copies:
        copy.wait_recv()
    out[...] = total + from_z[0] + from_z[1] + from_z[2]
    for step in range(4):
        y_copies[step].wait_send()
    for copy in z_copies:
        copy.wait_send()


def sum_kernel(parts, out, from_y, own_sum, from_z, *sems):
    place = whereabouts()
    greet(gather_partners(place))
    buffers = (from_y, own_sum, from_z)
    y_copies = start_sum(parts, place, buffers, sems)
    finish_sum(y_copies, parts, out, place, buffers, sems)


def shard_sum(parts, number):
    chunk = parts.shape[1:]
    return comm_call(
        sum_kernel,
        [jax.ShapeDtypeStruct(chunk, jnp.float32)],
        sum_buffers(chunk) + sum_sems(),
        number,
        (parts,),
        "v",
        "v",
        40 << 20,
    )[0]


def picked_kernel(parts, rows, facts, out, rows_all, facts_all, from_y, own_sum, from_z, *sems):
    place = whereabouts()
    rep, shard, core_twin, x_twin, _ = place
    sum_sem = sems[:4]
    send_row, recv_row, send_fact, recv_fact, own = sems[4:]
    rep_peers = [(lax.rem(rep + step, RG), shard) for step in range(1, RG)]
    greet(gather_partners(place) + rep_peers)
    buffers = (from_y, own_sum, from_z)
    y_copies = start_sum(parts, place, buffers, sum_sem)
    keep = pltpu.make_async_copy(rows, rows_all.at[rep], own)
    keep.start()
    to_x = remote(rows, rows_all.at[rep], send_row.at[0], recv_row.at[0], (x_twin, shard))
    to_core = remote(rows, rows_all.at[rep], send_row.at[1], recv_row.at[1], (core_twin, shard))
    to_x.start()
    to_core.start()
    fact_copies = [
        remote(facts, facts_all.at[rep], send_fact.at[at], recv_fact.at[at], peer) for at, peer in enumerate(rep_peers)
    ]
    for copy in fact_copies:
        copy.start()
    facts_all[rep] = facts[...]
    finish_sum(y_copies, parts, out, place, buffers, sum_sem)
    to_x.wait_recv()
    passed = remote(rows_all.at[x_twin], rows_all.at[x_twin], send_row.at[2], recv_row.at[2], (core_twin, shard))
    passed.start()
    keep.wait()
    to_x.wait_send()
    to_core.wait()
    for copy in fact_copies:
        copy.wait()
    passed.wait()


def sum_and_share(parts, rows, facts, number):
    dma = pltpu.SemaphoreType.DMA
    chunk = parts.shape[1:]
    return comm_call(
        picked_kernel,
        [
            jax.ShapeDtypeStruct(chunk, jnp.float32),
            jax.ShapeDtypeStruct((RG,) + rows.shape, rows.dtype),
            jax.ShapeDtypeStruct((RG,) + facts.shape, facts.dtype),
        ],
        sum_buffers(chunk) + sum_sems() + [dma((3,))] * 4 + [dma],
        number,
        (parts, rows, facts),
        "vvv",
        "vvv",
        40 << 20,
    )


def branch_kernel(rows, pieces, out, features, *sems):
    place = whereabouts()
    rep, shard, _, _, _ = place
    send, recv = sems[5:]
    peers = [(rep, shard_peer(shard, step)) for step in range(1, SG)]
    greet(peers)
    started = start_gather(rows, out, row_slot, place, sems[:5])
    copies = []
    for at, peer in enumerate(peers):
        copies.append(remote(pieces.at[peer[1]], features.at[shard], send.at[at], recv.at[at], peer))
        copies[-1].start()
    features[shard] = pieces[shard]
    finish_gather(started, out, row_slot, place, sems[:5])
    for copy in copies:
        copy.wait()


def share_branch(rows, pieces, number):
    dma = pltpu.SemaphoreType.DMA
    return comm_call(
        branch_kernel,
        [jax.ShapeDtypeStruct((SG * rows.shape[0], rows.shape[1]), rows.dtype), jax.ShapeDtypeStruct(pieces.shape, pieces.dtype)],
        GATHER_SEMS + [dma((SG - 1,))] * 2,
        number,
        (rows, pieces),
        "vv",
        "vv",
    )


def coded(rows, steps):
    inverse = jnp.where(steps > 0.0, 1.0 / steps, 0.0)
    return jnp.clip(jnp.round(rows * inverse), -32767.0, 32767.0).astype(jnp.int32).astype(jnp.int16)


def layer_kernel(
    vocab, parts, stats, base, unit, grad_in, grad_back, smalls, rows, facts, targets, head,
    rows_all, in_all, back_all, smalls_out, head_out, squares,
    low, sum_in, sum_back, turned, stats_all, steps_all, from_y, own_sum, from_z, pair_in, pair_back, half_in, half_back, far_in, far_back, small_rep, small_sum, small_shard,
    send_y, recv_y, send_z, recv_z, send_stat, recv_stat, send_pair, recv_pair, send_far, recv_far,
    send_rep, recv_rep, send_small, recv_small,
    send_row, recv_row, send_in, recv_in, send_back, recv_back, own,
):
    at = pl.program_id(0)
    last = pl.num_programs(0) - 1
    rep, shard, core_twin, x_twin, y_twin = whereabouts()
    core_far = lax.rem(core_twin + 2, RG)
    shard_peers = [(rep, shard_peer(shard, step)) for step in range(1, SG)]
    rep_peers = [(lax.rem(rep + step, RG), shard) for step in range(1, RG)]

    def rep_copies():
        return [
            remote(smalls, small_rep.at[k], send_rep.at[k], recv_rep.at[k], peer) for k, peer in enumerate(rep_peers)
        ]

    def pair_copies(which, slot):
        pairs = ((grad_in, pair_in), (grad_back, pair_back))
        return [
            remote(
                source.at[which], target.at[slot], send_pair.at[2 * slot + k], recv_pair.at[2 * slot + k],
                (core_twin, shard),
            )
            for k, (source, target) in enumerate(pairs)
        ]

    def y_copy(step):
        return remote(parts.at[z_peer(y_twin, step)], from_y.at[step], send_y.at[step], recv_y.at[step], (rep, y_twin))

    def z_copy(step):
        return remote(
            own_sum.at[step], from_z.at[step - 1], send_z.at[step - 1], recv_z.at[step - 1], (rep, z_peer(shard, step))
        )

    def stat_copies():
        return [
            remote(stats, stats_all.at[shard], send_stat.at[k], recv_stat.at[k], peer)
            for k, peer in enumerate(shard_peers)
        ]

    def far_copies():
        return [
            remote(half_in, far_in, send_far.at[0], recv_far.at[0], (x_twin, shard)),
            remote(half_back, far_back, send_far.at[1], recv_far.at[1], (x_twin, shard)),
        ]

    def small_copies():
        return [
            remote(small_sum.at[peer[1]], small_shard.at[k], send_small.at[k], recv_small.at[k], peer)
            for k, peer in enumerate(shard_peers)
        ]

    def in_copies():
        return [
            remote(sum_in.at[peer[1]], in_all.at[shard], send_in.at[k], recv_in.at[k], peer)
            for k, peer in enumerate(shard_peers)
        ]

    def own_in():
        return pltpu.make_async_copy(sum_in.at[shard], in_all.at[shard], own.at[0])

    def back_move(slot):
        tile = shard if slot == 0 else SG + 4 * shard + slot - 1
        owner, place = tile // 5, lax.rem(tile, 5)
        there = remote(sum_back.at[slot], back_all.at[place], send_back.at[slot], recv_back.at[place], (rep, owner))
        return owner, place, there

    def decoded(codes, steps):
        return codes.astype(jnp.int32).astype(jnp.float32) * steps

    def pair_sum(step):
        y_copy(step).wait_recv()
        own = decoded(parts[z_peer(shard, step)], steps_all[:, 0:1])
        return own + decoded(from_y[step], steps_all[:, 4:5])

    def pass_on(step):
        own_sum[step] = coded(pair_sum(step), steps_all[:, 0:1] + steps_all[:, 4:5])
        z_copy(step).start()

    @pl.when(at == 0)
    def _():
        greet(shard_peers + rep_peers)
        for copy in stat_copies():
            copy.start()
        for step in (2, 1, 3, 0):
            y_copy(step).start()
        for copy in pair_copies(core_far, 1) + pair_copies(core_twin, 0) + rep_copies():
            copy.start()
        stats_all[shard] = stats[...]
        squares[...] = jnp.zeros_like(squares)
        for group in range(RG):
            turned[group] = rows[group].T

    @pl.when(at == 1)
    def _():
        for copy in pair_copies(core_far, 1):
            copy.wait()
        half_in[...] = grad_in[x_twin] + pair_in[1]
        half_back[...] = grad_back[x_twin] + pair_back[1]
        for copy in far_copies():
            copy.start()
        for copy in rep_copies():
            copy.wait()
        small_sum[...] = smalls[...] + small_rep[0] + small_rep[1] + small_rep[2]
        for copy in small_copies():
            copy.start()

    @pl.when(at == 3)
    def _():
        for copy in stat_copies():
            copy.wait()
        near = [stats_all[z_peer(shard, k), 2:3, :] for k in range(4)]
        near += [stats_all[z_peer(y_twin, k), 2:3, :] for k in range(4)]
        sums = stats_all[0]
        for k in range(1, SG):
            sums = sums + stats_all[k]
        near += [sums[0:2, :], stats[3:4, :], jnp.zeros((5, sums.shape[1]), jnp.float32)]
        steps_all[:, 0:16] = jnp.concatenate(near, axis=0).T
        pass_on(2)

    pl.when(at == 6)(lambda: pass_on(1))
    pl.when(at == 8)(lambda: pass_on(3))

    @pl.when(at == 10)
    def _():
        for copy in pair_copies(core_twin, 0):
            copy.wait()
        for copy in far_copies():
            copy.wait()
        sum_in[...] = grad_in[rep] + pair_in[0] + far_in[...]
        sum_back[...] = grad_back[rep] + pair_back[0] + far_back[...]
        for copy in in_copies():
            copy.start()
        own_in().start()
        for slot in range(5):
            owner, place, there = back_move(slot)
            here = pltpu.make_async_copy(sum_back.at[slot], back_all.at[place], recv_back.at[place])
            pl.when(owner == shard)(here.start)
            pl.when(owner != shard)(there.start)

    def head_block(size):
        total = None
        for group in range(RG):
            base = at * VOCAB_BLOCK
            grads = logit_grads(head[:size], turned[group], facts[group, 0:1, :], targets[group, 0:1, :] - base)
            term = plain_dot(grads, rows[group])
            total = term if total is None else total + term
        head_out[:size] = total
        squares[0:1, :] += jnp.sum(total * total, axis=0, keepdims=True)

    vocab_blocks(vocab, VOCAB_BLOCK, head_block)

    @pl.when(at == last)
    def _():
        total = pair_sum(0)
        for step in (1, 2, 3):
            z_copy(step).wait()
            behind = 4 - step
            steps = steps_all[:, behind : behind + 1] + steps_all[:, 4 + behind : 5 + behind]
            total = total + decoded(from_z[step - 1], steps)
        mean, slope, scale = (steps_all[:, k : k + 1] for k in (8, 9, 10))
        d_rows = (total - mean / D - unit[...] * (slope / D)) * scale
        low[...] = (base[...] + d_rows).astype(low.dtype)
        to_x = remote(low, rows_all.at[rep], send_row.at[0], recv_row.at[0], (x_twin, shard))
        to_core = remote(low, rows_all.at[rep], send_row.at[1], recv_row.at[1], (core_twin, shard))
        keep = pltpu.make_async_copy(low, rows_all.at[rep], own.at[1])
        to_x.start()
        to_core.start()
        keep.start()
        for copy in small_copies():
            copy.wait()
        whole = small_sum[shard]
        for k in range(SG - 1):
            whole = whole + small_shard[k]
        smalls_out[...] = whole
        for step in range(4):
            y_copy(step).wait_send()
        to_x.wait_recv()
        passed = remote(rows_all.at[x_twin], rows_all.at[x_twin], send_row.at[2], recv_row.at[2], (core_twin, shard))
        passed.start()
        own_in().wait()
        for copy in in_copies():
            copy.wait()
        for place in range(5):
            pltpu.make_async_copy(sum_back.at[0], back_all.at[place], recv_back.at[place]).wait()
        for slot in range(5):
            owner, _, there = back_move(slot)
            pl.when(owner != shard)(there.wait_send)
        keep.wait()
        to_x.wait_send()
        to_core.wait()
        passed.wait()


def layer_sums(parts, stats, base, unit, grad_in, grad_back, smalls, rows, facts, targets, head, number):
    dma = pltpu.SemaphoreType.DMA
    chunk = parts.shape[1:]
    quarter_in, quarter_back, piece = grad_in.shape[1:], grad_back.shape[1:], smalls.shape[1:]
    vocab, depth = head.shape
    vmem = lambda shape: pltpu.VMEM(shape, jnp.float32)
    shape = lambda dims: jax.ShapeDtypeStruct(dims, jnp.float32)
    block = pl.BlockSpec((VOCAB_BLOCK, depth), lambda at: (at, 0))
    return comm_call(
        functools.partial(layer_kernel, vocab),
        [
            jax.ShapeDtypeStruct((RG,) + chunk, jnp.bfloat16),
            shape(quarter_in),
            shape(quarter_back),
            shape(piece),
            shape(head.shape),
            shape((8, depth)),
        ],
        [pltpu.VMEM(chunk, jnp.bfloat16), vmem(quarter_in), vmem(quarter_back)]
        + [pltpu.VMEM((RG, depth, rows.shape[1]), rows.dtype), vmem((SG,) + stats.shape), vmem((chunk[0], 128))]
        + [pltpu.VMEM((count,) + chunk, parts.dtype) for count in (4, 4, 3)]
        + [vmem((2,) + quarter_in), vmem((2,) + quarter_back), vmem(quarter_in), vmem(quarter_back), vmem(quarter_in), vmem(quarter_back)]
        + [vmem((3,) + smalls.shape), vmem(smalls.shape), vmem((SG - 1,) + piece)]
        + sum_sems()
        + [dma((SG - 1,))] * 2 + [dma((4,))] * 2 + [dma((2,))] * 2 + [dma((3,))] * 2 + [dma((SG - 1,))] * 2
        + [dma((3,))] * 2 + [dma((SG - 1,))] * 2 + [dma((5,))] * 2 + [dma((2,))],
        number,
        (parts, stats, base, unit, grad_in, grad_back, smalls, rows, facts, targets, head),
        ["v"] * 10 + [block],
        ["a"] * 3 + ["v", block, "v"],
        62 << 20,
        (pl.cdiv(vocab, VOCAB_BLOCK),),
    )


def total_kernel(value, out, from_rep, half, from_shard, send_rep, recv_rep, send_shard, recv_shard):
    rep, shard, _, _, _ = whereabouts()
    shard_peers = [(rep, shard_peer(shard, step)) for step in range(1, SG)]
    rep_peers = [(lax.rem(rep + step, RG), shard) for step in range(1, RG)]
    greet(shard_peers + rep_peers)
    copies = [
        remote(value, from_rep.at[rep], send_rep.at[k], recv_rep.at[k], peer) for k, peer in enumerate(rep_peers)
    ]
    for copy in copies:
        copy.start()
    from_rep[rep] = value[...]
    for copy in copies:
        copy.wait()
    half[...] = from_rep[0] + from_rep[1] + from_rep[2] + from_rep[3]
    copies = [
        remote(half, from_shard.at[shard], send_shard.at[k], recv_shard.at[k], peer)
        for k, peer in enumerate(shard_peers)
    ]
    for copy in copies:
        copy.start()
    from_shard[shard] = half[...]
    for copy in copies:
        copy.wait()
    total = from_shard[0]
    for k in range(1, SG):
        total = total + from_shard[k]
    out[...] = total


def total_everywhere(value, number):
    dma = pltpu.SemaphoreType.DMA
    return comm_call(
        total_kernel,
        [jax.ShapeDtypeStruct(value.shape, value.dtype)],
        [pltpu.VMEM((RG,) + value.shape, value.dtype), pltpu.VMEM(value.shape, value.dtype), pltpu.VMEM((SG,) + value.shape, value.dtype)]
        + [dma((RG - 1,))] * 2 + [dma((SG - 1,))] * 2,
        number,
        (value,),
        "v",
        "v",
    )[0]


GROUP_HEADS = H // SG
HEAD_COLS = GROUP_HEADS * HD
UNITS = FF // SG
OWN_COLS = 3 * HEAD_COLS + UNITS
VOCAB_BLOCK = 512
ROW_BLOCK = 1024
TABLE_BLOCK = 4096
CAST_BLOCK = 512
VMEM_LIMIT = 60 << 20


def transposed_dot(left, right):
    return lax.dot_general(left, right, (((1,), (1,)), ((), ())), preferred_element_type=jnp.float32)


def first_dot(left, right):
    return lax.dot_general(left, right, (((0,), (0,)), ((), ())), preferred_element_type=jnp.float32)


def plain_dot(left, right):
    return jnp.dot(left, right, preferred_element_type=jnp.float32)


def vocab_blocks(vocab, height, body):
    at = pl.program_id(0)
    full, tail = divmod(vocab, height)
    pl.when(at < full)(lambda: body(height))
    if tail > 0:
        pl.when(at == full)(lambda: body(tail))


def top_kernel(vocab, rows, targets, head, stats, turned, top, total, target):
    at = pl.program_id(0)

    @pl.when(at == 0)
    def _():
        turned[...] = rows[...].T
        top[...] = jnp.full_like(top, -1e30)
        total[...] = jnp.zeros_like(total)
        target[...] = jnp.zeros_like(target)

    def block(size):
        logits = plain_dot(head[:size], turned[...])
        hits = lax.broadcasted_iota(jnp.int32, logits.shape, 0) == targets[...] - at * ROW_BLOCK
        target[...] += jnp.sum(jnp.where(hits, logits, 0.0), axis=0, keepdims=True)
        highest = jnp.maximum(top[...], jnp.max(logits, axis=0, keepdims=True))
        weights = jnp.sum(jnp.exp(logits - highest), axis=0, keepdims=True)
        total[...] = total[...] * jnp.exp(top[...] - highest) + weights
        top[...] = highest

    vocab_blocks(vocab, ROW_BLOCK, block)

    @pl.when(at == pl.num_programs(0) - 1)
    def _():
        stats[...] = jnp.zeros_like(stats)
        stats[0:1, :] = top[...]
        stats[1:2, :] = total[...]
        stats[2:3, :] = target[...]


def logit_stats(rows, targets, head):
    vocab, depth = head.shape
    count = rows.shape[0]
    line = pltpu.VMEM((1, count), jnp.float32)
    return pl.pallas_call(
        functools.partial(top_kernel, vocab),
        grid=(pl.cdiv(vocab, ROW_BLOCK),),
        in_specs=[
            pl.BlockSpec((count, depth), lambda at: (0, 0)),
            pl.BlockSpec((1, count), lambda at: (0, 0)),
            pl.BlockSpec((ROW_BLOCK, depth), lambda at: (at, 0)),
        ],
        out_specs=pl.BlockSpec((8, count), lambda at: (0, 0)),
        out_shape=jax.ShapeDtypeStruct((8, count), jnp.float32),
        scratch_shapes=[pltpu.VMEM((depth, count), rows.dtype), line, line, line],
        compiler_params=pltpu.CompilerParams(vmem_limit_bytes=VMEM_LIMIT),
    )(rows, targets, head)


def logit_grads(low, turned, logsum, targets):
    logits = plain_dot(low, turned)
    hits = lax.broadcasted_iota(jnp.int32, logits.shape, 0) == targets
    weights = jnp.exp(logits - logsum)
    return jnp.where(hits, weights - 1.0, weights).astype(jnp.bfloat16)


def rows_kernel(vocab, rows, facts, targets, head, out, turned):
    at = pl.program_id(0)

    @pl.when(at == 0)
    def _():
        turned[...] = rows[...].T
        out[...] = jnp.zeros_like(out)

    def block(size):
        low = head[:size]
        out[...] += first_dot(logit_grads(low, turned[...], facts[0:1, :], targets[...] - at * ROW_BLOCK), low)

    vocab_blocks(vocab, ROW_BLOCK, block)


def picked_grads(rows, facts, targets, head):
    vocab, depth = head.shape
    count = rows.shape[0]
    return pl.pallas_call(
        functools.partial(rows_kernel, vocab),
        grid=(pl.cdiv(vocab, ROW_BLOCK),),
        in_specs=[
            pl.BlockSpec((count, depth), lambda at: (0, 0)),
            pl.BlockSpec((8, count), lambda at: (0, 0)),
            pl.BlockSpec((1, count), lambda at: (0, 0)),
            pl.BlockSpec((ROW_BLOCK, depth), lambda at: (at, 0)),
        ],
        out_specs=pl.BlockSpec((count, depth), lambda at: (0, 0)),
        out_shape=jax.ShapeDtypeStruct((count, depth), jnp.float32),
        scratch_shapes=[pltpu.VMEM((depth, count), rows.dtype)],
        compiler_params=pltpu.CompilerParams(vmem_limit_bytes=VMEM_LIMIT),
    )(rows, facts, targets, head)


def embed_grad_kernel(ids, rows, out, squares, table, wide):
    at = pl.program_id(0)
    width = out.shape[1]

    @pl.when(at == 0)
    def _():
        squares[...] = jnp.zeros_like(squares)
        wide[...] = rows[...].astype(jnp.float32)

        @pl.loop(0, table.shape[0] // 512)
        def _(part):
            table[pl.ds(pl.multiple_of(part * 512, 512), 512), :] = jnp.zeros((512, table.shape[1]), jnp.float32)

        @pl.loop(0, rows.shape[0] // 8)
        def _(group):
            for lane in range(8):
                token = group * 8 + lane
                here = pl.ds(ids[token], 1)
                table[here, :] = table[here, :] + wide[pl.ds(token, 1), :]

    block = table[pl.ds(pl.multiple_of(at * width, width), width), :]
    out[...] = block.T
    squares[...] += jnp.sum((block * block).reshape(width // 8, 8, block.shape[1]), axis=0)


def embed_grads(ids, rows, vocab):
    count, feats = rows.shape
    blocks = pl.cdiv(vocab, TABLE_BLOCK)
    return pl.pallas_call(
        embed_grad_kernel,
        grid=(blocks,),
        in_specs=[
            pl.BlockSpec(memory_space=pltpu.SMEM),
            pl.BlockSpec(memory_space=pltpu.VMEM),
        ],
        out_specs=[
            pl.BlockSpec((feats, TABLE_BLOCK), lambda at: (0, at)),
            pl.BlockSpec((8, feats), lambda at: (0, 0)),
        ],
        out_shape=[
            jax.ShapeDtypeStruct((feats, vocab), jnp.float32),
            jax.ShapeDtypeStruct((8, feats), jnp.float32),
        ],
        scratch_shapes=[
            pltpu.VMEM((blocks * TABLE_BLOCK, feats), jnp.float32),
            pltpu.VMEM((count, feats), jnp.float32),
        ],
        compiler_params=pltpu.CompilerParams(vmem_limit_bytes=VMEM_LIMIT),
    )(ids, rows)


def turn_tables(places):
    half_rot = ROT // 2
    lane = jnp.arange(HEAD_COLS) % HD
    exponent = (lane % half_rot).astype(jnp.float32) * (2.0 / ROT)
    angles = places[:, None] * jnp.exp(-exponent * jnp.log(10000.0))[None, :]
    cosine, sine = jnp.cos(angles), jnp.sin(angles)
    lane = lane[None, :]
    return (
        jnp.where(lane < ROT, cosine, 1.0),
        jnp.where(lane < half_rot, -sine, 0.0),
        jnp.where((lane >= half_rot) & (lane < ROT), sine, 0.0),
    )


def centred_rows(values):
    centred = values - jnp.mean(values, axis=-1, keepdims=True)
    spread = jnp.mean(centred * centred, axis=-1, keepdims=True)
    scale = lax.rsqrt(spread + NORM_EPS)
    return centred * scale, scale


def exact_dot(left, right, dims):
    return lax.dot_general(
        left, right, (dims, ((), ())), precision=lax.Precision.HIGHEST, preferred_element_type=jnp.float32
    )


def pick_matrix(places, tokens):
    token = lax.broadcasted_iota(jnp.int32, (tokens, places.shape[1]), 0)
    return (places == token).astype(jnp.float32)


def turn(rows, tables, sign):
    half_rot = ROT // 2
    own, after, before = tables
    width = rows.shape[1]
    return (
        rows * own
        + sign * (pltpu.roll(rows, width - half_rot, 1) * after)
        + sign * (pltpu.roll(rows, half_rot, 1) * before)
    )


def head_lanes(rows, head):
    lane = lax.broadcasted_iota(jnp.int32, rows.shape, 1)
    return jnp.where(lane // HD == head, rows, jnp.zeros_like(rows))


def head_probs(queries, keys, allowed, head):
    scores = transposed_dot(keys, head_lanes(queries, head)) * HD ** (-0.5)
    scores = jnp.where(allowed, scores, -1e30)
    exponent = jnp.exp(scores - jnp.max(scores, axis=0, keepdims=True))
    return exponent / jnp.sum(exponent, axis=0, keepdims=True)


def line_allowed(places, span, tokens):
    keys = lax.broadcasted_iota(jnp.int32, (tokens, places.shape[1]), 0)
    in_query = (places >= span) & (places < span + PIC)
    in_key = (keys >= span) & (keys < span + PIC)
    return (keys <= places) | (in_query & in_key)


def forward_kernel(
    spans, residual, places, scales, bias, own, after, before, weights, back,
    queries, keys, values, hidden, joined, picked_one, picked_two, picked_rows, branch,
):
    bf16 = jnp.bfloat16
    tokens = residual.shape[0]
    span = spans[pl.program_id(0)]
    gain_one, shift_one = scales[0:1, :], scales[1:2, :]
    gain_two, shift_two = scales[2:3, :], scales[3:4, :]
    unit, _ = centred_rows(residual[...].astype(jnp.float32))
    low_one = (unit * gain_one + shift_one).astype(bf16)
    slots = places[0:1, :]
    pick = pick_matrix(slots, tokens)
    rows = first_dot(pick.astype(bf16), residual[...])
    picked_rows[...] = rows.astype(bf16)
    unit, _ = centred_rows(rows)
    low_picked = (unit * gain_one + shift_one).astype(bf16)
    picked_one[...] = low_picked
    low_two = (unit * gain_two + shift_two).astype(bf16)
    picked_two[...] = low_two
    tables = (own[...], after[...], before[...])
    picked_tables = tuple(exact_dot(pick, table, ((0,), (0,))) for table in tables)
    two, three = 2 * HEAD_COLS, 3 * HEAD_COLS
    query = plain_dot(low_picked, weights[:, :HEAD_COLS]) + bias[:, :HEAD_COLS]
    query = turn(query, picked_tables, 1.0).astype(bf16)
    queries[...] = query
    key = plain_dot(low_one, weights[:, HEAD_COLS:two]) + bias[:, HEAD_COLS:two]
    key = turn(key, tables, 1.0).astype(bf16)
    keys[...] = key
    value = (plain_dot(low_one, weights[:, two:three]) + bias[:, two:three]).astype(bf16)
    values[...] = value
    allowed = line_allowed(slots, span, tokens)
    attended = None
    for head in range(GROUP_HEADS):
        probs = head_probs(query, key, allowed, head).astype(bf16)
        term = head_lanes(first_dot(probs, value), head)
        attended = term if attended is None else attended + term
    joined[:, :HEAD_COLS] = attended.astype(bf16)
    pre = plain_dot(low_two, weights[:, three:]) + bias[:, three:]
    hidden[...] = pre
    joined[:, HEAD_COLS:] = (0.5 * pre * (1.0 + lax.erf(pre * 0.5**0.5))).astype(bf16)
    branch[...] = plain_dot(joined[...], back[...])


def line_block(height, width):
    return pl.BlockSpec((height, width), lambda line: (line, 0))


def still(array):
    return pl.BlockSpec(array.shape, lambda line: (0,) * array.ndim)


def layer_forward(spans, residual, places, scales, bias, tables, weights, back):
    lines = spans.shape[0]
    tokens, slots = residual.shape[0] // lines, places.shape[1]
    depth = residual.shape[1]
    bf16, f32 = jnp.bfloat16, jnp.float32
    outs = [
        (slots, HEAD_COLS, bf16),
        (tokens, HEAD_COLS, bf16),
        (tokens, HEAD_COLS, bf16),
        (slots, UNITS, f32),
        (slots, HEAD_COLS + UNITS, bf16),
        (slots, depth, bf16),
        (slots, depth, bf16),
        (slots, depth, bf16),
        (slots, depth, f32),
    ]
    return pl.pallas_call(
        forward_kernel,
        grid=(lines,),
        in_specs=[
            pl.BlockSpec(memory_space=pltpu.SMEM),
            line_block(tokens, depth),
            line_block(8, slots),
            still(scales),
            still(bias),
            *[still(table) for table in tables],
            still(weights),
            still(back),
        ],
        out_specs=[line_block(height, width) for height, width, _ in outs],
        out_shape=[jax.ShapeDtypeStruct((lines * height, width), kind) for height, width, kind in outs],
        compiler_params=pltpu.CompilerParams(vmem_limit_bytes=VMEM_LIMIT),
    )(spans, residual, places, scales, bias, *tables, weights, back)


def backward_kernel(
    spans, residual, places, scales, own, after, before, weights, back,
    queries, keys, values, hidden, joined, picked_one, picked_two, d_branch, d_after,
    unit_parts, stats, base, own_unit, grad_in, grad_back, grad_scales, grad_bias, unit_rows,
):
    bf16 = jnp.bfloat16
    line = pl.program_id(0)
    tokens = residual.shape[0]
    span = spans[line]
    gain_one, shift_one = scales[0:1, :], scales[1:2, :]
    gain_two = scales[2:3, :]

    @pl.when(line == 0)
    def _():
        for total in (grad_in, grad_back, grad_scales, grad_bias):
            total[...] = jnp.zeros_like(total)

    slots = places[0:1, :]
    pick = pick_matrix(slots, tokens)
    base[...] = exact_dot(pick, d_after[...], ((1,), (0,)))
    tables = (own[...], after[...], before[...])
    picked_tables = tuple(exact_dot(pick, table, ((0,), (0,))) for table in tables)
    pick = pick.astype(bf16)
    d_rows = d_branch[...]
    d_joined = transposed_dot(d_rows, back[...])
    grad_back[...] += first_dot(joined[...], d_rows)
    d_attended = d_joined[:, :HEAD_COLS].astype(bf16)
    pre = hidden[...]
    slope = 0.5 * (1.0 + lax.erf(pre * 0.5**0.5)) + pre * jnp.exp(-0.5 * pre * pre) * (2.0 * 3.141592653589793) ** -0.5
    d_hidden = (d_joined[:, HEAD_COLS:] * slope).astype(bf16)
    allowed = line_allowed(slots, span, tokens)
    query, key, value = queries[...], keys[...], values[...]
    d_query = d_key = d_value = None
    for head in range(GROUP_HEADS):
        probs = head_probs(query, key, allowed, head)
        d_head = head_lanes(d_attended, head)
        d_probs = transposed_dot(value, d_head)
        d_scores = (probs * (d_probs - jnp.sum(probs * d_probs, axis=0, keepdims=True))).astype(bf16)
        terms = (
            head_lanes(first_dot(d_scores, key), head),
            plain_dot(d_scores, head_lanes(query, head)),
            plain_dot(probs.astype(bf16), d_head),
        )
        if d_query is None:
            d_query, d_key, d_value = terms
        else:
            d_query, d_key, d_value = d_query + terms[0], d_key + terms[1], d_value + terms[2]
    d_query = turn(d_query * HD ** (-0.5), picked_tables, -1.0).astype(bf16)
    d_key = turn(d_key * HD ** (-0.5), tables, -1.0).astype(bf16)
    d_value = d_value.astype(bf16)
    unit, unit_scale = centred_rows(residual[...].astype(jnp.float32))
    unit_rows[...] = unit
    feats = own_unit.shape[1]
    own_unit[...] = unit_rows[:, pl.ds(pl.multiple_of(lax.axis_index("shard") * feats, feats), feats)]
    low_one = (unit * gain_one + shift_one).astype(bf16)
    two, three = 2 * HEAD_COLS, 3 * HEAD_COLS
    grad_in[:, :HEAD_COLS] += first_dot(picked_one[...], d_query)
    grad_in[:, HEAD_COLS:two] += first_dot(low_one, d_key)
    grad_in[:, two:three] += first_dot(low_one, d_value)
    grad_in[:, three:] += first_dot(picked_two[...], d_hidden)

    def column_sum(rows):
        return jnp.sum(rows.astype(jnp.float32), axis=0, keepdims=True)

    grad_bias[0:1, :HEAD_COLS] += column_sum(d_query)
    grad_bias[0:1, HEAD_COLS:two] += column_sum(d_key)
    grad_bias[0:1, two:three] += column_sum(d_value)
    grad_bias[0:1, three:] += column_sum(d_hidden)
    d_normed = (
        transposed_dot(plain_dot(pick, d_query).astype(bf16), weights[:, :HEAD_COLS])
        + transposed_dot(d_key, weights[:, HEAD_COLS:two])
        + transposed_dot(d_value, weights[:, two:three])
    )
    d_unit = d_normed * gain_one
    grad_scales[0:1, :] += column_sum(d_normed * unit)
    grad_scales[1:2, :] += column_sum(d_normed)
    d_normed = transposed_dot(plain_dot(pick, d_hidden).astype(bf16), weights[:, three:])
    grad_scales[2:3, :] += column_sum(d_normed * unit)
    grad_scales[3:4, :] += column_sum(d_normed)
    d_unit = d_unit + d_normed * gain_two
    sum_one = jnp.sum(d_unit, axis=-1, keepdims=True)
    sum_two = jnp.sum(d_unit * unit, axis=-1, keepdims=True)
    steps = jnp.max(jnp.abs(d_unit), axis=-1, keepdims=True) * (1.0 / 32767.0)
    lane = lax.broadcasted_iota(jnp.int32, (tokens, 128), 1)
    columns = jnp.where(lane == 0, sum_one, jnp.where(lane == 1, sum_two, jnp.where(lane == 2, steps, unit_scale)))
    stats[...] = columns.T[:8, :]
    codes = coded(d_unit, steps)
    for part in range(unit_parts.shape[0]):
        unit_parts[part] = codes[:, part * feats : (part + 1) * feats]


def layer_backward(spans, residual, places, scales, tables, weights, back, kept, d_branch, d_after):
    lines = spans.shape[0]
    count, depth = residual.shape
    tokens, slots = count // lines, places.shape[1]
    feats = depth // SG
    f32 = jnp.float32
    whole = lambda height, width: pl.BlockSpec((height, width), lambda line: (0, 0))
    return pl.pallas_call(
        backward_kernel,
        grid=(lines,),
        in_specs=[
            pl.BlockSpec(memory_space=pltpu.SMEM),
            line_block(tokens, depth),
            line_block(8, slots),
            still(scales),
            *[still(table) for table in tables],
            still(weights),
            still(back),
            *[line_block(array.shape[0] // lines, array.shape[1]) for array in kept],
            line_block(slots, depth),
            line_block(slots, feats),
        ],
        out_specs=[
            pl.BlockSpec((SG, tokens, feats), lambda line: (0, line, 0)),
            pl.BlockSpec((8, tokens), lambda line: (0, line)),
            line_block(tokens, feats),
            line_block(tokens, feats),
            whole(depth, OWN_COLS),
            whole(HEAD_COLS + UNITS, depth),
            whole(8, depth),
            whole(8, OWN_COLS),
        ],
        out_shape=[
            jax.ShapeDtypeStruct((SG, count, feats), jnp.int16),
            jax.ShapeDtypeStruct((8, count), f32),
            jax.ShapeDtypeStruct((count, feats), f32),
            jax.ShapeDtypeStruct((count, feats), f32),
            jax.ShapeDtypeStruct((depth, OWN_COLS), f32),
            jax.ShapeDtypeStruct((HEAD_COLS + UNITS, depth), f32),
            jax.ShapeDtypeStruct((8, depth), f32),
            jax.ShapeDtypeStruct((8, OWN_COLS), f32),
        ],
        scratch_shapes=[pltpu.VMEM((tokens, depth), f32)],
        compiler_params=pltpu.CompilerParams(vmem_limit_bytes=VMEM_LIMIT),
    )(spans, residual, places, scales, *tables, weights, back, *kept, d_branch, d_after)


def group_plan(
    token_ids,
    pic_start,
    comp_pos,
    comp_tgt,
    proj_in,
    proj_back,
    small_params,
    head_table,
    embed_table,
    first_in,
    second_in,
    first_back,
    second_back,
    first_small,
    second_small,
    first_head,
    second_head,
    first_embed,
    second_embed,
):
    bf16 = jnp.bfloat16
    rep_at = lax.axis_index("rep")
    shard_at = lax.axis_index("shard")
    micro, _, seq_dev = token_ids.shape
    slots = comp_pos.shape[2]
    seq_len = seq_dev * RG
    lines = micro * SG // RG
    blocks = lines * RG
    own_blocks = blocks // SG
    tokens = lines * seq_len
    slot_count = blocks * slots
    own_slots = own_blocks * slots
    vocab_dev = head_table.shape[1]
    vocab = embed_table.shape[1]
    quarter = D // SG // RG

    place_line = jnp.concatenate([comp_pos[:, 0, :].reshape(-1), comp_tgt[:, 0, :].reshape(-1)])
    span_line = jnp.concatenate([pic_start[:, 0], jnp.zeros((seq_dev - micro,), jnp.int32)])
    ints = jnp.concatenate(
        [token_ids[:, 0, :], place_line[None], span_line[None], jnp.zeros((4, seq_dev), jnp.int32)]
    )
    small_low = small_params.astype(bf16).astype(jnp.float32).reshape(-1, 128)
    small_rows = small_low.shape[0]
    smalls = jnp.pad(small_low, ((0, 16 - small_rows), (0, 0)))
    ints_all, scales, own_bias, residual_low, in_all, back_all, head_low = share_entry(
        ints, smalls, proj_in, proj_back, embed_table, head_table.T, tokens, 1
    )
    own_in = in_all.reshape(D, OWN_COLS)
    own_back = back_all.reshape(5 * 128, D)
    gain_last, shift_last, bias_out = scales[4], scales[5], scales[6]

    by_group = ints_all.reshape(RG, RG, SG // RG, 8, seq_dev)
    ids_all = jnp.transpose(by_group[:, :, :, :micro], (1, 3, 2, 0, 4)).reshape(RG, tokens)
    slot_facts = jnp.transpose(
        by_group[:, :, :, 2].reshape(RG, RG, SG // RG, 2, micro, slots), (3, 1, 4, 2, 0, 5)
    ).reshape(2, RG, slot_count)
    used_all = slot_facts[0] < seq_dev
    targets_all = jnp.where(used_all, slot_facts[1] - shard_at * vocab_dev, -1)
    counted_all = used_all.astype(jnp.float32)
    pos_group = lax.dynamic_index_in_dim(slot_facts[0], rep_at, 0, False)
    targets_group = lax.dynamic_index_in_dim(targets_all, rep_at, 0, False)
    counted_group = lax.dynamic_index_in_dim(counted_all, rep_at, 0, False)
    spans = lax.dynamic_index_in_dim(by_group[0, :, :, 3, :micro], rep_at, 0, False).T.reshape(lines)

    slot_places = pos_group.reshape(lines, RG, slots)
    block_starts = (jnp.arange(RG) * seq_dev)[None, :, None]
    slot_places = jnp.where(slot_places < seq_dev, slot_places + block_starts, -1).reshape(lines, 1, RG * slots)
    slot_places = jnp.broadcast_to(slot_places, (lines, 8, RG * slots)).reshape(lines * 8, RG * slots)
    tables = turn_tables(jnp.arange(seq_len).astype(jnp.float32))
    *kept, picked_rows, branch_parts = layer_forward(
        spans, residual_low, slot_places, scales, own_bias, tables, own_in, own_back
    )
    branch = shard_sum(branch_parts.reshape(SG, own_slots, D), 3)

    own_residual = lax.dynamic_slice_in_dim(picked_rows, shard_at * own_slots, own_slots, 0).astype(jnp.float32)
    own_used = lax.dynamic_slice_in_dim(counted_group, shard_at * own_slots, own_slots, 0)
    after_add = own_residual + branch + bias_out
    final_rows, pull_last = jax.vjp(norm_rows, after_add, gain_last, shift_last)
    picked = (final_rows * own_used[:, None]).astype(bf16)
    rows_group = shard_gather(picked, 4)

    stats = logit_stats(rows_group, targets_group[None], head_low)
    stats_all = shard_stats(stats, 5)
    tops = stats_all[:, 0]
    top = jnp.max(tops, axis=0)
    logsum = top + jnp.log(jnp.sum(stats_all[:, 1] * jnp.exp(tops - top), axis=0))
    row_target = jnp.sum(stats_all[:, 2], axis=0)
    row_loss = jnp.where(counted_group > 0.0, logsum - row_target, 0.0)
    logsum = jnp.where(counted_group > 0.0, logsum, 1e30)
    facts = jnp.concatenate(
        [logsum[None], row_loss[None], counted_group[None], jnp.zeros((5, slot_count), jnp.float32)]
    )
    picked_parts = picked_grads(rows_group, facts, targets_group[None], head_low)
    d_picked, rows_all, facts_all = sum_and_share(
        picked_parts.reshape(SG, own_slots, D), rows_group, facts, 6
    )
    loss_sum = jnp.sum(facts_all[:, 1])
    count_sum = jnp.sum(facts_all[:, 2])
    targets_wide = jnp.broadcast_to(targets_all[:, None, :], (RG, 8, slot_count))

    d_after, d_gain_last, d_shift_last = pull_last(d_picked)
    d_branch_own = d_after.astype(bf16)
    d_bias_out = jnp.sum(d_branch_own.astype(jnp.float32), axis=0)
    pieces = jnp.transpose(d_after.reshape(own_slots, SG, D // SG), (1, 0, 2))
    d_branch, after_pieces = share_branch(d_branch_own, pieces, 7)
    d_after_feats = after_pieces.reshape(slot_count, D // SG)

    unit_parts, norm_stats, base, own_unit, grad_in, grad_back, grad_scales, grad_bias = layer_backward(
        spans, residual_low, slot_places, scales, tables, own_in, own_back, kept, d_branch, d_after_feats
    )

    def whole(columns, length):
        start = shard_at * columns.shape[0]
        return lax.dynamic_update_slice(jnp.zeros((length,), jnp.float32), columns, (start,))

    grad_small = jnp.concatenate(
        [
            grad_scales[:4].reshape(-1),
            d_gain_last,
            d_shift_last,
            *[whole(grad_bias[0, part * HEAD_COLS : (part + 1) * HEAD_COLS], D) for part in range(3)],
            whole(grad_bias[0, 3 * HEAD_COLS :], FF),
            d_bias_out,
        ]
    )
    grad_small = jnp.pad(grad_small.reshape(SG, small_rows, 128), ((0, 0), (0, 16 - small_rows), (0, 0)))
    in_quarters = jnp.transpose(grad_in.reshape(SG, RG, quarter, OWN_COLS), (1, 0, 2, 3))
    back_quarters = jnp.transpose(grad_back.reshape(5, RG, 32, D), (1, 0, 2, 3))
    d_rows_all, in_own, back_own, small_sum, grad_head, head_squares = layer_sums(
        unit_parts,
        norm_stats,
        base,
        own_unit,
        in_quarters,
        back_quarters,
        grad_small,
        rows_all,
        facts_all,
        targets_wide,
        head_low,
        8,
    )
    in_grads = lax.all_gather(in_own, "rep")
    back_grads = lax.all_gather(back_own, "rep")
    grad_embed, embed_squares = embed_grads(ids_all.reshape(-1), d_rows_all.reshape(RG * tokens, D // SG), vocab)

    in_grads = jnp.transpose(in_grads, (0, 2, 1, 3)).reshape(D // SG, SG, OWN_COLS)
    qkv_grads = jnp.transpose(
        in_grads[:, :, : 3 * HEAD_COLS].reshape(D // SG, SG, 3, HEAD_COLS), (0, 2, 1, 3)
    ).reshape(D // SG, 3 * D)
    grad_in = jnp.concatenate([qkv_grads, in_grads[:, :, 3 * HEAD_COLS :].reshape(D // SG, FF)], axis=1)
    grad_back = jnp.transpose(back_grads, (1, 0, 2, 3)).reshape(proj_back.shape)
    grad_small = small_sum[:small_rows].reshape(-1)

    repeated_square = jnp.sum(grad_small * grad_small) + jnp.sum(head_squares) + jnp.sum(embed_squares)
    local_square = repeated_square / RG + jnp.sum(in_own * in_own) + jnp.sum(back_own * back_own)
    norm_value = jnp.sqrt(total_everywhere(jnp.broadcast_to(local_square, (8, 128)), 10)[0, 0])
    factor = CLIP_LEVEL / jnp.maximum(norm_value, CLIP_LEVEL)
    next_in, moment_in, square_in = adamw(proj_in, grad_in * factor, first_in, second_in, RATE_IN)
    next_back, moment_back, square_back = adamw(
        proj_back, grad_back * factor, first_back, second_back, RATE_BACK
    )
    next_small, moment_small, square_small = adamw(
        small_params, grad_small * factor, first_small, second_small, RATE_SMALL
    )
    next_head, moment_head, square_head = adamw(
        head_table, grad_head.T * factor, first_head, second_head, RATE_HEAD
    )
    next_embed, moment_embed, square_embed = adamw(
        embed_table, grad_embed * factor, first_embed, second_embed, RATE_EMBED
    )
    return (
        jnp.stack([loss_sum, count_sum]),
        norm_value.reshape(1),
        next_in,
        moment_in,
        square_in,
        next_back,
        moment_back,
        square_back,
        next_small,
        moment_small,
        square_small,
        next_head,
        moment_head,
        square_head,
        next_embed,
        moment_embed,
        square_embed,
    )


def select_plan(mesh):
    if mesh.shape["rep"] == RG and mesh.shape["shard"] == SG:
        return group_plan
    return any_mesh


def solution(mesh):
    placed = (
        P(None, "shard", "rep"),
        P(None, "shard"),
        P(None, "shard", "rep"),
        P(None, "shard", "rep"),
        P("shard", None),
        P("shard", None),
        P("shard"),
        P(None, "shard"),
        P("shard", None),
        P("shard", None),
        P("shard", None),
        P("shard", None),
        P("shard", None),
        P("shard"),
        P("shard"),
        P(None, "shard"),
        P(None, "shard"),
        P("shard", None),
        P("shard", None),
    )
    return jax.shard_map(
        select_plan(mesh),
        mesh=mesh,
        in_specs=placed,
        out_specs=(
            P(),
            P(),
            P("shard", None),
            P("shard", None),
            P("shard", None),
            P("shard", None),
            P("shard", None),
            P("shard", None),
            P("shard"),
            P("shard"),
            P("shard"),
            P(None, "shard"),
            P(None, "shard"),
            P(None, "shard"),
            P("shard", None),
            P("shard", None),
            P("shard", None),
        ),
        check_vma=False,
    )
```

```python
import functools

import jax
import jax.numpy as jnp
from jax import lax
from jax.experimental import pallas as pl
from jax.experimental.pallas import tpu as pltpu
from jax.sharding import PartitionSpec as P

D = 1024
H = 16
HD = 64
ROT = 16
FF = 4096
PIC = 256
STEP = 10


NORM_EPS = 1e-05
CLIP_LEVEL = 1.0
BETA_FIRST = 0.9
BETA_SECOND = 0.95
ADAM_EPS = 1e-08
DECAY_RATE = 0.01
RATE_IN = 0.01
RATE_BACK = 0.05
RATE_SMALL = 0.3
RATE_HEAD = 0.01
RATE_EMBED = 0.3


def combined_all(part, axis, combine):
    gathered = jax.tree.map(lambda a: lax.all_gather(a, axis), part)

    def take(source):
        return jax.tree.map(lambda a: lax.dynamic_index_in_dim(a, source, 0, False), gathered)

    return lax.fori_loop(
        1, lax.axis_size(axis), lambda source, state: combine(state, take(source)), take(0)
    )


def norm_rows(values, gain_vec, shift_vec):
    centred = values - jnp.mean(values, axis=-1, keepdims=True)
    spread = jnp.mean(centred * centred, axis=-1, keepdims=True)
    return centred * lax.rsqrt(spread + NORM_EPS) * gain_vec + shift_vec


def rotate(head_rows, place_vec):
    half_rot = ROT // 2
    exponent = jnp.arange(half_rot).astype(jnp.float32) * (2.0 / ROT)
    angles = place_vec[:, None] * jnp.exp(-exponent * jnp.log(10000.0))
    cosine = jnp.cos(angles)[:, None, :]
    sine_part = jnp.sin(angles)[:, None, :]
    front_part = head_rows[..., :half_rot]
    back_part = head_rows[..., half_rot:ROT]
    return jnp.concatenate(
        [
            front_part * cosine - back_part * sine_part,
            back_part * cosine + front_part * sine_part,
            head_rows[..., ROT:],
        ],
        axis=-1,
    )


def split_small(gain_parts):
    marks = [0, D, 2 * D, 3 * D, 4 * D, 5 * D, 6 * D, 9 * D, 9 * D + FF, 10 * D + FF]
    return tuple((gain_parts[marks[number] : marks[number + 1]] for number in range(9)))


def gelu_exact(values):
    return jax.nn.gelu(values, approximate=False)


def combine_totals(earlier, later_part):
    highest = jnp.maximum(earlier[0], later_part[0])
    totals = earlier[1] * jnp.exp(earlier[0] - highest) + later_part[1] * jnp.exp(
        later_part[0] - highest
    )
    return (highest, totals, earlier[2] + later_part[2])


def allowed_mask(query_places, key_places, span_start):
    inside_query = (query_places >= span_start) & (query_places < span_start + PIC)
    inside_key = (key_places >= span_start) & (key_places < span_start + PIC)
    return (key_places[None, :] <= query_places[:, None]) | inside_query[:, None] & inside_key[
        None, :
    ]


def masked_scores(queries, keys_all, allowed):
    raw_scores = jnp.einsum(
        "qhd,khd->hqk", queries, keys_all, preferred_element_type=jnp.float32
    ) * HD ** (-0.5)
    return jnp.where(allowed[None], raw_scores, -1e30)


def adamw(weight, gradient, moment, square, rate_value):
    moment = BETA_FIRST * moment + (1.0 - BETA_FIRST) * gradient
    square = BETA_SECOND * square + (1.0 - BETA_SECOND) * gradient * gradient
    moment_hat = moment / (1.0 - BETA_FIRST**STEP)
    square_hat = square / (1.0 - BETA_SECOND**STEP)
    weight = weight - rate_value * (
        moment_hat / (jnp.sqrt(square_hat) + ADAM_EPS) + DECAY_RATE * weight
    )
    return (weight, moment, square)


def any_mesh(
    token_ids,
    pic_start,
    comp_pos,
    comp_tgt,
    proj_in,
    proj_back,
    small_params,
    head_table,
    embed_table,
    first_in,
    second_in,
    first_back,
    second_back,
    first_small,
    second_small,
    first_head,
    second_head,
    first_embed,
    second_embed,
):
    seq_dev = token_ids.shape[2]
    micro_count = token_ids.shape[0]
    vocab_dev = head_table.shape[1]
    rep_count = lax.axis_size("rep")
    seq_len = seq_dev * rep_count
    rep_at = lax.axis_index("rep")
    shard_at = lax.axis_index("shard")
    used_own = comp_pos[:, 0, :] < seq_dev
    marked = jnp.where(used_own, comp_tgt[:, 0, :], -1)
    ids_group, tgt_group = (
        lax.all_gather(token_ids[:, 0, :], "shard", axis=1, tiled=True),
        lax.all_gather(marked, "shard", axis=1, tiled=True),
    )
    in_low = proj_in.astype(jnp.bfloat16)
    back_low = proj_back.astype(jnp.bfloat16)
    small_low = small_params.astype(jnp.bfloat16)
    head_low = head_table.astype(jnp.bfloat16)
    table_low = embed_table.astype(jnp.bfloat16)
    own_places = rep_at * seq_dev + jnp.arange(seq_dev)
    key_places = jnp.arange(seq_len)
    own_float = own_places.astype(jnp.float32)
    vocab_ids = jnp.arange(vocab_dev)
    grad_in = jnp.zeros((D, 3 * D + FF), jnp.float32)
    grad_back = jnp.zeros((D + FF, D), jnp.float32)
    grad_small = jnp.zeros((10 * D + FF,), jnp.float32)
    grad_head = jnp.zeros(head_table.shape, jnp.float32)
    grad_embed = jnp.zeros(embed_table.shape, jnp.float32)
    loss_sum = jnp.zeros((), jnp.float32)
    count_sum = jnp.zeros((), jnp.float32)
    for micro_at in range(micro_count):
        wide_in, wide_back, wide_small = (
            lax.all_gather(in_low, "shard", axis=0, tiled=True),
            lax.all_gather(back_low, "shard", axis=0, tiled=True),
            lax.all_gather(small_low, "shard", axis=0, tiled=True),
        )
        (
            gain_one,
            shift_one,
            gain_two,
            shift_two,
            gain_last,
            shift_last,
            bias_qkv,
            bias_hidden,
            bias_out,
        ) = split_small(wide_small.astype(jnp.float32))
        columns = jnp.take(table_low, ids_group[micro_at], axis=1)
        arrived = lax.all_to_all(columns, "shard", split_axis=1, concat_axis=0, tiled=True)
        residual = arrived.T.astype(jnp.float32)
        normed_one = norm_rows(residual, gain_one, shift_one)
        normed_two = norm_rows(residual, gain_two, shift_two)
        low_one = normed_one.astype(jnp.bfloat16)
        low_two = normed_two.astype(jnp.bfloat16)
        projected = (
            jnp.dot(low_one, wide_in[:, : 3 * D], preferred_element_type=jnp.float32) + bias_qkv
        )
        queries = rotate(projected[:, :D].reshape(seq_dev, H, HD), own_float).astype(jnp.bfloat16)
        key_rows = (
            rotate(projected[:, D : 2 * D].reshape(seq_dev, H, HD), own_float)
            .astype(jnp.bfloat16)
            .reshape(seq_dev, D)
        )
        value_rows = projected[:, 2 * D :].astype(jnp.bfloat16)
        keys_all, values_all = (
            lax.all_gather(key_rows, "rep", axis=0, tiled=True),
            lax.all_gather(value_rows, "rep", axis=0, tiled=True),
        )
        keys_all = keys_all.reshape(seq_len, H, HD)
        values_all = values_all.reshape(seq_len, H, HD)
        allowed = allowed_mask(own_places, key_places, pic_start[micro_at, 0])
        scores = masked_scores(queries, keys_all, allowed)
        highest = jnp.max(scores, axis=-1, keepdims=True)
        exponent = jnp.exp(scores - highest)
        totals = jnp.sum(exponent, axis=-1, keepdims=True)
        logsum = highest + jnp.log(totals)
        attn_probs = (exponent / totals).astype(jnp.bfloat16)
        attended = (
            jnp.einsum("hqk,khd->qhd", attn_probs, values_all, preferred_element_type=jnp.float32)
            .reshape(seq_dev, D)
            .astype(jnp.bfloat16)
        )
        hidden_pre = (
            jnp.dot(low_two, wide_in[:, 3 * D :], preferred_element_type=jnp.float32) + bias_hidden
        )
        activation = gelu_exact(hidden_pre).astype(jnp.bfloat16)
        joined = jnp.concatenate([attended, activation], axis=1)
        after_add = (
            residual + jnp.dot(joined, wide_back, preferred_element_type=jnp.float32) + bias_out
        )
        final_rows = norm_rows(after_add, gain_last, shift_last)
        places = comp_pos[micro_at, 0]
        used_slots = (places < seq_dev).astype(jnp.float32)
        picked = (
            jnp.take(final_rows, jnp.minimum(places, seq_dev - 1), axis=0) * used_slots[:, None]
        ).astype(jnp.bfloat16)
        rows_all = lax.all_gather(picked, "shard", axis=0, tiled=True)
        logits = jnp.dot(rows_all, head_low, preferred_element_type=jnp.float32)
        targets = tgt_group[micro_at]
        matches = (targets - shard_at * vocab_dev)[:, None] == vocab_ids[None, :]
        row_top = jnp.max(logits, axis=1)
        row_total = jnp.sum(jnp.exp(logits - row_top[:, None]), axis=1)
        row_target = jnp.sum(jnp.where(matches, logits, 0.0), axis=1)
        row_top, row_total, row_target = combined_all(
            (row_top, row_total, row_target), "shard", combine_totals
        )
        logsum_rows = row_top + jnp.log(row_total)
        counted = (targets >= 0).astype(jnp.float32)
        loss_sum = loss_sum + jnp.sum((logsum_rows - row_target) * counted)
        count_sum = count_sum + jnp.sum(counted)
        d_logits = (
            (jnp.exp(logits - logsum_rows[:, None]) - matches.astype(jnp.float32))
            * counted[:, None]
        ).astype(jnp.bfloat16)
        grad_head = grad_head + jnp.einsum(
            "rd,rv->dv", rows_all, d_logits, preferred_element_type=jnp.float32
        )
        d_picked = lax.psum_scatter(
            jnp.einsum("rv,dv->rd", d_logits, head_low, preferred_element_type=jnp.float32),
            "shard",
            scatter_dimension=0,
            tiled=True,
        )
        d_final = jnp.zeros((seq_dev, D), jnp.float32).at[places].add(d_picked, mode="drop")
        back_in, back_back = (
            lax.all_gather(in_low, "shard", axis=0, tiled=True),
            lax.all_gather(back_low, "shard", axis=0, tiled=True),
        )
        _, pull_last = jax.vjp(norm_rows, after_add, gain_last, shift_last)
        d_after, d_gain_last, d_shift_last = pull_last(d_final)
        d_branch = d_after.astype(jnp.bfloat16)
        grad_back = grad_back + jnp.einsum(
            "sc,sd->cd", joined, d_branch, preferred_element_type=jnp.float32
        )
        d_joined = jnp.einsum("sd,cd->sc", d_branch, back_back, preferred_element_type=jnp.float32)
        d_attended = d_joined[:, :D].astype(jnp.bfloat16).reshape(seq_dev, H, HD)
        _, pull_gelu = jax.vjp(gelu_exact, hidden_pre)
        d_hidden = pull_gelu(d_joined[:, D:])[0].astype(jnp.bfloat16)
        probs_again = jnp.exp(masked_scores(queries, keys_all, allowed) - logsum)
        d_probs = jnp.einsum(
            "qhd,khd->hqk", d_attended, values_all, preferred_element_type=jnp.float32
        )
        d_scores = (
            probs_again * (d_probs - jnp.sum(probs_again * d_probs, axis=-1, keepdims=True))
        ).astype(jnp.bfloat16)
        d_queries = jnp.einsum(
            "hqk,khd->qhd", d_scores, keys_all, preferred_element_type=jnp.float32
        ) * HD ** (-0.5)
        low_probs = probs_again.astype(jnp.bfloat16)
        d_keys = jnp.einsum(
            "hqk,qhd->khd", d_scores, queries, preferred_element_type=jnp.float32
        ) * HD ** (-0.5)
        d_values = jnp.einsum(
            "hqk,qhd->khd", low_probs, d_attended, preferred_element_type=jnp.float32
        )
        key_grads = lax.psum_scatter(
            jnp.concatenate(
                [
                    d_keys.reshape(seq_dev * lax.axis_size("rep"), D),
                    d_values.reshape(seq_dev * lax.axis_size("rep"), D),
                ],
                axis=1,
            ),
            "rep",
            scatter_dimension=0,
            tiled=True,
        )
        d_key_rows = rotate(key_grads[:, :D].reshape(seq_dev, H, HD), -own_float).reshape(
            seq_dev, D
        )
        d_query_rows = rotate(d_queries, -own_float).reshape(seq_dev, D)
        d_projected = jnp.concatenate([d_query_rows, d_key_rows, key_grads[:, D:]], axis=1).astype(
            jnp.bfloat16
        )
        grad_in = grad_in + jnp.concatenate(
            [
                jnp.einsum("sd,sc->dc", low_one, d_projected, preferred_element_type=jnp.float32),
                jnp.einsum("sd,sc->dc", low_two, d_hidden, preferred_element_type=jnp.float32),
            ],
            axis=1,
        )
        d_normed_one = jnp.einsum(
            "sc,dc->sd", d_projected, back_in[:, : 3 * D], preferred_element_type=jnp.float32
        )
        d_normed_two = jnp.einsum(
            "sc,dc->sd", d_hidden, back_in[:, 3 * D :], preferred_element_type=jnp.float32
        )
        _, pull_one = jax.vjp(norm_rows, residual, gain_one, shift_one)
        d_resid_one, d_gain_one, d_shift_one = pull_one(d_normed_one)
        _, pull_two = jax.vjp(norm_rows, residual, gain_two, shift_two)
        d_resid_two, d_gain_two, d_shift_two = pull_two(d_normed_two)
        d_residual = (d_after + d_resid_one + d_resid_two).astype(jnp.bfloat16)
        returned = lax.all_to_all(d_residual.T, "shard", split_axis=0, concat_axis=1, tiled=True)
        grad_embed = grad_embed.at[:, ids_group[micro_at]].add(returned.astype(jnp.float32))
        grad_small = grad_small + jnp.concatenate(
            [
                d_gain_one,
                d_shift_one,
                d_gain_two,
                d_shift_two,
                d_gain_last,
                d_shift_last,
                jnp.sum(d_projected.astype(jnp.float32), axis=0),
                jnp.sum(d_hidden.astype(jnp.float32), axis=0),
                jnp.sum(d_branch.astype(jnp.float32), axis=0),
            ]
        )
    shard_in, shard_back, shard_small = (
        lax.psum_scatter(grad_in, "shard", scatter_dimension=0, tiled=True),
        lax.psum_scatter(grad_back, "shard", scatter_dimension=0, tiled=True),
        lax.psum_scatter(grad_small, "shard", scatter_dimension=0, tiled=True),
    )
    summed = lax.psum(
        (shard_in, shard_back, shard_small, grad_head, grad_embed, loss_sum, count_sum), "rep"
    )
    local_square = (
        jnp.sum(summed[0] * summed[0])
        + jnp.sum(summed[1] * summed[1])
        + jnp.sum(summed[2] * summed[2])
        + jnp.sum(summed[3] * summed[3])
        + jnp.sum(summed[4] * summed[4])
    )
    norm_value = jnp.sqrt(lax.psum(local_square, "shard"))
    factor = CLIP_LEVEL / jnp.maximum(norm_value, CLIP_LEVEL)
    next_in, moment_in, square_in = adamw(proj_in, summed[0] * factor, first_in, second_in, RATE_IN)
    next_back, moment_back, square_back = adamw(
        proj_back, summed[1] * factor, first_back, second_back, RATE_BACK
    )
    next_small, moment_small, square_small = adamw(
        small_params, summed[2] * factor, first_small, second_small, RATE_SMALL
    )
    next_head, moment_head, square_head = adamw(
        head_table, summed[3] * factor, first_head, second_head, RATE_HEAD
    )
    next_embed, moment_embed, square_embed = adamw(
        embed_table, summed[4] * factor, first_embed, second_embed, RATE_EMBED
    )
    return (
        jnp.stack([summed[5], summed[6]]),
        norm_value.reshape(1),
        next_in,
        moment_in,
        square_in,
        next_back,
        moment_back,
        square_back,
        next_small,
        moment_small,
        square_small,
        next_head,
        moment_head,
        square_head,
        next_embed,
        moment_embed,
        square_embed,
    )


MESH = pl.DeviceIdType.MESH
RG = 4
SG = 8


def whereabouts():
    rep = lax.axis_index("rep")
    shard = lax.axis_index("shard")
    core_twin = rep + 1 - 2 * lax.rem(rep, 2)
    x_twin = lax.rem(rep + 2, RG)
    y_twin = shard + 1 - 2 * lax.rem(shard, 2)
    return rep, shard, core_twin, x_twin, y_twin


def z_peer(shard, step):
    return lax.rem(shard + 2 * step, SG)


def shard_peer(shard, step):
    return lax.rem(shard + step, SG)


def greet(partners):
    barrier = pltpu.get_barrier_semaphore()
    for partner in partners:
        pl.semaphore_signal(barrier, inc=1, device_id=partner, device_id_type=MESH)
    pl.semaphore_wait(barrier, len(partners))


def remote(src, dst, send_sem, recv_sem, partner):
    return pltpu.make_async_remote_copy(
        src_ref=src,
        dst_ref=dst,
        send_sem=send_sem,
        recv_sem=recv_sem,
        device_id=partner,
        device_id_type=MESH,
    )


def comm_call(kernel, out_shape, scratch, number, args, spaces=None, out_spaces=None, limit=None, grid=()):
    pick = {
        "a": pl.BlockSpec(memory_space=pl.ANY),
        "v": pl.BlockSpec(memory_space=pltpu.VMEM),
    }
    choose = lambda space: pick[space] if isinstance(space, str) else space
    spaces = spaces or "a" * len(args)
    out_spaces = out_spaces or "a" * len(out_shape)
    return pl.pallas_call(
        kernel,
        grid=grid,
        out_shape=out_shape,
        in_specs=[choose(space) for space in spaces],
        out_specs=[choose(space) for space in out_spaces],
        scratch_shapes=scratch,
        compiler_params=pltpu.CompilerParams(
            collective_id=number, has_side_effects=True, vmem_limit_bytes=limit
        ),
    )(*args)


def start_gather(source, out, slot, place, sems):
    send_z, recv_z, send_y, recv_y, own = sems
    rep, shard, _, _, y_twin = place
    keep = pltpu.make_async_copy(source, slot(out, shard), own)
    keep.start()
    first_y = remote(source, slot(out, shard), send_y.at[0], recv_y.at[0], (rep, y_twin))
    z_copies = [
        remote(source, slot(out, shard), send_z.at[step - 1], recv_z.at[step - 1], (rep, z_peer(shard, step)))
        for step in range(1, 4)
    ]
    for copy in z_copies:
        copy.start()
    first_y.start()
    return keep, first_y, z_copies


def finish_gather(started, out, slot, place, sems):
    send_z, recv_z, send_y, recv_y, own = sems
    rep, shard, _, _, y_twin = place
    keep, first_y, z_copies = started
    passed = []
    for step in range(1, 4):
        z_copies[step - 1].wait_recv()
        came_from = z_peer(shard, SG // 2 - step)
        passed.append(
            remote(slot(out, came_from), slot(out, came_from), send_y.at[step], recv_y.at[step], (rep, y_twin))
        )
        passed[-1].start()
    keep.wait()
    for copy in z_copies:
        copy.wait_send()
    first_y.wait()
    for copy in passed:
        copy.wait()


def gather_partners(place):
    rep, shard, _, _, y_twin = place
    return [(rep, z_peer(shard, step)) for step in range(1, 4)] + [(rep, y_twin)]


GATHER_SEMS = [pltpu.SemaphoreType.DMA((3,)), pltpu.SemaphoreType.DMA((3,)), pltpu.SemaphoreType.DMA((4,)), pltpu.SemaphoreType.DMA((4,)), pltpu.SemaphoreType.DMA]


def row_slot(out, index):
    height = out.shape[0] // SG
    return out.at[pl.ds(pl.multiple_of(index * height, height), height)]


def tile_user(tile):
    return jnp.where(tile < SG, tile, (tile - SG) // 4)


def tile_slot(tile):
    return jnp.where(tile < SG, 0, 1 + lax.rem(tile - SG + SG, 4))


def entry_kernel(
    table_steps, head_rows, ints, smalls, weights_in, weights_back, table, head,
    ints_out, places, marks, scales, bias, out, in_all, back_all, head_low,
    ints_all, smalls_all, in_parts, back_tiles, turned, wide, low, ids,
    send_int, recv_int, send_small, recv_small, send_rep, recv_rep,
    send_in, recv_in, send_back, recv_back, send_far, recv_far, send_pair, recv_pair,
    send_up, recv_up, send_down, recv_down, send_y, recv_y, own,
):
    at = pl.program_id(0)
    last = pl.num_programs(0) - 1
    rep, shard, core_twin, x_twin, y_twin = whereabouts()
    level, side = shard // 2, lax.rem(shard, 2)
    shard_peers = [(rep, shard_peer(shard, step)) for step in range(1, SG)]
    rep_peers = [(lax.rem(rep + step, RG), shard) for step in range(1, RG)]
    lines, tokens, feats = low.shape
    small_rows = 14

    def int_copies():
        return [
            remote(ints, ints_all.at[rep, shard], send_int.at[k], recv_int.at[k], peer)
            for k, peer in enumerate(shard_peers)
        ]

    def small_copies():
        return [
            remote(smalls, smalls_all.at[shard], send_small.at[k], recv_small.at[k], peer)
            for k, peer in enumerate(shard_peers)
        ]

    def rep_copies():
        return [
            remote(ints_all.at[rep], ints_all.at[rep], send_rep.at[k], recv_rep.at[k], peer)
            for k, peer in enumerate(rep_peers)
        ]

    def in_copies():
        return [
            remote(in_parts.at[peer[1], rep], in_all.at[shard, rep], send_in.at[k], recv_in.at[k], peer)
            for k, peer in enumerate(shard_peers)
        ]

    def own_in():
        return pltpu.make_async_copy(in_parts.at[shard, rep], in_all.at[shard, rep], own.at[0])

    def back_move(k):
        tile = 5 * shard + k
        user, slot = tile_user(tile), tile_slot(tile)
        there = remote(
            back_tiles.at[k, rep], back_all.at[slot, rep], send_back.at[k], recv_back.at[slot], (rep, user)
        )
        return user, slot, there

    def quarter_copies(quarter, sends, recvs, base, peer):
        return [
            remote(array.at[:, quarter], array.at[:, quarter], sends.at[base + k], recvs.at[base + k], (peer, shard))
            for k, array in enumerate((in_all, back_all))
        ]

    def far_copies():
        return quarter_copies(rep, send_far, recv_far, 0, x_twin)

    def pair_copies():
        return quarter_copies(rep, send_pair, recv_pair, 0, core_twin) + quarter_copies(
            x_twin, send_pair, recv_pair, 2, core_twin
        )

    def slot(line, z_at, y_at):
        index = 2 * z_at + y_at
        return out.at[pl.ds(line * tokens, tokens), pl.ds(pl.multiple_of(index * feats, feats), feats)]

    def up_copy(line, hop):
        here = slot(line, level - hop, side)
        source = low.at[line] if hop == 0 else here
        return remote(source, here, send_up.at[line, hop], recv_up.at[line, hop], (rep, shard + 2))

    def down_copy(line, hop):
        here = slot(line, level + hop, side)
        source = low.at[line] if hop == 0 else here
        return remote(source, here, send_down.at[line, hop], recv_down.at[line, hop], (rep, shard - 2))

    def side_copy(line, z_at, source=None):
        here = slot(line, z_at, side)
        return remote(
            here if source is None else source, here, send_y.at[line, z_at], recv_y.at[line, z_at], (rep, y_twin)
        )

    def keep_copy(line):
        return pltpu.make_async_copy(low.at[line], slot(line, level, side), own.at[2 + line])

    def pass_on(line, hop):
        @pl.when(level >= hop)
        def _():
            pltpu.make_async_copy(low.at[line], slot(line, level - hop, side), recv_up.at[line, hop - 1]).wait()
            if hop < 3:
                pl.when(level < 3)(lambda: up_copy(line, hop).start())
            side_copy(line, level - hop).start()

        @pl.when(level + hop <= 3)
        def _():
            pltpu.make_async_copy(low.at[line], slot(line, level + hop, side), recv_down.at[line, hop - 1]).wait()
            if hop < 3:
                pl.when(level > 0)(lambda: down_copy(line, hop).start())
            side_copy(line, level + hop).start()

    @pl.when(at == 0)
    def _():
        greet(shard_peers + rep_peers)
        for copy in int_copies() + small_copies():
            copy.start()
        for target in range(SG):
            for part in range(3):
                columns = weights_in[:, part * D + target * HEAD_COLS : part * D + (target + 1) * HEAD_COLS]
                in_parts[target, :, :, part * HEAD_COLS : (part + 1) * HEAD_COLS] = columns.astype(
                    in_parts.dtype
                ).reshape(RG, in_parts.shape[2], HEAD_COLS)
            columns = weights_in[:, 3 * D + target * UNITS : 3 * D + (target + 1) * UNITS]
            in_parts[target, :, :, 3 * HEAD_COLS :] = columns.astype(in_parts.dtype).reshape(
                RG, in_parts.shape[2], UNITS
            )
        back_tiles[...] = weights_back[...].astype(back_tiles.dtype).reshape(back_tiles.shape)
        for copy in in_copies():
            copy.start()
        own_in().start()
        for k in range(5):
            user, slot_at, there = back_move(k)
            here = pltpu.make_async_copy(back_tiles.at[k, rep], back_all.at[slot_at, rep], recv_back.at[slot_at])
            pl.when(user == shard)(here.start)
            pl.when(user != shard)(there.start)
        ints_all[rep, shard] = ints[...]
        smalls_all[shard] = smalls[...]

    @pl.when(at < table_steps)
    def _():
        block = table[...].astype(jnp.bfloat16).astype(jnp.float32)
        width = block.shape[1]
        turned[pl.ds(pl.multiple_of(at * width, width), width), :] = block.T

    @pl.when(at == 5)
    def _():
        for copy in int_copies():
            copy.wait()
        for copy in rep_copies():
            copy.start()

    @pl.when(at == table_steps)
    def _():
        for copy in rep_copies():
            copy.wait()
        to_scalars = pltpu.make_async_copy(ints_all.at[:, pl.ds(2 * rep, 2)], ids, own.at[1])
        to_scalars.start()
        to_scalars.wait()
        for line in range(lines):
            micro, member = line // 2, line % 2
            for block_at in range(RG):

                @pl.loop(0, 16)
                def _(group):
                    for k in range(8):
                        lane = group * 8 + k
                        wide[pl.ds(block_at * 128 + lane, 1), :] = turned[
                            pl.ds(ids[block_at, member, micro, lane], 1), :
                        ]

            low[line] = wide[...].astype(jnp.bfloat16)
            pl.when(level < 3)(lambda: up_copy(line, 0).start())
            pl.when(level > 0)(lambda: down_copy(line, 0).start())
            side_copy(line, level, low.at[line]).start()
            keep_copy(line).start()
        own_in().wait()
        for copy in in_copies():
            copy.wait()
        for k in range(5):
            pltpu.make_async_copy(back_tiles.at[0, rep], back_all.at[k, rep], recv_back.at[k]).wait()
        for copy in far_copies():
            copy.start()

    @pl.when(at >= table_steps)
    def _():
        head_low[...] = head[...].astype(jnp.bfloat16)

    order = sorted(((line, hop) for line in range(lines) for hop in range(1, 4)), key=lambda item: (sum(item), item[1]))
    for step, (line, hop) in enumerate(order):
        pl.when(at == table_steps + 1 + step)(functools.partial(pass_on, line, hop))

    @pl.when(at == last - 2)
    def _():
        for copy in far_copies():
            copy.wait()
        for copy in pair_copies():
            copy.start()

    @pl.when(at == last)
    def _():
        for copy in small_copies():
            copy.wait()
        ints_out[...] = ints_all[...]

        seq_dev, slots = ints.shape[1], ints.shape[1] // 4
        for group in range(RG):
            for line in range(lines):
                micro, member = line // 2, line % 2
                for block_at in range(RG):
                    facts = ints_all[block_at, 2 * group + member, 2:3, :]
                    where = facts[:, slots * micro : slots * (micro + 1)]
                    goal = facts[:, slots * (2 + micro) : slots * (3 + micro)]
                    some = where < seq_dev
                    start = (line * RG + block_at) * slots
                    marks[group, 0:1, start : start + slots] = jnp.where(some, goal - shard * head_rows, -1)
                    marks[group, 1:2, start : start + slots] = some.astype(jnp.int32)
        for line in range(lines):
            micro, member = line // 2, line % 2
            for block_at in range(RG):
                where = ints_all[block_at, 2 * rep + member, 2:3, slots * micro : slots * (micro + 1)]
                places[8 * line : 8 * line + 1, block_at * slots : (block_at + 1) * slots] = jnp.where(
                    where < seq_dev, where + block_at * seq_dev, -1
                )
            span = ints_all[0, 2 * rep + member, 3:4, micro : micro + 1]
            places[8 * line + 1 : 8 * line + 2, :] = jnp.broadcast_to(span, (1, places.shape[1]))

        def small_row(row):
            return smalls_all[row // small_rows, pl.ds(lax.rem(row, small_rows), 1), :]

        scales[...] = jnp.zeros_like(scales)
        for vector, start in enumerate([8 * k for k in range(6)] + [8 * 13]):
            for part in range(8):
                row = start + part
                scales[vector : vector + 1, part * 128 : (part + 1) * 128] = smalls_all[
                    row // small_rows, row % small_rows : row % small_rows + 1, :
                ]
        for part in range(3):
            bias[:, part * 128 : (part + 1) * 128] = small_row(48 + 8 * part + shard)
        for part in range(4):
            bias[:, (3 + part) * 128 : (4 + part) * 128] = small_row(72 + 4 * shard + part)
        for k in range(5):
            user, _, there = back_move(k)
            pl.when(user != shard)(there.wait_send)
        for line in range(lines):
            keep_copy(line).wait()
            for hop in range(3):
                pl.when((level >= hop) & (level < 3))(lambda: up_copy(line, hop).wait_send())
                pl.when((level + hop <= 3) & (level > 0))(lambda: down_copy(line, hop).wait_send())
            for z_at in range(4):
                side_copy(line, z_at).wait()
        for copy in pair_copies():
            copy.wait()


def share_entry(ints, smalls, weights_in, weights_back, table, head, tokens, number):
    quarter = weights_in.shape[0] // RG
    in_shape = (SG, RG, quarter, OWN_COLS)
    back_shape = (5, RG, 32, weights_back.shape[1])
    dma = pltpu.SemaphoreType.DMA
    feats, vocab = table.shape
    blocks = pl.cdiv(vocab, TABLE_BLOCK)
    head_blocks = max(pl.cdiv(head.shape[0], CAST_BLOCK), 13)
    lines = 4
    per_line = tokens // lines
    head_spec = pl.BlockSpec(
        (CAST_BLOCK, head.shape[1]),
        lambda at: (jnp.clip(at - blocks, 0, pl.cdiv(head.shape[0], CAST_BLOCK) - 1), 0),
    )
    return comm_call(
        functools.partial(entry_kernel, blocks, head.shape[0]),
        [
            jax.ShapeDtypeStruct((RG, SG) + ints.shape, ints.dtype),
            jax.ShapeDtypeStruct((8 * lines, ints.shape[1]), ints.dtype),
            jax.ShapeDtypeStruct((RG, 8, ints.shape[1] * lines), ints.dtype),
            jax.ShapeDtypeStruct((8, SG * feats), jnp.float32),
            jax.ShapeDtypeStruct((1, OWN_COLS), jnp.float32),
            jax.ShapeDtypeStruct((tokens, SG * feats), jnp.bfloat16),
            jax.ShapeDtypeStruct(in_shape, jnp.bfloat16),
            jax.ShapeDtypeStruct(back_shape, jnp.bfloat16),
            jax.ShapeDtypeStruct(head.shape, jnp.bfloat16),
        ],
        [
            pltpu.VMEM((RG, SG) + ints.shape, ints.dtype),
            pltpu.VMEM((SG,) + smalls.shape, smalls.dtype),
            pltpu.VMEM(in_shape, jnp.bfloat16),
            pltpu.VMEM(back_shape, jnp.bfloat16),
            pltpu.VMEM((blocks * TABLE_BLOCK, feats), jnp.float32),
            pltpu.VMEM((per_line, feats), jnp.float32),
            pltpu.VMEM((lines, per_line, feats), jnp.bfloat16),
            pltpu.SMEM((RG, 2) + ints.shape, jnp.int32),
        ]
        + [dma((SG - 1,))] * 4
        + [dma((RG - 1,))] * 2
        + [dma((SG - 1,))] * 2
        + [dma((5,))] * 2
        + [dma((2,))] * 2
        + [dma((4,))] * 2
        + [dma((lines, 3))] * 4
        + [dma((lines, 4))] * 2
        + [dma((2 + lines,))],
        number,
        (ints, smalls, weights_in, weights_back, table, head),
        ["v", "v", "v", "v", pl.BlockSpec((feats, TABLE_BLOCK), lambda at: (0, jnp.minimum(at, blocks - 1))), head_spec],
        ["v"] * 5 + ["a", "a", "a", head_spec],
        VMEM_LIMIT,
        (blocks + head_blocks,),
    )


def loss_kernel(
    vocab, parts, picked_rows, scales, used, marks, head,
    rows_all, facts_out, branch, features_out, vectors,
    rows, turned, low, after, branch_y, branch_sum, branch_z, picked_y, picked_sum, picked_z, picked,
    stats, stats_all, facts, facts_all, features, pieces, low_branch, top, total, target,
    branch_send_y, branch_recv_y, branch_send_z, branch_recv_z,
    picked_send_y, picked_recv_y, picked_send_z, picked_recv_z,
    row_z_send, row_z_recv, row_y_send, row_y_recv, row_own,
    back_z_send, back_z_recv, back_y_send, back_y_recv, back_own,
    send_stat, recv_stat, send_row, recv_row, send_fact, recv_fact, send_feat, recv_feat, own,
):
    at = pl.program_id(0)
    blocks = pl.num_programs(0) // 2
    place = whereabouts()
    rep, shard, core_twin, x_twin, y_twin = place
    shard_peers = [(rep, shard_peer(shard, step)) for step in range(1, SG)]
    rep_peers = [(lax.rem(rep + step, RG), shard) for step in range(1, RG)]
    slots = after.shape[0]
    own_rows = pl.ds(pl.multiple_of(shard * slots, slots), slots)

    def shard_total(values, from_y, own_sum, from_z, send_y, recv_y, send_z, recv_z):
        y_copies = {}
        for step in (2, 1, 3, 0):
            y_copies[step] = remote(
                values.at[z_peer(y_twin, step)], from_y.at[step], send_y.at[step], recv_y.at[step], (rep, y_twin)
            )
            y_copies[step].start()
        z_copies = []
        for step in (2, 1, 3):
            y_copies[step].wait_recv()
            own_sum[step] = values[z_peer(shard, step)] + from_y[step]
            z_copies.append(
                remote(
                    own_sum.at[step], from_z.at[step - 1], send_z.at[step - 1], recv_z.at[step - 1],
                    (rep, z_peer(shard, step)),
                )
            )
            z_copies[-1].start()
        y_copies[0].wait_recv()
        result = values[shard] + from_y[0]
        for copy in z_copies:
            copy.wait()
        for step in range(4):
            y_copies[step].wait_send()
        return result + from_z[0] + from_z[1] + from_z[2]

    row_sems = (row_z_send, row_z_recv, row_y_send, row_y_recv, row_own)
    back_sems = (back_z_send, back_z_recv, back_y_send, back_y_recv, back_own)

    def stat_copies():
        return [
            remote(stats, stats_all.at[shard], send_stat.at[k], recv_stat.at[k], peer)
            for k, peer in enumerate(shard_peers)
        ]

    def row_copy(k, peer):
        return remote(rows, rows_all.at[rep], send_row.at[k], recv_row.at[k], (peer, shard))

    def passed_copy():
        return remote(rows_all.at[x_twin], rows_all.at[x_twin], send_row.at[2], recv_row.at[2], (core_twin, shard))

    def keep_rows():
        return pltpu.make_async_copy(rows, rows_all.at[rep], own)

    def fact_copies():
        return [
            remote(facts, facts_all.at[rep], send_fact.at[k], recv_fact.at[k], peer) for k, peer in enumerate(rep_peers)
        ]

    @pl.when(at == 0)
    def _():
        greet(shard_peers + rep_peers)
        sum_buffers = (branch_y, branch_sum, branch_z)
        whole = shard_total(parts, *sum_buffers, branch_send_y, branch_recv_y, branch_send_z, branch_recv_z)
        after[...] = picked_rows[own_rows, :].astype(jnp.float32) + whole + scales[6:7, :]
        unit, _ = centred_rows(after[...])
        final = unit * scales[4:5, :] + scales[5:6, :]
        low[...] = (final * used[own_rows, 0:1]).astype(low.dtype)
        started = start_gather(low, rows, row_slot, place, row_sems)
        finish_gather(started, rows, row_slot, place, row_sems)
        row_copy(0, x_twin).start()
        row_copy(1, core_twin).start()
        keep_rows().start()
        turned[...] = rows[...].T
        top[...] = jnp.full_like(top, -1e30)
        total[...] = jnp.zeros_like(total)
        target[...] = jnp.zeros_like(target)
        picked[...] = jnp.zeros_like(picked)

    full, tail = divmod(vocab, ROW_BLOCK)

    def each_block(start, body):
        pl.when((at >= start) & (at < start + full))(lambda: body(ROW_BLOCK))
        if tail > 0:
            pl.when(at == start + full)(lambda: body(tail))

    def top_block(size):
        logits = plain_dot(head[:size], turned[...])
        hits = lax.broadcasted_iota(jnp.int32, logits.shape, 0) == marks[rep, 0:1, :] - at * ROW_BLOCK
        target[...] += jnp.sum(jnp.where(hits, logits, 0.0), axis=0, keepdims=True)
        highest = jnp.maximum(top[...], jnp.max(logits, axis=0, keepdims=True))
        weights = jnp.sum(jnp.exp(logits - highest), axis=0, keepdims=True)
        total[...] = total[...] * jnp.exp(top[...] - highest) + weights
        top[...] = highest

    each_block(0, top_block)

    @pl.when(at == blocks - 1)
    def _():
        stats[...] = jnp.zeros_like(stats)
        stats[0:1, :] = top[...]
        stats[1:2, :] = total[...]
        stats[2:3, :] = target[...]
        for copy in stat_copies():
            copy.start()
        stats_all[shard] = stats[...]
        for copy in stat_copies():
            copy.wait()
        highest = stats_all[0, 0:1, :]
        for k in range(1, SG):
            highest = jnp.maximum(highest, stats_all[k, 0:1, :])
        weights = row_target = jnp.zeros_like(highest)
        for k in range(SG):
            weights = weights + stats_all[k, 1:2, :] * jnp.exp(stats_all[k, 0:1, :] - highest)
            row_target = row_target + stats_all[k, 2:3, :]
        logsum = highest + jnp.log(weights)
        some = marks[rep, 1:2, :] > 0
        facts[...] = jnp.zeros_like(facts)
        facts[0:1, :] = jnp.where(some, logsum, 1e30)
        facts[1:2, :] = jnp.where(some, logsum - row_target, 0.0)
        facts[2:3, :] = some.astype(jnp.float32)
        for copy in fact_copies():
            copy.start()
        facts_all[rep] = facts[...]
        row_copy(0, x_twin).wait_recv()
        passed_copy().start()

    def grad_block(size):
        block = head[:size]
        grads = logit_grads(block, turned[...], facts[0:1, :], marks[rep, 0:1, :] - (at - blocks) * ROW_BLOCK)
        picked[...] += first_dot(grads, block).reshape(picked.shape)

    each_block(blocks, grad_block)

    @pl.when(at == pl.num_programs(0) - 1)
    def _():
        sum_buffers = (picked_y, picked_sum, picked_z)
        d_final = shard_total(picked, *sum_buffers, picked_send_y, picked_recv_y, picked_send_z, picked_recv_z)
        unit, unit_scale = centred_rows(after[...])
        d_unit = d_final * scales[4:5, :]
        mean = jnp.mean(d_unit, axis=-1, keepdims=True)
        slope = jnp.mean(d_unit * unit, axis=-1, keepdims=True)
        d_after = (d_unit - mean - unit * slope) * unit_scale
        low_branch[...] = d_after.astype(low_branch.dtype)
        started = start_gather(low_branch, branch, row_slot, place, back_sems)
        width = pieces.shape[2]
        for k in range(SG):
            pieces[k] = d_after[:, k * width : (k + 1) * width]
        copies = [
            remote(pieces.at[peer[1]], features.at[shard], send_feat.at[k], recv_feat.at[k], peer)
            for k, peer in enumerate(shard_peers)
        ]
        for copy in copies:
            copy.start()
        features[shard] = pieces[shard]
        vectors[...] = jnp.zeros_like(vectors)
        vectors[0:1, :] = jnp.sum(d_final * unit, axis=0, keepdims=True)
        vectors[1:2, :] = jnp.sum(d_final, axis=0, keepdims=True)
        vectors[2:3, :] = jnp.sum(low_branch[...].astype(jnp.float32), axis=0, keepdims=True)
        finish_gather(started, branch, row_slot, place, back_sems)
        for copy in copies + fact_copies():
            copy.wait()
        facts_out[...] = facts_all[...]
        features_out[...] = features[...]
        row_copy(0, x_twin).wait_send()
        row_copy(1, core_twin).wait()
        passed_copy().wait()
        keep_rows().wait()


def loss_and_branch(parts, picked_rows, scales, used, marks, head, number):
    dma = pltpu.SemaphoreType.DMA
    f32, bf16 = jnp.float32, jnp.bfloat16
    _, slots, depth = parts.shape
    vocab = head.shape[0]
    count = SG * slots
    blocks = pl.cdiv(vocab, ROW_BLOCK)
    vmem = lambda *shape: pltpu.VMEM(shape, f32)
    return comm_call(
        functools.partial(loss_kernel, vocab),
        [
            jax.ShapeDtypeStruct((RG, count, depth), bf16),
            jax.ShapeDtypeStruct((RG, 8, count), f32),
            jax.ShapeDtypeStruct((count, depth), bf16),
            jax.ShapeDtypeStruct((SG, slots, depth // SG), f32),
            jax.ShapeDtypeStruct((8, depth), f32),
        ],
        [
            pltpu.VMEM((count, depth), bf16),
            pltpu.VMEM((depth, count), bf16),
            pltpu.VMEM((slots, depth), bf16),
            vmem(slots, depth),
        ]
        + [vmem(rounds, slots, depth) for rounds in (4, 4, 3, 4, 4, 3, SG)]
        + [vmem(8, count), vmem(SG, 8, count), vmem(8, count), vmem(RG, 8, count)]
        + [vmem(SG, slots, depth // SG)] * 2
        + [pltpu.VMEM((slots, depth), bf16)]
        + [vmem(1, count)] * 3
        + [dma((4,)), dma((4,)), dma((3,)), dma((3,))] * 2
        + GATHER_SEMS * 2
        + [dma((SG - 1,))] * 2
        + [dma((3,))] * 4
        + [dma((SG - 1,))] * 2
        + [dma],
        number,
        (parts, picked_rows, scales, used, marks, head),
        ["v"] * 5 + [pl.BlockSpec((ROW_BLOCK, depth), lambda at: (lax.rem(at, blocks), 0))],
        ["a", "v", "a", "v", "v"],
        VMEM_LIMIT,
        (2 * blocks,),
    )


def coded(rows, steps):
    inverse = jnp.where(steps > 0.0, 1.0 / steps, 0.0)
    return jnp.clip(jnp.round(rows * inverse), -32767.0, 32767.0).astype(jnp.int32).astype(jnp.int16)


def layer_kernel(
    vocab, parts, stats, base, unit, grad_in, grad_back, grad_scales, grad_bias, vectors, rows, facts, targets, head,
    rows_all, in_all, back_all, smalls_out, head_out, squares,
    smalls, low, sum_in, sum_back, turned, stats_all, steps_all, from_y, own_sum, from_z, pair_in, pair_back, half_in, half_back, far_in, far_back, small_rep, small_sum, small_shard,
    send_y, recv_y, send_z, recv_z, send_stat, recv_stat, send_pair, recv_pair, send_far, recv_far,
    send_rep, recv_rep, send_small, recv_small,
    send_row, recv_row, send_in, recv_in, send_back, recv_back, own,
):
    at = pl.program_id(0)
    last = pl.num_programs(0) - 1
    rep, shard, core_twin, x_twin, y_twin = whereabouts()
    core_far = lax.rem(core_twin + 2, RG)
    small_rows = 14
    shard_peers = [(rep, shard_peer(shard, step)) for step in range(1, SG)]
    rep_peers = [(lax.rem(rep + step, RG), shard) for step in range(1, RG)]

    def rep_copies():
        return [
            remote(smalls, small_rep.at[k], send_rep.at[k], recv_rep.at[k], peer) for k, peer in enumerate(rep_peers)
        ]

    def pair_copies(which, slot):
        pairs = ((grad_in, pair_in), (grad_back, pair_back))
        return [
            remote(
                source.at[:, which], target.at[slot], send_pair.at[2 * slot + k], recv_pair.at[2 * slot + k],
                (core_twin, shard),
            )
            for k, (source, target) in enumerate(pairs)
        ]

    def y_copy(step):
        return remote(parts.at[z_peer(y_twin, step)], from_y.at[step], send_y.at[step], recv_y.at[step], (rep, y_twin))

    def z_copy(step):
        return remote(
            own_sum.at[step], from_z.at[step - 1], send_z.at[step - 1], recv_z.at[step - 1], (rep, z_peer(shard, step))
        )

    def stat_copies():
        return [
            remote(stats, stats_all.at[shard], send_stat.at[k], recv_stat.at[k], peer)
            for k, peer in enumerate(shard_peers)
        ]

    def far_copies():
        return [
            remote(half_in, far_in, send_far.at[0], recv_far.at[0], (x_twin, shard)),
            remote(half_back, far_back, send_far.at[1], recv_far.at[1], (x_twin, shard)),
        ]

    def small_copies():
        return [
            remote(small_sum.at[peer[1]], small_shard.at[k], send_small.at[k], recv_small.at[k], peer)
            for k, peer in enumerate(shard_peers)
        ]

    def in_copies():
        return [
            remote(sum_in.at[peer[1]], in_all.at[shard], send_in.at[k], recv_in.at[k], peer)
            for k, peer in enumerate(shard_peers)
        ]

    def own_in():
        return pltpu.make_async_copy(sum_in.at[shard], in_all.at[shard], own.at[0])

    def back_move(slot):
        tile = shard if slot == 0 else SG + 4 * shard + slot - 1
        owner, place = tile // 5, lax.rem(tile, 5)
        there = remote(sum_back.at[slot], back_all.at[place], send_back.at[slot], recv_back.at[place], (rep, owner))
        return owner, place, there

    def decoded(codes, steps):
        return codes.astype(jnp.int32).astype(jnp.float32) * steps

    def pair_sum(step):
        y_copy(step).wait_recv()
        own = decoded(parts[z_peer(shard, step)], steps_all[:, 0:1])
        return own + decoded(from_y[step], steps_all[:, 4:5])

    def pass_on(step):
        own_sum[step] = coded(pair_sum(step), steps_all[:, 0:1] + steps_all[:, 4:5])
        z_copy(step).start()

    @pl.when(at == 0)
    def _():
        greet(shard_peers + rep_peers)
        for copy in stat_copies():
            copy.start()
        for step in (2, 1, 3, 0):
            y_copy(step).start()
        for copy in pair_copies(core_far, 1) + pair_copies(core_twin, 0):
            copy.start()
        smalls[...] = jnp.zeros_like(smalls)

        def put(row, values):
            smalls[row // small_rows, pl.ds(lax.rem(row, small_rows), 1), :] = values

        for k in range(8):
            lanes = slice(k * 128, (k + 1) * 128)
            for vector in range(4):
                put(8 * vector + k, grad_scales[vector : vector + 1, lanes])
            put(8 * 4 + k, vectors[0:1, lanes])
            put(8 * 5 + k, vectors[1:2, lanes])
            put(8 * 13 + k, vectors[2:3, lanes])
        for k in range(7):
            row = 48 + 8 * k + shard if k < 3 else 72 + 4 * shard + k - 3
            put(row, grad_bias[0:1, k * 128 : (k + 1) * 128])
        for copy in rep_copies():
            copy.start()
        stats_all[shard] = stats[...]
        squares[...] = jnp.zeros_like(squares)
        for group in range(RG):
            turned[group] = rows[group].T

    @pl.when(at == 1)
    def _():
        for copy in pair_copies(core_far, 1):
            copy.wait()
        half_in[...] = grad_in[:, x_twin] + pair_in[1]
        half_back[...] = grad_back[:, x_twin] + pair_back[1]
        for copy in far_copies():
            copy.start()
        for copy in rep_copies():
            copy.wait()
        small_sum[...] = smalls[...] + small_rep[0] + small_rep[1] + small_rep[2]
        for copy in small_copies():
            copy.start()

    @pl.when(at == 3)
    def _():
        for copy in stat_copies():
            copy.wait()
        near = [stats_all[z_peer(shard, k), 2:3, :] for k in range(4)]
        near += [stats_all[z_peer(y_twin, k), 2:3, :] for k in range(4)]
        sums = stats_all[0]
        for k in range(1, SG):
            sums = sums + stats_all[k]
        near += [sums[0:2, :], stats[3:4, :], jnp.zeros((5, sums.shape[1]), jnp.float32)]
        steps_all[:, 0:16] = jnp.concatenate(near, axis=0).T
        pass_on(2)

    pl.when(at == 6)(lambda: pass_on(1))
    pl.when(at == 8)(lambda: pass_on(3))

    @pl.when(at == 10)
    def _():
        for copy in pair_copies(core_twin, 0):
            copy.wait()
        for copy in far_copies():
            copy.wait()
        sum_in[...] = grad_in[:, rep] + pair_in[0] + far_in[...]
        sum_back[...] = grad_back[:, rep] + pair_back[0] + far_back[...]
        for copy in in_copies():
            copy.start()
        own_in().start()
        for slot in range(5):
            owner, place, there = back_move(slot)
            here = pltpu.make_async_copy(sum_back.at[slot], back_all.at[place], recv_back.at[place])
            pl.when(owner == shard)(here.start)
            pl.when(owner != shard)(there.start)

    def head_block(size):
        total = None
        for group in range(RG):
            base = at * VOCAB_BLOCK
            grads = logit_grads(head[:size], turned[group], facts[group, 0:1, :], targets[group, 0:1, :] - base)
            term = plain_dot(grads, rows[group])
            total = term if total is None else total + term
        head_out[:size] = total
        squares[0:1, :] += jnp.sum(total * total, axis=0, keepdims=True)

    vocab_blocks(vocab, VOCAB_BLOCK, head_block)

    @pl.when(at == last)
    def _():
        total = pair_sum(0)
        for step in (1, 2, 3):
            z_copy(step).wait()
            behind = 4 - step
            steps = steps_all[:, behind : behind + 1] + steps_all[:, 4 + behind : 5 + behind]
            total = total + decoded(from_z[step - 1], steps)
        mean, slope, scale = (steps_all[:, k : k + 1] for k in (8, 9, 10))
        d_rows = (total - mean / D - unit[...] * (slope / D)) * scale
        low[...] = (base[...] + d_rows).astype(low.dtype)
        to_x = remote(low, rows_all.at[rep], send_row.at[0], recv_row.at[0], (x_twin, shard))
        to_core = remote(low, rows_all.at[rep], send_row.at[1], recv_row.at[1], (core_twin, shard))
        keep = pltpu.make_async_copy(low, rows_all.at[rep], own.at[1])
        to_x.start()
        to_core.start()
        keep.start()
        for copy in small_copies():
            copy.wait()
        whole = small_sum[shard]
        for k in range(SG - 1):
            whole = whole + small_shard[k]
        smalls_out[...] = whole
        for step in range(4):
            y_copy(step).wait_send()
        to_x.wait_recv()
        passed = remote(rows_all.at[x_twin], rows_all.at[x_twin], send_row.at[2], recv_row.at[2], (core_twin, shard))
        passed.start()
        own_in().wait()
        for copy in in_copies():
            copy.wait()
        for place in range(5):
            pltpu.make_async_copy(sum_back.at[0], back_all.at[place], recv_back.at[place]).wait()
        for slot in range(5):
            owner, _, there = back_move(slot)
            pl.when(owner != shard)(there.wait_send)
        keep.wait()
        to_x.wait_send()
        to_core.wait()
        passed.wait()


def layer_sums(
    parts, stats, base, unit, grad_in, grad_back, grad_scales, grad_bias, vectors, rows, facts, targets, head, number
):
    dma = pltpu.SemaphoreType.DMA
    chunk = parts.shape[1:]
    quarter_in, quarter_back = (array.shape[:1] + array.shape[2:] for array in (grad_in, grad_back))
    piece = (16, 128)
    vocab, depth = head.shape
    vmem = lambda shape: pltpu.VMEM(shape, jnp.float32)
    shape = lambda dims: jax.ShapeDtypeStruct(dims, jnp.float32)
    block = pl.BlockSpec((VOCAB_BLOCK, depth), lambda at: (at, 0))
    return comm_call(
        functools.partial(layer_kernel, vocab),
        [
            jax.ShapeDtypeStruct((RG,) + chunk, jnp.bfloat16),
            shape(quarter_in),
            shape(quarter_back),
            shape(piece),
            shape(head.shape),
            shape((8, depth)),
        ],
        [vmem((SG,) + piece), pltpu.VMEM(chunk, jnp.bfloat16), vmem(quarter_in), vmem(quarter_back)]
        + [pltpu.VMEM((RG, depth, rows.shape[1]), rows.dtype), vmem((SG,) + stats.shape), vmem((chunk[0], 128))]
        + [pltpu.VMEM((count,) + chunk, parts.dtype) for count in (4, 4, 3)]
        + [vmem((2,) + quarter_in), vmem((2,) + quarter_back), vmem(quarter_in), vmem(quarter_back), vmem(quarter_in), vmem(quarter_back)]
        + [vmem((3, SG) + piece), vmem((SG,) + piece), vmem((SG - 1,) + piece)]
        + [dma((4,)), dma((4,)), dma((3,)), dma((3,))]
        + [dma((SG - 1,))] * 2 + [dma((4,))] * 2 + [dma((2,))] * 2 + [dma((3,))] * 2 + [dma((SG - 1,))] * 2
        + [dma((3,))] * 2 + [dma((SG - 1,))] * 2 + [dma((5,))] * 2 + [dma((2,))],
        number,
        (parts, stats, base, unit, grad_in, grad_back, grad_scales, grad_bias, vectors, rows, facts, targets, head),
        ["v"] * 12 + [block],
        ["a"] * 3 + ["v", block, "v"],
        62 << 20,
        (pl.cdiv(vocab, VOCAB_BLOCK),),
    )


def norm_kernel(
    head_squares, embed_squares, smalls, grad_in, grad_back, out,
    value, from_rep, half, from_shard, send_rep, recv_rep, send_shard, recv_shard,
):
    rep, shard, _, _, _ = whereabouts()
    shard_peers = [(rep, shard_peer(shard, step)) for step in range(1, SG)]
    rep_peers = [(lax.rem(rep + step, RG), shard) for step in range(1, RG)]
    greet(shard_peers + rep_peers)

    def squares(rows):
        return jnp.sum(rows * rows, axis=0, keepdims=True)

    def lanes(row):
        return sum(row[:, k * 128 : (k + 1) * 128] for k in range(row.shape[1] // 128))

    repeated = jnp.sum(embed_squares[...], axis=0, keepdims=True) + squares(smalls[...])
    repeated = repeated + lanes(jnp.sum(head_squares[...], axis=0, keepdims=True))
    total = repeated * (1.0 / RG)
    for rows in (grad_in, grad_back):
        for k in range(rows.shape[0]):
            total = total + lanes(squares(rows[k]))
    value[...] = jnp.broadcast_to(jnp.sum(total, axis=1, keepdims=True), value.shape)
    copies = [
        remote(value, from_rep.at[rep], send_rep.at[k], recv_rep.at[k], peer) for k, peer in enumerate(rep_peers)
    ]
    for copy in copies:
        copy.start()
    from_rep[rep] = value[...]
    for copy in copies:
        copy.wait()
    half[...] = from_rep[0] + from_rep[1] + from_rep[2] + from_rep[3]
    copies = [
        remote(half, from_shard.at[shard], send_shard.at[k], recv_shard.at[k], peer)
        for k, peer in enumerate(shard_peers)
    ]
    for copy in copies:
        copy.start()
    from_shard[shard] = half[...]
    for copy in copies:
        copy.wait()
    total = from_shard[0]
    for k in range(1, SG):
        total = total + from_shard[k]
    norm = jnp.sqrt(total)
    row = lax.broadcasted_iota(jnp.int32, norm.shape, 0)
    out[...] = jnp.where(row == 0, norm, CLIP_LEVEL / jnp.maximum(norm, CLIP_LEVEL))


def global_norm(head_squares, embed_squares, smalls, grad_in, grad_back, number):
    dma = pltpu.SemaphoreType.DMA
    tile = (8, 128)
    vmem = lambda *shape: pltpu.VMEM(shape, jnp.float32)
    return comm_call(
        norm_kernel,
        [jax.ShapeDtypeStruct(tile, jnp.float32)],
        [vmem(*tile), vmem(RG, *tile), vmem(*tile), vmem(SG, *tile)] + [dma((RG - 1,))] * 2 + [dma((SG - 1,))] * 2,
        number,
        (head_squares, embed_squares, smalls, grad_in, grad_back),
        "vvvvv",
        "v",
        12 << 20,
    )[0]


GROUP_HEADS = H // SG
HEAD_COLS = GROUP_HEADS * HD
UNITS = FF // SG
OWN_COLS = 3 * HEAD_COLS + UNITS
VOCAB_BLOCK = 512
ROW_BLOCK = 1024
TABLE_BLOCK = 4096
CAST_BLOCK = 512
VMEM_LIMIT = 60 << 20
EMBED_LIMIT = 30 << 20


def transposed_dot(left, right):
    return lax.dot_general(left, right, (((1,), (1,)), ((), ())), preferred_element_type=jnp.float32)


def first_dot(left, right):
    return lax.dot_general(left, right, (((0,), (0,)), ((), ())), preferred_element_type=jnp.float32)


def plain_dot(left, right):
    return jnp.dot(left, right, preferred_element_type=jnp.float32)


def vocab_blocks(vocab, height, body):
    at = pl.program_id(0)
    full, tail = divmod(vocab, height)
    pl.when(at < full)(lambda: body(height))
    if tail > 0:
        pl.when(at == full)(lambda: body(tail))


def logit_grads(low, turned, logsum, targets):
    logits = plain_dot(low, turned)
    hits = lax.broadcasted_iota(jnp.int32, logits.shape, 0) == targets
    weights = jnp.exp(logits - logsum)
    return jnp.where(hits, weights - 1.0, weights).astype(jnp.bfloat16)


def embed_grad_kernel(ids, rows, table, squares, wide):
    wide[...] = rows[...].astype(jnp.float32)
    squares[...] = jnp.zeros_like(squares)
    parts = table.shape[0] // 512

    def part_rows(part):
        return pl.ds(pl.multiple_of(part * 512, 512), 512)

    @pl.loop(0, parts)
    def _(part):
        table[part_rows(part), :] = jnp.zeros((512, table.shape[1]), jnp.float32)

    @pl.loop(0, rows.shape[0] // 8)
    def _(group):
        for lane in range(8):
            token = group * 8 + lane
            here = pl.ds(ids[token], 1)
            table[here, :] = table[here, :] + wide[pl.ds(token, 1), :]

    @pl.loop(0, parts)
    def _(part):
        block = table[part_rows(part), :]
        squares[...] += jnp.sum((block * block).reshape(64, 8, block.shape[1]), axis=0)


def embed_grads(ids, rows, vocab):
    count, feats = rows.shape
    height = pl.cdiv(vocab, TABLE_BLOCK) * TABLE_BLOCK
    return pl.pallas_call(
        embed_grad_kernel,
        in_specs=[pl.BlockSpec(memory_space=pltpu.SMEM), pl.BlockSpec(memory_space=pltpu.VMEM)],
        out_specs=[pl.BlockSpec(memory_space=pltpu.VMEM)] * 2,
        out_shape=[pltpu.VMEM((height, feats), jnp.float32), jax.ShapeDtypeStruct((8, feats), jnp.float32)],
        scratch_shapes=[pltpu.VMEM((count, feats), jnp.float32)],
        compiler_params=pltpu.CompilerParams(vmem_limit_bytes=EMBED_LIMIT),
    )(ids, rows)


def embed_update_kernel(norm, grads, weight, moment, square, next_weight, next_moment, next_square):
    width = weight.shape[1]
    here = pl.ds(pl.multiple_of(pl.program_id(0) * width, width), width)
    gradient = grads[here, :].T * norm[1:2, 0:1]
    next_weight[...], next_moment[...], next_square[...] = adamw(
        weight[...], gradient, moment[...], square[...], RATE_EMBED
    )


def update_embed(norm, grads, state):
    feats, vocab = state[0].shape
    block = pl.BlockSpec((feats, TABLE_BLOCK), lambda at: (0, at))
    return pl.pallas_call(
        embed_update_kernel,
        grid=(pl.cdiv(vocab, TABLE_BLOCK),),
        in_specs=[pl.BlockSpec(norm.shape, lambda at: (0, 0)), pl.BlockSpec(memory_space=pltpu.VMEM)] + [block] * 3,
        out_specs=[block] * 3,
        out_shape=[jax.ShapeDtypeStruct(state[0].shape, jnp.float32)] * 3,
        compiler_params=pltpu.CompilerParams(vmem_limit_bytes=EMBED_LIMIT),
    )(norm, pltpu.with_memory_space_constraint(grads, pltpu.VMEM), *state)


def update_kernel(
    norm, grads_in, grads_back, *refs
):
    factor = norm[1:2, 0:1]
    ins, backs = refs[0:3], refs[3:6]
    out_ins, out_backs = refs[6:9], refs[9:12]

    def update(here, gradient, sources, targets, rate):
        results = adamw(sources[0][here], gradient * factor, sources[1][here], sources[2][here], rate)
        for target, result in zip(targets, results):
            target[here] = result

    for source in range(SG):
        for part in range(3):
            first = part * D + source * HEAD_COLS
            gradient = grads_in[0, source, :, part * HEAD_COLS : (part + 1) * HEAD_COLS]
            update((slice(None), slice(first, first + HEAD_COLS)), gradient, ins, out_ins, RATE_IN)
        first = 3 * D + source * UNITS
        gradient = grads_in[0, source, :, 3 * HEAD_COLS :]
        update((slice(None), slice(first, first + UNITS)), gradient, ins, out_ins, RATE_IN)
    for tile in range(5):
        update((tile, 0), grads_back[0, tile], backs, out_backs, RATE_BACK)


def update_layer(norm, grads_in, grads_back, state_in, state_back):
    quarters, sources, rows, columns = grads_in.shape
    _, tiles, back_rows, depth = grads_back.shape
    wide = state_in[0].shape
    tall = state_back[0].shape
    back_shape = (tiles, quarters, back_rows, depth)
    in_block = pl.BlockSpec((rows, wide[1]), lambda at: (at, 0))
    back_block = pl.BlockSpec((tiles, 1, back_rows, depth), lambda at: (0, at, 0, 0))
    f32 = jnp.float32
    results = pl.pallas_call(
        update_kernel,
        grid=(quarters,),
        in_specs=[
            pl.BlockSpec(norm.shape, lambda at: (0, 0)),
            pl.BlockSpec((1, sources, rows, columns), lambda at: (at, 0, 0, 0)),
            pl.BlockSpec((1, tiles, back_rows, depth), lambda at: (at, 0, 0, 0)),
        ]
        + [in_block] * 3
        + [back_block] * 3,
        out_specs=[in_block] * 3 + [back_block] * 3,
        out_shape=[jax.ShapeDtypeStruct(wide, f32)] * 3 + [jax.ShapeDtypeStruct(back_shape, f32)] * 3,
        compiler_params=pltpu.CompilerParams(vmem_limit_bytes=VMEM_LIMIT),
    )(norm, grads_in, grads_back, *state_in, *[array.reshape(back_shape) for array in state_back])
    return (*results[:3], *[array.reshape(tall) for array in results[3:]])


def turn_tables(places):
    half_rot = ROT // 2
    lane = jnp.arange(HEAD_COLS) % HD
    exponent = (lane % half_rot).astype(jnp.float32) * (2.0 / ROT)
    angles = places[:, None] * jnp.exp(-exponent * jnp.log(10000.0))[None, :]
    cosine, sine = jnp.cos(angles), jnp.sin(angles)
    lane = lane[None, :]
    return (
        jnp.where(lane < ROT, cosine, 1.0),
        jnp.where(lane < half_rot, -sine, 0.0),
        jnp.where((lane >= half_rot) & (lane < ROT), sine, 0.0),
    )


def centred_rows(values):
    centred = values - jnp.mean(values, axis=-1, keepdims=True)
    spread = jnp.mean(centred * centred, axis=-1, keepdims=True)
    scale = lax.rsqrt(spread + NORM_EPS)
    return centred * scale, scale


def exact_dot(left, right, dims):
    return lax.dot_general(
        left, right, (dims, ((), ())), precision=lax.Precision.HIGHEST, preferred_element_type=jnp.float32
    )


def pick_matrix(places, tokens):
    token = lax.broadcasted_iota(jnp.int32, (tokens, places.shape[1]), 0)
    return (places == token).astype(jnp.float32)


def turn(rows, tables, sign):
    half_rot = ROT // 2
    own, after, before = tables
    width = rows.shape[1]
    return (
        rows * own
        + sign * (pltpu.roll(rows, width - half_rot, 1) * after)
        + sign * (pltpu.roll(rows, half_rot, 1) * before)
    )


def head_lanes(rows, head):
    lane = lax.broadcasted_iota(jnp.int32, rows.shape, 1)
    return jnp.where(lane // HD == head, rows, jnp.zeros_like(rows))


def head_probs(queries, keys, allowed, head):
    scores = transposed_dot(keys, head_lanes(queries, head)) * HD ** (-0.5)
    scores = jnp.where(allowed, scores, -1e30)
    exponent = jnp.exp(scores - jnp.max(scores, axis=0, keepdims=True))
    return exponent / jnp.sum(exponent, axis=0, keepdims=True)


def line_allowed(places, span, tokens):
    keys = lax.broadcasted_iota(jnp.int32, (tokens, places.shape[1]), 0)
    in_query = (places >= span) & (places < span + PIC)
    in_key = (keys >= span) & (keys < span + PIC)
    return (keys <= places) | (in_query & in_key)


def forward_kernel(
    residual, places, scales, bias, own, after, before, weights, back,
    queries, keys, values, hidden, joined, picked_one, picked_two, picked_rows, used, branch,
):
    bf16 = jnp.bfloat16
    tokens = residual.shape[0]
    span = places[1:2, :]
    gain_one, shift_one = scales[0:1, :], scales[1:2, :]
    gain_two, shift_two = scales[2:3, :], scales[3:4, :]
    unit, _ = centred_rows(residual[...].astype(jnp.float32))
    low_one = (unit * gain_one + shift_one).astype(bf16)
    slots = places[0:1, :]
    pick = pick_matrix(slots, tokens)
    rows = first_dot(pick.astype(bf16), residual[...])
    picked_rows[...] = rows.astype(bf16)
    used[...] = first_dot(pick.astype(bf16), jnp.ones((tokens, used.shape[1]), bf16))
    unit, _ = centred_rows(rows)
    low_picked = (unit * gain_one + shift_one).astype(bf16)
    picked_one[...] = low_picked
    low_two = (unit * gain_two + shift_two).astype(bf16)
    picked_two[...] = low_two
    tables = (own[...], after[...], before[...])
    picked_tables = tuple(exact_dot(pick, table, ((0,), (0,))) for table in tables)
    two, three = 2 * HEAD_COLS, 3 * HEAD_COLS
    query = plain_dot(low_picked, weights[:, :HEAD_COLS]) + bias[:, :HEAD_COLS]
    query = turn(query, picked_tables, 1.0).astype(bf16)
    queries[...] = query
    key = plain_dot(low_one, weights[:, HEAD_COLS:two]) + bias[:, HEAD_COLS:two]
    key = turn(key, tables, 1.0).astype(bf16)
    keys[...] = key
    value = (plain_dot(low_one, weights[:, two:three]) + bias[:, two:three]).astype(bf16)
    values[...] = value
    allowed = line_allowed(slots, span, tokens)
    attended = None
    for head in range(GROUP_HEADS):
        probs = head_probs(query, key, allowed, head).astype(bf16)
        term = head_lanes(first_dot(probs, value), head)
        attended = term if attended is None else attended + term
    joined[:, :HEAD_COLS] = attended.astype(bf16)
    pre = plain_dot(low_two, weights[:, three:]) + bias[:, three:]
    hidden[...] = pre
    joined[:, HEAD_COLS:] = (0.5 * pre * (1.0 + lax.erf(pre * 0.5**0.5))).astype(bf16)
    branch[...] = plain_dot(joined[...], back[...])


def line_block(height, width):
    return pl.BlockSpec((height, width), lambda line: (line, 0))


def still(array):
    return pl.BlockSpec(array.shape, lambda line: (0,) * array.ndim)


def layer_forward(residual, places, scales, bias, tables, weights, back):
    lines = places.shape[0] // 8
    tokens, slots = residual.shape[0] // lines, places.shape[1]
    depth = residual.shape[1]
    bf16, f32 = jnp.bfloat16, jnp.float32
    outs = [
        (slots, HEAD_COLS, bf16),
        (tokens, HEAD_COLS, bf16),
        (tokens, HEAD_COLS, bf16),
        (slots, UNITS, f32),
        (slots, HEAD_COLS + UNITS, bf16),
        (slots, depth, bf16),
        (slots, depth, bf16),
        (slots, depth, bf16),
        (slots, 128, f32),
        (slots, depth, f32),
    ]
    return pl.pallas_call(
        forward_kernel,
        grid=(lines,),
        in_specs=[
            line_block(tokens, depth),
            line_block(8, slots),
            still(scales),
            still(bias),
            *[still(table) for table in tables],
            still(weights),
            still(back),
        ],
        out_specs=[line_block(height, width) for height, width, _ in outs],
        out_shape=[jax.ShapeDtypeStruct((lines * height, width), kind) for height, width, kind in outs],
        compiler_params=pltpu.CompilerParams(vmem_limit_bytes=VMEM_LIMIT),
    )(residual, places, scales, bias, *tables, weights, back)


def backward_kernel(
    residual, places, scales, own, after, before, weights, back,
    queries, keys, values, hidden, joined, picked_one, picked_two, d_branch, d_after,
    unit_parts, stats, base, own_unit, grad_in, grad_back, grad_scales, grad_bias, unit_rows,
):
    bf16 = jnp.bfloat16
    line = pl.program_id(0)
    tokens = residual.shape[0]
    span = places[1:2, :]
    gain_one, shift_one = scales[0:1, :], scales[1:2, :]
    gain_two = scales[2:3, :]

    @pl.when(line == 0)
    def _():
        for total in (grad_in, grad_back, grad_scales, grad_bias):
            total[...] = jnp.zeros_like(total)

    slots = places[0:1, :]
    pick = pick_matrix(slots, tokens)
    base[...] = exact_dot(pick, d_after[...], ((1,), (0,)))
    tables = (own[...], after[...], before[...])
    picked_tables = tuple(exact_dot(pick, table, ((0,), (0,))) for table in tables)
    pick = pick.astype(bf16)
    d_rows = d_branch[...]
    d_joined = transposed_dot(d_rows, back[...])
    grad_back[...] += first_dot(joined[...], d_rows)
    d_attended = d_joined[:, :HEAD_COLS].astype(bf16)
    pre = hidden[...]
    slope = 0.5 * (1.0 + lax.erf(pre * 0.5**0.5)) + pre * jnp.exp(-0.5 * pre * pre) * (2.0 * 3.141592653589793) ** -0.5
    d_hidden = (d_joined[:, HEAD_COLS:] * slope).astype(bf16)
    allowed = line_allowed(slots, span, tokens)
    query, key, value = queries[...], keys[...], values[...]
    d_query = d_key = d_value = None
    for head in range(GROUP_HEADS):
        probs = head_probs(query, key, allowed, head)
        d_head = head_lanes(d_attended, head)
        d_probs = transposed_dot(value, d_head)
        d_scores = (probs * (d_probs - jnp.sum(probs * d_probs, axis=0, keepdims=True))).astype(bf16)
        terms = (
            head_lanes(first_dot(d_scores, key), head),
            plain_dot(d_scores, head_lanes(query, head)),
            plain_dot(probs.astype(bf16), d_head),
        )
        if d_query is None:
            d_query, d_key, d_value = terms
        else:
            d_query, d_key, d_value = d_query + terms[0], d_key + terms[1], d_value + terms[2]
    d_query = turn(d_query * HD ** (-0.5), picked_tables, -1.0).astype(bf16)
    d_key = turn(d_key * HD ** (-0.5), tables, -1.0).astype(bf16)
    d_value = d_value.astype(bf16)
    unit, unit_scale = centred_rows(residual[...].astype(jnp.float32))
    unit_rows[...] = unit
    feats = own_unit.shape[1]
    own_unit[...] = unit_rows[:, pl.ds(pl.multiple_of(lax.axis_index("shard") * feats, feats), feats)]
    low_one = (unit * gain_one + shift_one).astype(bf16)
    three = 3 * HEAD_COLS
    grad_in[:, :HEAD_COLS] += first_dot(picked_one[...], d_query)
    d_both = jnp.concatenate([d_key, d_value], axis=1)
    grad_in[:, HEAD_COLS:three] += first_dot(low_one, d_both)
    grad_in[:, three:] += first_dot(picked_two[...], d_hidden)

    def column_sum(rows):
        return jnp.sum(rows.astype(jnp.float32), axis=0, keepdims=True)

    grad_bias[0:1, :HEAD_COLS] += column_sum(d_query)
    grad_bias[0:1, HEAD_COLS:three] += column_sum(d_both)
    grad_bias[0:1, three:] += column_sum(d_hidden)
    d_projected = jnp.concatenate([plain_dot(pick, d_query).astype(bf16), d_both], axis=1)
    d_normed = transposed_dot(d_projected, weights[:, :three])
    d_unit = d_normed * gain_one
    grad_scales[0:1, :] += column_sum(d_normed * unit)
    grad_scales[1:2, :] += column_sum(d_normed)
    d_normed = transposed_dot(plain_dot(pick, d_hidden).astype(bf16), weights[:, three:])
    grad_scales[2:3, :] += column_sum(d_normed * unit)
    grad_scales[3:4, :] += column_sum(d_normed)
    d_unit = d_unit + d_normed * gain_two
    sum_one = jnp.sum(d_unit, axis=-1, keepdims=True)
    sum_two = jnp.sum(d_unit * unit, axis=-1, keepdims=True)
    steps = jnp.max(jnp.abs(d_unit), axis=-1, keepdims=True) * (1.0 / 32767.0)
    lane = lax.broadcasted_iota(jnp.int32, (tokens, 128), 1)
    columns = jnp.where(lane == 0, sum_one, jnp.where(lane == 1, sum_two, jnp.where(lane == 2, steps, unit_scale)))
    stats[...] = columns.T[:8, :]
    codes = coded(d_unit, steps)
    for part in range(unit_parts.shape[0]):
        unit_parts[part] = codes[:, part * feats : (part + 1) * feats]


def layer_backward(residual, places, scales, tables, weights, back, kept, d_branch, d_after):
    lines = places.shape[0] // 8
    count, depth = residual.shape
    tokens, slots = count // lines, places.shape[1]
    feats = depth // SG
    f32 = jnp.float32
    whole = lambda height, width: pl.BlockSpec((height, width), lambda line: (0, 0))
    return pl.pallas_call(
        backward_kernel,
        grid=(lines,),
        in_specs=[
            line_block(tokens, depth),
            line_block(8, slots),
            still(scales),
            *[still(table) for table in tables],
            still(weights),
            still(back),
            *[line_block(array.shape[0] // lines, array.shape[1]) for array in kept],
            line_block(slots, depth),
            line_block(slots, feats),
        ],
        out_specs=[
            pl.BlockSpec((SG, tokens, feats), lambda line: (0, line, 0)),
            pl.BlockSpec((8, tokens), lambda line: (0, line)),
            line_block(tokens, feats),
            line_block(tokens, feats),
            whole(depth, OWN_COLS),
            whole(HEAD_COLS + UNITS, depth),
            whole(8, depth),
            whole(8, OWN_COLS),
        ],
        out_shape=[
            jax.ShapeDtypeStruct((SG, count, feats), jnp.int16),
            jax.ShapeDtypeStruct((8, count), f32),
            jax.ShapeDtypeStruct((count, feats), f32),
            jax.ShapeDtypeStruct((count, feats), f32),
            jax.ShapeDtypeStruct((depth, OWN_COLS), f32),
            jax.ShapeDtypeStruct((HEAD_COLS + UNITS, depth), f32),
            jax.ShapeDtypeStruct((8, depth), f32),
            jax.ShapeDtypeStruct((8, OWN_COLS), f32),
        ],
        scratch_shapes=[pltpu.VMEM((tokens, depth), f32)],
        compiler_params=pltpu.CompilerParams(vmem_limit_bytes=VMEM_LIMIT),
    )(residual, places, scales, *tables, weights, back, *kept, d_branch, d_after)


def group_plan(
    token_ids,
    pic_start,
    comp_pos,
    comp_tgt,
    proj_in,
    proj_back,
    small_params,
    head_table,
    embed_table,
    first_in,
    second_in,
    first_back,
    second_back,
    first_small,
    second_small,
    first_head,
    second_head,
    first_embed,
    second_embed,
):
    bf16 = jnp.bfloat16
    rep_at = lax.axis_index("rep")
    shard_at = lax.axis_index("shard")
    micro, _, seq_dev = token_ids.shape
    slots = comp_pos.shape[2]
    seq_len = seq_dev * RG
    lines = micro * SG // RG
    blocks = lines * RG
    own_blocks = blocks // SG
    tokens = lines * seq_len
    slot_count = blocks * slots
    own_slots = own_blocks * slots
    vocab_dev = head_table.shape[1]
    vocab = embed_table.shape[1]
    quarter = D // SG // RG

    place_line = jnp.concatenate([comp_pos[:, 0, :].reshape(-1), comp_tgt[:, 0, :].reshape(-1)])
    span_line = jnp.concatenate([pic_start[:, 0], jnp.zeros((seq_dev - micro,), jnp.int32)])
    ints = jnp.concatenate(
        [token_ids[:, 0, :], place_line[None], span_line[None], jnp.zeros((4, seq_dev), jnp.int32)]
    )
    small_low = small_params.astype(bf16).astype(jnp.float32).reshape(-1, 128)
    small_rows = small_low.shape[0]
    smalls = jnp.pad(small_low, ((0, 16 - small_rows), (0, 0)))
    ints_all, places, marks, scales, own_bias, residual_low, in_all, back_all, head_low = share_entry(
        ints, smalls, proj_in, proj_back, embed_table, head_table.T, tokens, 1
    )
    own_in = in_all.reshape(D, OWN_COLS)
    own_back = back_all.reshape(5 * 128, D)

    tables = turn_tables(jnp.arange(seq_len).astype(jnp.float32))
    *kept, picked_rows, used, branch_parts = layer_forward(
        residual_low, places, scales, own_bias, tables, own_in, own_back
    )
    rows_all, facts_all, d_branch, after_pieces, vectors = loss_and_branch(
        branch_parts.reshape(SG, own_slots, D),
        picked_rows,
        scales,
        used,
        marks,
        head_low,
        3,
    )
    loss_sum = jnp.sum(facts_all[:, 1])
    count_sum = jnp.sum(facts_all[:, 2])
    d_after_feats = after_pieces.reshape(slot_count, D // SG)

    unit_parts, norm_stats, base, own_unit, grad_in, grad_back, grad_scales, grad_bias = layer_backward(
        residual_low, places, scales, tables, own_in, own_back, kept, d_branch, d_after_feats
    )

    in_quarters = grad_in.reshape(SG, RG, quarter, OWN_COLS)
    back_quarters = grad_back.reshape(5, RG, 32, D)
    d_rows_all, in_own, back_own, small_sum, grad_head, head_squares = layer_sums(
        unit_parts,
        norm_stats,
        base,
        own_unit,
        in_quarters,
        back_quarters,
        grad_scales,
        grad_bias,
        vectors,
        rows_all,
        facts_all,
        marks,
        head_low,
        8,
    )
    in_grads = lax.all_gather(in_own, "rep")
    back_grads = lax.all_gather(back_own, "rep")
    by_group = ints_all.reshape(RG, RG, SG // RG, 8, seq_dev)[:, :, :, :micro]
    ids_all = jnp.transpose(by_group, (1, 3, 2, 0, 4)).reshape(-1)
    grad_embed, embed_squares = embed_grads(ids_all, d_rows_all.reshape(RG * tokens, D // SG), vocab)

    norm_rows_out = global_norm(head_squares, embed_squares, small_sum, in_own, back_own, 10)
    norm_value, factor = norm_rows_out[0, 0], norm_rows_out[1, 0]
    next_in, moment_in, square_in, next_back, moment_back, square_back = update_layer(
        norm_rows_out, in_grads, back_grads, (proj_in, first_in, second_in), (proj_back, first_back, second_back)
    )
    grad_small = small_sum[:small_rows].reshape(-1)
    next_small, moment_small, square_small = adamw(
        small_params, grad_small * factor, first_small, second_small, RATE_SMALL
    )
    next_head, moment_head, square_head = adamw(
        head_table, grad_head.T * factor, first_head, second_head, RATE_HEAD
    )
    next_embed, moment_embed, square_embed = update_embed(
        norm_rows_out, grad_embed, (embed_table, first_embed, second_embed)
    )
    return (
        jnp.stack([loss_sum, count_sum]),
        norm_value.reshape(1),
        next_in,
        moment_in,
        square_in,
        next_back,
        moment_back,
        square_back,
        next_small,
        moment_small,
        square_small,
        next_head,
        moment_head,
        square_head,
        next_embed,
        moment_embed,
        square_embed,
    )


def select_plan(mesh):
    if mesh.shape["rep"] == RG and mesh.shape["shard"] == SG:
        return group_plan
    return any_mesh


def solution(mesh):
    placed = (
        P(None, "shard", "rep"),
        P(None, "shard"),
        P(None, "shard", "rep"),
        P(None, "shard", "rep"),
        P("shard", None),
        P("shard", None),
        P("shard"),
        P(None, "shard"),
        P("shard", None),
        P("shard", None),
        P("shard", None),
        P("shard", None),
        P("shard", None),
        P("shard"),
        P("shard"),
        P(None, "shard"),
        P(None, "shard"),
        P("shard", None),
        P("shard", None),
    )
    return jax.shard_map(
        select_plan(mesh),
        mesh=mesh,
        in_specs=placed,
        out_specs=(
            P(),
            P(),
            P("shard", None),
            P("shard", None),
            P("shard", None),
            P("shard", None),
            P("shard", None),
            P("shard", None),
            P("shard"),
            P("shard"),
            P("shard"),
            P(None, "shard"),
            P(None, "shard"),
            P(None, "shard"),
            P("shard", None),
            P("shard", None),
            P("shard", None),
        ),
        check_vma=False,
    )
```

```python
import functools

import jax
import jax.numpy as jnp
from jax import lax
from jax.experimental import pallas as pl
from jax.experimental.pallas import tpu as pltpu
from jax.sharding import PartitionSpec as P

D = 1024
H = 16
HD = 64
ROT = 16
FF = 4096
PIC = 256
STEP = 10


NORM_EPS = 1e-05
CLIP_LEVEL = 1.0
BETA_FIRST = 0.9
BETA_SECOND = 0.95
ADAM_EPS = 1e-08
DECAY_RATE = 0.01
RATE_IN = 0.01
RATE_BACK = 0.05
RATE_SMALL = 0.3
RATE_HEAD = 0.01
RATE_EMBED = 0.3


def combined_all(part, axis, combine):
    gathered = jax.tree.map(lambda a: lax.all_gather(a, axis), part)

    def take(source):
        return jax.tree.map(lambda a: lax.dynamic_index_in_dim(a, source, 0, False), gathered)

    return lax.fori_loop(
        1, lax.axis_size(axis), lambda source, state: combine(state, take(source)), take(0)
    )


def norm_rows(values, gain_vec, shift_vec):
    centred = values - jnp.mean(values, axis=-1, keepdims=True)
    spread = jnp.mean(centred * centred, axis=-1, keepdims=True)
    return centred * lax.rsqrt(spread + NORM_EPS) * gain_vec + shift_vec


def rotate(head_rows, place_vec):
    half_rot = ROT // 2
    exponent = jnp.arange(half_rot).astype(jnp.float32) * (2.0 / ROT)
    angles = place_vec[:, None] * jnp.exp(-exponent * jnp.log(10000.0))
    cosine = jnp.cos(angles)[:, None, :]
    sine_part = jnp.sin(angles)[:, None, :]
    front_part = head_rows[..., :half_rot]
    back_part = head_rows[..., half_rot:ROT]
    return jnp.concatenate(
        [
            front_part * cosine - back_part * sine_part,
            back_part * cosine + front_part * sine_part,
            head_rows[..., ROT:],
        ],
        axis=-1,
    )


def split_small(gain_parts):
    marks = [0, D, 2 * D, 3 * D, 4 * D, 5 * D, 6 * D, 9 * D, 9 * D + FF, 10 * D + FF]
    return tuple((gain_parts[marks[number] : marks[number + 1]] for number in range(9)))


def gelu_exact(values):
    return jax.nn.gelu(values, approximate=False)


def combine_totals(earlier, later_part):
    highest = jnp.maximum(earlier[0], later_part[0])
    totals = earlier[1] * jnp.exp(earlier[0] - highest) + later_part[1] * jnp.exp(
        later_part[0] - highest
    )
    return (highest, totals, earlier[2] + later_part[2])


def allowed_mask(query_places, key_places, span_start):
    inside_query = (query_places >= span_start) & (query_places < span_start + PIC)
    inside_key = (key_places >= span_start) & (key_places < span_start + PIC)
    return (key_places[None, :] <= query_places[:, None]) | inside_query[:, None] & inside_key[
        None, :
    ]


def masked_scores(queries, keys_all, allowed):
    raw_scores = jnp.einsum(
        "qhd,khd->hqk", queries, keys_all, preferred_element_type=jnp.float32
    ) * HD ** (-0.5)
    return jnp.where(allowed[None], raw_scores, -1e30)


def adamw(weight, gradient, moment, square, rate_value):
    moment = BETA_FIRST * moment + (1.0 - BETA_FIRST) * gradient
    square = BETA_SECOND * square + (1.0 - BETA_SECOND) * gradient * gradient
    moment_hat = moment / (1.0 - BETA_FIRST**STEP)
    square_hat = square / (1.0 - BETA_SECOND**STEP)
    weight = weight - rate_value * (
        moment_hat / (jnp.sqrt(square_hat) + ADAM_EPS) + DECAY_RATE * weight
    )
    return (weight, moment, square)


def any_mesh(
    token_ids,
    pic_start,
    comp_pos,
    comp_tgt,
    proj_in,
    proj_back,
    small_params,
    head_table,
    embed_table,
    first_in,
    second_in,
    first_back,
    second_back,
    first_small,
    second_small,
    first_head,
    second_head,
    first_embed,
    second_embed,
):
    seq_dev = token_ids.shape[2]
    micro_count = token_ids.shape[0]
    vocab_dev = head_table.shape[1]
    rep_count = lax.axis_size("rep")
    seq_len = seq_dev * rep_count
    rep_at = lax.axis_index("rep")
    shard_at = lax.axis_index("shard")
    used_own = comp_pos[:, 0, :] < seq_dev
    marked = jnp.where(used_own, comp_tgt[:, 0, :], -1)
    ids_group, tgt_group = (
        lax.all_gather(token_ids[:, 0, :], "shard", axis=1, tiled=True),
        lax.all_gather(marked, "shard", axis=1, tiled=True),
    )
    in_low = proj_in.astype(jnp.bfloat16)
    back_low = proj_back.astype(jnp.bfloat16)
    small_low = small_params.astype(jnp.bfloat16)
    head_low = head_table.astype(jnp.bfloat16)
    table_low = embed_table.astype(jnp.bfloat16)
    own_places = rep_at * seq_dev + jnp.arange(seq_dev)
    key_places = jnp.arange(seq_len)
    own_float = own_places.astype(jnp.float32)
    vocab_ids = jnp.arange(vocab_dev)
    grad_in = jnp.zeros((D, 3 * D + FF), jnp.float32)
    grad_back = jnp.zeros((D + FF, D), jnp.float32)
    grad_small = jnp.zeros((10 * D + FF,), jnp.float32)
    grad_head = jnp.zeros(head_table.shape, jnp.float32)
    grad_embed = jnp.zeros(embed_table.shape, jnp.float32)
    loss_sum = jnp.zeros((), jnp.float32)
    count_sum = jnp.zeros((), jnp.float32)
    for micro_at in range(micro_count):
        wide_in, wide_back, wide_small = (
            lax.all_gather(in_low, "shard", axis=0, tiled=True),
            lax.all_gather(back_low, "shard", axis=0, tiled=True),
            lax.all_gather(small_low, "shard", axis=0, tiled=True),
        )
        (
            gain_one,
            shift_one,
            gain_two,
            shift_two,
            gain_last,
            shift_last,
            bias_qkv,
            bias_hidden,
            bias_out,
        ) = split_small(wide_small.astype(jnp.float32))
        columns = jnp.take(table_low, ids_group[micro_at], axis=1)
        arrived = lax.all_to_all(columns, "shard", split_axis=1, concat_axis=0, tiled=True)
        residual = arrived.T.astype(jnp.float32)
        normed_one = norm_rows(residual, gain_one, shift_one)
        normed_two = norm_rows(residual, gain_two, shift_two)
        low_one = normed_one.astype(jnp.bfloat16)
        low_two = normed_two.astype(jnp.bfloat16)
        projected = (
            jnp.dot(low_one, wide_in[:, : 3 * D], preferred_element_type=jnp.float32) + bias_qkv
        )
        queries = rotate(projected[:, :D].reshape(seq_dev, H, HD), own_float).astype(jnp.bfloat16)
        key_rows = (
            rotate(projected[:, D : 2 * D].reshape(seq_dev, H, HD), own_float)
            .astype(jnp.bfloat16)
            .reshape(seq_dev, D)
        )
        value_rows = projected[:, 2 * D :].astype(jnp.bfloat16)
        keys_all, values_all = (
            lax.all_gather(key_rows, "rep", axis=0, tiled=True),
            lax.all_gather(value_rows, "rep", axis=0, tiled=True),
        )
        keys_all = keys_all.reshape(seq_len, H, HD)
        values_all = values_all.reshape(seq_len, H, HD)
        allowed = allowed_mask(own_places, key_places, pic_start[micro_at, 0])
        scores = masked_scores(queries, keys_all, allowed)
        highest = jnp.max(scores, axis=-1, keepdims=True)
        exponent = jnp.exp(scores - highest)
        totals = jnp.sum(exponent, axis=-1, keepdims=True)
        logsum = highest + jnp.log(totals)
        attn_probs = (exponent / totals).astype(jnp.bfloat16)
        attended = (
            jnp.einsum("hqk,khd->qhd", attn_probs, values_all, preferred_element_type=jnp.float32)
            .reshape(seq_dev, D)
            .astype(jnp.bfloat16)
        )
        hidden_pre = (
            jnp.dot(low_two, wide_in[:, 3 * D :], preferred_element_type=jnp.float32) + bias_hidden
        )
        activation = gelu_exact(hidden_pre).astype(jnp.bfloat16)
        joined = jnp.concatenate([attended, activation], axis=1)
        after_add = (
            residual + jnp.dot(joined, wide_back, preferred_element_type=jnp.float32) + bias_out
        )
        final_rows = norm_rows(after_add, gain_last, shift_last)
        places = comp_pos[micro_at, 0]
        used_slots = (places < seq_dev).astype(jnp.float32)
        picked = (
            jnp.take(final_rows, jnp.minimum(places, seq_dev - 1), axis=0) * used_slots[:, None]
        ).astype(jnp.bfloat16)
        rows_all = lax.all_gather(picked, "shard", axis=0, tiled=True)
        logits = jnp.dot(rows_all, head_low, preferred_element_type=jnp.float32)
        targets = tgt_group[micro_at]
        matches = (targets - shard_at * vocab_dev)[:, None] == vocab_ids[None, :]
        row_top = jnp.max(logits, axis=1)
        row_total = jnp.sum(jnp.exp(logits - row_top[:, None]), axis=1)
        row_target = jnp.sum(jnp.where(matches, logits, 0.0), axis=1)
        row_top, row_total, row_target = combined_all(
            (row_top, row_total, row_target), "shard", combine_totals
        )
        logsum_rows = row_top + jnp.log(row_total)
        counted = (targets >= 0).astype(jnp.float32)
        loss_sum = loss_sum + jnp.sum((logsum_rows - row_target) * counted)
        count_sum = count_sum + jnp.sum(counted)
        d_logits = (
            (jnp.exp(logits - logsum_rows[:, None]) - matches.astype(jnp.float32))
            * counted[:, None]
        ).astype(jnp.bfloat16)
        grad_head = grad_head + jnp.einsum(
            "rd,rv->dv", rows_all, d_logits, preferred_element_type=jnp.float32
        )
        d_picked = lax.psum_scatter(
            jnp.einsum("rv,dv->rd", d_logits, head_low, preferred_element_type=jnp.float32),
            "shard",
            scatter_dimension=0,
            tiled=True,
        )
        d_final = jnp.zeros((seq_dev, D), jnp.float32).at[places].add(d_picked, mode="drop")
        back_in, back_back = (
            lax.all_gather(in_low, "shard", axis=0, tiled=True),
            lax.all_gather(back_low, "shard", axis=0, tiled=True),
        )
        _, pull_last = jax.vjp(norm_rows, after_add, gain_last, shift_last)
        d_after, d_gain_last, d_shift_last = pull_last(d_final)
        d_branch = d_after.astype(jnp.bfloat16)
        grad_back = grad_back + jnp.einsum(
            "sc,sd->cd", joined, d_branch, preferred_element_type=jnp.float32
        )
        d_joined = jnp.einsum("sd,cd->sc", d_branch, back_back, preferred_element_type=jnp.float32)
        d_attended = d_joined[:, :D].astype(jnp.bfloat16).reshape(seq_dev, H, HD)
        _, pull_gelu = jax.vjp(gelu_exact, hidden_pre)
        d_hidden = pull_gelu(d_joined[:, D:])[0].astype(jnp.bfloat16)
        probs_again = jnp.exp(masked_scores(queries, keys_all, allowed) - logsum)
        d_probs = jnp.einsum(
            "qhd,khd->hqk", d_attended, values_all, preferred_element_type=jnp.float32
        )
        d_scores = (
            probs_again * (d_probs - jnp.sum(probs_again * d_probs, axis=-1, keepdims=True))
        ).astype(jnp.bfloat16)
        d_queries = jnp.einsum(
            "hqk,khd->qhd", d_scores, keys_all, preferred_element_type=jnp.float32
        ) * HD ** (-0.5)
        low_probs = probs_again.astype(jnp.bfloat16)
        d_keys = jnp.einsum(
            "hqk,qhd->khd", d_scores, queries, preferred_element_type=jnp.float32
        ) * HD ** (-0.5)
        d_values = jnp.einsum(
            "hqk,qhd->khd", low_probs, d_attended, preferred_element_type=jnp.float32
        )
        key_grads = lax.psum_scatter(
            jnp.concatenate(
                [
                    d_keys.reshape(seq_dev * lax.axis_size("rep"), D),
                    d_values.reshape(seq_dev * lax.axis_size("rep"), D),
                ],
                axis=1,
            ),
            "rep",
            scatter_dimension=0,
            tiled=True,
        )
        d_key_rows = rotate(key_grads[:, :D].reshape(seq_dev, H, HD), -own_float).reshape(
            seq_dev, D
        )
        d_query_rows = rotate(d_queries, -own_float).reshape(seq_dev, D)
        d_projected = jnp.concatenate([d_query_rows, d_key_rows, key_grads[:, D:]], axis=1).astype(
            jnp.bfloat16
        )
        grad_in = grad_in + jnp.concatenate(
            [
                jnp.einsum("sd,sc->dc", low_one, d_projected, preferred_element_type=jnp.float32),
                jnp.einsum("sd,sc->dc", low_two, d_hidden, preferred_element_type=jnp.float32),
            ],
            axis=1,
        )
        d_normed_one = jnp.einsum(
            "sc,dc->sd", d_projected, back_in[:, : 3 * D], preferred_element_type=jnp.float32
        )
        d_normed_two = jnp.einsum(
            "sc,dc->sd", d_hidden, back_in[:, 3 * D :], preferred_element_type=jnp.float32
        )
        _, pull_one = jax.vjp(norm_rows, residual, gain_one, shift_one)
        d_resid_one, d_gain_one, d_shift_one = pull_one(d_normed_one)
        _, pull_two = jax.vjp(norm_rows, residual, gain_two, shift_two)
        d_resid_two, d_gain_two, d_shift_two = pull_two(d_normed_two)
        d_residual = (d_after + d_resid_one + d_resid_two).astype(jnp.bfloat16)
        returned = lax.all_to_all(d_residual.T, "shard", split_axis=0, concat_axis=1, tiled=True)
        grad_embed = grad_embed.at[:, ids_group[micro_at]].add(returned.astype(jnp.float32))
        grad_small = grad_small + jnp.concatenate(
            [
                d_gain_one,
                d_shift_one,
                d_gain_two,
                d_shift_two,
                d_gain_last,
                d_shift_last,
                jnp.sum(d_projected.astype(jnp.float32), axis=0),
                jnp.sum(d_hidden.astype(jnp.float32), axis=0),
                jnp.sum(d_branch.astype(jnp.float32), axis=0),
            ]
        )
    shard_in, shard_back, shard_small = (
        lax.psum_scatter(grad_in, "shard", scatter_dimension=0, tiled=True),
        lax.psum_scatter(grad_back, "shard", scatter_dimension=0, tiled=True),
        lax.psum_scatter(grad_small, "shard", scatter_dimension=0, tiled=True),
    )
    summed = lax.psum(
        (shard_in, shard_back, shard_small, grad_head, grad_embed, loss_sum, count_sum), "rep"
    )
    local_square = (
        jnp.sum(summed[0] * summed[0])
        + jnp.sum(summed[1] * summed[1])
        + jnp.sum(summed[2] * summed[2])
        + jnp.sum(summed[3] * summed[3])
        + jnp.sum(summed[4] * summed[4])
    )
    norm_value = jnp.sqrt(lax.psum(local_square, "shard"))
    factor = CLIP_LEVEL / jnp.maximum(norm_value, CLIP_LEVEL)
    next_in, moment_in, square_in = adamw(proj_in, summed[0] * factor, first_in, second_in, RATE_IN)
    next_back, moment_back, square_back = adamw(
        proj_back, summed[1] * factor, first_back, second_back, RATE_BACK
    )
    next_small, moment_small, square_small = adamw(
        small_params, summed[2] * factor, first_small, second_small, RATE_SMALL
    )
    next_head, moment_head, square_head = adamw(
        head_table, summed[3] * factor, first_head, second_head, RATE_HEAD
    )
    next_embed, moment_embed, square_embed = adamw(
        embed_table, summed[4] * factor, first_embed, second_embed, RATE_EMBED
    )
    return (
        jnp.stack([summed[5], summed[6]]),
        norm_value.reshape(1),
        next_in,
        moment_in,
        square_in,
        next_back,
        moment_back,
        square_back,
        next_small,
        moment_small,
        square_small,
        next_head,
        moment_head,
        square_head,
        next_embed,
        moment_embed,
        square_embed,
    )


MESH = pl.DeviceIdType.MESH
RG = 4
SG = 8


def whereabouts():
    rep = lax.axis_index("rep")
    shard = lax.axis_index("shard")
    core_twin = rep + 1 - 2 * lax.rem(rep, 2)
    x_twin = lax.rem(rep + 2, RG)
    y_twin = shard + 1 - 2 * lax.rem(shard, 2)
    return rep, shard, core_twin, x_twin, y_twin


def z_peer(shard, step):
    return lax.rem(shard + 2 * step, SG)


def shard_peer(shard, step):
    return lax.rem(shard + step, SG)


def greet(partners):
    barrier = pltpu.get_barrier_semaphore()
    for partner in partners:
        pl.semaphore_signal(barrier, inc=1, device_id=partner, device_id_type=MESH)
    pl.semaphore_wait(barrier, len(partners))


def remote(src, dst, send_sem, recv_sem, partner):
    return pltpu.make_async_remote_copy(
        src_ref=src,
        dst_ref=dst,
        send_sem=send_sem,
        recv_sem=recv_sem,
        device_id=partner,
        device_id_type=MESH,
    )


def comm_call(kernel, out_shape, scratch, number, args, spaces=None, out_spaces=None, limit=None, grid=()):
    pick = {
        "a": pl.BlockSpec(memory_space=pl.ANY),
        "v": pl.BlockSpec(memory_space=pltpu.VMEM),
    }
    choose = lambda space: pick[space] if isinstance(space, str) else space
    spaces = spaces or "a" * len(args)
    out_spaces = out_spaces or "a" * len(out_shape)
    return pl.pallas_call(
        kernel,
        grid=grid,
        out_shape=out_shape,
        in_specs=[choose(space) for space in spaces],
        out_specs=[choose(space) for space in out_spaces],
        scratch_shapes=scratch,
        compiler_params=pltpu.CompilerParams(
            collective_id=number, has_side_effects=True, vmem_limit_bytes=limit
        ),
    )(*args)


def start_gather(source, out, slot, place, sems):
    send_z, recv_z, send_y, recv_y, own = sems
    rep, shard, _, _, y_twin = place
    keep = pltpu.make_async_copy(source, slot(out, shard), own)
    keep.start()
    first_y = remote(source, slot(out, shard), send_y.at[0], recv_y.at[0], (rep, y_twin))
    z_copies = [
        remote(source, slot(out, shard), send_z.at[step - 1], recv_z.at[step - 1], (rep, z_peer(shard, step)))
        for step in range(1, 4)
    ]
    for copy in z_copies:
        copy.start()
    first_y.start()
    return keep, first_y, z_copies


def finish_gather(started, out, slot, place, sems):
    send_z, recv_z, send_y, recv_y, own = sems
    rep, shard, _, _, y_twin = place
    keep, first_y, z_copies = started
    passed = []
    for step in range(1, 4):
        z_copies[step - 1].wait_recv()
        came_from = z_peer(shard, SG // 2 - step)
        passed.append(
            remote(slot(out, came_from), slot(out, came_from), send_y.at[step], recv_y.at[step], (rep, y_twin))
        )
        passed[-1].start()
    keep.wait()
    for copy in z_copies:
        copy.wait_send()
    first_y.wait()
    for copy in passed:
        copy.wait()


def gather_partners(place):
    rep, shard, _, _, y_twin = place
    return [(rep, z_peer(shard, step)) for step in range(1, 4)] + [(rep, y_twin)]


GATHER_SEMS = [pltpu.SemaphoreType.DMA((3,)), pltpu.SemaphoreType.DMA((3,)), pltpu.SemaphoreType.DMA((4,)), pltpu.SemaphoreType.DMA((4,)), pltpu.SemaphoreType.DMA]


def row_slot(out, index):
    height = out.shape[0] // SG
    return out.at[pl.ds(pl.multiple_of(index * height, height), height)]


def tile_user(tile):
    return jnp.where(tile < SG, tile, (tile - SG) // 4)


def tile_slot(tile):
    return jnp.where(tile < SG, 0, 1 + lax.rem(tile - SG + SG, 4))


def entry_kernel(
    table_steps, head_rows, ints, smalls, weights_in, weights_back, table, head,
    ints_out, places, marks, scales, bias, out, in_all, back_all, head_low,
    ints_all, smalls_all, in_parts, back_tiles, turned, wide, low, ids,
    send_int, recv_int, send_small, recv_small, send_rep, recv_rep,
    send_in, recv_in, send_back, recv_back, send_far, recv_far, send_pair, recv_pair,
    send_up, recv_up, send_down, recv_down, send_y, recv_y, own,
):
    at = pl.program_id(0)
    last = pl.num_programs(0) - 1
    rep, shard, core_twin, x_twin, y_twin = whereabouts()
    level, side = shard // 2, lax.rem(shard, 2)
    shard_peers = [(rep, shard_peer(shard, step)) for step in range(1, SG)]
    rep_peers = [(lax.rem(rep + step, RG), shard) for step in range(1, RG)]
    lines, tokens, feats = low.shape
    small_rows = 14

    def int_copies():
        return [
            remote(ints, ints_all.at[rep, shard], send_int.at[k], recv_int.at[k], peer)
            for k, peer in enumerate(shard_peers)
        ]

    def small_copies():
        return [
            remote(smalls, smalls_all.at[shard], send_small.at[k], recv_small.at[k], peer)
            for k, peer in enumerate(shard_peers)
        ]

    def rep_copies():
        return [
            remote(ints_all.at[rep], ints_all.at[rep], send_rep.at[k], recv_rep.at[k], peer)
            for k, peer in enumerate(rep_peers)
        ]

    def in_copies():
        return [
            remote(in_parts.at[peer[1], rep], in_all.at[shard, rep], send_in.at[k], recv_in.at[k], peer)
            for k, peer in enumerate(shard_peers)
        ]

    def own_in():
        return pltpu.make_async_copy(in_parts.at[shard, rep], in_all.at[shard, rep], own.at[0])

    def back_move(k):
        tile = 5 * shard + k
        user, slot = tile_user(tile), tile_slot(tile)
        there = remote(
            back_tiles.at[k, rep], back_all.at[slot, rep], send_back.at[k], recv_back.at[slot], (rep, user)
        )
        return user, slot, there

    def quarter_copies(quarter, sends, recvs, base, peer):
        return [
            remote(array.at[:, quarter], array.at[:, quarter], sends.at[base + k], recvs.at[base + k], (peer, shard))
            for k, array in enumerate((in_all, back_all))
        ]

    def far_copies():
        return quarter_copies(rep, send_far, recv_far, 0, x_twin)

    def pair_copies():
        return quarter_copies(rep, send_pair, recv_pair, 0, core_twin) + quarter_copies(
            x_twin, send_pair, recv_pair, 2, core_twin
        )

    def slot(line, z_at, y_at):
        index = 2 * z_at + y_at
        return out.at[pl.ds(line * tokens, tokens), pl.ds(pl.multiple_of(index * feats, feats), feats)]

    def up_copy(line, hop):
        here = slot(line, level - hop, side)
        source = low.at[line] if hop == 0 else here
        return remote(source, here, send_up.at[line, hop], recv_up.at[line, hop], (rep, shard + 2))

    def down_copy(line, hop):
        here = slot(line, level + hop, side)
        source = low.at[line] if hop == 0 else here
        return remote(source, here, send_down.at[line, hop], recv_down.at[line, hop], (rep, shard - 2))

    def side_copy(line, z_at, source=None):
        here = slot(line, z_at, side)
        return remote(
            here if source is None else source, here, send_y.at[line, z_at], recv_y.at[line, z_at], (rep, y_twin)
        )

    def keep_copy(line):
        return pltpu.make_async_copy(low.at[line], slot(line, level, side), own.at[2 + line])

    def pass_on(line, hop):
        @pl.when(level >= hop)
        def _():
            pltpu.make_async_copy(low.at[line], slot(line, level - hop, side), recv_up.at[line, hop - 1]).wait()
            if hop < 3:
                pl.when(level < 3)(lambda: up_copy(line, hop).start())
            side_copy(line, level - hop).start()

        @pl.when(level + hop <= 3)
        def _():
            pltpu.make_async_copy(low.at[line], slot(line, level + hop, side), recv_down.at[line, hop - 1]).wait()
            if hop < 3:
                pl.when(level > 0)(lambda: down_copy(line, hop).start())
            side_copy(line, level + hop).start()

    @pl.when(at == 0)
    def _():
        greet(shard_peers + rep_peers)
        for copy in int_copies() + small_copies():
            copy.start()
        for target in range(SG):
            for part in range(3):
                columns = weights_in[:, part * D + target * HEAD_COLS : part * D + (target + 1) * HEAD_COLS]
                in_parts[target, :, :, part * HEAD_COLS : (part + 1) * HEAD_COLS] = columns.astype(
                    in_parts.dtype
                ).reshape(RG, in_parts.shape[2], HEAD_COLS)
            columns = weights_in[:, 3 * D + target * UNITS : 3 * D + (target + 1) * UNITS]
            in_parts[target, :, :, 3 * HEAD_COLS :] = columns.astype(in_parts.dtype).reshape(
                RG, in_parts.shape[2], UNITS
            )
        back_tiles[...] = weights_back[...].astype(back_tiles.dtype).reshape(back_tiles.shape)
        for copy in in_copies():
            copy.start()
        own_in().start()
        for k in range(5):
            user, slot_at, there = back_move(k)
            here = pltpu.make_async_copy(back_tiles.at[k, rep], back_all.at[slot_at, rep], recv_back.at[slot_at])
            pl.when(user == shard)(here.start)
            pl.when(user != shard)(there.start)
        ints_all[rep, shard] = ints[...]
        smalls_all[shard] = smalls[...]

    @pl.when(at < table_steps)
    def _():
        block = table[...].astype(jnp.bfloat16).astype(jnp.float32)
        width = block.shape[1]
        turned[pl.ds(pl.multiple_of(at * width, width), width), :] = block.T

    @pl.when(at == 5)
    def _():
        for copy in int_copies():
            copy.wait()
        for copy in rep_copies():
            copy.start()

    @pl.when(at == table_steps)
    def _():
        for copy in rep_copies():
            copy.wait()
        to_scalars = pltpu.make_async_copy(ints_all.at[:, pl.ds(2 * rep, 2)], ids, own.at[1])
        to_scalars.start()
        to_scalars.wait()
        for line in range(lines):
            micro, member = line // 2, line % 2
            for block_at in range(RG):

                @pl.loop(0, 16)
                def _(group):
                    for k in range(8):
                        lane = group * 8 + k
                        wide[pl.ds(block_at * 128 + lane, 1), :] = turned[
                            pl.ds(ids[block_at, member, micro, lane], 1), :
                        ]

            low[line] = wide[...].astype(jnp.bfloat16)
            pl.when(level < 3)(lambda: up_copy(line, 0).start())
            pl.when(level > 0)(lambda: down_copy(line, 0).start())
            side_copy(line, level, low.at[line]).start()
            keep_copy(line).start()
        own_in().wait()
        for copy in in_copies():
            copy.wait()
        for k in range(5):
            pltpu.make_async_copy(back_tiles.at[0, rep], back_all.at[k, rep], recv_back.at[k]).wait()
        for copy in far_copies():
            copy.start()

    @pl.when(at >= table_steps)
    def _():
        head_low[...] = head[...].astype(jnp.bfloat16)

    order = sorted(((line, hop) for line in range(lines) for hop in range(1, 4)), key=lambda item: (sum(item), item[1]))
    for step, (line, hop) in enumerate(order):
        pl.when(at == table_steps + 1 + step)(functools.partial(pass_on, line, hop))

    @pl.when(at == last - 2)
    def _():
        for copy in far_copies():
            copy.wait()
        for copy in pair_copies():
            copy.start()

    @pl.when(at == last)
    def _():
        for copy in small_copies():
            copy.wait()
        ints_out[...] = ints_all[...]

        seq_dev, slots = ints.shape[1], ints.shape[1] // 4
        for group in range(RG):
            for line in range(lines):
                micro, member = line // 2, line % 2
                for block_at in range(RG):
                    facts = ints_all[block_at, 2 * group + member, 2:3, :]
                    where = facts[:, slots * micro : slots * (micro + 1)]
                    goal = facts[:, slots * (2 + micro) : slots * (3 + micro)]
                    some = where < seq_dev
                    start = (line * RG + block_at) * slots
                    marks[group, 0:1, start : start + slots] = jnp.where(some, goal - shard * head_rows, -1)
                    marks[group, 1:2, start : start + slots] = some.astype(jnp.int32)
        for line in range(lines):
            micro, member = line // 2, line % 2
            for block_at in range(RG):
                where = ints_all[block_at, 2 * rep + member, 2:3, slots * micro : slots * (micro + 1)]
                places[8 * line : 8 * line + 1, block_at * slots : (block_at + 1) * slots] = jnp.where(
                    where < seq_dev, where + block_at * seq_dev, -1
                )
            span = ints_all[0, 2 * rep + member, 3:4, micro : micro + 1]
            places[8 * line + 1 : 8 * line + 2, :] = jnp.broadcast_to(span, (1, places.shape[1]))

        def small_row(row):
            return smalls_all[row // small_rows, pl.ds(lax.rem(row, small_rows), 1), :]

        scales[...] = jnp.zeros_like(scales)
        for vector, start in enumerate([8 * k for k in range(6)] + [8 * 13]):
            for part in range(8):
                row = start + part
                scales[vector : vector + 1, part * 128 : (part + 1) * 128] = smalls_all[
                    row // small_rows, row % small_rows : row % small_rows + 1, :
                ]
        for part in range(3):
            bias[:, part * 128 : (part + 1) * 128] = small_row(48 + 8 * part + shard)
        for part in range(4):
            bias[:, (3 + part) * 128 : (4 + part) * 128] = small_row(72 + 4 * shard + part)
        for k in range(5):
            user, _, there = back_move(k)
            pl.when(user != shard)(there.wait_send)
        for line in range(lines):
            keep_copy(line).wait()
            for hop in range(3):
                pl.when((level >= hop) & (level < 3))(lambda: up_copy(line, hop).wait_send())
                pl.when((level + hop <= 3) & (level > 0))(lambda: down_copy(line, hop).wait_send())
            for z_at in range(4):
                side_copy(line, z_at).wait()
        for copy in pair_copies():
            copy.wait()


def share_entry(ints, smalls, weights_in, weights_back, table, head, tokens, number):
    quarter = weights_in.shape[0] // RG
    in_shape = (SG, RG, quarter, OWN_COLS)
    back_shape = (5, RG, 32, weights_back.shape[1])
    dma = pltpu.SemaphoreType.DMA
    feats, vocab = table.shape
    blocks = pl.cdiv(vocab, TABLE_BLOCK)
    head_blocks = max(pl.cdiv(head.shape[0], CAST_BLOCK), 13)
    lines = 4
    per_line = tokens // lines
    head_spec = pl.BlockSpec(
        (CAST_BLOCK, head.shape[1]),
        lambda at: (jnp.clip(at - blocks, 0, pl.cdiv(head.shape[0], CAST_BLOCK) - 1), 0),
    )
    return comm_call(
        functools.partial(entry_kernel, blocks, head.shape[0]),
        [
            jax.ShapeDtypeStruct((RG, SG) + ints.shape, ints.dtype),
            jax.ShapeDtypeStruct((8 * lines, ints.shape[1]), ints.dtype),
            jax.ShapeDtypeStruct((RG, 8, ints.shape[1] * lines), ints.dtype),
            jax.ShapeDtypeStruct((8, SG * feats), jnp.float32),
            jax.ShapeDtypeStruct((1, OWN_COLS), jnp.float32),
            jax.ShapeDtypeStruct((tokens, SG * feats), jnp.bfloat16),
            jax.ShapeDtypeStruct(in_shape, jnp.bfloat16),
            jax.ShapeDtypeStruct(back_shape, jnp.bfloat16),
            jax.ShapeDtypeStruct(head.shape, jnp.bfloat16),
        ],
        [
            pltpu.VMEM((RG, SG) + ints.shape, ints.dtype),
            pltpu.VMEM((SG,) + smalls.shape, smalls.dtype),
            pltpu.VMEM(in_shape, jnp.bfloat16),
            pltpu.VMEM(back_shape, jnp.bfloat16),
            pltpu.VMEM((blocks * TABLE_BLOCK, feats), jnp.float32),
            pltpu.VMEM((per_line, feats), jnp.float32),
            pltpu.VMEM((lines, per_line, feats), jnp.bfloat16),
            pltpu.SMEM((RG, 2) + ints.shape, jnp.int32),
        ]
        + [dma((SG - 1,))] * 4
        + [dma((RG - 1,))] * 2
        + [dma((SG - 1,))] * 2
        + [dma((5,))] * 2
        + [dma((2,))] * 2
        + [dma((4,))] * 2
        + [dma((lines, 3))] * 4
        + [dma((lines, 4))] * 2
        + [dma((2 + lines,))],
        number,
        (ints, smalls, weights_in, weights_back, table, head),
        ["v", "v", "v", "v", pl.BlockSpec((feats, TABLE_BLOCK), lambda at: (0, jnp.minimum(at, blocks - 1))), head_spec],
        ["v"] * 5 + ["a", "a", "a", head_spec],
        VMEM_LIMIT,
        (blocks + head_blocks,),
    )


def loss_kernel(
    vocab, parts, picked_rows, scales, used, marks, head,
    rows_all, facts_out, branch, features_out, vectors,
    rows, turned, low, after, branch_y, branch_sum, branch_z, picked_y, picked_sum, picked_z, picked,
    send_codes, stats, stats_all, facts, facts_all, features, pieces, low_branch, top, total, target,
    branch_send_y, branch_recv_y, branch_send_z, branch_recv_z,
    picked_send_y, picked_recv_y, picked_send_z, picked_recv_z,
    row_z_send, row_z_recv, row_y_send, row_y_recv, row_own,
    back_z_send, back_z_recv, back_y_send, back_y_recv, back_own,
    send_stat, recv_stat, send_row, recv_row, send_fact, recv_fact, send_feat, recv_feat, own,
):
    at = pl.program_id(0)
    blocks = pl.num_programs(0) // 2
    place = whereabouts()
    rep, shard, core_twin, x_twin, y_twin = place
    shard_peers = [(rep, shard_peer(shard, step)) for step in range(1, SG)]
    rep_peers = [(lax.rem(rep + step, RG), shard) for step in range(1, RG)]
    slots = after.shape[0]
    own_rows = pl.ds(pl.multiple_of(shard * slots, slots), slots)

    def shard_total(values, from_y, own_sum, from_z, send_y, recv_y, send_z, recv_z):
        y_copies = {}
        for step in (2, 1, 3, 0):
            send_codes[step] = row_codes(values[z_peer(y_twin, step)])
            y_copies[step] = remote(
                send_codes.at[step], from_y.at[step], send_y.at[step], recv_y.at[step], (rep, y_twin)
            )
            y_copies[step].start()
        z_copies = []
        for step in (2, 1, 3):
            y_copies[step].wait_recv()
            own_sum[step] = row_codes(values[z_peer(shard, step)] + row_values(from_y[step]))
            z_copies.append(
                remote(
                    own_sum.at[step], from_z.at[step - 1], send_z.at[step - 1], recv_z.at[step - 1],
                    (rep, z_peer(shard, step)),
                )
            )
            z_copies[-1].start()
        y_copies[0].wait_recv()
        result = values[shard] + row_values(from_y[0])
        for copy in z_copies:
            copy.wait()
        for step in range(4):
            y_copies[step].wait_send()
        return result + row_values(from_z[0]) + row_values(from_z[1]) + row_values(from_z[2])

    row_sems = (row_z_send, row_z_recv, row_y_send, row_y_recv, row_own)
    back_sems = (back_z_send, back_z_recv, back_y_send, back_y_recv, back_own)

    def stat_copies():
        return [
            remote(stats, stats_all.at[shard], send_stat.at[k], recv_stat.at[k], peer)
            for k, peer in enumerate(shard_peers)
        ]

    def row_copy(k, peer):
        return remote(rows, rows_all.at[rep], send_row.at[k], recv_row.at[k], (peer, shard))

    def passed_copy():
        return remote(rows_all.at[x_twin], rows_all.at[x_twin], send_row.at[2], recv_row.at[2], (core_twin, shard))

    def keep_rows():
        return pltpu.make_async_copy(rows, rows_all.at[rep], own)

    def fact_copies():
        return [
            remote(facts, facts_all.at[rep], send_fact.at[k], recv_fact.at[k], peer) for k, peer in enumerate(rep_peers)
        ]

    @pl.when(at == 0)
    def _():
        greet(shard_peers + rep_peers)
        sum_buffers = (branch_y, branch_sum, branch_z)
        whole = shard_total(parts, *sum_buffers, branch_send_y, branch_recv_y, branch_send_z, branch_recv_z)
        after[...] = picked_rows[own_rows, :].astype(jnp.float32) + whole + scales[6:7, :]
        unit, _ = centred_rows(after[...])
        final = unit * scales[4:5, :] + scales[5:6, :]
        low[...] = (final * used[own_rows, 0:1]).astype(low.dtype)
        started = start_gather(low, rows, row_slot, place, row_sems)
        finish_gather(started, rows, row_slot, place, row_sems)
        row_copy(0, x_twin).start()
        row_copy(1, core_twin).start()
        keep_rows().start()
        turned[...] = rows[...].T
        top[...] = jnp.full_like(top, -1e30)
        total[...] = jnp.zeros_like(total)
        target[...] = jnp.zeros_like(target)
        picked[...] = jnp.zeros_like(picked)

    full, tail = divmod(vocab, ROW_BLOCK)

    def each_block(start, body):
        pl.when((at >= start) & (at < start + full))(lambda: body(ROW_BLOCK))
        if tail > 0:
            pl.when(at == start + full)(lambda: body(tail))

    def top_block(size):
        logits = plain_dot(head[:size], turned[...])
        hits = lax.broadcasted_iota(jnp.int32, logits.shape, 0) == marks[rep, 0:1, :] - at * ROW_BLOCK
        target[...] += jnp.sum(jnp.where(hits, logits, 0.0), axis=0, keepdims=True)
        highest = jnp.maximum(top[...], jnp.max(logits, axis=0, keepdims=True))
        weights = jnp.sum(jnp.exp(logits - highest), axis=0, keepdims=True)
        total[...] = total[...] * jnp.exp(top[...] - highest) + weights
        top[...] = highest

    each_block(0, top_block)

    @pl.when(at == blocks - 1)
    def _():
        stats[...] = jnp.zeros_like(stats)
        stats[0:1, :] = top[...]
        stats[1:2, :] = total[...]
        stats[2:3, :] = target[...]
        for copy in stat_copies():
            copy.start()
        stats_all[shard] = stats[...]
        for copy in stat_copies():
            copy.wait()
        highest = stats_all[0, 0:1, :]
        for k in range(1, SG):
            highest = jnp.maximum(highest, stats_all[k, 0:1, :])
        weights = row_target = jnp.zeros_like(highest)
        for k in range(SG):
            weights = weights + stats_all[k, 1:2, :] * jnp.exp(stats_all[k, 0:1, :] - highest)
            row_target = row_target + stats_all[k, 2:3, :]
        logsum = highest + jnp.log(weights)
        some = marks[rep, 1:2, :] > 0
        facts[...] = jnp.zeros_like(facts)
        facts[0:1, :] = jnp.where(some, logsum, 1e30)
        facts[1:2, :] = jnp.where(some, logsum - row_target, 0.0)
        facts[2:3, :] = some.astype(jnp.float32)
        for copy in fact_copies():
            copy.start()
        facts_all[rep] = facts[...]
        row_copy(0, x_twin).wait_recv()
        passed_copy().start()

    def grad_block(size):
        block = head[:size]
        grads = logit_grads(block, turned[...], facts[0:1, :], marks[rep, 0:1, :] - (at - blocks) * ROW_BLOCK, plain_dot)
        picked[...] += first_dot(grads, block).reshape(picked.shape)

    each_block(blocks, grad_block)

    @pl.when(at == pl.num_programs(0) - 1)
    def _():
        sum_buffers = (picked_y, picked_sum, picked_z)
        d_final = shard_total(picked, *sum_buffers, picked_send_y, picked_recv_y, picked_send_z, picked_recv_z)
        unit, unit_scale = centred_rows(after[...])
        d_unit = d_final * scales[4:5, :]
        mean = jnp.mean(d_unit, axis=-1, keepdims=True)
        slope = jnp.mean(d_unit * unit, axis=-1, keepdims=True)
        d_after = (d_unit - mean - unit * slope) * unit_scale
        low_branch[...] = d_after.astype(low_branch.dtype)
        started = start_gather(low_branch, branch, row_slot, place, back_sems)
        width = pieces.shape[2]
        for k in range(SG):
            pieces[k] = d_after[:, k * width : (k + 1) * width]
        copies = [
            remote(pieces.at[peer[1]], features.at[shard], send_feat.at[k], recv_feat.at[k], peer)
            for k, peer in enumerate(shard_peers)
        ]
        for copy in copies:
            copy.start()
        features[shard] = pieces[shard]
        vectors[...] = jnp.zeros_like(vectors)
        vectors[0:1, :] = jnp.sum(d_final * unit, axis=0, keepdims=True)
        vectors[1:2, :] = jnp.sum(d_final, axis=0, keepdims=True)
        vectors[2:3, :] = jnp.sum(low_branch[...].astype(jnp.float32), axis=0, keepdims=True)
        finish_gather(started, branch, row_slot, place, back_sems)
        for copy in copies + fact_copies():
            copy.wait()
        facts_out[...] = facts_all[...]
        features_out[...] = features[...]
        row_copy(0, x_twin).wait_send()
        row_copy(1, core_twin).wait()
        passed_copy().wait()
        keep_rows().wait()


def loss_and_branch(parts, picked_rows, scales, used, marks, head, number):
    dma = pltpu.SemaphoreType.DMA
    f32, bf16 = jnp.float32, jnp.bfloat16
    _, slots, depth = parts.shape
    vocab = head.shape[0]
    count = SG * slots
    blocks = pl.cdiv(vocab, ROW_BLOCK)
    vmem = lambda *shape: pltpu.VMEM(shape, f32)
    return comm_call(
        functools.partial(loss_kernel, vocab),
        [
            jax.ShapeDtypeStruct((RG, count, depth), bf16),
            jax.ShapeDtypeStruct((RG, 8, count), f32),
            jax.ShapeDtypeStruct((count, depth), bf16),
            jax.ShapeDtypeStruct((SG, slots, depth // SG), f32),
            jax.ShapeDtypeStruct((8, depth), f32),
        ],
        [
            pltpu.VMEM((count, depth), bf16),
            pltpu.VMEM((depth, count), bf16),
            pltpu.VMEM((slots, depth), bf16),
            vmem(slots, depth),
        ]
        + [pltpu.VMEM((rounds, slots, depth + 128), jnp.int16) for rounds in (4, 4, 3, 4, 4, 3)]
        + [vmem(SG, slots, depth), pltpu.VMEM((4, slots, depth + 128), jnp.int16)]
        + [vmem(8, count), vmem(SG, 8, count), vmem(8, count), vmem(RG, 8, count)]
        + [vmem(SG, slots, depth // SG)] * 2
        + [pltpu.VMEM((slots, depth), bf16)]
        + [vmem(1, count)] * 3
        + [dma((4,)), dma((4,)), dma((3,)), dma((3,))] * 2
        + GATHER_SEMS * 2
        + [dma((SG - 1,))] * 2
        + [dma((3,))] * 4
        + [dma((SG - 1,))] * 2
        + [dma],
        number,
        (parts, picked_rows, scales, used, marks, head),
        ["v"] * 5 + [pl.BlockSpec((ROW_BLOCK, depth), lambda at: (lax.rem(at, blocks), 0))],
        ["a", "v", "a", "v", "v"],
        VMEM_LIMIT,
        (2 * blocks,),
    )


def coded(rows, steps):
    inverse = jnp.where(steps > 0.0, 1.0 / steps, 0.0)
    return jnp.clip(jnp.round(rows * inverse), -32767.0, 32767.0).astype(jnp.int32).astype(jnp.int16)


def row_codes(rows):
    largest = jnp.maximum(jnp.max(jnp.abs(rows), axis=-1, keepdims=True), 1e-30)
    power = jnp.ceil(jnp.log(largest) * (1.0 / LOG_TWO) - 14.99)
    codes = coded(rows, jnp.exp(power * LOG_TWO))
    tail = jnp.broadcast_to(power, (rows.shape[0], 128)).astype(jnp.int32).astype(jnp.int16)
    return jnp.concatenate([codes, tail], axis=1)


def row_values(codes):
    depth = codes.shape[1] - 128
    power = codes[:, depth : depth + 1].astype(jnp.int32).astype(jnp.float32)
    return codes[:, :depth].astype(jnp.int32).astype(jnp.float32) * jnp.exp(power * LOG_TWO)


def backward_line(
    residual, places, scales, own, after, before, weights, back,
    queries, keys, values, hidden, joined, picked_one, picked_two, d_branch, d_after,
    parts, stats, base, own_unit, grad_in, grad_back, grad_scales, grad_bias, line,
):
    bf16 = jnp.bfloat16
    shard = lax.axis_index("shard")
    tokens = residual.shape[0]
    here = pl.ds(pl.multiple_of(line * tokens, tokens), tokens)
    feats = own_unit.shape[1]
    span = places[1:2, :]
    gain_one, shift_one = scales[0:1, :], scales[1:2, :]
    gain_two = scales[2:3, :]
    slots = places[0:1, :]
    pick = pick_matrix(slots, tokens)
    base[here, :] = exact_dot(pick, d_after[...], ((1,), (0,)))
    tables = (own[...], after[...], before[...])
    picked_tables = tuple(exact_dot(pick, table, ((0,), (0,))) for table in tables)
    pick = pick.astype(bf16)
    d_rows = d_branch[...]
    d_joined = transposed_dot(d_rows, back[...])
    grad_back[...] += first_dot(joined[...], d_rows).reshape(grad_back.shape)
    d_attended = d_joined[:, :HEAD_COLS].astype(bf16)
    pre = hidden[...]
    slope = 0.5 * (1.0 + lax.erf(pre * 0.5**0.5)) + pre * jnp.exp(-0.5 * pre * pre) * (2.0 * 3.141592653589793) ** -0.5
    d_hidden = (d_joined[:, HEAD_COLS:] * slope).astype(bf16)
    allowed = line_allowed(slots, span, tokens)
    query, key, value = queries[...], keys[...], values[...]
    d_query = d_key = d_value = None
    for head in range(GROUP_HEADS):
        probs = head_probs(query, key, allowed, head)
        d_head = head_lanes(d_attended, head)
        d_probs = transposed_dot(value, d_head)
        d_scores = (probs * (d_probs - jnp.sum(probs * d_probs, axis=0, keepdims=True))).astype(bf16)
        terms = (
            head_lanes(first_dot(d_scores, key), head),
            plain_dot(d_scores, head_lanes(query, head)),
            plain_dot(probs.astype(bf16), d_head),
        )
        if d_query is None:
            d_query, d_key, d_value = terms
        else:
            d_query, d_key, d_value = d_query + terms[0], d_key + terms[1], d_value + terms[2]
    d_query = turn(d_query * HD ** (-0.5), picked_tables, -1.0).astype(bf16)
    d_key = turn(d_key * HD ** (-0.5), tables, -1.0).astype(bf16)
    d_both = jnp.concatenate([d_key, d_value.astype(bf16)], axis=1)
    wide = residual[...].astype(jnp.float32)
    row_mean = jnp.mean(wide, axis=-1, keepdims=True)
    unit, unit_scale = centred_rows(wide)
    own_lanes = residual[:, pl.ds(pl.multiple_of(shard * feats, feats), feats)].astype(jnp.float32)
    own_unit[here, :] = (own_lanes - row_mean) * unit_scale
    low_one = (unit * gain_one + shift_one).astype(bf16)
    three = 3 * HEAD_COLS

    def add_in(first, width, term):
        grad_in[:, :, :, first : first + width] += term.reshape(grad_in.shape[:3] + (width,))

    add_in(0, HEAD_COLS, first_dot(picked_one[...], d_query))
    add_in(HEAD_COLS, 2 * HEAD_COLS, first_dot(low_one, d_both))
    add_in(three, UNITS, first_dot(picked_two[...], d_hidden))

    def column_sum(rows):
        return jnp.sum(rows.astype(jnp.float32), axis=0, keepdims=True)

    grad_bias[0:1, :HEAD_COLS] += column_sum(d_query)
    grad_bias[0:1, HEAD_COLS:three] += column_sum(d_both)
    grad_bias[0:1, three:] += column_sum(d_hidden)
    d_projected = jnp.concatenate([plain_dot(pick, d_query).astype(bf16), d_both], axis=1)
    d_normed = transposed_dot(d_projected, weights[:, :three])
    d_unit = d_normed * gain_one
    grad_scales[0:1, :] += column_sum(d_normed * unit)
    grad_scales[1:2, :] += column_sum(d_normed)
    d_normed = transposed_dot(plain_dot(pick, d_hidden).astype(bf16), weights[:, three:])
    grad_scales[2:3, :] += column_sum(d_normed * unit)
    grad_scales[3:4, :] += column_sum(d_normed)
    d_unit = d_unit + d_normed * gain_two
    sum_one = jnp.sum(d_unit, axis=-1, keepdims=True)
    sum_two = jnp.sum(d_unit * unit, axis=-1, keepdims=True)
    steps = jnp.max(jnp.abs(d_unit), axis=-1, keepdims=True) * (1.0 / 32767.0)
    lane = lax.broadcasted_iota(jnp.int32, (tokens, 128), 1)
    columns = jnp.where(lane == 0, sum_one, jnp.where(lane == 1, sum_two, jnp.where(lane == 2, steps, unit_scale)))
    stats[:, here] = columns.T[:8, :]
    codes = coded(d_unit, steps)
    for part in range(SG):
        parts[part, here, :] = codes[:, part * feats : (part + 1) * feats]


def layer_kernel(
    vocab, lines,
    residual, places, scales, table_own, table_after, table_before, weights, back,
    queries, keys, values, hidden, joined, picked_one, picked_two, d_branch, d_after,
    vectors, rows, facts, targets, head,
    rows_all, in_out, back_out, smalls_out, head_out, squares,
    parts, stats, base, unit, grad_in, grad_back, grad_scales, grad_bias,
    smalls, low, sum_in, sum_back, stats_all, steps_all, from_y, own_sum, from_z, pair_in, pair_back,
    send_in_codes, send_in_steps, send_back_codes, send_back_steps,
    far_in_codes, far_in_steps, far_back_codes, far_back_steps,
    in_codes, in_steps, back_codes, back_steps,
    small_rep, small_sum, small_shard,
    send_y, recv_y, send_z, recv_z, send_stat, recv_stat, send_pair, recv_pair, send_far, recv_far,
    send_rep, recv_rep, send_small, recv_small,
    send_row, recv_row, send_in, recv_in, send_back, recv_back, own,
):
    at = pl.program_id(0)
    last = pl.num_programs(0) - 1
    rep, shard, core_twin, x_twin, y_twin = whereabouts()
    core_far = lax.rem(core_twin + 2, RG)
    small_rows = 14
    tokens = residual.shape[0]
    shard_peers = [(rep, shard_peer(shard, step)) for step in range(1, SG)]
    rep_peers = [(lax.rem(rep + step, RG), shard) for step in range(1, RG)]

    def rep_copies():
        return [
            remote(smalls, small_rep.at[k], send_rep.at[k], recv_rep.at[k], peer) for k, peer in enumerate(rep_peers)
        ]

    def pair_copies(which, slot):
        pairs = ((grad_in, pair_in), (grad_back, pair_back))
        return [
            remote(
                source.at[:, which], target.at[slot], send_pair.at[2 * slot + k], recv_pair.at[2 * slot + k],
                (core_twin, shard),
            )
            for k, (source, target) in enumerate(pairs)
        ]

    def y_copy(line, step):
        here = pl.ds(pl.multiple_of(line * tokens, tokens), tokens)
        return remote(
            parts.at[z_peer(y_twin, step), here], from_y.at[step, here],
            send_y.at[line, step], recv_y.at[line, step], (rep, y_twin),
        )

    def z_copy(line, step):
        here = pl.ds(line * tokens, tokens)
        return remote(
            own_sum.at[step, here], from_z.at[step - 1, here],
            send_z.at[line, step - 1], recv_z.at[line, step - 1], (rep, z_peer(shard, step)),
        )

    def stat_copies(line):
        here = pl.ds(pl.multiple_of(line * tokens, tokens), tokens)
        return [
            remote(stats.at[:, here], stats_all.at[shard, :, here], send_stat.at[line, k], recv_stat.at[line, k], peer)
            for k, peer in enumerate(shard_peers)
        ]

    def far_copies():
        pairs = (
            (send_in_codes, far_in_codes), (send_in_steps, far_in_steps),
            (send_back_codes, far_back_codes), (send_back_steps, far_back_steps),
        )
        return [
            remote(source, target, send_far.at[k], recv_far.at[k], (x_twin, shard))
            for k, (source, target) in enumerate(pairs)
        ]

    def small_copies():
        return [
            remote(small_sum.at[peer[1]], small_shard.at[k], send_small.at[k], recv_small.at[k], peer)
            for k, peer in enumerate(shard_peers)
        ]

    def in_copies():
        return [
            remote(source.at[peer[1]], target.at[shard], send_in.at[which, k], recv_in.at[which, k], peer)
            for k, peer in enumerate(shard_peers)
            for which, (source, target) in enumerate(((send_in_codes, in_codes), (send_in_steps, in_steps)))
        ]

    back_pairs = ((send_back_codes, back_codes), (send_back_steps, back_steps))

    def back_move(slot, which):
        tile = shard if slot == 0 else SG + 4 * shard + slot - 1
        owner, place = tile // 5, lax.rem(tile, 5)
        source, target = back_pairs[which]
        there = remote(
            source.at[slot], target.at[place], send_back.at[which, slot], recv_back.at[which, place], (rep, owner)
        )
        return owner, place, there

    def row_copy(line, k, peer):
        here = pl.ds(line * tokens, tokens)
        return remote(low.at[here], rows_all.at[rep, here], send_row.at[line, k], recv_row.at[line, k], (peer, shard))

    def passed_copy(line):
        there = rows_all.at[x_twin, pl.ds(line * tokens, tokens)]
        return remote(there, there, send_row.at[line, 2], recv_row.at[line, 2], (core_twin, shard))

    def keep_rows(line):
        here = pl.ds(line * tokens, tokens)
        return pltpu.make_async_copy(low.at[here], rows_all.at[rep, here], own.at[line])

    def pass_rows(line):
        row_copy(line, 0, x_twin).wait_recv()
        passed_copy(line).start()

    def finish(line):
        here = pl.ds(line * tokens, tokens)
        total = pair_sum(line, 0)
        for step in (1, 2, 3):
            z_copy(line, step).wait()
            behind = 4 - step
            steps = steps_all[here, behind : behind + 1] + steps_all[here, 4 + behind : 5 + behind]
            total = total + decoded(from_z[step - 1, here, :], steps)
        mean, slope, scale = (steps_all[here, k : k + 1] for k in (8, 9, 10))
        d_rows = (total - mean / D - unit[here, :] * (slope / D)) * scale
        low[here, :] = (base[here, :] + d_rows).astype(low.dtype)
        row_copy(line, 0, x_twin).start()
        row_copy(line, 1, core_twin).start()
        keep_rows(line).start()
        if line > 0:
            pass_rows(line - 1)

    def decoded(codes, steps):
        return codes.astype(jnp.int32).astype(jnp.float32) * steps

    def encode(values, codes, steps):
        for k in range(values.shape[0]):
            row_steps = jnp.max(jnp.abs(values[k]), axis=-1, keepdims=True) * (1.0 / 32767.0)
            steps[k] = jnp.broadcast_to(row_steps, steps.shape[1:])
            codes[k] = coded(values[k], row_steps)

    def pair_sum(line, step):
        here = pl.ds(line * tokens, tokens)
        y_copy(line, step).wait_recv()
        own_codes = decoded(parts[z_peer(shard, step), here, :], steps_all[here, 0:1])
        return own_codes + decoded(from_y[step, here, :], steps_all[here, 4:5])

    def pass_on(line):
        here = pl.ds(line * tokens, tokens)
        for copy in stat_copies(line):
            copy.wait()
        near = [stats_all[z_peer(shard, k), 2:3, here] for k in range(4)]
        near += [stats_all[z_peer(y_twin, k), 2:3, here] for k in range(4)]
        sums = stats_all[0, :, here]
        for k in range(1, SG):
            sums = sums + stats_all[k, :, here]
        near += [sums[0:2, :], stats[3:4, here], jnp.zeros((5, tokens), jnp.float32)]
        steps_all[here, 0:16] = jnp.concatenate(near, axis=0).T
        for step in (2, 1, 3):
            own_sum[step, here, :] = coded(pair_sum(line, step), steps_all[here, 0:1] + steps_all[here, 4:5])
            z_copy(line, step).start()

    @pl.when(at == 0)
    def _():
        greet(shard_peers + rep_peers)
        for total in (grad_in, grad_back, grad_scales, grad_bias, squares, smalls):
            total[...] = jnp.zeros_like(total)

    for line, step_at in enumerate(PASS_STEPS):
        pl.when(at == step_at)(functools.partial(pass_on, line))

    @pl.when(at < lines)
    def _():
        backward_line(
            residual, places, scales, table_own, table_after, table_before, weights, back,
            queries, keys, values, hidden, joined, picked_one, picked_two, d_branch, d_after,
            parts, stats, base, unit, grad_in, grad_back, grad_scales, grad_bias, at,
        )
        for copy in stat_copies(at):
            copy.start()
        for step in (2, 1, 3, 0):
            y_copy(at, step).start()
        here = pl.ds(pl.multiple_of(at * tokens, tokens), tokens)
        stats_all[shard, :, here] = stats[:, here]

    @pl.when(at == lines - 1)
    def _():
        for copy in pair_copies(core_far, 1) + pair_copies(core_twin, 0):
            copy.start()

        def put(row, values):
            smalls[row // small_rows, pl.ds(lax.rem(row, small_rows), 1), :] = values

        for k in range(8):
            lanes = slice(k * 128, (k + 1) * 128)
            for vector in range(4):
                put(8 * vector + k, grad_scales[vector : vector + 1, lanes])
            put(8 * 4 + k, vectors[0:1, lanes])
            put(8 * 5 + k, vectors[1:2, lanes])
            put(8 * 13 + k, vectors[2:3, lanes])
        for k in range(7):
            row = 48 + 8 * k + shard if k < 3 else 72 + 4 * shard + k - 3
            put(row, grad_bias[0:1, k * 128 : (k + 1) * 128])
        for copy in rep_copies():
            copy.start()

    @pl.when(at == lines + 1)
    def _():
        for copy in pair_copies(core_far, 1):
            copy.wait()
        sum_in[...] = grad_in[:, x_twin] + pair_in[1]
        sum_back[...] = grad_back[:, x_twin] + pair_back[1]
        encode(sum_in, send_in_codes, send_in_steps)
        encode(sum_back, send_back_codes, send_back_steps)
        for copy in far_copies():
            copy.start()
        for copy in rep_copies():
            copy.wait()
        small_sum[...] = smalls[...] + small_rep[0] + small_rep[1] + small_rep[2]
        for copy in small_copies():
            copy.start()

    @pl.when(at == lines + 6)
    def _():
        for copy in pair_copies(core_twin, 0) + far_copies():
            copy.wait()
        sum_in[...] = grad_in[:, rep] + pair_in[0]
        sum_back[...] = grad_back[:, rep] + pair_back[0]
        for k in range(sum_in.shape[0]):
            sum_in[k] = sum_in[k] + decoded(far_in_codes[k], far_in_steps[k, :, 0:1])
        for k in range(sum_back.shape[0]):
            sum_back[k] = sum_back[k] + decoded(far_back_codes[k], far_back_steps[k, :, 0:1])
        encode(sum_in, send_in_codes, send_in_steps)
        encode(sum_back, send_back_codes, send_back_steps)
        for copy in in_copies():
            copy.start()
        in_codes[shard] = send_in_codes[shard]
        in_steps[shard] = send_in_steps[shard]
        for slot in range(5):
            for which, (source, target) in enumerate(back_pairs):
                owner, place, there = back_move(slot, which)
                here = pltpu.make_async_copy(source.at[slot], target.at[place], recv_back.at[which, place])
                pl.when(owner == shard)(here.start)
                pl.when(owner != shard)(there.start)

    for line, step_at in enumerate(FINISH_STEPS):
        pl.when(at == step_at)(functools.partial(finish, line))

    pl.when(at == last)(lambda: pass_rows(lines - 1))

    @pl.when(at >= lines)
    def _():
        block_at = at - lines

        def head_block(size):
            total = None
            for group in range(RG):
                base_row = block_at * VOCAB_BLOCK
                grads = logit_grads(
                    head[:size], rows[group], facts[group, 0:1, :], targets[group, 0:1, :] - base_row, transposed_dot
                )
                term = plain_dot(grads, rows[group])
                total = term if total is None else total + term
            head_out[:size] = total
            squares[0:1, :] += jnp.sum(total * total, axis=0, keepdims=True)

        full, tail = divmod(vocab, VOCAB_BLOCK)
        pl.when(block_at < full)(lambda: head_block(VOCAB_BLOCK))
        if tail > 0:
            pl.when(block_at == full)(lambda: head_block(tail))

    @pl.when(at == last)
    def _():
        for copy in small_copies():
            copy.wait()
        whole = small_sum[shard]
        for k in range(SG - 1):
            whole = whole + small_shard[k]
        smalls_out[...] = whole
        for copy in in_copies():
            copy.wait()
        for k in range(in_codes.shape[0]):
            in_out[k] = decoded(in_codes[k], in_steps[k, :, 0:1])
        for place in range(5):
            for which, (source, target) in enumerate(back_pairs):
                pltpu.make_async_copy(source.at[0], target.at[place], recv_back.at[which, place]).wait()
        for place in range(5):
            back_out[place] = decoded(back_codes[place], back_steps[place, :, 0:1])
        for slot in range(5):
            for which in range(2):
                owner, _, there = back_move(slot, which)
                pl.when(owner != shard)(there.wait_send)
        for line in range(lines):
            for step in range(4):
                y_copy(line, step).wait_send()
            keep_rows(line).wait()
            row_copy(line, 0, x_twin).wait_send()
            row_copy(line, 1, core_twin).wait()
            passed_copy(line).wait()


def layer_backward(residual, places, scales, tables, weights, back, kept, d_branch, d_after, vectors, rows, facts, targets, head, number):
    dma = pltpu.SemaphoreType.DMA
    f32, bf16, i16 = jnp.float32, jnp.bfloat16, jnp.int16
    lines = places.shape[0] // 8
    count, depth = residual.shape
    tokens, slots = count // lines, places.shape[1]
    feats = depth // SG
    vocab = head.shape[0]
    quarter = feats // RG
    piece = (16, 128)
    blocks = pl.cdiv(vocab, VOCAB_BLOCK)
    vmem = lambda *shape: pltpu.VMEM(shape, f32)
    short = lambda *shape: pltpu.VMEM(shape, i16)
    shape = lambda *dims: jax.ShapeDtypeStruct(dims, f32)

    def by_line(height, width):
        return pl.BlockSpec((height, width), lambda at: (jnp.minimum(at, lines - 1), 0))

    head_block = pl.BlockSpec((VOCAB_BLOCK, depth), lambda at: (jnp.clip(at - lines, 0, blocks - 1), 0))
    in_dims, back_dims = (SG, quarter, OWN_COLS), (5, 32, depth)
    in_step, back_step = (SG, quarter, 128), (5, 32, 128)
    coded_buffers = [short(*in_dims), vmem(*in_step), short(*back_dims), vmem(*back_step)]
    return comm_call(
        functools.partial(layer_kernel, vocab, lines),
        [
            jax.ShapeDtypeStruct((RG, count, feats), bf16),
            shape(*in_dims),
            shape(*back_dims),
            shape(*piece),
            shape(vocab, depth),
            shape(8, depth),
        ],
        [
            short(SG, count, feats),
            vmem(8, count),
            vmem(count, feats),
            vmem(count, feats),
            vmem(SG, RG, quarter, OWN_COLS),
            vmem(5, RG, 32, depth),
            vmem(8, depth),
            vmem(8, OWN_COLS),
            vmem(SG, *piece),
            pltpu.VMEM((count, feats), bf16),
            vmem(*in_dims),
            vmem(*back_dims),
            vmem(SG, 8, count),
            vmem(count, 128),
            short(4, count, feats),
            short(4, count, feats),
            short(3, count, feats),
            vmem(2, *in_dims),
            vmem(2, *back_dims),
        ]
        + coded_buffers * 3
        + [vmem(3, SG, *piece), vmem(SG, *piece), vmem(SG - 1, *piece)]
        + [dma((lines, 4))] * 2
        + [dma((lines, 3))] * 2
        + [dma((lines, SG - 1))] * 2
        + [dma((4,))] * 4
        + [dma((3,))] * 2
        + [dma((SG - 1,))] * 2
        + [dma((lines, 3))] * 2
        + [dma((2, SG - 1))] * 2
        + [dma((2, 5))] * 2
        + [dma((lines,))],
        number,
        (residual, places, scales, *tables, weights, back, *kept, d_branch, d_after, vectors, rows, facts, targets, head),
        [by_line(tokens, depth), by_line(8, slots)]
        + ["v"] * 6
        + [by_line(array.shape[0] // lines, array.shape[1]) for array in kept]
        + [by_line(slots, depth), by_line(slots, feats)]
        + ["v"] * 4
        + [head_block],
        ["a", "v", "v", "v", head_block, "v"],
        LAYER_LIMIT,
        (lines + blocks,),
    )


def norm_kernel(
    head_squares, embed_squares, smalls, grad_in, grad_back, out,
    value, from_rep, half, from_shard, send_rep, recv_rep, send_shard, recv_shard,
):
    rep, shard, _, _, _ = whereabouts()
    shard_peers = [(rep, shard_peer(shard, step)) for step in range(1, SG)]
    rep_peers = [(lax.rem(rep + step, RG), shard) for step in range(1, RG)]
    greet(shard_peers + rep_peers)

    def squares(rows):
        return jnp.sum(rows * rows, axis=0, keepdims=True)

    def lanes(row):
        return sum(row[:, k * 128 : (k + 1) * 128] for k in range(row.shape[1] // 128))

    repeated = jnp.sum(embed_squares[...], axis=0, keepdims=True) + squares(smalls[...])
    repeated = repeated + lanes(jnp.sum(head_squares[...], axis=0, keepdims=True))
    total = repeated * (1.0 / RG)
    for rows in (grad_in, grad_back):
        for k in range(rows.shape[0]):
            total = total + lanes(squares(rows[k]))
    value[...] = jnp.broadcast_to(jnp.sum(total, axis=1, keepdims=True), value.shape)
    copies = [
        remote(value, from_rep.at[rep], send_rep.at[k], recv_rep.at[k], peer) for k, peer in enumerate(rep_peers)
    ]
    for copy in copies:
        copy.start()
    from_rep[rep] = value[...]
    for copy in copies:
        copy.wait()
    half[...] = from_rep[0] + from_rep[1] + from_rep[2] + from_rep[3]
    copies = [
        remote(half, from_shard.at[shard], send_shard.at[k], recv_shard.at[k], peer)
        for k, peer in enumerate(shard_peers)
    ]
    for copy in copies:
        copy.start()
    from_shard[shard] = half[...]
    for copy in copies:
        copy.wait()
    total = from_shard[0]
    for k in range(1, SG):
        total = total + from_shard[k]
    norm = jnp.sqrt(total)
    row = lax.broadcasted_iota(jnp.int32, norm.shape, 0)
    out[...] = jnp.where(row == 0, norm, CLIP_LEVEL / jnp.maximum(norm, CLIP_LEVEL))


def global_norm(head_squares, embed_squares, smalls, grad_in, grad_back, number):
    dma = pltpu.SemaphoreType.DMA
    tile = (8, 128)
    vmem = lambda *shape: pltpu.VMEM(shape, jnp.float32)
    return comm_call(
        norm_kernel,
        [jax.ShapeDtypeStruct(tile, jnp.float32)],
        [vmem(*tile), vmem(RG, *tile), vmem(*tile), vmem(SG, *tile)] + [dma((RG - 1,))] * 2 + [dma((SG - 1,))] * 2,
        number,
        (head_squares, embed_squares, smalls, grad_in, grad_back),
        "vvvvv",
        "v",
        12 << 20,
    )[0]


GROUP_HEADS = H // SG
HEAD_COLS = GROUP_HEADS * HD
UNITS = FF // SG
OWN_COLS = 3 * HEAD_COLS + UNITS
VOCAB_BLOCK = 512
ROW_BLOCK = 1024
TABLE_BLOCK = 4096
CAST_BLOCK = 512
VMEM_LIMIT = 60 << 20
EMBED_LIMIT = 30 << 20
LAYER_LIMIT = 63 << 20
PASS_STEPS = (3, 5, 7, 9)
FINISH_STEPS = (8, 11, 13, 15)
LOG_TWO = 0.6931471805599453


def transposed_dot(left, right):
    return lax.dot_general(left, right, (((1,), (1,)), ((), ())), preferred_element_type=jnp.float32)


def first_dot(left, right):
    return lax.dot_general(left, right, (((0,), (0,)), ((), ())), preferred_element_type=jnp.float32)


def plain_dot(left, right):
    return jnp.dot(left, right, preferred_element_type=jnp.float32)


def logit_grads(low, rows, logsum, targets, dot):
    logits = dot(low, rows)
    hits = lax.broadcasted_iota(jnp.int32, logits.shape, 0) == targets
    weights = jnp.exp(logits - logsum)
    return jnp.where(hits, weights - 1.0, weights).astype(jnp.bfloat16)


def embed_grad_kernel(ids, rows, table, squares, wide):
    wide[...] = rows[...].astype(jnp.float32)
    squares[...] = jnp.zeros_like(squares)
    parts = table.shape[0] // 512

    def part_rows(part):
        return pl.ds(pl.multiple_of(part * 512, 512), 512)

    @pl.loop(0, parts)
    def _(part):
        table[part_rows(part), :] = jnp.zeros((512, table.shape[1]), jnp.float32)

    @pl.loop(0, rows.shape[0] // 8)
    def _(group):
        for lane in range(8):
            token = group * 8 + lane
            here = pl.ds(ids[token], 1)
            table[here, :] = table[here, :] + wide[pl.ds(token, 1), :]

    @pl.loop(0, parts)
    def _(part):
        block = table[part_rows(part), :]
        squares[...] += jnp.sum((block * block).reshape(64, 8, block.shape[1]), axis=0)


def embed_grads(ids, rows, vocab):
    count, feats = rows.shape
    height = pl.cdiv(vocab, TABLE_BLOCK) * TABLE_BLOCK
    return pl.pallas_call(
        embed_grad_kernel,
        in_specs=[pl.BlockSpec(memory_space=pltpu.SMEM), pl.BlockSpec(memory_space=pltpu.VMEM)],
        out_specs=[pl.BlockSpec(memory_space=pltpu.VMEM)] * 2,
        out_shape=[pltpu.VMEM((height, feats), jnp.float32), jax.ShapeDtypeStruct((8, feats), jnp.float32)],
        scratch_shapes=[pltpu.VMEM((count, feats), jnp.float32)],
        compiler_params=pltpu.CompilerParams(vmem_limit_bytes=EMBED_LIMIT),
    )(ids, rows)


def embed_update_kernel(norm, grads, weight, moment, square, next_weight, next_moment, next_square):
    width = weight.shape[1]
    here = pl.ds(pl.multiple_of(pl.program_id(0) * width, width), width)
    gradient = grads[here, :].T * norm[1:2, 0:1]
    next_weight[...], next_moment[...], next_square[...] = adamw(
        weight[...], gradient, moment[...], square[...], RATE_EMBED
    )


def update_embed(norm, grads, state):
    feats, vocab = state[0].shape
    block = pl.BlockSpec((feats, TABLE_BLOCK), lambda at: (0, at))
    return pl.pallas_call(
        embed_update_kernel,
        grid=(pl.cdiv(vocab, TABLE_BLOCK),),
        in_specs=[pl.BlockSpec(norm.shape, lambda at: (0, 0)), pl.BlockSpec(memory_space=pltpu.VMEM)] + [block] * 3,
        out_specs=[block] * 3,
        out_shape=[jax.ShapeDtypeStruct(state[0].shape, jnp.float32)] * 3,
        compiler_params=pltpu.CompilerParams(vmem_limit_bytes=EMBED_LIMIT),
    )(norm, pltpu.with_memory_space_constraint(grads, pltpu.VMEM), *state)


def update_kernel(
    norm, grads_in, grads_back, *refs
):
    factor = norm[1:2, 0:1]
    ins, backs = refs[0:3], refs[3:6]
    out_ins, out_backs = refs[6:9], refs[9:12]

    def update(here, gradient, sources, targets, rate):
        results = adamw(sources[0][here], gradient * factor, sources[1][here], sources[2][here], rate)
        for target, result in zip(targets, results):
            target[here] = result

    for source in range(SG):
        for part in range(3):
            first = part * D + source * HEAD_COLS
            gradient = grads_in[0, source, :, part * HEAD_COLS : (part + 1) * HEAD_COLS]
            update((slice(None), slice(first, first + HEAD_COLS)), gradient, ins, out_ins, RATE_IN)
        first = 3 * D + source * UNITS
        gradient = grads_in[0, source, :, 3 * HEAD_COLS :]
        update((slice(None), slice(first, first + UNITS)), gradient, ins, out_ins, RATE_IN)
    for tile in range(5):
        update((tile, 0), grads_back[0, tile], backs, out_backs, RATE_BACK)


def update_layer(norm, grads_in, grads_back, state_in, state_back):
    quarters, sources, rows, columns = grads_in.shape
    _, tiles, back_rows, depth = grads_back.shape
    wide = state_in[0].shape
    tall = state_back[0].shape
    back_shape = (tiles, quarters, back_rows, depth)
    in_block = pl.BlockSpec((rows, wide[1]), lambda at: (at, 0))
    back_block = pl.BlockSpec((tiles, 1, back_rows, depth), lambda at: (0, at, 0, 0))
    f32 = jnp.float32
    results = pl.pallas_call(
        update_kernel,
        grid=(quarters,),
        in_specs=[
            pl.BlockSpec(norm.shape, lambda at: (0, 0)),
            pl.BlockSpec((1, sources, rows, columns), lambda at: (at, 0, 0, 0)),
            pl.BlockSpec((1, tiles, back_rows, depth), lambda at: (at, 0, 0, 0)),
        ]
        + [in_block] * 3
        + [back_block] * 3,
        out_specs=[in_block] * 3 + [back_block] * 3,
        out_shape=[jax.ShapeDtypeStruct(wide, f32)] * 3 + [jax.ShapeDtypeStruct(back_shape, f32)] * 3,
        compiler_params=pltpu.CompilerParams(vmem_limit_bytes=VMEM_LIMIT),
    )(norm, grads_in, grads_back, *state_in, *[array.reshape(back_shape) for array in state_back])
    return (*results[:3], *[array.reshape(tall) for array in results[3:]])


def turn_tables(places):
    half_rot = ROT // 2
    lane = jnp.arange(HEAD_COLS) % HD
    exponent = (lane % half_rot).astype(jnp.float32) * (2.0 / ROT)
    angles = places[:, None] * jnp.exp(-exponent * jnp.log(10000.0))[None, :]
    cosine, sine = jnp.cos(angles), jnp.sin(angles)
    lane = lane[None, :]
    return (
        jnp.where(lane < ROT, cosine, 1.0),
        jnp.where(lane < half_rot, -sine, 0.0),
        jnp.where((lane >= half_rot) & (lane < ROT), sine, 0.0),
    )


def centred_rows(values):
    centred = values - jnp.mean(values, axis=-1, keepdims=True)
    spread = jnp.mean(centred * centred, axis=-1, keepdims=True)
    scale = lax.rsqrt(spread + NORM_EPS)
    return centred * scale, scale


def exact_dot(left, right, dims):
    return lax.dot_general(
        left, right, (dims, ((), ())), precision=lax.Precision.HIGHEST, preferred_element_type=jnp.float32
    )


def pick_matrix(places, tokens):
    token = lax.broadcasted_iota(jnp.int32, (tokens, places.shape[1]), 0)
    return (places == token).astype(jnp.float32)


def turn(rows, tables, sign):
    half_rot = ROT // 2
    own, after, before = tables
    width = rows.shape[1]
    return (
        rows * own
        + sign * (pltpu.roll(rows, width - half_rot, 1) * after)
        + sign * (pltpu.roll(rows, half_rot, 1) * before)
    )


def head_lanes(rows, head):
    lane = lax.broadcasted_iota(jnp.int32, rows.shape, 1)
    return jnp.where(lane // HD == head, rows, jnp.zeros_like(rows))


def head_probs(queries, keys, allowed, head):
    scores = transposed_dot(keys, head_lanes(queries, head)) * HD ** (-0.5)
    scores = jnp.where(allowed, scores, -1e30)
    exponent = jnp.exp(scores - jnp.max(scores, axis=0, keepdims=True))
    return exponent / jnp.sum(exponent, axis=0, keepdims=True)


def line_allowed(places, span, tokens):
    keys = lax.broadcasted_iota(jnp.int32, (tokens, places.shape[1]), 0)
    in_query = (places >= span) & (places < span + PIC)
    in_key = (keys >= span) & (keys < span + PIC)
    return (keys <= places) | (in_query & in_key)


def forward_kernel(
    residual, places, scales, bias, own, after, before, weights, back,
    queries, keys, values, hidden, joined, picked_one, picked_two, picked_rows, used, branch,
):
    bf16 = jnp.bfloat16
    tokens = residual.shape[0]
    span = places[1:2, :]
    gain_one, shift_one = scales[0:1, :], scales[1:2, :]
    gain_two, shift_two = scales[2:3, :], scales[3:4, :]
    unit, _ = centred_rows(residual[...].astype(jnp.float32))
    low_one = (unit * gain_one + shift_one).astype(bf16)
    slots = places[0:1, :]
    pick = pick_matrix(slots, tokens)
    rows = first_dot(pick.astype(bf16), residual[...])
    picked_rows[...] = rows.astype(bf16)
    used[...] = first_dot(pick.astype(bf16), jnp.ones((tokens, used.shape[1]), bf16))
    unit, _ = centred_rows(rows)
    low_picked = (unit * gain_one + shift_one).astype(bf16)
    picked_one[...] = low_picked
    low_two = (unit * gain_two + shift_two).astype(bf16)
    picked_two[...] = low_two
    tables = (own[...], after[...], before[...])
    picked_tables = tuple(exact_dot(pick, table, ((0,), (0,))) for table in tables)
    two, three = 2 * HEAD_COLS, 3 * HEAD_COLS
    query = plain_dot(low_picked, weights[:, :HEAD_COLS]) + bias[:, :HEAD_COLS]
    query = turn(query, picked_tables, 1.0).astype(bf16)
    queries[...] = query
    key = plain_dot(low_one, weights[:, HEAD_COLS:two]) + bias[:, HEAD_COLS:two]
    key = turn(key, tables, 1.0).astype(bf16)
    keys[...] = key
    value = (plain_dot(low_one, weights[:, two:three]) + bias[:, two:three]).astype(bf16)
    values[...] = value
    allowed = line_allowed(slots, span, tokens)
    attended = None
    for head in range(GROUP_HEADS):
        probs = head_probs(query, key, allowed, head).astype(bf16)
        term = head_lanes(first_dot(probs, value), head)
        attended = term if attended is None else attended + term
    joined[:, :HEAD_COLS] = attended.astype(bf16)
    pre = plain_dot(low_two, weights[:, three:]) + bias[:, three:]
    hidden[...] = pre
    joined[:, HEAD_COLS:] = (0.5 * pre * (1.0 + lax.erf(pre * 0.5**0.5))).astype(bf16)
    branch[...] = plain_dot(joined[...], back[...])


def line_block(height, width):
    return pl.BlockSpec((height, width), lambda line: (line, 0))


def still(array):
    return pl.BlockSpec(array.shape, lambda line: (0,) * array.ndim)


def layer_forward(residual, places, scales, bias, tables, weights, back):
    lines = places.shape[0] // 8
    tokens, slots = residual.shape[0] // lines, places.shape[1]
    depth = residual.shape[1]
    bf16, f32 = jnp.bfloat16, jnp.float32
    outs = [
        (slots, HEAD_COLS, bf16),
        (tokens, HEAD_COLS, bf16),
        (tokens, HEAD_COLS, bf16),
        (slots, UNITS, f32),
        (slots, HEAD_COLS + UNITS, bf16),
        (slots, depth, bf16),
        (slots, depth, bf16),
        (slots, depth, bf16),
        (slots, 128, f32),
        (slots, depth, f32),
    ]
    return pl.pallas_call(
        forward_kernel,
        grid=(lines,),
        in_specs=[
            line_block(tokens, depth),
            line_block(8, slots),
            still(scales),
            still(bias),
            *[still(table) for table in tables],
            still(weights),
            still(back),
        ],
        out_specs=[line_block(height, width) for height, width, _ in outs],
        out_shape=[jax.ShapeDtypeStruct((lines * height, width), kind) for height, width, kind in outs],
        compiler_params=pltpu.CompilerParams(vmem_limit_bytes=VMEM_LIMIT),
    )(residual, places, scales, bias, *tables, weights, back)


def group_plan(
    token_ids,
    pic_start,
    comp_pos,
    comp_tgt,
    proj_in,
    proj_back,
    small_params,
    head_table,
    embed_table,
    first_in,
    second_in,
    first_back,
    second_back,
    first_small,
    second_small,
    first_head,
    second_head,
    first_embed,
    second_embed,
):
    bf16 = jnp.bfloat16
    rep_at = lax.axis_index("rep")
    shard_at = lax.axis_index("shard")
    micro, _, seq_dev = token_ids.shape
    slots = comp_pos.shape[2]
    seq_len = seq_dev * RG
    lines = micro * SG // RG
    blocks = lines * RG
    own_blocks = blocks // SG
    tokens = lines * seq_len
    slot_count = blocks * slots
    own_slots = own_blocks * slots
    vocab_dev = head_table.shape[1]
    vocab = embed_table.shape[1]
    quarter = D // SG // RG

    place_line = jnp.concatenate([comp_pos[:, 0, :].reshape(-1), comp_tgt[:, 0, :].reshape(-1)])
    span_line = jnp.concatenate([pic_start[:, 0], jnp.zeros((seq_dev - micro,), jnp.int32)])
    ints = jnp.concatenate(
        [token_ids[:, 0, :], place_line[None], span_line[None], jnp.zeros((4, seq_dev), jnp.int32)]
    )
    small_low = small_params.astype(bf16).astype(jnp.float32).reshape(-1, 128)
    small_rows = small_low.shape[0]
    smalls = jnp.pad(small_low, ((0, 16 - small_rows), (0, 0)))
    ints_all, places, marks, scales, own_bias, residual_low, in_all, back_all, head_low = share_entry(
        ints, smalls, proj_in, proj_back, embed_table, head_table.T, tokens, 1
    )
    own_in = in_all.reshape(D, OWN_COLS)
    own_back = back_all.reshape(5 * 128, D)

    tables = turn_tables(jnp.arange(seq_len).astype(jnp.float32))
    *kept, picked_rows, used, branch_parts = layer_forward(
        residual_low, places, scales, own_bias, tables, own_in, own_back
    )
    rows_all, facts_all, d_branch, after_pieces, vectors = loss_and_branch(
        branch_parts.reshape(SG, own_slots, D),
        picked_rows,
        scales,
        used,
        marks,
        head_low,
        3,
    )
    loss_sum = jnp.sum(facts_all[:, 1])
    count_sum = jnp.sum(facts_all[:, 2])
    d_after_feats = after_pieces.reshape(slot_count, D // SG)

    d_rows_all, in_own, back_own, small_sum, grad_head, head_squares = layer_backward(
        residual_low,
        places,
        scales,
        tables,
        own_in,
        own_back,
        kept,
        d_branch,
        d_after_feats,
        vectors,
        rows_all,
        facts_all,
        marks,
        head_low,
        8,
    )
    in_grads = lax.all_gather(in_own, "rep")
    back_grads = lax.all_gather(back_own, "rep")
    by_group = ints_all.reshape(RG, RG, SG // RG, 8, seq_dev)[:, :, :, :micro]
    ids_all = jnp.transpose(by_group, (1, 3, 2, 0, 4)).reshape(-1)
    grad_embed, embed_squares = embed_grads(ids_all, d_rows_all.reshape(RG * tokens, D // SG), vocab)

    norm_rows_out = global_norm(head_squares, embed_squares, small_sum, in_own, back_own, 10)
    norm_value, factor = norm_rows_out[0, 0], norm_rows_out[1, 0]
    next_in, moment_in, square_in, next_back, moment_back, square_back = update_layer(
        norm_rows_out, in_grads, back_grads, (proj_in, first_in, second_in), (proj_back, first_back, second_back)
    )
    grad_small = small_sum[:small_rows].reshape(-1)
    next_small, moment_small, square_small = adamw(
        small_params, grad_small * factor, first_small, second_small, RATE_SMALL
    )
    next_head, moment_head, square_head = adamw(
        head_table, grad_head.T * factor, first_head, second_head, RATE_HEAD
    )
    next_embed, moment_embed, square_embed = update_embed(
        norm_rows_out, grad_embed, (embed_table, first_embed, second_embed)
    )
    return (
        jnp.stack([loss_sum, count_sum]),
        norm_value.reshape(1),
        next_in,
        moment_in,
        square_in,
        next_back,
        moment_back,
        square_back,
        next_small,
        moment_small,
        square_small,
        next_head,
        moment_head,
        square_head,
        next_embed,
        moment_embed,
        square_embed,
    )


def select_plan(mesh):
    if mesh.shape["rep"] == RG and mesh.shape["shard"] == SG:
        return group_plan
    return any_mesh


def solution(mesh):
    placed = (
        P(None, "shard", "rep"),
        P(None, "shard"),
        P(None, "shard", "rep"),
        P(None, "shard", "rep"),
        P("shard", None),
        P("shard", None),
        P("shard"),
        P(None, "shard"),
        P("shard", None),
        P("shard", None),
        P("shard", None),
        P("shard", None),
        P("shard", None),
        P("shard"),
        P("shard"),
        P(None, "shard"),
        P(None, "shard"),
        P("shard", None),
        P("shard", None),
    )
    return jax.shard_map(
        select_plan(mesh),
        mesh=mesh,
        in_specs=placed,
        out_specs=(
            P(),
            P(),
            P("shard", None),
            P("shard", None),
            P("shard", None),
            P("shard", None),
            P("shard", None),
            P("shard", None),
            P("shard"),
            P("shard"),
            P("shard"),
            P(None, "shard"),
            P(None, "shard"),
            P(None, "shard"),
            P("shard", None),
            P("shard", None),
            P("shard", None),
        ),
        check_vma=False,
    )
```

```python
import functools

import jax
import jax.numpy as jnp
import numpy as np
from jax import lax
from jax.experimental import pallas as pl
from jax.experimental.pallas import tpu as pltpu
from jax.sharding import PartitionSpec as P

D = 1024
H = 16
HD = 64
ROT = 16
FF = 4096
PIC = 256
STEP = 10


NORM_EPS = 1e-05
CLIP_LEVEL = 1.0
BETA_FIRST = 0.9
BETA_SECOND = 0.95
ADAM_EPS = 1e-08
DECAY_RATE = 0.01
RATE_IN = 0.01
RATE_BACK = 0.05
RATE_SMALL = 0.3
RATE_HEAD = 0.01
RATE_EMBED = 0.3


def combined_all(part, axis, combine):
    gathered = jax.tree.map(lambda a: lax.all_gather(a, axis), part)

    def take(source):
        return jax.tree.map(lambda a: lax.dynamic_index_in_dim(a, source, 0, False), gathered)

    return lax.fori_loop(
        1, lax.axis_size(axis), lambda source, state: combine(state, take(source)), take(0)
    )


def norm_rows(values, gain_vec, shift_vec):
    centred = values - jnp.mean(values, axis=-1, keepdims=True)
    spread = jnp.mean(centred * centred, axis=-1, keepdims=True)
    return centred * lax.rsqrt(spread + NORM_EPS) * gain_vec + shift_vec


def rotate(head_rows, place_vec):
    half_rot = ROT // 2
    exponent = jnp.arange(half_rot).astype(jnp.float32) * (2.0 / ROT)
    angles = place_vec[:, None] * jnp.exp(-exponent * jnp.log(10000.0))
    cosine = jnp.cos(angles)[:, None, :]
    sine_part = jnp.sin(angles)[:, None, :]
    front_part = head_rows[..., :half_rot]
    back_part = head_rows[..., half_rot:ROT]
    return jnp.concatenate(
        [
            front_part * cosine - back_part * sine_part,
            back_part * cosine + front_part * sine_part,
            head_rows[..., ROT:],
        ],
        axis=-1,
    )


def split_small(gain_parts):
    marks = [0, D, 2 * D, 3 * D, 4 * D, 5 * D, 6 * D, 9 * D, 9 * D + FF, 10 * D + FF]
    return tuple((gain_parts[marks[number] : marks[number + 1]] for number in range(9)))


def gelu_exact(values):
    return jax.nn.gelu(values, approximate=False)


def combine_totals(earlier, later_part):
    highest = jnp.maximum(earlier[0], later_part[0])
    totals = earlier[1] * jnp.exp(earlier[0] - highest) + later_part[1] * jnp.exp(
        later_part[0] - highest
    )
    return (highest, totals, earlier[2] + later_part[2])


def allowed_mask(query_places, key_places, span_start):
    inside_query = (query_places >= span_start) & (query_places < span_start + PIC)
    inside_key = (key_places >= span_start) & (key_places < span_start + PIC)
    return (key_places[None, :] <= query_places[:, None]) | inside_query[:, None] & inside_key[
        None, :
    ]


def masked_scores(queries, keys_all, allowed):
    raw_scores = jnp.einsum(
        "qhd,khd->hqk", queries, keys_all, preferred_element_type=jnp.float32
    ) * HD ** (-0.5)
    return jnp.where(allowed[None], raw_scores, -1e30)


def adamw(weight, gradient, moment, square, rate_value):
    moment = BETA_FIRST * moment + (1.0 - BETA_FIRST) * gradient
    square = BETA_SECOND * square + (1.0 - BETA_SECOND) * gradient * gradient
    moment_hat = moment / (1.0 - BETA_FIRST**STEP)
    square_hat = square / (1.0 - BETA_SECOND**STEP)
    weight = weight - rate_value * (
        moment_hat / (jnp.sqrt(square_hat) + ADAM_EPS) + DECAY_RATE * weight
    )
    return (weight, moment, square)


def any_mesh(
    token_ids,
    pic_start,
    comp_pos,
    comp_tgt,
    proj_in,
    proj_back,
    small_params,
    head_table,
    embed_table,
    first_in,
    second_in,
    first_back,
    second_back,
    first_small,
    second_small,
    first_head,
    second_head,
    first_embed,
    second_embed,
):
    seq_dev = token_ids.shape[2]
    micro_count = token_ids.shape[0]
    vocab_dev = head_table.shape[1]
    rep_count = lax.axis_size("rep")
    seq_len = seq_dev * rep_count
    rep_at = lax.axis_index("rep")
    shard_at = lax.axis_index("shard")
    used_own = comp_pos[:, 0, :] < seq_dev
    marked = jnp.where(used_own, comp_tgt[:, 0, :], -1)
    ids_group, tgt_group = (
        lax.all_gather(token_ids[:, 0, :], "shard", axis=1, tiled=True),
        lax.all_gather(marked, "shard", axis=1, tiled=True),
    )
    in_low = proj_in.astype(jnp.bfloat16)
    back_low = proj_back.astype(jnp.bfloat16)
    small_low = small_params.astype(jnp.bfloat16)
    head_low = head_table.astype(jnp.bfloat16)
    table_low = embed_table.astype(jnp.bfloat16)
    own_places = rep_at * seq_dev + jnp.arange(seq_dev)
    key_places = jnp.arange(seq_len)
    own_float = own_places.astype(jnp.float32)
    vocab_ids = jnp.arange(vocab_dev)
    grad_in = jnp.zeros((D, 3 * D + FF), jnp.float32)
    grad_back = jnp.zeros((D + FF, D), jnp.float32)
    grad_small = jnp.zeros((10 * D + FF,), jnp.float32)
    grad_head = jnp.zeros(head_table.shape, jnp.float32)
    grad_embed = jnp.zeros(embed_table.shape, jnp.float32)
    loss_sum = jnp.zeros((), jnp.float32)
    count_sum = jnp.zeros((), jnp.float32)
    for micro_at in range(micro_count):
        wide_in, wide_back, wide_small = (
            lax.all_gather(in_low, "shard", axis=0, tiled=True),
            lax.all_gather(back_low, "shard", axis=0, tiled=True),
            lax.all_gather(small_low, "shard", axis=0, tiled=True),
        )
        (
            gain_one,
            shift_one,
            gain_two,
            shift_two,
            gain_last,
            shift_last,
            bias_qkv,
            bias_hidden,
            bias_out,
        ) = split_small(wide_small.astype(jnp.float32))
        columns = jnp.take(table_low, ids_group[micro_at], axis=1)
        arrived = lax.all_to_all(columns, "shard", split_axis=1, concat_axis=0, tiled=True)
        residual = arrived.T.astype(jnp.float32)
        normed_one = norm_rows(residual, gain_one, shift_one)
        normed_two = norm_rows(residual, gain_two, shift_two)
        low_one = normed_one.astype(jnp.bfloat16)
        low_two = normed_two.astype(jnp.bfloat16)
        projected = (
            jnp.dot(low_one, wide_in[:, : 3 * D], preferred_element_type=jnp.float32) + bias_qkv
        )
        queries = rotate(projected[:, :D].reshape(seq_dev, H, HD), own_float).astype(jnp.bfloat16)
        key_rows = (
            rotate(projected[:, D : 2 * D].reshape(seq_dev, H, HD), own_float)
            .astype(jnp.bfloat16)
            .reshape(seq_dev, D)
        )
        value_rows = projected[:, 2 * D :].astype(jnp.bfloat16)
        keys_all, values_all = (
            lax.all_gather(key_rows, "rep", axis=0, tiled=True),
            lax.all_gather(value_rows, "rep", axis=0, tiled=True),
        )
        keys_all = keys_all.reshape(seq_len, H, HD)
        values_all = values_all.reshape(seq_len, H, HD)
        allowed = allowed_mask(own_places, key_places, pic_start[micro_at, 0])
        scores = masked_scores(queries, keys_all, allowed)
        highest = jnp.max(scores, axis=-1, keepdims=True)
        exponent = jnp.exp(scores - highest)
        totals = jnp.sum(exponent, axis=-1, keepdims=True)
        logsum = highest + jnp.log(totals)
        attn_probs = (exponent / totals).astype(jnp.bfloat16)
        attended = (
            jnp.einsum("hqk,khd->qhd", attn_probs, values_all, preferred_element_type=jnp.float32)
            .reshape(seq_dev, D)
            .astype(jnp.bfloat16)
        )
        hidden_pre = (
            jnp.dot(low_two, wide_in[:, 3 * D :], preferred_element_type=jnp.float32) + bias_hidden
        )
        activation = gelu_exact(hidden_pre).astype(jnp.bfloat16)
        joined = jnp.concatenate([attended, activation], axis=1)
        after_add = (
            residual + jnp.dot(joined, wide_back, preferred_element_type=jnp.float32) + bias_out
        )
        final_rows = norm_rows(after_add, gain_last, shift_last)
        places = comp_pos[micro_at, 0]
        used_slots = (places < seq_dev).astype(jnp.float32)
        picked = (
            jnp.take(final_rows, jnp.minimum(places, seq_dev - 1), axis=0) * used_slots[:, None]
        ).astype(jnp.bfloat16)
        rows_all = lax.all_gather(picked, "shard", axis=0, tiled=True)
        logits = jnp.dot(rows_all, head_low, preferred_element_type=jnp.float32)
        targets = tgt_group[micro_at]
        matches = (targets - shard_at * vocab_dev)[:, None] == vocab_ids[None, :]
        row_top = jnp.max(logits, axis=1)
        row_total = jnp.sum(jnp.exp(logits - row_top[:, None]), axis=1)
        row_target = jnp.sum(jnp.where(matches, logits, 0.0), axis=1)
        row_top, row_total, row_target = combined_all(
            (row_top, row_total, row_target), "shard", combine_totals
        )
        logsum_rows = row_top + jnp.log(row_total)
        counted = (targets >= 0).astype(jnp.float32)
        loss_sum = loss_sum + jnp.sum((logsum_rows - row_target) * counted)
        count_sum = count_sum + jnp.sum(counted)
        d_logits = (
            (jnp.exp(logits - logsum_rows[:, None]) - matches.astype(jnp.float32))
            * counted[:, None]
        ).astype(jnp.bfloat16)
        grad_head = grad_head + jnp.einsum(
            "rd,rv->dv", rows_all, d_logits, preferred_element_type=jnp.float32
        )
        d_picked = lax.psum_scatter(
            jnp.einsum("rv,dv->rd", d_logits, head_low, preferred_element_type=jnp.float32),
            "shard",
            scatter_dimension=0,
            tiled=True,
        )
        d_final = jnp.zeros((seq_dev, D), jnp.float32).at[places].add(d_picked, mode="drop")
        back_in, back_back = (
            lax.all_gather(in_low, "shard", axis=0, tiled=True),
            lax.all_gather(back_low, "shard", axis=0, tiled=True),
        )
        _, pull_last = jax.vjp(norm_rows, after_add, gain_last, shift_last)
        d_after, d_gain_last, d_shift_last = pull_last(d_final)
        d_branch = d_after.astype(jnp.bfloat16)
        grad_back = grad_back + jnp.einsum(
            "sc,sd->cd", joined, d_branch, preferred_element_type=jnp.float32
        )
        d_joined = jnp.einsum("sd,cd->sc", d_branch, back_back, preferred_element_type=jnp.float32)
        d_attended = d_joined[:, :D].astype(jnp.bfloat16).reshape(seq_dev, H, HD)
        _, pull_gelu = jax.vjp(gelu_exact, hidden_pre)
        d_hidden = pull_gelu(d_joined[:, D:])[0].astype(jnp.bfloat16)
        probs_again = jnp.exp(masked_scores(queries, keys_all, allowed) - logsum)
        d_probs = jnp.einsum(
            "qhd,khd->hqk", d_attended, values_all, preferred_element_type=jnp.float32
        )
        d_scores = (
            probs_again * (d_probs - jnp.sum(probs_again * d_probs, axis=-1, keepdims=True))
        ).astype(jnp.bfloat16)
        d_queries = jnp.einsum(
            "hqk,khd->qhd", d_scores, keys_all, preferred_element_type=jnp.float32
        ) * HD ** (-0.5)
        low_probs = probs_again.astype(jnp.bfloat16)
        d_keys = jnp.einsum(
            "hqk,qhd->khd", d_scores, queries, preferred_element_type=jnp.float32
        ) * HD ** (-0.5)
        d_values = jnp.einsum(
            "hqk,qhd->khd", low_probs, d_attended, preferred_element_type=jnp.float32
        )
        key_grads = lax.psum_scatter(
            jnp.concatenate(
                [
                    d_keys.reshape(seq_dev * lax.axis_size("rep"), D),
                    d_values.reshape(seq_dev * lax.axis_size("rep"), D),
                ],
                axis=1,
            ),
            "rep",
            scatter_dimension=0,
            tiled=True,
        )
        d_key_rows = rotate(key_grads[:, :D].reshape(seq_dev, H, HD), -own_float).reshape(
            seq_dev, D
        )
        d_query_rows = rotate(d_queries, -own_float).reshape(seq_dev, D)
        d_projected = jnp.concatenate([d_query_rows, d_key_rows, key_grads[:, D:]], axis=1).astype(
            jnp.bfloat16
        )
        grad_in = grad_in + jnp.concatenate(
            [
                jnp.einsum("sd,sc->dc", low_one, d_projected, preferred_element_type=jnp.float32),
                jnp.einsum("sd,sc->dc", low_two, d_hidden, preferred_element_type=jnp.float32),
            ],
            axis=1,
        )
        d_normed_one = jnp.einsum(
            "sc,dc->sd", d_projected, back_in[:, : 3 * D], preferred_element_type=jnp.float32
        )
        d_normed_two = jnp.einsum(
            "sc,dc->sd", d_hidden, back_in[:, 3 * D :], preferred_element_type=jnp.float32
        )
        _, pull_one = jax.vjp(norm_rows, residual, gain_one, shift_one)
        d_resid_one, d_gain_one, d_shift_one = pull_one(d_normed_one)
        _, pull_two = jax.vjp(norm_rows, residual, gain_two, shift_two)
        d_resid_two, d_gain_two, d_shift_two = pull_two(d_normed_two)
        d_residual = (d_after + d_resid_one + d_resid_two).astype(jnp.bfloat16)
        returned = lax.all_to_all(d_residual.T, "shard", split_axis=0, concat_axis=1, tiled=True)
        grad_embed = grad_embed.at[:, ids_group[micro_at]].add(returned.astype(jnp.float32))
        grad_small = grad_small + jnp.concatenate(
            [
                d_gain_one,
                d_shift_one,
                d_gain_two,
                d_shift_two,
                d_gain_last,
                d_shift_last,
                jnp.sum(d_projected.astype(jnp.float32), axis=0),
                jnp.sum(d_hidden.astype(jnp.float32), axis=0),
                jnp.sum(d_branch.astype(jnp.float32), axis=0),
            ]
        )
    shard_in, shard_back, shard_small = (
        lax.psum_scatter(grad_in, "shard", scatter_dimension=0, tiled=True),
        lax.psum_scatter(grad_back, "shard", scatter_dimension=0, tiled=True),
        lax.psum_scatter(grad_small, "shard", scatter_dimension=0, tiled=True),
    )
    summed = lax.psum(
        (shard_in, shard_back, shard_small, grad_head, grad_embed, loss_sum, count_sum), "rep"
    )
    local_square = (
        jnp.sum(summed[0] * summed[0])
        + jnp.sum(summed[1] * summed[1])
        + jnp.sum(summed[2] * summed[2])
        + jnp.sum(summed[3] * summed[3])
        + jnp.sum(summed[4] * summed[4])
    )
    norm_value = jnp.sqrt(lax.psum(local_square, "shard"))
    factor = CLIP_LEVEL / jnp.maximum(norm_value, CLIP_LEVEL)
    next_in, moment_in, square_in = adamw(proj_in, summed[0] * factor, first_in, second_in, RATE_IN)
    next_back, moment_back, square_back = adamw(
        proj_back, summed[1] * factor, first_back, second_back, RATE_BACK
    )
    next_small, moment_small, square_small = adamw(
        small_params, summed[2] * factor, first_small, second_small, RATE_SMALL
    )
    next_head, moment_head, square_head = adamw(
        head_table, summed[3] * factor, first_head, second_head, RATE_HEAD
    )
    next_embed, moment_embed, square_embed = adamw(
        embed_table, summed[4] * factor, first_embed, second_embed, RATE_EMBED
    )
    return (
        jnp.stack([summed[5], summed[6]]),
        norm_value.reshape(1),
        next_in,
        moment_in,
        square_in,
        next_back,
        moment_back,
        square_back,
        next_small,
        moment_small,
        square_small,
        next_head,
        moment_head,
        square_head,
        next_embed,
        moment_embed,
        square_embed,
    )


MESH = pl.DeviceIdType.MESH
RG = 4
SG = 8


def whereabouts():
    rep = lax.axis_index("rep")
    shard = lax.axis_index("shard")
    core_twin = rep + 1 - 2 * lax.rem(rep, 2)
    x_twin = lax.rem(rep + 2, RG)
    y_twin = shard + 1 - 2 * lax.rem(shard, 2)
    return rep, shard, core_twin, x_twin, y_twin


def z_peer(shard, step):
    return lax.rem(shard + 2 * step, SG)


def shard_peer(shard, step):
    return lax.rem(shard + step, SG)


def greet(partners):
    barrier = pltpu.get_barrier_semaphore()
    for partner in partners:
        pl.semaphore_signal(barrier, inc=1, device_id=partner, device_id_type=MESH)
    pl.semaphore_wait(barrier, len(partners))


def remote(src, dst, send_sem, recv_sem, partner):
    return pltpu.make_async_remote_copy(
        src_ref=src,
        dst_ref=dst,
        send_sem=send_sem,
        recv_sem=recv_sem,
        device_id=partner,
        device_id_type=MESH,
    )


def comm_call(kernel, out_shape, scratch, number, args, spaces=None, out_spaces=None, limit=None, grid=()):
    pick = {
        "a": pl.BlockSpec(memory_space=pl.ANY),
        "v": pl.BlockSpec(memory_space=pltpu.VMEM),
    }
    choose = lambda space: pick[space] if isinstance(space, str) else space
    spaces = spaces or "a" * len(args)
    out_spaces = out_spaces or "a" * len(out_shape)
    return pl.pallas_call(
        kernel,
        grid=grid,
        out_shape=out_shape,
        in_specs=[choose(space) for space in spaces],
        out_specs=[choose(space) for space in out_spaces],
        scratch_shapes=scratch,
        compiler_params=pltpu.CompilerParams(
            collective_id=number, has_side_effects=True, vmem_limit_bytes=limit
        ),
    )(*args)


def start_gather(source, out, slot, place, sems):
    send_z, recv_z, send_y, recv_y, own = sems
    rep, shard, _, _, y_twin = place
    keep = pltpu.make_async_copy(source, slot(out, shard), own)
    keep.start()
    first_y = remote(source, slot(out, shard), send_y.at[0], recv_y.at[0], (rep, y_twin))
    z_copies = [
        remote(source, slot(out, shard), send_z.at[step - 1], recv_z.at[step - 1], (rep, z_peer(shard, step)))
        for step in range(1, 4)
    ]
    for copy in z_copies:
        copy.start()
    first_y.start()
    return keep, first_y, z_copies


def finish_gather(started, out, slot, place, sems):
    send_z, recv_z, send_y, recv_y, own = sems
    rep, shard, _, _, y_twin = place
    keep, first_y, z_copies = started
    passed = []
    for step in range(1, 4):
        z_copies[step - 1].wait_recv()
        came_from = z_peer(shard, SG // 2 - step)
        passed.append(
            remote(slot(out, came_from), slot(out, came_from), send_y.at[step], recv_y.at[step], (rep, y_twin))
        )
        passed[-1].start()
    keep.wait()
    for copy in z_copies:
        copy.wait_send()
    first_y.wait()
    for copy in passed:
        copy.wait()


def gather_partners(place):
    rep, shard, _, _, y_twin = place
    return [(rep, z_peer(shard, step)) for step in range(1, 4)] + [(rep, y_twin)]


GATHER_SEMS = [pltpu.SemaphoreType.DMA((3,)), pltpu.SemaphoreType.DMA((3,)), pltpu.SemaphoreType.DMA((4,)), pltpu.SemaphoreType.DMA((4,)), pltpu.SemaphoreType.DMA]


def row_slot(out, index):
    height = out.shape[0] // SG
    return out.at[pl.ds(pl.multiple_of(index * height, height), height)]


def tile_user(tile):
    return jnp.where(tile < SG, tile, (tile - SG) // 4)


def tile_slot(tile):
    return jnp.where(tile < SG, 0, 1 + lax.rem(tile - SG + SG, 4))


def entry_kernel(
    table_steps, head_rows, token_ids, comp_pos, comp_tgt, pic_start, small_params, weights_in, weights_back, table, head,
    ints_out, places, marks, scales, bias, out, in_all, back_all, head_low,
    ints, smalls, ints_all, smalls_all, in_parts, back_tiles, turned, wide, low, ids,
    send_int, recv_int, send_small, recv_small, send_rep, recv_rep,
    send_in, recv_in, send_back, recv_back, send_far, recv_far, send_pair, recv_pair,
    send_up, recv_up, send_down, recv_down, send_y, recv_y, own,
):
    at = pl.program_id(0)
    last = pl.num_programs(0) - 1
    rep, shard, core_twin, x_twin, y_twin = whereabouts()
    level, side = shard // 2, lax.rem(shard, 2)
    shard_peers = [(rep, shard_peer(shard, step)) for step in range(1, SG)]
    rep_peers = [(lax.rem(rep + step, RG), shard) for step in range(1, RG)]
    lines, tokens, feats = low.shape
    small_rows = 14

    def int_copies():
        return [
            remote(ints, ints_all.at[rep, shard], send_int.at[k], recv_int.at[k], peer)
            for k, peer in enumerate(shard_peers)
        ]

    def small_copies():
        return [
            remote(smalls, smalls_all.at[shard], send_small.at[k], recv_small.at[k], peer)
            for k, peer in enumerate(shard_peers)
        ]

    def rep_copies():
        return [
            remote(ints_all.at[rep], ints_all.at[rep], send_rep.at[k], recv_rep.at[k], peer)
            for k, peer in enumerate(rep_peers)
        ]

    def in_copies():
        return [
            remote(in_parts.at[peer[1], rep], in_all.at[shard, rep], send_in.at[k], recv_in.at[k], peer)
            for k, peer in enumerate(shard_peers)
        ]

    def own_in():
        return pltpu.make_async_copy(in_parts.at[shard, rep], in_all.at[shard, rep], own.at[0])

    def back_move(k):
        tile = 5 * shard + k
        user, slot = tile_user(tile), tile_slot(tile)
        there = remote(
            back_tiles.at[k, rep], back_all.at[slot, rep], send_back.at[k], recv_back.at[slot], (rep, user)
        )
        return user, slot, there

    def quarter_copies(quarter, sends, recvs, base, peer):
        return [
            remote(array.at[:, quarter], array.at[:, quarter], sends.at[base + k], recvs.at[base + k], (peer, shard))
            for k, array in enumerate((in_all, back_all))
        ]

    def far_copies():
        return quarter_copies(rep, send_far, recv_far, 0, x_twin)

    def pair_copies():
        return quarter_copies(rep, send_pair, recv_pair, 0, core_twin) + quarter_copies(
            x_twin, send_pair, recv_pair, 2, core_twin
        )

    def slot(line, z_at, y_at):
        index = 2 * z_at + y_at
        return out.at[pl.ds(line * tokens, tokens), pl.ds(pl.multiple_of(index * feats, feats), feats)]

    def up_copy(line, hop):
        here = slot(line, level - hop, side)
        source = low.at[line] if hop == 0 else here
        return remote(source, here, send_up.at[line, hop], recv_up.at[line, hop], (rep, shard + 2))

    def down_copy(line, hop):
        here = slot(line, level + hop, side)
        source = low.at[line] if hop == 0 else here
        return remote(source, here, send_down.at[line, hop], recv_down.at[line, hop], (rep, shard - 2))

    def side_copy(line, z_at, source=None):
        here = slot(line, z_at, side)
        return remote(
            here if source is None else source, here, send_y.at[line, z_at], recv_y.at[line, z_at], (rep, y_twin)
        )

    def keep_copy(line):
        return pltpu.make_async_copy(low.at[line], slot(line, level, side), own.at[2 + line])

    def pass_on(line, hop):
        @pl.when(level >= hop)
        def _():
            pltpu.make_async_copy(low.at[line], slot(line, level - hop, side), recv_up.at[line, hop - 1]).wait()
            if hop < 3:
                pl.when(level < 3)(lambda: up_copy(line, hop).start())
            side_copy(line, level - hop).start()

        @pl.when(level + hop <= 3)
        def _():
            pltpu.make_async_copy(low.at[line], slot(line, level + hop, side), recv_down.at[line, hop - 1]).wait()
            if hop < 3:
                pl.when(level > 0)(lambda: down_copy(line, hop).start())
            side_copy(line, level + hop).start()

    @pl.when(at == 0)
    def _():
        ints[...] = jnp.zeros_like(ints)
        smalls[...] = jnp.zeros_like(smalls)
        smalls[:small_rows, :] = small_params[...].astype(jnp.bfloat16).astype(jnp.float32)
        places_wide = comp_pos.shape[2]
        for micro in range(2):
            ints[micro : micro + 1, :] = token_ids[micro]
            ints[2:3, places_wide * micro : places_wide * (micro + 1)] = comp_pos[micro]
            ints[2:3, places_wide * (2 + micro) : places_wide * (3 + micro)] = comp_tgt[micro]
            ints[3:4, micro : micro + 1] = pic_start[micro : micro + 1, :]
        greet(shard_peers + rep_peers)
        for copy in int_copies() + small_copies():
            copy.start()
        for target in range(SG):
            for part in range(3):
                columns = weights_in[:, part * D + target * HEAD_COLS : part * D + (target + 1) * HEAD_COLS]
                in_parts[target, :, :, part * HEAD_COLS : (part + 1) * HEAD_COLS] = columns.astype(
                    in_parts.dtype
                ).reshape(RG, in_parts.shape[2], HEAD_COLS)
            columns = weights_in[:, 3 * D + target * UNITS : 3 * D + (target + 1) * UNITS]
            in_parts[target, :, :, 3 * HEAD_COLS :] = columns.astype(in_parts.dtype).reshape(
                RG, in_parts.shape[2], UNITS
            )
        back_tiles[...] = weights_back[...].astype(back_tiles.dtype).reshape(back_tiles.shape)
        for copy in in_copies():
            copy.start()
        own_in().start()
        for k in range(5):
            user, slot_at, there = back_move(k)
            here = pltpu.make_async_copy(back_tiles.at[k, rep], back_all.at[slot_at, rep], recv_back.at[slot_at])
            pl.when(user == shard)(here.start)
            pl.when(user != shard)(there.start)
        ints_all[rep, shard] = ints[...]
        smalls_all[shard] = smalls[...]

    @pl.when(at < table_steps)
    def _():
        block = table[...].astype(jnp.bfloat16).astype(jnp.float32)
        width = block.shape[1]
        turned[pl.ds(pl.multiple_of(at * width, width), width), :] = block.T

    @pl.when(at == 5)
    def _():
        for copy in int_copies():
            copy.wait()
        for copy in rep_copies():
            copy.start()

    @pl.when(at == table_steps)
    def _():
        for copy in rep_copies():
            copy.wait()
        to_scalars = pltpu.make_async_copy(ints_all.at[:, pl.ds(2 * rep, 2)], ids, own.at[1])
        to_scalars.start()
        to_scalars.wait()
        for line in range(lines):
            micro, member = line // 2, line % 2
            for block_at in range(RG):

                @pl.loop(0, 16)
                def _(group):
                    for k in range(8):
                        lane = group * 8 + k
                        wide[pl.ds(block_at * 128 + lane, 1), :] = turned[
                            pl.ds(ids[block_at, member, micro, lane], 1), :
                        ]

            low[line] = wide[...].astype(jnp.bfloat16)
            pl.when(level < 3)(lambda: up_copy(line, 0).start())
            pl.when(level > 0)(lambda: down_copy(line, 0).start())
            side_copy(line, level, low.at[line]).start()
            keep_copy(line).start()
        own_in().wait()
        for copy in in_copies():
            copy.wait()
        for k in range(5):
            pltpu.make_async_copy(back_tiles.at[0, rep], back_all.at[k, rep], recv_back.at[k]).wait()
        for copy in far_copies():
            copy.start()

    @pl.when(at >= table_steps)
    def _():
        head_low[...] = head[...].astype(jnp.bfloat16)

    order = sorted(((line, hop) for line in range(lines) for hop in range(1, 4)), key=lambda item: (sum(item), item[1]))
    for step, (line, hop) in enumerate(order):
        pl.when(at == table_steps + 1 + step)(functools.partial(pass_on, line, hop))

    @pl.when(at == last - 2)
    def _():
        for copy in far_copies():
            copy.wait()
        for copy in pair_copies():
            copy.start()

    @pl.when(at == last)
    def _():
        for copy in small_copies():
            copy.wait()
        ints_out[...] = ints_all[...]

        seq_dev, slots = ints.shape[1], ints.shape[1] // 4
        for group in range(RG):
            for line in range(lines):
                micro, member = line // 2, line % 2
                for block_at in range(RG):
                    facts = ints_all[block_at, 2 * group + member, 2:3, :]
                    where = facts[:, slots * micro : slots * (micro + 1)]
                    goal = facts[:, slots * (2 + micro) : slots * (3 + micro)]
                    some = where < seq_dev
                    start = (line * RG + block_at) * slots
                    marks[group, 0:1, start : start + slots] = jnp.where(some, goal - shard * head_rows, -1)
                    marks[group, 1:2, start : start + slots] = some.astype(jnp.int32)
        for line in range(lines):
            micro, member = line // 2, line % 2
            for block_at in range(RG):
                where = ints_all[block_at, 2 * rep + member, 2:3, slots * micro : slots * (micro + 1)]
                places[8 * line : 8 * line + 1, block_at * slots : (block_at + 1) * slots] = jnp.where(
                    where < seq_dev, where + block_at * seq_dev, -1
                )
            span = ints_all[0, 2 * rep + member, 3:4, micro : micro + 1]
            places[8 * line + 1 : 8 * line + 2, :] = jnp.broadcast_to(span, (1, places.shape[1]))

        def small_row(row):
            return smalls_all[row // small_rows, pl.ds(lax.rem(row, small_rows), 1), :]

        scales[...] = jnp.zeros_like(scales)
        for vector, start in enumerate([8 * k for k in range(6)] + [8 * 13]):
            for part in range(8):
                row = start + part
                scales[vector : vector + 1, part * 128 : (part + 1) * 128] = smalls_all[
                    row // small_rows, row % small_rows : row % small_rows + 1, :
                ]
        for part in range(3):
            bias[:, part * 128 : (part + 1) * 128] = small_row(48 + 8 * part + shard)
        for part in range(4):
            bias[:, (3 + part) * 128 : (4 + part) * 128] = small_row(72 + 4 * shard + part)
        for k in range(5):
            user, _, there = back_move(k)
            pl.when(user != shard)(there.wait_send)
        for line in range(lines):
            keep_copy(line).wait()
            for hop in range(3):
                pl.when((level >= hop) & (level < 3))(lambda: up_copy(line, hop).wait_send())
                pl.when((level + hop <= 3) & (level > 0))(lambda: down_copy(line, hop).wait_send())
            for z_at in range(4):
                side_copy(line, z_at).wait()
        for copy in pair_copies():
            copy.wait()


def share_entry(token_ids, comp_pos, comp_tgt, pic_start, small_params, weights_in, weights_back, table, head, tokens, number):
    quarter = weights_in.shape[0] // RG
    ints = jax.ShapeDtypeStruct((8, token_ids.shape[2]), jnp.int32)
    smalls = jax.ShapeDtypeStruct((16, 128), jnp.float32)
    in_shape = (SG, RG, quarter, OWN_COLS)
    back_shape = (5, RG, 32, weights_back.shape[1])
    dma = pltpu.SemaphoreType.DMA
    feats, vocab = table.shape
    blocks = pl.cdiv(vocab, TABLE_BLOCK)
    head_blocks = max(pl.cdiv(head.shape[0], CAST_BLOCK), 13)
    lines = 4
    per_line = tokens // lines
    head_spec = pl.BlockSpec(
        (CAST_BLOCK, head.shape[1]),
        lambda at: (jnp.clip(at - blocks, 0, pl.cdiv(head.shape[0], CAST_BLOCK) - 1), 0),
    )
    return comm_call(
        functools.partial(entry_kernel, blocks, head.shape[0]),
        [
            jax.ShapeDtypeStruct((RG, SG) + ints.shape, ints.dtype),
            jax.ShapeDtypeStruct((8 * lines, ints.shape[1]), ints.dtype),
            jax.ShapeDtypeStruct((RG, 8, ints.shape[1] * lines), ints.dtype),
            jax.ShapeDtypeStruct((8, SG * feats), jnp.float32),
            jax.ShapeDtypeStruct((1, OWN_COLS), jnp.float32),
            jax.ShapeDtypeStruct((tokens, SG * feats), jnp.bfloat16),
            jax.ShapeDtypeStruct(in_shape, jnp.bfloat16),
            jax.ShapeDtypeStruct(back_shape, jnp.bfloat16),
            jax.ShapeDtypeStruct(head.shape, jnp.bfloat16),
        ],
        [
            pltpu.VMEM(ints.shape, ints.dtype),
            pltpu.VMEM(smalls.shape, smalls.dtype),
            pltpu.VMEM((RG, SG) + ints.shape, ints.dtype),
            pltpu.VMEM((SG,) + smalls.shape, smalls.dtype),
            pltpu.VMEM(in_shape, jnp.bfloat16),
            pltpu.VMEM(back_shape, jnp.bfloat16),
            pltpu.VMEM((blocks * TABLE_BLOCK, feats), jnp.float32),
            pltpu.VMEM((per_line, feats), jnp.float32),
            pltpu.VMEM((lines, per_line, feats), jnp.bfloat16),
            pltpu.SMEM((RG, 2) + ints.shape, jnp.int32),
        ]
        + [dma((SG - 1,))] * 4
        + [dma((RG - 1,))] * 2
        + [dma((SG - 1,))] * 2
        + [dma((5,))] * 2
        + [dma((2,))] * 2
        + [dma((4,))] * 2
        + [dma((lines, 3))] * 4
        + [dma((lines, 4))] * 2
        + [dma((2 + lines,))],
        number,
        (token_ids, comp_pos, comp_tgt, pic_start, small_params, weights_in, weights_back, table, head),
        ["v"] * 7 + [pl.BlockSpec((feats, TABLE_BLOCK), lambda at: (0, jnp.minimum(at, blocks - 1))), head_spec],
        ["v"] * 5 + ["a", "a", "a", head_spec],
        VMEM_LIMIT,
        (blocks + head_blocks,),
    )


def loss_kernel(
    vocab, parts, picked_rows, scales, used, marks, head,
    rows_all, facts_out, branch, features_out, vectors, loss_parts,
    rows, turned, low, after, branch_y, branch_sum, branch_z, picked_y, picked_sum, picked_z, picked,
    send_codes, stats, stats_all, facts, facts_all, features, pieces, low_branch, top, total, target,
    branch_send_y, branch_recv_y, branch_send_z, branch_recv_z,
    picked_send_y, picked_recv_y, picked_send_z, picked_recv_z,
    row_z_send, row_z_recv, row_y_send, row_y_recv, row_own,
    back_z_send, back_z_recv, back_y_send, back_y_recv, back_own,
    send_stat, recv_stat, send_row, recv_row, send_fact, recv_fact, send_feat, recv_feat, own,
):
    at = pl.program_id(0)
    blocks = pl.num_programs(0) // 2
    place = whereabouts()
    rep, shard, core_twin, x_twin, y_twin = place
    shard_peers = [(rep, shard_peer(shard, step)) for step in range(1, SG)]
    rep_peers = [(lax.rem(rep + step, RG), shard) for step in range(1, RG)]
    slots = after.shape[0]
    own_rows = pl.ds(pl.multiple_of(shard * slots, slots), slots)

    def shard_total(values, from_y, own_sum, from_z, send_y, recv_y, send_z, recv_z):
        y_copies = {}
        for step in (2, 1, 3, 0):
            send_codes[step] = row_codes(values[z_peer(y_twin, step)])
            y_copies[step] = remote(
                send_codes.at[step], from_y.at[step], send_y.at[step], recv_y.at[step], (rep, y_twin)
            )
            y_copies[step].start()
        z_copies = []
        for step in (2, 1, 3):
            y_copies[step].wait_recv()
            own_sum[step] = row_codes(values[z_peer(shard, step)] + row_values(from_y[step]))
            z_copies.append(
                remote(
                    own_sum.at[step], from_z.at[step - 1], send_z.at[step - 1], recv_z.at[step - 1],
                    (rep, z_peer(shard, step)),
                )
            )
            z_copies[-1].start()
        y_copies[0].wait_recv()
        result = values[shard] + row_values(from_y[0])
        for copy in z_copies:
            copy.wait()
        for step in range(4):
            y_copies[step].wait_send()
        return result + row_values(from_z[0]) + row_values(from_z[1]) + row_values(from_z[2])

    row_sems = (row_z_send, row_z_recv, row_y_send, row_y_recv, row_own)
    back_sems = (back_z_send, back_z_recv, back_y_send, back_y_recv, back_own)

    def stat_copies():
        return [
            remote(stats, stats_all.at[shard], send_stat.at[k], recv_stat.at[k], peer)
            for k, peer in enumerate(shard_peers)
        ]

    def row_copy(k, peer):
        return remote(rows, rows_all.at[rep], send_row.at[k], recv_row.at[k], (peer, shard))

    def passed_copy():
        return remote(rows_all.at[x_twin], rows_all.at[x_twin], send_row.at[2], recv_row.at[2], (core_twin, shard))

    def keep_rows():
        return pltpu.make_async_copy(rows, rows_all.at[rep], own)

    def fact_copies():
        return [
            remote(facts, facts_all.at[rep], send_fact.at[k], recv_fact.at[k], peer) for k, peer in enumerate(rep_peers)
        ]

    @pl.when(at == 0)
    def _():
        greet(shard_peers + rep_peers)
        sum_buffers = (branch_y, branch_sum, branch_z)
        whole = shard_total(parts, *sum_buffers, branch_send_y, branch_recv_y, branch_send_z, branch_recv_z)
        after[...] = picked_rows[own_rows, :].astype(jnp.float32) + whole + scales[6:7, :]
        unit, _ = centred_rows(after[...])
        final = unit * scales[4:5, :] + scales[5:6, :]
        low[...] = (final * used[own_rows, 0:1]).astype(low.dtype)
        started = start_gather(low, rows, row_slot, place, row_sems)
        finish_gather(started, rows, row_slot, place, row_sems)
        row_copy(0, x_twin).start()
        row_copy(1, core_twin).start()
        keep_rows().start()
        turned[...] = rows[...].T
        top[...] = jnp.full_like(top, -1e30)
        total[...] = jnp.zeros_like(total)
        target[...] = jnp.zeros_like(target)
        picked[...] = jnp.zeros_like(picked)

    full, tail = divmod(vocab, ROW_BLOCK)

    def each_block(start, body):
        pl.when((at >= start) & (at < start + full))(lambda: body(ROW_BLOCK))
        if tail > 0:
            pl.when(at == start + full)(lambda: body(tail))

    def top_block(size):
        logits = plain_dot(head[:size], turned[...])
        hits = lax.broadcasted_iota(jnp.int32, logits.shape, 0) == marks[rep, 0:1, :] - at * ROW_BLOCK
        target[...] += jnp.sum(jnp.where(hits, logits, 0.0), axis=0, keepdims=True)
        highest = jnp.maximum(top[...], jnp.max(logits, axis=0, keepdims=True))
        weights = jnp.sum(jnp.exp(logits - highest), axis=0, keepdims=True)
        total[...] = total[...] * jnp.exp(top[...] - highest) + weights
        top[...] = highest

    each_block(0, top_block)

    @pl.when(at == blocks - 1)
    def _():
        stats[...] = jnp.zeros_like(stats)
        stats[0:1, :] = top[...]
        stats[1:2, :] = total[...]
        stats[2:3, :] = target[...]
        for copy in stat_copies():
            copy.start()
        stats_all[shard] = stats[...]
        for copy in stat_copies():
            copy.wait()
        highest = stats_all[0, 0:1, :]
        for k in range(1, SG):
            highest = jnp.maximum(highest, stats_all[k, 0:1, :])
        weights = row_target = jnp.zeros_like(highest)
        for k in range(SG):
            weights = weights + stats_all[k, 1:2, :] * jnp.exp(stats_all[k, 0:1, :] - highest)
            row_target = row_target + stats_all[k, 2:3, :]
        logsum = highest + jnp.log(weights)
        some = marks[rep, 1:2, :] > 0
        facts[...] = jnp.zeros_like(facts)
        facts[0:1, :] = jnp.where(some, logsum, 1e30)
        facts[1:2, :] = jnp.where(some, logsum - row_target, 0.0)
        facts[2:3, :] = some.astype(jnp.float32)
        for copy in fact_copies():
            copy.start()
        facts_all[rep] = facts[...]
        row_copy(0, x_twin).wait_recv()
        passed_copy().start()

    def grad_block(size):
        block = head[:size]
        grads = logit_grads(block, turned[...], facts[0:1, :], marks[rep, 0:1, :] - (at - blocks) * ROW_BLOCK, plain_dot)
        picked[...] += first_dot(grads, block).reshape(picked.shape)

    each_block(blocks, grad_block)

    @pl.when(at == pl.num_programs(0) - 1)
    def _():
        sum_buffers = (picked_y, picked_sum, picked_z)
        d_final = shard_total(picked, *sum_buffers, picked_send_y, picked_recv_y, picked_send_z, picked_recv_z)
        unit, unit_scale = centred_rows(after[...])
        d_unit = d_final * scales[4:5, :]
        mean = jnp.mean(d_unit, axis=-1, keepdims=True)
        slope = jnp.mean(d_unit * unit, axis=-1, keepdims=True)
        d_after = (d_unit - mean - unit * slope) * unit_scale
        low_branch[...] = d_after.astype(low_branch.dtype)
        started = start_gather(low_branch, branch, row_slot, place, back_sems)
        width = pieces.shape[2]
        for k in range(SG):
            pieces[k] = d_after[:, k * width : (k + 1) * width]
        copies = [
            remote(pieces.at[peer[1]], features.at[shard], send_feat.at[k], recv_feat.at[k], peer)
            for k, peer in enumerate(shard_peers)
        ]
        for copy in copies:
            copy.start()
        features[shard] = pieces[shard]
        vectors[...] = jnp.zeros_like(vectors)
        vectors[0:1, :] = jnp.sum(d_final * unit, axis=0, keepdims=True)
        vectors[1:2, :] = jnp.sum(d_final, axis=0, keepdims=True)
        vectors[2:3, :] = jnp.sum(low_branch[...].astype(jnp.float32), axis=0, keepdims=True)
        finish_gather(started, branch, row_slot, place, back_sems)
        for copy in copies + fact_copies():
            copy.wait()
        facts_out[...] = facts_all[...]
        lane = lax.broadcasted_iota(jnp.int32, loss_parts.shape, 1)
        sums = facts_all[0] + facts_all[1] + facts_all[2] + facts_all[3]
        losses = jnp.sum(sums[1:2, :], axis=1, keepdims=True)
        loss_parts[...] = jnp.where(lane == 0, losses, jnp.sum(sums[2:3, :], axis=1, keepdims=True))
        features_out[...] = features[...]
        row_copy(0, x_twin).wait_send()
        row_copy(1, core_twin).wait()
        passed_copy().wait()
        keep_rows().wait()


def loss_and_branch(parts, picked_rows, scales, used, marks, head, number):
    dma = pltpu.SemaphoreType.DMA
    f32, bf16 = jnp.float32, jnp.bfloat16
    _, slots, depth = parts.shape
    vocab = head.shape[0]
    count = SG * slots
    blocks = pl.cdiv(vocab, ROW_BLOCK)
    vmem = lambda *shape: pltpu.VMEM(shape, f32)
    return comm_call(
        functools.partial(loss_kernel, vocab),
        [
            jax.ShapeDtypeStruct((RG, count, depth), bf16),
            jax.ShapeDtypeStruct((RG, 8, count), f32),
            jax.ShapeDtypeStruct((count, depth), bf16),
            jax.ShapeDtypeStruct((SG, slots, depth // SG), f32),
            jax.ShapeDtypeStruct((8, depth), f32),
            jax.ShapeDtypeStruct((8, 128), f32),
        ],
        [
            pltpu.VMEM((count, depth), bf16),
            pltpu.VMEM((depth, count), bf16),
            pltpu.VMEM((slots, depth), bf16),
            vmem(slots, depth),
        ]
        + [pltpu.VMEM((rounds, slots, depth + 128), jnp.int16) for rounds in (4, 4, 3, 4, 4, 3)]
        + [vmem(SG, slots, depth), pltpu.VMEM((4, slots, depth + 128), jnp.int16)]
        + [vmem(8, count), vmem(SG, 8, count), vmem(8, count), vmem(RG, 8, count)]
        + [vmem(SG, slots, depth // SG)] * 2
        + [pltpu.VMEM((slots, depth), bf16)]
        + [vmem(1, count)] * 3
        + [dma((4,)), dma((4,)), dma((3,)), dma((3,))] * 2
        + GATHER_SEMS * 2
        + [dma((SG - 1,))] * 2
        + [dma((3,))] * 4
        + [dma((SG - 1,))] * 2
        + [dma],
        number,
        (parts, picked_rows, scales, used, marks, head),
        ["v"] * 5 + [pl.BlockSpec((ROW_BLOCK, depth), lambda at: (lax.rem(at, blocks), 0))],
        ["a", "v", "a", "v", "v", "v"],
        VMEM_LIMIT,
        (2 * blocks,),
    )


def coded(rows, steps):
    inverse = jnp.where(steps > 0.0, 1.0 / steps, 0.0)
    return jnp.clip(jnp.round(rows * inverse), -32767.0, 32767.0).astype(jnp.int32).astype(jnp.int16)


def row_codes(rows):
    largest = jnp.maximum(jnp.max(jnp.abs(rows), axis=-1, keepdims=True), 1e-30)
    power = jnp.ceil(jnp.log(largest) * (1.0 / LOG_TWO) - 14.99)
    codes = coded(rows, jnp.exp(power * LOG_TWO))
    tail = jnp.broadcast_to(power, (rows.shape[0], 128)).astype(jnp.int32).astype(jnp.int16)
    return jnp.concatenate([codes, tail], axis=1)


def row_values(codes):
    depth = codes.shape[1] - 128
    power = codes[:, depth : depth + 1].astype(jnp.int32).astype(jnp.float32)
    return codes[:, :depth].astype(jnp.int32).astype(jnp.float32) * jnp.exp(power * LOG_TWO)


def backward_line(
    residual, places, scales, own, after, before, weights, back,
    queries, keys, values, hidden, joined, picked_one, picked_two, d_branch, d_after,
    parts, stats, base, own_unit, grad_in, grad_back, grad_scales, grad_bias, line,
):
    bf16 = jnp.bfloat16
    shard = lax.axis_index("shard")
    tokens = residual.shape[0]
    here = pl.ds(pl.multiple_of(line * tokens, tokens), tokens)
    feats = own_unit.shape[1]
    span = places[1:2, :]
    gain_one, shift_one = scales[0:1, :], scales[1:2, :]
    gain_two = scales[2:3, :]
    slots = places[0:1, :]
    pick = pick_matrix(slots, tokens)
    base[here, :] = exact_dot(pick, d_after[...], ((1,), (0,)))
    tables = (own[...], after[...], before[...])
    picked_tables = tuple(exact_dot(pick, table, ((0,), (0,))) for table in tables)
    pick = pick.astype(bf16)
    d_rows = d_branch[...]
    d_joined = transposed_dot(d_rows, back[...])
    grad_back[...] += first_dot(joined[...], d_rows).reshape(grad_back.shape)
    d_attended = d_joined[:, :HEAD_COLS].astype(bf16)
    pre = hidden[...]
    slope = 0.5 * (1.0 + lax.erf(pre * 0.5**0.5)) + pre * jnp.exp(-0.5 * pre * pre) * (2.0 * 3.141592653589793) ** -0.5
    d_hidden = (d_joined[:, HEAD_COLS:] * slope).astype(bf16)
    allowed = line_allowed(slots, span, tokens)
    query, key, value = queries[...], keys[...], values[...]
    d_query = d_key = d_value = None
    for head in range(GROUP_HEADS):
        probs = head_probs(query, key, allowed, head)
        d_head = head_lanes(d_attended, head)
        d_probs = transposed_dot(value, d_head)
        d_scores = (probs * (d_probs - jnp.sum(probs * d_probs, axis=0, keepdims=True))).astype(bf16)
        terms = (
            head_lanes(first_dot(d_scores, key), head),
            plain_dot(d_scores, head_lanes(query, head)),
            plain_dot(probs.astype(bf16), d_head),
        )
        if d_query is None:
            d_query, d_key, d_value = terms
        else:
            d_query, d_key, d_value = d_query + terms[0], d_key + terms[1], d_value + terms[2]
    d_query = turn(d_query * HD ** (-0.5), picked_tables, -1.0).astype(bf16)
    d_key = turn(d_key * HD ** (-0.5), tables, -1.0).astype(bf16)
    d_both = jnp.concatenate([d_key, d_value.astype(bf16)], axis=1)
    wide = residual[...].astype(jnp.float32)
    row_mean = jnp.mean(wide, axis=-1, keepdims=True)
    unit, unit_scale = centred_rows(wide)
    own_lanes = residual[:, pl.ds(pl.multiple_of(shard * feats, feats), feats)].astype(jnp.float32)
    own_unit[here, :] = (own_lanes - row_mean) * unit_scale
    low_one = (unit * gain_one + shift_one).astype(bf16)
    three = 3 * HEAD_COLS

    def add_in(first, width, term):
        grad_in[:, :, :, first : first + width] += term.reshape(grad_in.shape[:3] + (width,))

    add_in(0, HEAD_COLS, first_dot(picked_one[...], d_query))
    add_in(HEAD_COLS, 2 * HEAD_COLS, first_dot(low_one, d_both))
    add_in(three, UNITS, first_dot(picked_two[...], d_hidden))

    def column_sum(rows):
        return jnp.sum(rows.astype(jnp.float32), axis=0, keepdims=True)

    grad_bias[0:1, :HEAD_COLS] += column_sum(d_query)
    grad_bias[0:1, HEAD_COLS:three] += column_sum(d_both)
    grad_bias[0:1, three:] += column_sum(d_hidden)
    d_projected = jnp.concatenate([plain_dot(pick, d_query).astype(bf16), d_both], axis=1)
    d_normed = transposed_dot(d_projected, weights[:, :three])
    d_unit = d_normed * gain_one
    grad_scales[0:1, :] += column_sum(d_normed * unit)
    grad_scales[1:2, :] += column_sum(d_normed)
    d_normed = transposed_dot(plain_dot(pick, d_hidden).astype(bf16), weights[:, three:])
    grad_scales[2:3, :] += column_sum(d_normed * unit)
    grad_scales[3:4, :] += column_sum(d_normed)
    d_unit = d_unit + d_normed * gain_two
    sum_one = jnp.sum(d_unit, axis=-1, keepdims=True)
    sum_two = jnp.sum(d_unit * unit, axis=-1, keepdims=True)
    steps = jnp.max(jnp.abs(d_unit), axis=-1, keepdims=True) * (1.0 / 32767.0)
    lane = lax.broadcasted_iota(jnp.int32, (tokens, 128), 1)
    columns = jnp.where(lane == 0, sum_one, jnp.where(lane == 1, sum_two, jnp.where(lane == 2, steps, unit_scale)))
    stats[:, here] = columns.T[:8, :]
    codes = coded(d_unit, steps)
    for part in range(SG):
        parts[part, here, :] = codes[:, part * feats : (part + 1) * feats]


def layer_kernel(
    vocab, lines,
    residual, places, scales, table_own, table_after, table_before, weights, back,
    queries, keys, values, hidden, joined, picked_one, picked_two, d_branch, d_after,
    vectors, rows, facts, targets, head,
    rows_all, in_out, back_out, smalls_out, head_out, squares,
    parts, stats, base, unit, grad_in, grad_back, grad_scales, grad_bias,
    smalls, low, sum_in, sum_back, stats_all, steps_all, from_y, own_sum, from_z, pair_in, pair_back,
    send_in_codes, send_in_steps, send_back_codes, send_back_steps,
    far_in_codes, far_in_steps, far_back_codes, far_back_steps,
    in_codes, in_steps, back_codes, back_steps,
    small_rep, small_sum, small_shard,
    send_y, recv_y, send_z, recv_z, send_stat, recv_stat, send_pair, recv_pair, send_far, recv_far,
    send_rep, recv_rep, send_small, recv_small,
    send_row, recv_row, send_in, recv_in, send_back, recv_back, own,
):
    at = pl.program_id(0)
    last = pl.num_programs(0) - 1
    rep, shard, core_twin, x_twin, y_twin = whereabouts()
    core_far = lax.rem(core_twin + 2, RG)
    small_rows = 14
    tokens = residual.shape[0]
    shard_peers = [(rep, shard_peer(shard, step)) for step in range(1, SG)]
    rep_peers = [(lax.rem(rep + step, RG), shard) for step in range(1, RG)]

    def rep_copies():
        return [
            remote(smalls, small_rep.at[k], send_rep.at[k], recv_rep.at[k], peer) for k, peer in enumerate(rep_peers)
        ]

    def pair_copies(which, slot):
        pairs = ((grad_in, pair_in), (grad_back, pair_back))
        return [
            remote(
                source.at[:, which], target.at[slot], send_pair.at[2 * slot + k], recv_pair.at[2 * slot + k],
                (core_twin, shard),
            )
            for k, (source, target) in enumerate(pairs)
        ]

    def y_copy(line, step):
        here = pl.ds(pl.multiple_of(line * tokens, tokens), tokens)
        return remote(
            parts.at[z_peer(y_twin, step), here], from_y.at[step, here],
            send_y.at[line, step], recv_y.at[line, step], (rep, y_twin),
        )

    def z_copy(line, step):
        here = pl.ds(line * tokens, tokens)
        return remote(
            own_sum.at[step, here], from_z.at[step - 1, here],
            send_z.at[line, step - 1], recv_z.at[line, step - 1], (rep, z_peer(shard, step)),
        )

    def stat_copies(line):
        here = pl.ds(pl.multiple_of(line * tokens, tokens), tokens)
        return [
            remote(stats.at[:, here], stats_all.at[shard, :, here], send_stat.at[line, k], recv_stat.at[line, k], peer)
            for k, peer in enumerate(shard_peers)
        ]

    def far_copies():
        pairs = (
            (send_in_codes, far_in_codes), (send_in_steps, far_in_steps),
            (send_back_codes, far_back_codes), (send_back_steps, far_back_steps),
        )
        return [
            remote(source, target, send_far.at[k], recv_far.at[k], (x_twin, shard))
            for k, (source, target) in enumerate(pairs)
        ]

    def small_copies():
        return [
            remote(small_sum.at[peer[1]], small_shard.at[k], send_small.at[k], recv_small.at[k], peer)
            for k, peer in enumerate(shard_peers)
        ]

    def in_copies():
        return [
            remote(source.at[peer[1]], target.at[shard], send_in.at[which, k], recv_in.at[which, k], peer)
            for k, peer in enumerate(shard_peers)
            for which, (source, target) in enumerate(((send_in_codes, in_codes), (send_in_steps, in_steps)))
        ]

    back_pairs = ((send_back_codes, back_codes), (send_back_steps, back_steps))

    def back_move(slot, which):
        tile = shard if slot == 0 else SG + 4 * shard + slot - 1
        owner, place = tile // 5, lax.rem(tile, 5)
        source, target = back_pairs[which]
        there = remote(
            source.at[slot], target.at[place], send_back.at[which, slot], recv_back.at[which, place], (rep, owner)
        )
        return owner, place, there

    def row_copy(line, k, peer):
        here = pl.ds(line * tokens, tokens)
        return remote(low.at[here], rows_all.at[rep, here], send_row.at[line, k], recv_row.at[line, k], (peer, shard))

    def passed_copy(line):
        there = rows_all.at[x_twin, pl.ds(line * tokens, tokens)]
        return remote(there, there, send_row.at[line, 2], recv_row.at[line, 2], (core_twin, shard))

    def keep_rows(line):
        here = pl.ds(line * tokens, tokens)
        return pltpu.make_async_copy(low.at[here], rows_all.at[rep, here], own.at[line])

    def pass_rows(line):
        row_copy(line, 0, x_twin).wait_recv()
        passed_copy(line).start()

    def finish(line):
        here = pl.ds(line * tokens, tokens)
        total = pair_sum(line, 0)
        for step in (1, 2, 3):
            z_copy(line, step).wait()
            behind = 4 - step
            steps = steps_all[here, behind : behind + 1] + steps_all[here, 4 + behind : 5 + behind]
            total = total + decoded(from_z[step - 1, here, :], steps)
        mean, slope, scale = (steps_all[here, k : k + 1] for k in (8, 9, 10))
        d_rows = (total - mean / D - unit[here, :] * (slope / D)) * scale
        low[here, :] = (base[here, :] + d_rows).astype(low.dtype)
        row_copy(line, 0, x_twin).start()
        row_copy(line, 1, core_twin).start()
        keep_rows(line).start()
        if line > 0:
            pass_rows(line - 1)

    def decoded(codes, steps):
        return codes.astype(jnp.int32).astype(jnp.float32) * steps

    def encode(values, codes, steps):
        for k in range(values.shape[0]):
            row_steps = jnp.max(jnp.abs(values[k]), axis=-1, keepdims=True) * (1.0 / 32767.0)
            steps[k] = jnp.broadcast_to(row_steps, steps.shape[1:])
            codes[k] = coded(values[k], row_steps)

    def pair_sum(line, step):
        here = pl.ds(line * tokens, tokens)
        y_copy(line, step).wait_recv()
        own_codes = decoded(parts[z_peer(shard, step), here, :], steps_all[here, 0:1])
        return own_codes + decoded(from_y[step, here, :], steps_all[here, 4:5])

    def pass_on(line):
        here = pl.ds(line * tokens, tokens)
        for copy in stat_copies(line):
            copy.wait()
        near = [stats_all[z_peer(shard, k), 2:3, here] for k in range(4)]
        near += [stats_all[z_peer(y_twin, k), 2:3, here] for k in range(4)]
        sums = stats_all[0, :, here]
        for k in range(1, SG):
            sums = sums + stats_all[k, :, here]
        near += [sums[0:2, :], stats[3:4, here], jnp.zeros((5, tokens), jnp.float32)]
        steps_all[here, 0:16] = jnp.concatenate(near, axis=0).T
        for step in (2, 1, 3):
            own_sum[step, here, :] = coded(pair_sum(line, step), steps_all[here, 0:1] + steps_all[here, 4:5])
            z_copy(line, step).start()

    @pl.when(at == 0)
    def _():
        greet(shard_peers + rep_peers)
        for total in (grad_in, grad_back, grad_scales, grad_bias, squares, smalls):
            total[...] = jnp.zeros_like(total)

    for line, step_at in enumerate(PASS_STEPS):
        pl.when(at == step_at)(functools.partial(pass_on, line))

    @pl.when(at < lines)
    def _():
        backward_line(
            residual, places, scales, table_own, table_after, table_before, weights, back,
            queries, keys, values, hidden, joined, picked_one, picked_two, d_branch, d_after,
            parts, stats, base, unit, grad_in, grad_back, grad_scales, grad_bias, at,
        )
        for copy in stat_copies(at):
            copy.start()
        for step in (2, 1, 3, 0):
            y_copy(at, step).start()
        here = pl.ds(pl.multiple_of(at * tokens, tokens), tokens)
        stats_all[shard, :, here] = stats[:, here]

    @pl.when(at == lines - 1)
    def _():
        for copy in pair_copies(core_far, 1) + pair_copies(core_twin, 0):
            copy.start()

        def put(row, values):
            smalls[row // small_rows, pl.ds(lax.rem(row, small_rows), 1), :] = values

        for k in range(8):
            lanes = slice(k * 128, (k + 1) * 128)
            for vector in range(4):
                put(8 * vector + k, grad_scales[vector : vector + 1, lanes])
            put(8 * 4 + k, vectors[0:1, lanes])
            put(8 * 5 + k, vectors[1:2, lanes])
            put(8 * 13 + k, vectors[2:3, lanes])
        for k in range(7):
            row = 48 + 8 * k + shard if k < 3 else 72 + 4 * shard + k - 3
            put(row, grad_bias[0:1, k * 128 : (k + 1) * 128])
        for copy in rep_copies():
            copy.start()

    @pl.when(at == lines + 1)
    def _():
        for copy in pair_copies(core_far, 1):
            copy.wait()
        sum_in[...] = grad_in[:, x_twin] + pair_in[1]
        sum_back[...] = grad_back[:, x_twin] + pair_back[1]
        encode(sum_in, send_in_codes, send_in_steps)
        encode(sum_back, send_back_codes, send_back_steps)
        for copy in far_copies():
            copy.start()
        for copy in rep_copies():
            copy.wait()
        small_sum[...] = smalls[...] + small_rep[0] + small_rep[1] + small_rep[2]
        for copy in small_copies():
            copy.start()

    @pl.when(at == lines + 6)
    def _():
        for copy in pair_copies(core_twin, 0) + far_copies():
            copy.wait()
        sum_in[...] = grad_in[:, rep] + pair_in[0]
        sum_back[...] = grad_back[:, rep] + pair_back[0]
        for k in range(sum_in.shape[0]):
            sum_in[k] = sum_in[k] + decoded(far_in_codes[k], far_in_steps[k, :, 0:1])
        for k in range(sum_back.shape[0]):
            sum_back[k] = sum_back[k] + decoded(far_back_codes[k], far_back_steps[k, :, 0:1])
        encode(sum_in, send_in_codes, send_in_steps)
        encode(sum_back, send_back_codes, send_back_steps)
        for copy in in_copies():
            copy.start()
        in_codes[shard] = send_in_codes[shard]
        in_steps[shard] = send_in_steps[shard]
        for slot in range(5):
            for which, (source, target) in enumerate(back_pairs):
                owner, place, there = back_move(slot, which)
                here = pltpu.make_async_copy(source.at[slot], target.at[place], recv_back.at[which, place])
                pl.when(owner == shard)(here.start)
                pl.when(owner != shard)(there.start)

    for line, step_at in enumerate(FINISH_STEPS):
        pl.when(at == step_at)(functools.partial(finish, line))

    pl.when(at == last)(lambda: pass_rows(lines - 1))

    @pl.when(at >= lines)
    def _():
        block_at = at - lines

        def head_block(size):
            total = None
            for group in range(RG):
                base_row = block_at * VOCAB_BLOCK
                grads = logit_grads(
                    head[:size], rows[group], facts[group, 0:1, :], targets[group, 0:1, :] - base_row, transposed_dot
                )
                term = plain_dot(grads, rows[group])
                total = term if total is None else total + term
            head_out[:size] = total
            squares[0:1, :] += jnp.sum(total * total, axis=0, keepdims=True)

        full, tail = divmod(vocab, VOCAB_BLOCK)
        pl.when(block_at < full)(lambda: head_block(VOCAB_BLOCK))
        if tail > 0:
            pl.when(block_at == full)(lambda: head_block(tail))

    @pl.when(at == last)
    def _():
        for copy in small_copies():
            copy.wait()
        whole = small_sum[shard]
        for k in range(SG - 1):
            whole = whole + small_shard[k]
        smalls_out[...] = whole
        for copy in in_copies():
            copy.wait()
        for k in range(in_codes.shape[0]):
            in_out[k] = decoded(in_codes[k], in_steps[k, :, 0:1])
        for place in range(5):
            for which, (source, target) in enumerate(back_pairs):
                pltpu.make_async_copy(source.at[0], target.at[place], recv_back.at[which, place]).wait()
        for place in range(5):
            back_out[place] = decoded(back_codes[place], back_steps[place, :, 0:1])
        for slot in range(5):
            for which in range(2):
                owner, _, there = back_move(slot, which)
                pl.when(owner != shard)(there.wait_send)
        for line in range(lines):
            for step in range(4):
                y_copy(line, step).wait_send()
            keep_rows(line).wait()
            row_copy(line, 0, x_twin).wait_send()
            row_copy(line, 1, core_twin).wait()
            passed_copy(line).wait()


def layer_backward(residual, places, scales, tables, weights, back, kept, d_branch, d_after, vectors, rows, facts, targets, head, number):
    dma = pltpu.SemaphoreType.DMA
    f32, bf16, i16 = jnp.float32, jnp.bfloat16, jnp.int16
    lines = places.shape[0] // 8
    count, depth = residual.shape
    tokens, slots = count // lines, places.shape[1]
    feats = depth // SG
    vocab = head.shape[0]
    quarter = feats // RG
    piece = (16, 128)
    blocks = pl.cdiv(vocab, VOCAB_BLOCK)
    vmem = lambda *shape: pltpu.VMEM(shape, f32)
    short = lambda *shape: pltpu.VMEM(shape, i16)
    shape = lambda *dims: jax.ShapeDtypeStruct(dims, f32)

    def by_line(height, width):
        return pl.BlockSpec((height, width), lambda at: (jnp.minimum(at, lines - 1), 0))

    head_block = pl.BlockSpec((VOCAB_BLOCK, depth), lambda at: (jnp.clip(at - lines, 0, blocks - 1), 0))
    in_dims, back_dims = (SG, quarter, OWN_COLS), (5, 32, depth)
    in_step, back_step = (SG, quarter, 128), (5, 32, 128)
    coded_buffers = [short(*in_dims), vmem(*in_step), short(*back_dims), vmem(*back_step)]
    return comm_call(
        functools.partial(layer_kernel, vocab, lines),
        [
            jax.ShapeDtypeStruct((RG, count, feats), bf16),
            shape(*in_dims),
            shape(*back_dims),
            shape(*piece),
            shape(vocab, depth),
            shape(8, depth),
        ],
        [
            short(SG, count, feats),
            vmem(8, count),
            vmem(count, feats),
            vmem(count, feats),
            vmem(SG, RG, quarter, OWN_COLS),
            vmem(5, RG, 32, depth),
            vmem(8, depth),
            vmem(8, OWN_COLS),
            vmem(SG, *piece),
            pltpu.VMEM((count, feats), bf16),
            vmem(*in_dims),
            vmem(*back_dims),
            vmem(SG, 8, count),
            vmem(count, 128),
            short(4, count, feats),
            short(4, count, feats),
            short(3, count, feats),
            vmem(2, *in_dims),
            vmem(2, *back_dims),
        ]
        + coded_buffers * 3
        + [vmem(3, SG, *piece), vmem(SG, *piece), vmem(SG - 1, *piece)]
        + [dma((lines, 4))] * 2
        + [dma((lines, 3))] * 2
        + [dma((lines, SG - 1))] * 2
        + [dma((4,))] * 4
        + [dma((3,))] * 2
        + [dma((SG - 1,))] * 2
        + [dma((lines, 3))] * 2
        + [dma((2, SG - 1))] * 2
        + [dma((2, 5))] * 2
        + [dma((lines,))],
        number,
        (residual, places, scales, *tables, weights, back, *kept, d_branch, d_after, vectors, rows, facts, targets, head),
        [by_line(tokens, depth), by_line(8, slots)]
        + ["v"] * 6
        + [by_line(array.shape[0] // lines, array.shape[1]) for array in kept]
        + [by_line(slots, depth), by_line(slots, feats)]
        + ["v"] * 4
        + [head_block],
        ["a", "v", "v", "v", head_block, "v"],
        LAYER_LIMIT,
        (lines + blocks,),
    )


def norm_kernel(
    head_squares, embed_squares, smalls, grad_in, grad_back, out,
    value, from_rep, half, from_shard, send_rep, recv_rep, send_shard, recv_shard,
):
    rep, shard, _, _, _ = whereabouts()
    shard_peers = [(rep, shard_peer(shard, step)) for step in range(1, SG)]
    rep_peers = [(lax.rem(rep + step, RG), shard) for step in range(1, RG)]
    greet(shard_peers + rep_peers)

    def squares(rows):
        return jnp.sum(rows * rows, axis=0, keepdims=True)

    def lanes(row):
        return sum(row[:, k * 128 : (k + 1) * 128] for k in range(row.shape[1] // 128))

    repeated = jnp.sum(embed_squares[...], axis=0, keepdims=True) + squares(smalls[...])
    repeated = repeated + lanes(jnp.sum(head_squares[...], axis=0, keepdims=True))
    total = repeated * (1.0 / RG)
    for rows in (grad_in, grad_back):
        for k in range(rows.shape[0]):
            total = total + lanes(squares(rows[k]))
    value[...] = jnp.broadcast_to(jnp.sum(total, axis=1, keepdims=True), value.shape)
    copies = [
        remote(value, from_rep.at[rep], send_rep.at[k], recv_rep.at[k], peer) for k, peer in enumerate(rep_peers)
    ]
    for copy in copies:
        copy.start()
    from_rep[rep] = value[...]
    for copy in copies:
        copy.wait()
    half[...] = from_rep[0] + from_rep[1] + from_rep[2] + from_rep[3]
    copies = [
        remote(half, from_shard.at[shard], send_shard.at[k], recv_shard.at[k], peer)
        for k, peer in enumerate(shard_peers)
    ]
    for copy in copies:
        copy.start()
    from_shard[shard] = half[...]
    for copy in copies:
        copy.wait()
    total = from_shard[0]
    for k in range(1, SG):
        total = total + from_shard[k]
    norm = jnp.sqrt(total)
    row = lax.broadcasted_iota(jnp.int32, norm.shape, 0)
    out[...] = jnp.where(row == 0, norm, CLIP_LEVEL / jnp.maximum(norm, CLIP_LEVEL))


def global_norm(head_squares, embed_squares, smalls, grad_in, grad_back, number):
    dma = pltpu.SemaphoreType.DMA
    tile = (8, 128)
    vmem = lambda *shape: pltpu.VMEM(shape, jnp.float32)
    return comm_call(
        norm_kernel,
        [jax.ShapeDtypeStruct(tile, jnp.float32)],
        [vmem(*tile), vmem(RG, *tile), vmem(*tile), vmem(SG, *tile)] + [dma((RG - 1,))] * 2 + [dma((SG - 1,))] * 2,
        number,
        (head_squares, embed_squares, smalls, grad_in, grad_back),
        "vvvvv",
        "v",
        12 << 20,
    )[0]


GROUP_HEADS = H // SG
HEAD_COLS = GROUP_HEADS * HD
UNITS = FF // SG
OWN_COLS = 3 * HEAD_COLS + UNITS
VOCAB_BLOCK = 512
ROW_BLOCK = 1024
TABLE_BLOCK = 4096
CAST_BLOCK = 512
VMEM_LIMIT = 60 << 20
EMBED_LIMIT = 30 << 20
LAYER_LIMIT = 63 << 20
PASS_STEPS = (3, 5, 7, 9)
FINISH_STEPS = (8, 11, 13, 15)
LOG_TWO = 0.6931471805599453


def transposed_dot(left, right):
    return lax.dot_general(left, right, (((1,), (1,)), ((), ())), preferred_element_type=jnp.float32)


def first_dot(left, right):
    return lax.dot_general(left, right, (((0,), (0,)), ((), ())), preferred_element_type=jnp.float32)


def plain_dot(left, right):
    return jnp.dot(left, right, preferred_element_type=jnp.float32)


def logit_grads(low, rows, logsum, targets, dot):
    logits = dot(low, rows)
    hits = lax.broadcasted_iota(jnp.int32, logits.shape, 0) == targets
    weights = jnp.exp(logits - logsum)
    return jnp.where(hits, weights - 1.0, weights).astype(jnp.bfloat16)


def embed_grad_kernel(ids, rows, table, squares, wide):
    wide[...] = rows[...].astype(jnp.float32)
    squares[...] = jnp.zeros_like(squares)
    parts = table.shape[0] // 512

    def part_rows(part):
        return pl.ds(pl.multiple_of(part * 512, 512), 512)

    @pl.loop(0, parts)
    def _(part):
        table[part_rows(part), :] = jnp.zeros((512, table.shape[1]), jnp.float32)

    @pl.loop(0, rows.shape[0] // 8)
    def _(group):
        for lane in range(8):
            token = group * 8 + lane
            here = pl.ds(ids[token], 1)
            table[here, :] = table[here, :] + wide[pl.ds(token, 1), :]

    @pl.loop(0, parts)
    def _(part):
        block = table[part_rows(part), :]
        squares[...] += jnp.sum((block * block).reshape(64, 8, block.shape[1]), axis=0)


def embed_grads(ids, rows, vocab):
    count, feats = rows.shape
    height = pl.cdiv(vocab, TABLE_BLOCK) * TABLE_BLOCK
    return pl.pallas_call(
        embed_grad_kernel,
        in_specs=[pl.BlockSpec(memory_space=pltpu.SMEM), pl.BlockSpec(memory_space=pltpu.VMEM)],
        out_specs=[pl.BlockSpec(memory_space=pltpu.VMEM)] * 2,
        out_shape=[pltpu.VMEM((height, feats), jnp.float32), jax.ShapeDtypeStruct((8, feats), jnp.float32)],
        scratch_shapes=[pltpu.VMEM((count, feats), jnp.float32)],
        compiler_params=pltpu.CompilerParams(vmem_limit_bytes=EMBED_LIMIT),
    )(ids, rows)


def embed_update_kernel(norm, grads, weight, moment, square, next_weight, next_moment, next_square):
    width = weight.shape[1]
    here = pl.ds(pl.multiple_of(pl.program_id(0) * width, width), width)
    gradient = grads[here, :].T * norm[1:2, 0:1]
    next_weight[...], next_moment[...], next_square[...] = adamw(
        weight[...], gradient, moment[...], square[...], RATE_EMBED
    )


def update_embed(norm, grads, state):
    feats, vocab = state[0].shape
    block = pl.BlockSpec((feats, TABLE_BLOCK), lambda at: (0, at))
    return pl.pallas_call(
        embed_update_kernel,
        grid=(pl.cdiv(vocab, TABLE_BLOCK),),
        in_specs=[pl.BlockSpec(norm.shape, lambda at: (0, 0)), pl.BlockSpec(memory_space=pltpu.VMEM)] + [block] * 3,
        out_specs=[block] * 3,
        out_shape=[jax.ShapeDtypeStruct(state[0].shape, jnp.float32)] * 3,
        compiler_params=pltpu.CompilerParams(vmem_limit_bytes=EMBED_LIMIT),
    )(norm, pltpu.with_memory_space_constraint(grads, pltpu.VMEM), *state)


def update_kernel(
    norm, grads_in, grads_back, *refs
):
    factor = norm[1:2, 0:1]
    ins, backs = refs[0:3], refs[3:6]
    out_ins, out_backs = refs[6:9], refs[9:12]

    def update(here, gradient, sources, targets, rate):
        results = adamw(sources[0][here], gradient * factor, sources[1][here], sources[2][here], rate)
        for target, result in zip(targets, results):
            target[here] = result

    for source in range(SG):
        for part in range(3):
            first = part * D + source * HEAD_COLS
            gradient = grads_in[0, source, :, part * HEAD_COLS : (part + 1) * HEAD_COLS]
            update((slice(None), slice(first, first + HEAD_COLS)), gradient, ins, out_ins, RATE_IN)
        first = 3 * D + source * UNITS
        gradient = grads_in[0, source, :, 3 * HEAD_COLS :]
        update((slice(None), slice(first, first + UNITS)), gradient, ins, out_ins, RATE_IN)
    for tile in range(5):
        update((tile, 0), grads_back[0, tile], backs, out_backs, RATE_BACK)


def update_layer(norm, grads_in, grads_back, state_in, state_back):
    quarters, sources, rows, columns = grads_in.shape
    _, tiles, back_rows, depth = grads_back.shape
    wide = state_in[0].shape
    tall = state_back[0].shape
    back_shape = (tiles, quarters, back_rows, depth)
    in_block = pl.BlockSpec((rows, wide[1]), lambda at: (at, 0))
    back_block = pl.BlockSpec((tiles, 1, back_rows, depth), lambda at: (0, at, 0, 0))
    f32 = jnp.float32
    results = pl.pallas_call(
        update_kernel,
        grid=(quarters,),
        in_specs=[
            pl.BlockSpec(norm.shape, lambda at: (0, 0)),
            pl.BlockSpec((1, sources, rows, columns), lambda at: (at, 0, 0, 0)),
            pl.BlockSpec((1, tiles, back_rows, depth), lambda at: (at, 0, 0, 0)),
        ]
        + [in_block] * 3
        + [back_block] * 3,
        out_specs=[in_block] * 3 + [back_block] * 3,
        out_shape=[jax.ShapeDtypeStruct(wide, f32)] * 3 + [jax.ShapeDtypeStruct(back_shape, f32)] * 3,
        compiler_params=pltpu.CompilerParams(vmem_limit_bytes=VMEM_LIMIT),
    )(norm, grads_in, grads_back, *state_in, *[array.reshape(back_shape) for array in state_back])
    return (*results[:3], *[array.reshape(tall) for array in results[3:]])


def turn_tables(length):
    half_rot = ROT // 2
    lane = np.arange(HEAD_COLS) % HD
    exponent = (lane % half_rot).astype(np.float32) * np.float32(2.0 / ROT)
    speeds = np.exp(-exponent * np.log(np.float32(10000.0))).astype(np.float32)
    angles = np.arange(length, dtype=np.float32)[:, None] * speeds[None, :]
    cosine, sine = np.cos(angles), np.sin(angles)
    lane = lane[None, :]
    tables = (
        np.where(lane < ROT, cosine, 1.0),
        np.where(lane < half_rot, -sine, 0.0),
        np.where((lane >= half_rot) & (lane < ROT), sine, 0.0),
    )
    return tuple(jnp.asarray(table.astype(np.float32)) for table in tables)


def centred_rows(values):
    centred = values - jnp.mean(values, axis=-1, keepdims=True)
    spread = jnp.mean(centred * centred, axis=-1, keepdims=True)
    scale = lax.rsqrt(spread + NORM_EPS)
    return centred * scale, scale


def exact_dot(left, right, dims):
    return lax.dot_general(
        left, right, (dims, ((), ())), precision=lax.Precision.HIGHEST, preferred_element_type=jnp.float32
    )


def pick_matrix(places, tokens):
    token = lax.broadcasted_iota(jnp.int32, (tokens, places.shape[1]), 0)
    return (places == token).astype(jnp.float32)


def turn(rows, tables, sign):
    half_rot = ROT // 2
    own, after, before = tables
    width = rows.shape[1]
    return (
        rows * own
        + sign * (pltpu.roll(rows, width - half_rot, 1) * after)
        + sign * (pltpu.roll(rows, half_rot, 1) * before)
    )


def head_lanes(rows, head):
    lane = lax.broadcasted_iota(jnp.int32, rows.shape, 1)
    return jnp.where(lane // HD == head, rows, jnp.zeros_like(rows))


def head_probs(queries, keys, allowed, head):
    scores = transposed_dot(keys, head_lanes(queries, head)) * HD ** (-0.5)
    scores = jnp.where(allowed, scores, -1e30)
    exponent = jnp.exp(scores - jnp.max(scores, axis=0, keepdims=True))
    return exponent / jnp.sum(exponent, axis=0, keepdims=True)


def line_allowed(places, span, tokens):
    keys = lax.broadcasted_iota(jnp.int32, (tokens, places.shape[1]), 0)
    in_query = (places >= span) & (places < span + PIC)
    in_key = (keys >= span) & (keys < span + PIC)
    return (keys <= places) | (in_query & in_key)


def forward_kernel(
    residual, places, scales, bias, own, after, before, weights, back,
    queries, keys, values, hidden, joined, picked_one, picked_two, picked_rows, used, branch,
):
    bf16 = jnp.bfloat16
    tokens = residual.shape[0]
    span = places[1:2, :]
    gain_one, shift_one = scales[0:1, :], scales[1:2, :]
    gain_two, shift_two = scales[2:3, :], scales[3:4, :]
    unit, _ = centred_rows(residual[...].astype(jnp.float32))
    low_one = (unit * gain_one + shift_one).astype(bf16)
    slots = places[0:1, :]
    pick = pick_matrix(slots, tokens)
    rows = first_dot(pick.astype(bf16), residual[...])
    picked_rows[...] = rows.astype(bf16)
    used[...] = first_dot(pick.astype(bf16), jnp.ones((tokens, used.shape[1]), bf16))
    unit, _ = centred_rows(rows)
    low_picked = (unit * gain_one + shift_one).astype(bf16)
    picked_one[...] = low_picked
    low_two = (unit * gain_two + shift_two).astype(bf16)
    picked_two[...] = low_two
    tables = (own[...], after[...], before[...])
    picked_tables = tuple(exact_dot(pick, table, ((0,), (0,))) for table in tables)
    two, three = 2 * HEAD_COLS, 3 * HEAD_COLS
    query = plain_dot(low_picked, weights[:, :HEAD_COLS]) + bias[:, :HEAD_COLS]
    query = turn(query, picked_tables, 1.0).astype(bf16)
    queries[...] = query
    key = plain_dot(low_one, weights[:, HEAD_COLS:two]) + bias[:, HEAD_COLS:two]
    key = turn(key, tables, 1.0).astype(bf16)
    keys[...] = key
    value = (plain_dot(low_one, weights[:, two:three]) + bias[:, two:three]).astype(bf16)
    values[...] = value
    allowed = line_allowed(slots, span, tokens)
    attended = None
    for head in range(GROUP_HEADS):
        probs = head_probs(query, key, allowed, head).astype(bf16)
        term = head_lanes(first_dot(probs, value), head)
        attended = term if attended is None else attended + term
    joined[:, :HEAD_COLS] = attended.astype(bf16)
    pre = plain_dot(low_two, weights[:, three:]) + bias[:, three:]
    hidden[...] = pre
    joined[:, HEAD_COLS:] = (0.5 * pre * (1.0 + lax.erf(pre * 0.5**0.5))).astype(bf16)
    branch[...] = plain_dot(joined[...], back[...])


def line_block(height, width):
    return pl.BlockSpec((height, width), lambda line: (line, 0))


def still(array):
    return pl.BlockSpec(array.shape, lambda line: (0,) * array.ndim)


def layer_forward(residual, places, scales, bias, tables, weights, back):
    lines = places.shape[0] // 8
    tokens, slots = residual.shape[0] // lines, places.shape[1]
    depth = residual.shape[1]
    bf16, f32 = jnp.bfloat16, jnp.float32
    outs = [
        (slots, HEAD_COLS, bf16),
        (tokens, HEAD_COLS, bf16),
        (tokens, HEAD_COLS, bf16),
        (slots, UNITS, f32),
        (slots, HEAD_COLS + UNITS, bf16),
        (slots, depth, bf16),
        (slots, depth, bf16),
        (slots, depth, bf16),
        (slots, 128, f32),
        (slots, depth, f32),
    ]
    return pl.pallas_call(
        forward_kernel,
        grid=(lines,),
        in_specs=[
            line_block(tokens, depth),
            line_block(8, slots),
            still(scales),
            still(bias),
            *[still(table) for table in tables],
            still(weights),
            still(back),
        ],
        out_specs=[line_block(height, width) for height, width, _ in outs],
        out_shape=[jax.ShapeDtypeStruct((lines * height, width), kind) for height, width, kind in outs],
        compiler_params=pltpu.CompilerParams(vmem_limit_bytes=VMEM_LIMIT),
    )(residual, places, scales, bias, *tables, weights, back)


def group_plan(
    token_ids,
    pic_start,
    comp_pos,
    comp_tgt,
    proj_in,
    proj_back,
    small_params,
    head_table,
    embed_table,
    first_in,
    second_in,
    first_back,
    second_back,
    first_small,
    second_small,
    first_head,
    second_head,
    first_embed,
    second_embed,
):
    micro, _, seq_dev = token_ids.shape
    slots = comp_pos.shape[2]
    seq_len = seq_dev * RG
    lines = micro * SG // RG
    blocks = lines * RG
    own_blocks = blocks // SG
    tokens = lines * seq_len
    slot_count = blocks * slots
    own_slots = own_blocks * slots
    vocab_dev = head_table.shape[1]
    vocab = embed_table.shape[1]
    quarter = D // SG // RG

    small_rows = small_params.shape[0] // 128
    ints_all, places, marks, scales, own_bias, residual_low, in_all, back_all, head_low = share_entry(
        token_ids,
        comp_pos,
        comp_tgt,
        pic_start,
        small_params.reshape(small_rows, 128),
        proj_in,
        proj_back,
        embed_table,
        head_table.T,
        tokens,
        1,
    )
    own_in = in_all.reshape(D, OWN_COLS)
    own_back = back_all.reshape(5 * 128, D)

    tables = turn_tables(seq_len)
    *kept, picked_rows, used, branch_parts = layer_forward(
        residual_low, places, scales, own_bias, tables, own_in, own_back
    )
    rows_all, facts_all, d_branch, after_pieces, vectors, loss_tile = loss_and_branch(
        branch_parts.reshape(SG, own_slots, D),
        picked_rows,
        scales,
        used,
        marks,
        head_low,
        3,
    )
    d_after_feats = after_pieces.reshape(slot_count, D // SG)

    d_rows_all, in_own, back_own, small_sum, grad_head, head_squares = layer_backward(
        residual_low,
        places,
        scales,
        tables,
        own_in,
        own_back,
        kept,
        d_branch,
        d_after_feats,
        vectors,
        rows_all,
        facts_all,
        marks,
        head_low,
        8,
    )
    in_grads = lax.all_gather(in_own, "rep")
    back_grads = lax.all_gather(back_own, "rep")
    by_group = ints_all.reshape(RG, RG, SG // RG, 8, seq_dev)[:, :, :, :micro]
    ids_all = jnp.transpose(by_group, (1, 3, 2, 0, 4)).reshape(-1)
    grad_embed, embed_squares = embed_grads(ids_all, d_rows_all.reshape(RG * tokens, D // SG), vocab)

    norm_rows_out = global_norm(head_squares, embed_squares, small_sum, in_own, back_own, 10)
    factor = norm_rows_out[1, 0]
    next_in, moment_in, square_in, next_back, moment_back, square_back = update_layer(
        norm_rows_out, in_grads, back_grads, (proj_in, first_in, second_in), (proj_back, first_back, second_back)
    )
    grad_small = small_sum[:small_rows].reshape(-1)
    next_small, moment_small, square_small = adamw(
        small_params, grad_small * factor, first_small, second_small, RATE_SMALL
    )
    next_head, moment_head, square_head = adamw(
        head_table, grad_head.T * factor, first_head, second_head, RATE_HEAD
    )
    next_embed, moment_embed, square_embed = update_embed(
        norm_rows_out, grad_embed, (embed_table, first_embed, second_embed)
    )
    return (
        loss_tile[0, :2],
        norm_rows_out[0, :1],
        next_in,
        moment_in,
        square_in,
        next_back,
        moment_back,
        square_back,
        next_small,
        moment_small,
        square_small,
        next_head,
        moment_head,
        square_head,
        next_embed,
        moment_embed,
        square_embed,
    )


def select_plan(mesh):
    if mesh.shape["rep"] == RG and mesh.shape["shard"] == SG:
        return group_plan
    return any_mesh


def solution(mesh):
    placed = (
        P(None, "shard", "rep"),
        P(None, "shard"),
        P(None, "shard", "rep"),
        P(None, "shard", "rep"),
        P("shard", None),
        P("shard", None),
        P("shard"),
        P(None, "shard"),
        P("shard", None),
        P("shard", None),
        P("shard", None),
        P("shard", None),
        P("shard", None),
        P("shard"),
        P("shard"),
        P(None, "shard"),
        P(None, "shard"),
        P("shard", None),
        P("shard", None),
    )
    return jax.shard_map(
        select_plan(mesh),
        mesh=mesh,
        in_specs=placed,
        out_specs=(
            P(),
            P(),
            P("shard", None),
            P("shard", None),
            P("shard", None),
            P("shard", None),
            P("shard", None),
            P("shard", None),
            P("shard"),
            P("shard"),
            P("shard"),
            P(None, "shard"),
            P(None, "shard"),
            P(None, "shard"),
            P("shard", None),
            P("shard", None),
            P("shard", None),
        ),
        check_vma=False,
    )
```
